32 devices in a mesh: set: 1, kb: 32 (over z, y, x, core).
Axes of the slice: x: 2, y: 2, z: 4, core: 2. Of those that a mesh axis runs over, the one named last changes fastest.
Arguments:
- green_momentum_grid: float32 [2, 4, 4096, 512], P('set', None, 'kb'), may hold values from -6 to 6
- pair_table: int32 [8, 2], replicated, may hold values from 0 to 3, as said below
- mirror_map: int32 [3, 16], P('set'), may hold values from 0 to 15, as said below
Outputs:
- chi_out: float32 [2, 8, 4096, 512], P('set', None, 'kb')
The draws below stay inside these ranges and needn't reach their ends.
Inputs may be any that keep to these rules, and one draw needn't show every extreme that they name: `pair_table`: each of the two columns names every entry number 0 to 3 at least once. Each row d is a reflection: mirror_map[d,x] = (c_d - x) mod 16 for a centre c_d of that row.
All inputs are finite; a program needn't handle non-finite values.
Results may differ from the reference program's by a relative error of at most 0.0003.
Values sent between devices are 32-bit elements; how exact they have to be, the bound alone decides.
No kernel may reach another device: no remote copies, remote signals or barrier semaphores. Data moves between devices by JAX's collectives and lax.ppermute only.
A program may use at most 128 MiB of HBM per device.

```python
import math
import jax
import jax.numpy as jnp
from jax import lax

SIDE = 16
KPTS = 4096
NFREQ = 512
NENT = 4
NCHI = 8


def draw_pair_table(key, part):
    column_one = jax.random.permutation(jax.random.fold_in(key, 11), jnp.arange(NCHI, dtype=jnp.int32) % NENT)
    column_two = jax.random.permutation(jax.random.fold_in(key, 12), jnp.arange(NCHI, dtype=jnp.int32) % NENT)
    return jnp.stack([column_one, column_two], axis=1).astype(jnp.int32)


def draw_mirror_map(key, part):
    centres = jax.random.randint(jax.random.fold_in(key, 21), (3,), 0, SIDE, dtype=jnp.int32)
    coords = jnp.arange(SIDE, dtype=jnp.int32)
    return ((centres[:, None] - coords[None, :]) % SIDE).astype(jnp.int32)


def steps_of(stream_key, shape, pieces, least, high):
    gain = 1.0
    for dim, shards_of in pieces:
        steps = jax.random.uniform(jax.random.fold_in(jax.random.fold_in(stream_key, 6), dim), (shards_of,), jnp.float32, least / len(pieces), high / len(pieces))
        gain = gain * jnp.repeat(jnp.exp(steps), shape[dim] // shards_of).reshape((-1,) + (1,) * (len(shape) - 1 - dim))
    return gain


def gaussian(rng, shape, width, limit, cuts=(), kind=jnp.bfloat16):
    result = jax.random.normal(rng, shape, jnp.float32) * width
    if len(cuts) > 0:
        result = steps_of(rng, shape, cuts, -0.22, 0.18) * result
    return jnp.clip(result, min=-limit, max=limit).astype(kind)


def setup_inputs(seed: int = 0, part: int = 0) -> dict:
    key_of = jax.random.split(jax.random.key(seed), 4)
    own_keys = jax.random.split(jax.random.fold_in(key_of[3], part), 4)
    green_momentum_grid = gaussian(own_keys[0], (2, NENT, KPTS, NFREQ), 1.0, 6.0, ((2, 32),), jnp.float32)
    pair_table = draw_pair_table(jax.random.fold_in(key_of[3], 71), part)
    mirror_map = draw_mirror_map(jax.random.fold_in(jax.random.fold_in(key_of[3], part), 71), part)
    return {"green_momentum_grid": green_momentum_grid, "pair_table": pair_table, "mirror_map": mirror_map}


def trig_pair(angle_int, period, scale):
    angle = (2.0 * math.pi / period) * angle_int.astype(jnp.float32)
    return scale * jnp.cos(angle), scale * jnp.sin(angle)


def complex_combine(formula, cosine, sine, real_part, imag_part):
    first_term = jnp.einsum(formula, cosine, real_part + imag_part, precision=lax.Precision.HIGHEST)
    second_term = jnp.einsum(formula, cosine + sine, imag_part, precision=lax.Precision.HIGHEST)
    third_term = jnp.einsum(formula, sine - cosine, real_part, precision=lax.Precision.HIGHEST)
    return first_term - second_term, first_term + third_term


def forward_imaginary_time(tau_rows, frequency_count):
    freq_index = jnp.arange(frequency_count, dtype=jnp.int32)
    angle_int = ((2 * freq_index[None, :] - frequency_count + 1) * (2 * tau_rows[:, None] + 1)) % (4 * frequency_count)
    cosine, sine = trig_pair(angle_int, 4 * frequency_count, frequency_count ** -0.5)
    return cosine, -sine


def tau_backward(tau_rows, frequency_count):
    freq_index = jnp.arange(frequency_count, dtype=jnp.int32)
    angle_int = ((freq_index[:, None] - frequency_count // 2) * (2 * tau_rows[None, :] + 1)) % (2 * frequency_count)
    return trig_pair(angle_int, 2 * frequency_count, frequency_count ** -0.5)


def grid_transform(real_part, imag_part, grid_side, direction):
    shape = real_part.shape
    plane = jnp.arange(grid_side * grid_side, dtype=jnp.int32)
    upper = plane // grid_side
    lower = plane % grid_side
    plane_int = (upper[:, None] * upper[None, :] + lower[:, None] * lower[None, :]) % grid_side
    plane_cos, plane_sin = trig_pair(plane_int, grid_side, 1.0 / grid_side)
    line = jnp.arange(grid_side, dtype=jnp.int32)
    line_cos, line_sin = trig_pair((line[:, None] * line[None, :]) % grid_side, grid_side, grid_side ** -0.5)
    real_part = real_part.reshape(shape[:-1] + (grid_side, grid_side * grid_side))
    imag_part = imag_part.reshape(shape[:-1] + (grid_side, grid_side * grid_side))
    real_part, imag_part = complex_combine('pq,...xq->...xp', plane_cos, direction * plane_sin, real_part, imag_part)
    real_part, imag_part = complex_combine('ax,...xp->...ap', line_cos, direction * line_sin, real_part, imag_part)
    return real_part.reshape(shape), imag_part.reshape(shape)


def mirror_index(mirror_map, grid_side):
    index_x = mirror_map[0][:, None, None]
    index_y = mirror_map[1][None, :, None]
    index_z = mirror_map[2][None, None, :]
    return (index_x * grid_side * grid_side + index_y * grid_side + index_z).reshape(-1).astype(jnp.int32)


def bubble(gr_re, gr_im, mirror_re, mirror_im, pair_table, entries):
    entry_ids = jnp.arange(entries, dtype=jnp.int32)
    pick_left = (pair_table[:, 0][:, None] == entry_ids[None, :]).astype(jnp.float32)
    pick_right = (pair_table[:, 1][:, None] == entry_ids[None, :]).astype(jnp.float32)
    left_re = jnp.einsum('me,e...->m...', pick_left, gr_re, precision=lax.Precision.HIGHEST)
    left_im = jnp.einsum('me,e...->m...', pick_left, gr_im, precision=lax.Precision.HIGHEST)
    right_re = jnp.einsum('me,e...->m...', pick_right, mirror_re, precision=lax.Precision.HIGHEST)
    right_im = jnp.einsum('me,e...->m...', pick_right, mirror_im, precision=lax.Precision.HIGHEST)
    return left_re * right_re - left_im * right_im, left_re * right_im + left_im * right_re


def reference(green_momentum_grid, pair_table, mirror_map):
    tau_rows = jnp.arange(NFREQ, dtype=jnp.int32)
    fwd_cos, fwd_sin = forward_imaginary_time(tau_rows, NFREQ)
    tau_re, tau_im = complex_combine('qa,fsa->fqs', fwd_cos, fwd_sin, green_momentum_grid[0], green_momentum_grid[1])
    mirror_flat = mirror_index(mirror_map, SIDE)

    def one_time(time_index):
        other_index = (NFREQ - 1 - time_index).astype(jnp.int32)
        here_re = lax.dynamic_index_in_dim(tau_re, time_index, 1, keepdims=False)
        here_im = lax.dynamic_index_in_dim(tau_im, time_index, 1, keepdims=False)
        there_re = lax.dynamic_index_in_dim(tau_re, other_index, 1, keepdims=False)
        there_im = lax.dynamic_index_in_dim(tau_im, other_index, 1, keepdims=False)
        here_re, here_im = grid_transform(here_re, here_im, SIDE, 1.0)
        there_re, there_im = grid_transform(there_re, there_im, SIDE, 1.0)
        there_re = jnp.take(there_re, mirror_flat, axis=1)
        there_im = jnp.take(there_im, mirror_flat, axis=1)
        chi_re, chi_im = bubble(here_re, here_im, there_re, there_im, pair_table, NENT)
        chi_re, chi_im = grid_transform(chi_re, chi_im, SIDE, -1.0)
        return jnp.stack([chi_re, chi_im])

    momenta = lax.map(one_time, jnp.arange(NFREQ, dtype=jnp.int32))
    momenta = jnp.transpose(momenta, (1, 2, 0, 3))
    back_cos, back_sin = tau_backward(tau_rows, NFREQ)
    out_re, out_im = complex_combine('vj,ejk->ekv', back_cos, back_sin, momenta[0], momenta[1])
    return jnp.stack([out_re, out_im])
```

```python
import functools

import jax
import jax.numpy as jnp
import ml_dtypes
import numpy as np
from jax import lax
from jax.experimental import pallas as pl
from jax.experimental.pallas import tpu as pltpu
from jax.sharding import PartitionSpec as P

LANES = 128
ROWS = 8
GROUPS = 1


def split_constant(matrix):
    high = matrix.astype(np.float32).astype(ml_dtypes.bfloat16)
    low = (matrix - high.astype(np.float64)).astype(np.float32).astype(ml_dtypes.bfloat16)
    return high, low


def split_value(value):
    high = value.astype(jnp.bfloat16)
    low = (value - high.astype(jnp.float32)).astype(jnp.bfloat16)
    return high, low


def dot3(left, right, dims):
    def one(a, b):
        return lax.dot_general(a, b, (dims, ((), ())), preferred_element_type=jnp.float32)

    return one(left[0], right[0]) + (one(left[0], right[1]) + one(left[1], right[0]))


def time_rows(devices, pairs, padded):
    rows = np.full((devices, padded), -1, np.int64)
    rows[:, :pairs] = np.arange(devices * pairs).reshape(devices, pairs)
    return rows.reshape(-1)


def fermion_matrix(rows, count):
    n = np.arange(count, dtype=np.int64)
    angle = ((2 * n[None, :] - count + 1) * (2 * rows[:, None] + 1)) % (4 * count)
    angle = np.pi * angle / (2 * count)
    used = (rows >= 0)[:, None] * count**-0.5
    return np.concatenate([np.cos(angle) * used, np.sin(angle) * used], axis=0)


def boson_matrix(rows, count):
    v = np.arange(count, dtype=np.int64)
    angle = ((v[None, :] - count // 2) * (2 * rows[:, None] + 1)) % (2 * count)
    angle = np.pi * angle / count
    used = (rows >= 0)[:, None] * count**-0.5
    return np.concatenate([np.cos(angle) * used, np.sin(angle) * used], axis=0)


def plane_parts(side):
    p = np.arange(side * side, dtype=np.int64)
    angle = ((p[:, None] // side) * (p[None, :] // side) + (p[:, None] % side) * (p[None, :] % side)) % side
    angle = 2 * np.pi * angle / side
    scale = side**-1.5
    return np.cos(angle) * scale, np.sin(angle) * scale


def plane_matrix(side):
    cosine, sine = plane_parts(side)
    return np.block([[cosine, sine], [-sine, cosine]])


def times_w4(re, im, power, sign):
    power = (power * sign) % 4
    if power == 0:
        return re, im
    if power == 1:
        return -im, re
    if power == 2:
        return -re, -im
    return im, -re


def dft4(values, sign):
    (r0, i0), (r1, i1), (r2, i2), (r3, i3) = values
    sr, si, dr, di = r0 + r2, i0 + i2, r0 - r2, i0 - i2
    tr, ti, er, ei = r1 + r3, i1 + i3, r1 - r3, i1 - i3
    if sign > 0:
        return [(sr + tr, si + ti), (dr - ei, di + er), (sr - tr, si - ti), (dr + ei, di - er)]
    return [(sr + tr, si + ti), (dr + ei, di - er), (sr - tr, si - ti), (dr - ei, di + er)]


def twiddle(value, power, sign, side):
    re, im = value
    if power % (side // 4) == 0:
        return times_w4(re, im, power // (side // 4), sign)
    angle = 2.0 * np.pi * power / side
    c, s = float(np.cos(angle)), float(sign * np.sin(angle))
    return re * c - im * s, re * s + im * c


def dft_line(values, sign):
    side = len(values)
    if side == 1:
        return values
    if side == 2:
        (r0, i0), (r1, i1) = values
        return [(r0 + r1, i0 + i1), (r0 - r1, i0 - i1)]
    if side == 4:
        return dft4(values, sign)
    inner = side // 4
    parts = [dft_line(values[b::4], sign) for b in range(4)]
    out = [None] * side
    for k1 in range(inner):
        column = [twiddle(parts[b][k1], b * k1, sign, side) for b in range(4)]
        for k2, value in enumerate(dft4(column, sign)):
            out[k1 + inner * k2] = value
    return out


def times_kernel(g_ref, mh_ref, ml_ref, out_ref):
    lanes = g_ref.shape[2]
    groups, _, _, _, rows, _ = out_ref.shape
    half = groups * rows
    g = jnp.concatenate([g_ref[0, 0], g_ref[1, 0]], axis=0)
    d = dot3((mh_ref[...], ml_ref[...]), split_value(g), ((1,), (1,)))
    c_re, c_im = d[:half, :lanes], d[:half, lanes:]
    s_re, s_im = d[half:, :lanes], d[half:, lanes:]
    for where, value in (
        ((0, 0), c_re + s_im),
        ((0, 1), c_im - s_re),
        ((1, 0), s_im - c_re),
        ((1, 1), -(c_im + s_re)),
    ):
        out_ref[:, where[0], where[1], 0] = value.reshape(groups, rows, lanes)


def to_times(green, devices, padded, matrix):
    _, entries, lanes, count = green.shape
    return pl.pallas_call(
        times_kernel,
        grid=(entries,),
        in_specs=[
            pl.BlockSpec((2, 1, lanes, count), lambda e: (0, e, 0, 0)),
            pl.BlockSpec(matrix[0].shape, lambda e: (0, 0)),
            pl.BlockSpec(matrix[1].shape, lambda e: (0, 0)),
        ],
        out_specs=pl.BlockSpec((devices, 2, 2, 1, padded, lanes), lambda e: (0, 0, 0, e, 0, 0)),
        out_shape=jax.ShapeDtypeStruct((devices, 2, 2, entries, padded, lanes), jnp.float32),
        compiler_params=pltpu.CompilerParams(vmem_limit_bytes=32 << 20),
        name="to_times",
    )(green, *matrix)


def mirror_kernel(index_ref, ch_ref, cl_ref, sh_ref, sl_ref, fh_ref, fl_ref, bh_ref, bl_ref):
    plane = ch_ref.shape[0]
    row = lax.broadcasted_iota(jnp.int32, (plane, plane), 0)
    pick = (row == index_ref[...]).astype(jnp.float32).astype(jnp.bfloat16)

    def dot(a, b):
        return jnp.dot(a, b, preferred_element_type=jnp.float32)

    for c_ref, s_ref, f_ref, b_ref in ((ch_ref, sh_ref, fh_ref, bh_ref), (cl_ref, sl_ref, fl_ref, bl_ref)):
        cosine, sine = dot(c_ref[...], pick), dot(s_ref[...], pick)
        f_ref[:plane, :plane] = cosine.astype(jnp.bfloat16)
        f_ref[plane:, plane:] = cosine.astype(jnp.bfloat16)
        f_ref[:plane, plane:] = sine.astype(jnp.bfloat16)
        f_ref[plane:, :plane] = (-sine).astype(jnp.bfloat16)
        cosine, sine = dot(pick, c_ref[...]), dot(pick, s_ref[...])
        b_ref[:plane, :plane] = cosine.astype(jnp.bfloat16)
        b_ref[plane:, plane:] = cosine.astype(jnp.bfloat16)
        b_ref[:plane, plane:] = (-sine).astype(jnp.bfloat16)
        b_ref[plane:, :plane] = sine.astype(jnp.bfloat16)


def mirror_matrices(mirror_map, side):
    plane = side * side
    index = (mirror_map[1][:, None] * side + mirror_map[2][None, :]).reshape(1, plane)
    cosine, sine = plane_parts(side)
    parts = split_constant(cosine) + split_constant(sine)
    square = jax.ShapeDtypeStruct((2 * plane, 2 * plane), jnp.bfloat16)
    return pl.pallas_call(
        mirror_kernel,
        out_shape=[square] * 4,
        compiler_params=pltpu.CompilerParams(vmem_limit_bytes=32 << 20),
        name="mirror_matrices",
    )(index, *[jnp.asarray(part) for part in parts])


def space_kernel(x_ref, ph_ref, pl_ref, mh_ref, ml_ref, out_ref, mid):
    side, _, halves, _, entries, rows, lanes = x_ref.shape
    plane = 2 * lanes
    for half in range(halves):
        pieces = [
            x_ref[:, h, half, ri].reshape(side * entries * rows, lanes) for ri in range(2) for h in range(2)
        ]
        matrix = (ph_ref[...], pl_ref[...]) if half == 0 else (mh_ref[...], ml_ref[...])
        d = dot3(split_value(jnp.concatenate(pieces, axis=1)), matrix, ((1,), (0,)))
        for ri in range(2):
            mid[half, :, ri] = d[:, ri * plane : (ri + 1) * plane].reshape(side, entries, rows, plane)
    for half in range(halves):

        @pl.loop(0, entries)
        def _(e):
            for block in range(2):
                cut = pl.ds(block * lanes, lanes)
                values = [(mid[half, x, 0, e, :, cut], mid[half, x, 1, e, :, cut]) for x in range(side)]
                for x, (re, im) in enumerate(dft_line(values, 1)):
                    out_ref[half, x, 0, e, :, cut] = re
                    out_ref[half, x, 1, e, :, cut] = im


def to_space(x, plain, mirrored):
    side, _, halves, _, entries, rows, lanes = x.shape
    shape = (halves, side, 2, entries, rows, 2 * lanes)
    return pl.pallas_call(
        space_kernel,
        out_shape=jax.ShapeDtypeStruct(shape, jnp.float32),
        scratch_shapes=[pltpu.VMEM(shape, jnp.float32)],
        compiler_params=pltpu.CompilerParams(vmem_limit_bytes=40 << 20),
        name="to_space",
    )(x, *plain, *mirrored)


def bubble_kernel(first, table_ref, mirror_ref, g_ref, ph_ref, pl_ref, mh_ref, ml_ref, out_ref, mid):
    halves, side, _, _, rows, plane = g_ref.shape
    members = out_ref.shape[4]
    lanes = plane // 2

    @pl.loop(0, members)
    def _(c):
        left, right = table_ref[first + c, 0], table_ref[first + c, 1]
        for half in range(halves):
            for block in range(2):
                cut = pl.ds(block * lanes, lanes)
                values = []
                for x in range(side):
                    other = mirror_ref[0, x]
                    a_re = g_ref[half, x, 0, left, :, cut]
                    a_im = g_ref[half, x, 1, left, :, cut]
                    b_re = g_ref[1 - half, other, 0, right, :, cut]
                    b_im = g_ref[1 - half, other, 1, right, :, cut]
                    values.append((a_re * b_re - a_im * b_im, a_re * b_im + a_im * b_re))
                for x, (re, im) in enumerate(dft_line(values, -1)):
                    mid[half, x, c, 0, :, cut] = re
                    mid[half, x, c, 1, :, cut] = im

    for half in range(halves):
        matrix = (ph_ref[...], pl_ref[...]) if half == 0 else (mh_ref[...], ml_ref[...])
        count = side * members * rows
        value = jnp.concatenate([mid[half, :, :, ri].reshape(count, plane) for ri in range(2)], axis=1)
        d = dot3(split_value(value), matrix, ((1,), (0,)))
        for ri in range(2):
            for h in range(2):
                start = ri * plane + h * lanes
                out_ref[:, h, half, ri] = d[:, start : start + lanes].reshape(side, members, rows, lanes)


def bubbles(first, members, table, mirror_map, space, plain, mirrored):
    halves, side, _, _, rows, plane = space.shape
    smem = pl.BlockSpec(memory_space=pltpu.SMEM)
    vmem = pl.BlockSpec(memory_space=pltpu.VMEM)
    return pl.pallas_call(
        functools.partial(bubble_kernel, first),
        in_specs=[smem, smem] + [vmem] * 5,
        out_shape=jax.ShapeDtypeStruct((side, 2, halves, 2, members, rows, plane // 2), jnp.float32),
        scratch_shapes=[pltpu.VMEM((halves, side, members, 2, rows, plane), jnp.float32)],
        compiler_params=pltpu.CompilerParams(vmem_limit_bytes=48 << 20),
        name="bubbles",
    )(table, mirror_map, space, *plain, *mirrored)


def frequency_kernel(y_ref, mh_ref, ml_ref, *refs):
    out_ref = refs[-1]
    devices, _, _, _, rows, lanes = y_ref.shape
    count = devices * rows

    def part(half, ri):
        return y_ref[:, half, ri, 0].reshape(count, lanes)

    sums = [part(0, ri) + part(1, ri) for ri in range(2)]
    differences = [part(0, ri) - part(1, ri) for ri in range(2)]
    upper = jnp.concatenate([sums[0], -differences[1]], axis=0)
    lower = jnp.concatenate([sums[1], differences[0]], axis=0)
    value = jnp.concatenate([upper.T, lower.T], axis=0)
    d = dot3(split_value(value), (mh_ref[...], ml_ref[...]), ((1,), (0,)))
    out_ref[0, 0] = d[:lanes]
    out_ref[1, 0] = d[lanes:]


def to_frequencies(y, matrix, first, total, earlier):
    devices, _, _, members, rows, lanes = y.shape
    count = matrix[0].shape[1]
    whole = pl.BlockSpec(matrix[0].shape, lambda c: (0, 0))
    args = (y,) + tuple(matrix)
    specs = [pl.BlockSpec((devices, 2, 2, 1, rows, lanes), lambda c: (0, 0, 0, c, 0, 0)), whole, whole]
    aliases = {}
    if earlier is not None:
        args += (earlier,)
        specs.append(pl.BlockSpec(memory_space=pl.ANY))
        aliases = {3: 0}
    return pl.pallas_call(
        frequency_kernel,
        grid=(members,),
        in_specs=specs,
        out_specs=pl.BlockSpec((2, 1, lanes, count), lambda c: (0, first + c, 0, 0)),
        out_shape=jax.ShapeDtypeStruct((2, total, lanes, count), jnp.float32),
        input_output_aliases=aliases,
        compiler_params=pltpu.CompilerParams(vmem_limit_bytes=32 << 20),
        name="to_frequencies",
    )(*args)


def exchange(x):
    shape = x.shape
    flat = x.reshape(shape[0], -1, shape[-1])
    return lax.all_to_all(flat, "kb", split_axis=0, concat_axis=0, tiled=True).reshape(shape)


def local(green, pair_table, mirror_map):
    side = mirror_map.shape[1]
    plane = side * side
    lanes, count = green.shape[2], green.shape[3]
    devices = side * plane // lanes
    pairs = count // (2 * devices)
    padded = -(-pairs // ROWS) * ROWS
    strips = plane // 2 // lanes
    components = pair_table.shape[0]
    rows = time_rows(devices, pairs, padded)
    forward = [jnp.asarray(part) for part in split_constant(fermion_matrix(rows, count))]
    backward = [jnp.asarray(part) for part in split_constant(boson_matrix(rows, count))]
    flat = plane_matrix(side)
    plain = [jnp.asarray(part) for part in split_constant(flat)]
    plain_back = [jnp.asarray(part) for part in split_constant(flat.T)]

    def arrived(x):
        x = exchange(x[..., :pairs, :])
        x = jnp.pad(x, ((0, 0),) * 4 + ((0, padded - pairs), (0, 0)))
        x = x.reshape((side, 2, strips) + x.shape[1:])
        x = jnp.moveaxis(x, 2, -2)
        return x.reshape(x.shape[:-2] + (strips * lanes,))

    def returned(x):
        x = x[..., :pairs, :]
        x = x.reshape(x.shape[:-1] + (strips, lanes))
        x = jnp.moveaxis(x, -2, 2)
        x = exchange(x.reshape((devices,) + x.shape[3:]))
        return jnp.pad(x, ((0, 0),) * 4 + ((0, padded - pairs), (0, 0)))

    mirrored = mirror_matrices(mirror_map, side)
    space = to_space(arrived(to_times(green, devices, padded, forward)), plain, mirrored[:2])
    members = components // GROUPS
    out = None
    for group in range(GROUPS):
        first = group * members
        chi = bubbles(first, members, pair_table, mirror_map, space, plain_back, mirrored[2:])
        out = to_frequencies(returned(chi), backward, first, components, out)
    return out


def solution(mesh):
    placed = (P("set", None, "kb", None), P(), P("set", None))
    return jax.shard_map(
        local, mesh=mesh, in_specs=placed, out_specs=P("set", None, "kb", None), check_vma=False
    )
```

```python
import jax
import jax.numpy as jnp
import ml_dtypes
import numpy as np
from jax import lax
from jax.experimental import pallas as pl
from jax.experimental.pallas import tpu as pltpu
from jax.sharding import PartitionSpec as P

LANES = 128
ROWS = 8
GROUPS = 2


def split_constant(matrix):
    high = matrix.astype(np.float32).astype(ml_dtypes.bfloat16)
    low = (matrix - high.astype(np.float64)).astype(np.float32).astype(ml_dtypes.bfloat16)
    return high, low


def split_value(value):
    high = value.astype(jnp.bfloat16)
    low = (value - high.astype(jnp.float32)).astype(jnp.bfloat16)
    return high, low


def dot3(left, right, dims):
    def one(a, b):
        return lax.dot_general(a, b, (dims, ((), ())), preferred_element_type=jnp.float32)

    return one(left[0], right[0]) + (one(left[0], right[1]) + one(left[1], right[0]))


def time_rows(devices, pairs, padded):
    rows = np.full((devices, padded), -1, np.int64)
    rows[:, :pairs] = np.arange(devices * pairs).reshape(devices, pairs)
    return rows.reshape(-1)


def fermion_matrix(rows, count):
    n = np.arange(count, dtype=np.int64)
    angle = ((2 * n[None, :] - count + 1) * (2 * rows[:, None] + 1)) % (4 * count)
    angle = np.pi * angle / (2 * count)
    used = (rows >= 0)[:, None] * count**-0.5
    return np.concatenate([np.cos(angle) * used, np.sin(angle) * used], axis=0)


def boson_matrix(rows, count):
    v = np.arange(count, dtype=np.int64)
    angle = ((v[None, :] - count // 2) * (2 * rows[:, None] + 1)) % (2 * count)
    angle = np.pi * angle / count
    used = (rows >= 0)[:, None] * count**-0.5
    return np.concatenate([np.cos(angle) * used, np.sin(angle) * used], axis=0)


def plane_parts(side):
    p = np.arange(side * side, dtype=np.int64)
    angle = ((p[:, None] // side) * (p[None, :] // side) + (p[:, None] % side) * (p[None, :] % side)) % side
    angle = 2 * np.pi * angle / side
    scale = side**-1.5
    return np.cos(angle) * scale, np.sin(angle) * scale


def times_w4(re, im, power, sign):
    power = (power * sign) % 4
    if power == 0:
        return re, im
    if power == 1:
        return -im, re
    if power == 2:
        return -re, -im
    return im, -re


def dft4(values, sign):
    (r0, i0), (r1, i1), (r2, i2), (r3, i3) = values
    sr, si, dr, di = r0 + r2, i0 + i2, r0 - r2, i0 - i2
    tr, ti, er, ei = r1 + r3, i1 + i3, r1 - r3, i1 - i3
    if sign > 0:
        return [(sr + tr, si + ti), (dr - ei, di + er), (sr - tr, si - ti), (dr + ei, di - er)]
    return [(sr + tr, si + ti), (dr + ei, di - er), (sr - tr, si - ti), (dr - ei, di + er)]


def twiddle(value, power, sign, side):
    re, im = value
    if power % (side // 4) == 0:
        return times_w4(re, im, power // (side // 4), sign)
    angle = 2.0 * np.pi * power / side
    c, s = float(np.cos(angle)), float(sign * np.sin(angle))
    return re * c - im * s, re * s + im * c


def dft_line(values, sign):
    side = len(values)
    if side == 1:
        return values
    if side == 2:
        (r0, i0), (r1, i1) = values
        return [(r0 + r1, i0 + i1), (r0 - r1, i0 - i1)]
    if side == 4:
        return dft4(values, sign)
    inner = side // 4
    parts = [dft_line(values[b::4], sign) for b in range(4)]
    out = [None] * side
    for k1 in range(inner):
        column = [twiddle(parts[b][k1], b * k1, sign, side) for b in range(4)]
        for k2, value in enumerate(dft4(column, sign)):
            out[k1 + inner * k2] = value
    return out


def times_kernel(g_ref, mh_ref, ml_ref, out_ref):
    lanes = g_ref.shape[2]
    groups, _, _, _, rows, _ = out_ref.shape
    half = groups * rows
    g = jnp.concatenate([g_ref[0, 0], g_ref[1, 0]], axis=0)
    d = dot3((mh_ref[...], ml_ref[...]), split_value(g), ((1,), (1,)))
    c_re, c_im = d[:half, :lanes], d[:half, lanes:]
    s_re, s_im = d[half:, :lanes], d[half:, lanes:]
    for where, value in (
        ((0, 0), c_re + s_im),
        ((0, 1), c_im - s_re),
        ((1, 0), s_im - c_re),
        ((1, 1), -(c_im + s_re)),
    ):
        out_ref[:, where[0], where[1], 0] = value.reshape(groups, rows, lanes)


def to_times(green, devices, padded, matrix):
    _, entries, lanes, count = green.shape
    return pl.pallas_call(
        times_kernel,
        grid=(entries,),
        in_specs=[
            pl.BlockSpec((2, 1, lanes, count), lambda e: (0, e, 0, 0)),
            pl.BlockSpec(matrix[0].shape, lambda e: (0, 0)),
            pl.BlockSpec(matrix[1].shape, lambda e: (0, 0)),
        ],
        out_specs=pl.BlockSpec((devices, 2, 2, 1, padded, lanes), lambda e: (0, 0, 0, e, 0, 0)),
        out_shape=jax.ShapeDtypeStruct((devices, 2, 2, entries, padded, lanes), jnp.float32),
        compiler_params=pltpu.CompilerParams(vmem_limit_bytes=60 << 20),
        name="to_times",
    )(green, *matrix)


def fill_block(ref, cosine, sine):
    plane = cosine.shape[0]
    ref[:plane, :plane] = cosine.astype(jnp.bfloat16)
    ref[plane:, plane:] = cosine.astype(jnp.bfloat16)
    ref[:plane, plane:] = sine.astype(jnp.bfloat16)
    ref[plane:, :plane] = (-sine).astype(jnp.bfloat16)


def middle_kernel(
    table_ref, mirror_ref, index_ref, x_ref, ch_ref, cl_ref, sh_ref, sl_ref, out_ref,
    forward, backward, mid, space, chi, stage, sems,
):
    side, _, halves, _, entries, rows, lanes = x_ref.shape
    plane = 2 * lanes
    units, _, _, _, members, _, _ = stage.shape
    row = lax.broadcasted_iota(jnp.int32, (plane, plane), 0)
    pick = (row == index_ref[...]).astype(jnp.float32).astype(jnp.bfloat16)

    def dot(a, b):
        return jnp.dot(a, b, preferred_element_type=jnp.float32)

    for part, (c_ref, s_ref) in enumerate(((ch_ref, sh_ref), (cl_ref, sl_ref))):
        cosine, sine = c_ref[...].astype(jnp.float32), s_ref[...].astype(jnp.float32)
        fill_block(forward.at[0, part], cosine, sine)
        fill_block(backward.at[0, part], cosine, -sine)
        fill_block(forward.at[1, part], dot(c_ref[...], pick), dot(s_ref[...], pick))
        fill_block(backward.at[1, part], dot(pick, c_ref[...]), -dot(pick, s_ref[...]))

    for half in range(halves):
        pieces = [
            x_ref[:, h, half, ri].reshape(side * entries * rows, lanes) for ri in range(2) for h in range(2)
        ]
        value = split_value(jnp.concatenate(pieces, axis=1))
        d = dot3(value, (forward[half, 0], forward[half, 1]), ((1,), (0,)))
        for ri in range(2):
            mid[half, :, ri] = d[:, ri * plane : (ri + 1) * plane].reshape(side, entries, rows, plane)
    for half in range(halves):
        for e in range(entries):
            for block in range(2):
                cut = slice(block * lanes, (block + 1) * lanes)
                values = [(mid[half, x, 0, e, :, cut], mid[half, x, 1, e, :, cut]) for x in range(side)]
                for x, (re, im) in enumerate(dft_line(values, 1)):
                    space[half, x, 0, e, :, cut] = re
                    space[half, x, 1, e, :, cut] = im

    copies = []
    for unit in range(units):
        half, first = unit % halves, unit // halves * members
        for c in range(members):
            left, right = table_ref[first + c, 0], table_ref[first + c, 1]
            for block in range(2):
                cut = slice(block * lanes, (block + 1) * lanes)
                values = []
                for x in range(side):
                    other = mirror_ref[0, x]
                    a_re = space[half, x, 0, left, :, cut]
                    a_im = space[half, x, 1, left, :, cut]
                    b_re = space[1 - half, other, 0, right, :, cut]
                    b_im = space[1 - half, other, 1, right, :, cut]
                    values.append((a_re * b_re - a_im * b_im, a_re * b_im + a_im * b_re))
                for x, (re, im) in enumerate(dft_line(values, -1)):
                    chi[unit, 0, x, c, :, cut] = re
                    chi[unit, 1, x, c, :, cut] = im
        count = side * members * rows
        value = jnp.concatenate([chi[unit, ri].reshape(count, plane) for ri in range(2)], axis=1)
        d = dot3(split_value(value), (backward[half, 0], backward[half, 1]), ((1,), (0,)))
        for ri in range(2):
            for h in range(2):
                start = ri * plane + h * lanes
                stage[unit, :, h, ri] = d[:, start : start + lanes].reshape(side, members, rows, lanes)
        target = out_ref.at[:, :, half, :, pl.ds(first, members)]
        copies.append(pltpu.make_async_copy(stage.at[unit], target, sems.at[unit]))
        copies[-1].start()
    for copy in copies:
        copy.wait()


def middle(x, table, mirror_map):
    side, _, halves, _, entries, rows, lanes = x.shape
    plane = 2 * lanes
    components = table.shape[0]
    members = components // GROUPS
    units = halves * GROUPS
    index = (mirror_map[1][:, None] * side + mirror_map[2][None, :]).reshape(1, plane)
    cosine, sine = plane_parts(side)
    parts = [jnp.asarray(part) for part in split_constant(cosine) + split_constant(sine)]
    smem = pl.BlockSpec(memory_space=pltpu.SMEM)
    vmem = pl.BlockSpec(memory_space=pltpu.VMEM)
    matrices = pltpu.VMEM((halves, 2, 2 * plane, 2 * plane), jnp.bfloat16)
    spatial = pltpu.VMEM((halves, side, 2, entries, rows, plane), jnp.float32)
    return pl.pallas_call(
        middle_kernel,
        in_specs=[smem, smem] + [vmem] * 6,
        out_specs=pl.BlockSpec(memory_space=pltpu.HBM),
        out_shape=jax.ShapeDtypeStruct((side, 2, halves, 2, components, rows, lanes), jnp.float32),
        scratch_shapes=[
            matrices,
            matrices,
            spatial,
            spatial,
            pltpu.VMEM((units, 2, side, members, rows, plane), jnp.float32),
            pltpu.VMEM((units, side, 2, 2, members, rows, lanes), jnp.float32),
            pltpu.SemaphoreType.DMA((units,)),
        ],
        compiler_params=pltpu.CompilerParams(vmem_limit_bytes=48 << 20),
        name="middle",
    )(table, mirror_map, index, x, *parts)


def frequency_kernel(y_ref, mh_ref, ml_ref, out_ref, stage, sems):
    devices, _, _, components, rows, lanes = y_ref.shape
    count = devices * rows
    groups = sems.shape[0]
    members = components // groups
    matrix = (mh_ref[...], ml_ref[...])
    copies = []
    for group in range(groups):
        pieces = []
        for c in range(group * members, (group + 1) * members):
            part = [[y_ref[:, half, ri, c].reshape(count, lanes) for ri in range(2)] for half in range(2)]
            sums = [part[0][ri] + part[1][ri] for ri in range(2)]
            differences = [part[0][ri] - part[1][ri] for ri in range(2)]
            pieces.append(jnp.concatenate([sums[0], -differences[1]], axis=0).T)
            pieces.append(jnp.concatenate([sums[1], differences[0]], axis=0).T)
        d = dot3(split_value(jnp.concatenate(pieces, axis=0)), matrix, ((1,), (0,)))
        d = d.reshape(members, 2, lanes, d.shape[1])
        for ri in range(2):
            stage[ri, group * members : (group + 1) * members] = d[:, ri]
        cut = pl.ds(group * members, members)
        copies.append(pltpu.make_async_copy(stage.at[:, cut], out_ref.at[:, cut], sems.at[group]))
        copies[-1].start()
    for copy in copies:
        copy.wait()


def to_frequencies(y, matrix):
    components, lanes = y.shape[3], y.shape[5]
    shape = (2, components, lanes, matrix[0].shape[1])
    vmem = pl.BlockSpec(memory_space=pltpu.VMEM)
    return pl.pallas_call(
        frequency_kernel,
        in_specs=[vmem] * 3,
        out_specs=pl.BlockSpec(memory_space=pltpu.HBM),
        out_shape=jax.ShapeDtypeStruct(shape, jnp.float32),
        scratch_shapes=[pltpu.VMEM(shape, jnp.float32), pltpu.SemaphoreType.DMA((components // 2,))],
        compiler_params=pltpu.CompilerParams(vmem_limit_bytes=40 << 20),
        name="to_frequencies",
    )(y, *matrix)


def exchange(x):
    shape = x.shape
    flat = x.reshape(shape[0], -1, shape[-1])
    return lax.all_to_all(flat, "kb", split_axis=0, concat_axis=0, tiled=True).reshape(shape)


def local(green, pair_table, mirror_map):
    side = mirror_map.shape[1]
    plane = side * side
    lanes, count = green.shape[2], green.shape[3]
    devices = side * plane // lanes
    pairs = count // (2 * devices)
    padded = -(-pairs // ROWS) * ROWS
    strips = plane // 2 // lanes
    rows = time_rows(devices, pairs, padded)
    forward = [jnp.asarray(part) for part in split_constant(fermion_matrix(rows, count))]
    backward = [jnp.asarray(part) for part in split_constant(boson_matrix(rows, count))]

    def arrived(x):
        x = exchange(x[..., :pairs, :])
        x = jnp.pad(x, ((0, 0),) * 4 + ((0, padded - pairs), (0, 0)))
        x = x.reshape((side, 2, strips) + x.shape[1:])
        x = jnp.moveaxis(x, 2, -2)
        return x.reshape(x.shape[:-2] + (strips * lanes,))

    def returned(x):
        x = x[..., :pairs, :]
        x = x.reshape(x.shape[:-1] + (strips, lanes))
        x = jnp.moveaxis(x, -2, 2)
        x = exchange(x.reshape((devices,) + x.shape[3:]))
        return jnp.pad(x, ((0, 0),) * 4 + ((0, padded - pairs), (0, 0)))

    chi = middle(arrived(to_times(green, devices, padded, forward)), pair_table, mirror_map)
    return to_frequencies(returned(chi), backward)


def solution(mesh):
    placed = (P("set", None, "kb", None), P(), P("set", None))
    return jax.shard_map(
        local, mesh=mesh, in_specs=placed, out_specs=P("set", None, "kb", None), check_vma=False
    )
```

```python
import jax
import jax.numpy as jnp
import ml_dtypes
import numpy as np
from jax import lax
from jax.experimental import pallas as pl
from jax.experimental.pallas import tpu as pltpu
from jax.sharding import PartitionSpec as P

LANES = 128
ROWS = 8
GROUPS = 2


def split_constant(matrix):
    high = matrix.astype(np.float32).astype(ml_dtypes.bfloat16)
    low = (matrix - high.astype(np.float64)).astype(np.float32).astype(ml_dtypes.bfloat16)
    return high, low


def split_value(value):
    high = value.astype(jnp.bfloat16)
    low = (value - high.astype(jnp.float32)).astype(jnp.bfloat16)
    return high, low


def dot3(left, right, dims):
    (k_left,), (k_right,) = dims
    a = jnp.concatenate([left[0], left[0], left[1]], axis=k_left)
    b = jnp.concatenate([right[0], right[1], right[0]], axis=k_right)
    return lax.dot_general(a, b, (dims, ((), ())), preferred_element_type=jnp.float32)


def time_rows(devices, pairs, padded):
    rows = np.full((devices, padded), -1, np.int64)
    rows[:, :pairs] = np.arange(devices * pairs).reshape(devices, pairs)
    return rows.reshape(-1)


def fermion_matrix(rows, count):
    n = np.arange(count, dtype=np.int64)
    angle = ((2 * n[None, :] - count + 1) * (2 * rows[:, None] + 1)) % (4 * count)
    angle = np.pi * angle / (2 * count)
    used = (rows >= 0)[:, None] * count**-0.5
    return np.concatenate([np.cos(angle) * used, np.sin(angle) * used], axis=0)


def boson_matrix(rows, count):
    v = np.arange(count, dtype=np.int64)
    angle = ((v[None, :] - count // 2) * (2 * rows[:, None] + 1)) % (2 * count)
    angle = np.pi * angle / count
    used = (rows >= 0)[:, None] * count**-0.5
    return np.concatenate([np.cos(angle) * used, np.sin(angle) * used], axis=0)


def plane_parts(side):
    p = np.arange(side * side, dtype=np.int64)
    angle = ((p[:, None] // side) * (p[None, :] // side) + (p[:, None] % side) * (p[None, :] % side)) % side
    angle = 2 * np.pi * angle / side
    scale = side**-1.5
    return np.cos(angle) * scale, np.sin(angle) * scale


def times_w4(re, im, power, sign):
    power = (power * sign) % 4
    if power == 0:
        return re, im
    if power == 1:
        return -im, re
    if power == 2:
        return -re, -im
    return im, -re


def dft4(values, sign):
    (r0, i0), (r1, i1), (r2, i2), (r3, i3) = values
    sr, si, dr, di = r0 + r2, i0 + i2, r0 - r2, i0 - i2
    tr, ti, er, ei = r1 + r3, i1 + i3, r1 - r3, i1 - i3
    if sign > 0:
        return [(sr + tr, si + ti), (dr - ei, di + er), (sr - tr, si - ti), (dr + ei, di - er)]
    return [(sr + tr, si + ti), (dr + ei, di - er), (sr - tr, si - ti), (dr - ei, di + er)]


def twiddle(value, power, sign, side):
    re, im = value
    if power % (side // 4) == 0:
        return times_w4(re, im, power // (side // 4), sign)
    angle = 2.0 * np.pi * power / side
    c, s = float(np.cos(angle)), float(sign * np.sin(angle))
    return re * c - im * s, re * s + im * c


def dft_line(values, sign):
    side = len(values)
    if side == 1:
        return values
    if side == 2:
        (r0, i0), (r1, i1) = values
        return [(r0 + r1, i0 + i1), (r0 - r1, i0 - i1)]
    if side == 4:
        return dft4(values, sign)
    inner = side // 4
    parts = [dft_line(values[b::4], sign) for b in range(4)]
    out = [None] * side
    for k1 in range(inner):
        column = [twiddle(parts[b][k1], b * k1, sign, side) for b in range(4)]
        for k2, value in enumerate(dft4(column, sign)):
            out[k1 + inner * k2] = value
    return out


def times_kernel(g_hbm, mh_hbm, ml_hbm, out_ref, g_ref, mh_ref, ml_ref, stage, in_sems, m_sems, out_sems):
    entries, lanes = g_ref.shape[1:3]
    groups, _, _, _, rows, _ = stage.shape
    half = groups * rows
    loads = [
        pltpu.make_async_copy(mh_hbm, mh_ref, m_sems.at[0]),
        pltpu.make_async_copy(ml_hbm, ml_ref, m_sems.at[1]),
    ]
    pieces = [
        pltpu.make_async_copy(g_hbm.at[:, pl.ds(e, 1)], g_ref.at[:, pl.ds(e, 1)], in_sems.at[e])
        for e in range(entries)
    ]
    for copy in [pieces[0]] + loads + pieces[1:]:
        copy.start()
    for copy in loads:
        copy.wait()
    matrix = (mh_ref[...], ml_ref[...])
    copies = []
    for e in range(entries):
        pieces[e].wait()
        g = jnp.concatenate([g_ref[0, e], g_ref[1, e]], axis=0)
        d = dot3(matrix, split_value(g), ((1,), (1,)))
        c_re, c_im = d[:half, :lanes], d[:half, lanes:]
        s_re, s_im = d[half:, :lanes], d[half:, lanes:]
        for where, value in (
            ((0, 0), c_re + s_im),
            ((0, 1), c_im - s_re),
            ((1, 0), s_im - c_re),
            ((1, 1), -(c_im + s_re)),
        ):
            stage[:, where[0], where[1], e] = value.reshape(groups, rows, lanes)
        cut = pl.ds(e, 1)
        copies.append(pltpu.make_async_copy(stage.at[:, :, :, cut], out_ref.at[:, :, :, cut], out_sems.at[e]))
        copies[-1].start()
    for copy in copies:
        copy.wait()


def to_times(green, devices, padded, matrix):
    _, entries, lanes, count = green.shape
    shape = (devices, 2, 2, entries, padded, lanes)
    hbm = pl.BlockSpec(memory_space=pltpu.HBM)
    return pl.pallas_call(
        times_kernel,
        in_specs=[hbm] * 3,
        out_specs=hbm,
        out_shape=jax.ShapeDtypeStruct(shape, jnp.float32),
        scratch_shapes=[
            pltpu.VMEM(green.shape, jnp.float32),
            pltpu.VMEM(matrix[0].shape, jnp.bfloat16),
            pltpu.VMEM(matrix[1].shape, jnp.bfloat16),
            pltpu.VMEM(shape, jnp.float32),
            pltpu.SemaphoreType.DMA((entries,)),
            pltpu.SemaphoreType.DMA((2,)),
            pltpu.SemaphoreType.DMA((entries,)),
        ],
        compiler_params=pltpu.CompilerParams(vmem_limit_bytes=32 << 20),
        name="to_times",
    )(green, *matrix)


def fill_block(ref, cosine, sine):
    plane = cosine.shape[0]
    lanes = plane // 2
    for block in range(2):
        cut = slice(block * lanes, (block + 1) * lanes)
        re = slice(2 * block * lanes, (2 * block + 1) * lanes)
        im = slice((2 * block + 1) * lanes, (2 * block + 2) * lanes)
        ref[:plane, re] = cosine[:, cut].astype(jnp.bfloat16)
        ref[plane:, im] = cosine[:, cut].astype(jnp.bfloat16)
        ref[:plane, im] = sine[:, cut].astype(jnp.bfloat16)
        ref[plane:, re] = (-sine[:, cut]).astype(jnp.bfloat16)


def middle_kernel(
    table_ref, mirror_ref, index_ref, x_ref, ch_ref, cl_ref, sh_ref, sl_ref, out_ref,
    forward, backward, mid, space, chi, stage, sems,
):
    side, _, halves, _, entries, rows, lanes = x_ref.shape
    plane = 2 * lanes
    units, _, _, _, members, _, _ = stage.shape
    row = lax.broadcasted_iota(jnp.int32, (plane, plane), 0)
    pick = (row == index_ref[...]).astype(jnp.float32).astype(jnp.bfloat16)

    def dot(a, b):
        return jnp.dot(a, b, preferred_element_type=jnp.float32)

    for part, (c_ref, s_ref) in enumerate(((ch_ref, sh_ref), (cl_ref, sl_ref))):
        cosine, sine = c_ref[...].astype(jnp.float32), s_ref[...].astype(jnp.float32)
        fill_block(forward.at[0, part], cosine, sine)
        fill_block(backward.at[0, part], cosine, -sine)
        fill_block(forward.at[1, part], dot(c_ref[...], pick), dot(s_ref[...], pick))
        fill_block(backward.at[1, part], dot(pick, c_ref[...]), -dot(pick, s_ref[...]))

    def plane_dot(value, matrix, half, block):
        cut = slice(2 * block * lanes, 2 * (block + 1) * lanes)
        return dot3(value, (matrix[half, 0, :, cut], matrix[half, 1, :, cut]), ((1,), (0,)))

    def arrive(half):
        pieces = [
            x_ref[:, h, half, ri].reshape(side * entries * rows, lanes) for ri in range(2) for h in range(2)
        ]
        return split_value(jnp.concatenate(pieces, axis=1))

    def to_plane(value, half, block):
        d = plane_dot(value, forward, half, block)
        for ri in range(2):
            piece = d[:, ri * lanes : (ri + 1) * lanes]
            mid[half, block, ri] = piece.reshape(side, entries, rows, lanes)

    def along_line(half, block, e):
        values = [(mid[half, block, 0, x, e], mid[half, block, 1, x, e]) for x in range(side)]
        for x, (re, im) in enumerate(dft_line(values, 1)):
            space[half, block, x, 0, e] = re
            space[half, block, x, 1, e] = im

    def product(unit, block, c):
        half, first = unit % halves, unit // halves * members
        left, right = table_ref[first + c, 0], table_ref[first + c, 1]
        values = []
        for x in range(side):
            other = mirror_ref[0, x]
            a_re, a_im = space[half, block, x, 0, left], space[half, block, x, 1, left]
            b_re, b_im = space[1 - half, block, other, 0, right], space[1 - half, block, other, 1, right]
            values.append((a_re * b_re - a_im * b_im, a_re * b_im + a_im * b_re))
        cut = slice(block * lanes, (block + 1) * lanes)
        for x, (re, im) in enumerate(dft_line(values, -1)):
            chi[unit, 0, x, c, :, cut] = re
            chi[unit, 1, x, c, :, cut] = im

    def from_plane(unit, value, h):
        d = plane_dot(value, backward, unit % halves, h)
        for ri in range(2):
            piece = d[:, ri * lanes : (ri + 1) * lanes]
            stage[unit, :, h, ri] = piece.reshape(side, members, rows, lanes)

    def collect(unit):
        count = side * members * rows
        return split_value(jnp.concatenate([chi[unit, ri].reshape(count, plane) for ri in range(2)], axis=1))

    copies = []

    def send(unit):
        target = out_ref.at[:, :, unit % halves, :, pl.ds(unit // halves * members, members)]
        copies.append(pltpu.make_async_copy(stage.at[unit], target, sems.at[unit]))
        copies[-1].start()

    order = [(half, block) for half in range(halves) for block in range(2)]
    for step in range(len(order) + 1):
        if step < len(order):
            half, block = order[step]
            if block == 0:
                value = arrive(half)
            to_plane(value, half, block)
        if step > 0:
            for e in range(entries):
                along_line(*order[step - 1], e)

    for unit in range(units + 1):
        tasks = [(block, c) for block in range(2) for c in range(members)] if unit < units else []
        if unit > 0:
            value = collect(unit - 1)
        for h in range(2):
            if unit > 0:
                from_plane(unit - 1, value, h)
            for block, c in tasks[h * members : (h + 1) * members]:
                product(unit, block, c)
        if unit > 0:
            send(unit - 1)
    for copy in copies:
        copy.wait()


def middle(x, table, mirror_map):
    side, _, halves, _, entries, rows, lanes = x.shape
    plane = 2 * lanes
    components = table.shape[0]
    members = components // GROUPS
    units = halves * GROUPS
    index = (mirror_map[1][:, None] * side + mirror_map[2][None, :]).reshape(1, plane)
    cosine, sine = plane_parts(side)
    parts = [jnp.asarray(part) for part in split_constant(cosine) + split_constant(sine)]
    smem = pl.BlockSpec(memory_space=pltpu.SMEM)
    vmem = pl.BlockSpec(memory_space=pltpu.VMEM)
    matrices = pltpu.VMEM((halves, 2, 2 * plane, 2 * plane), jnp.bfloat16)
    return pl.pallas_call(
        middle_kernel,
        in_specs=[smem, smem] + [vmem] * 6,
        out_specs=pl.BlockSpec(memory_space=pltpu.HBM),
        out_shape=jax.ShapeDtypeStruct((side, 2, halves, 2, components, rows, lanes), jnp.float32),
        scratch_shapes=[
            matrices,
            matrices,
            pltpu.VMEM((halves, 2, 2, side, entries, rows, lanes), jnp.float32),
            pltpu.VMEM((halves, 2, side, 2, entries, rows, lanes), jnp.float32),
            pltpu.VMEM((units, 2, side, members, rows, plane), jnp.float32),
            pltpu.VMEM((units, side, 2, 2, members, rows, lanes), jnp.float32),
            pltpu.SemaphoreType.DMA((units,)),
        ],
        compiler_params=pltpu.CompilerParams(vmem_limit_bytes=48 << 20),
        name="middle",
    )(table, mirror_map, index, x, *parts)


def frequency_kernel(y_ref, mh_ref, ml_ref, out_ref, stage, sems):
    devices, _, _, components, rows, lanes = y_ref.shape
    count = devices * rows
    groups = sems.shape[0]
    members = components // groups
    matrix = (mh_ref[...], ml_ref[...])
    copies = []
    for group in range(groups):
        pieces = []
        for c in range(group * members, (group + 1) * members):
            part = [[y_ref[:, half, ri, c].reshape(count, lanes) for ri in range(2)] for half in range(2)]
            sums = [part[0][ri] + part[1][ri] for ri in range(2)]
            differences = [part[0][ri] - part[1][ri] for ri in range(2)]
            pieces.append(jnp.concatenate([sums[0], -differences[1]], axis=0).T)
            pieces.append(jnp.concatenate([sums[1], differences[0]], axis=0).T)
        d = dot3(split_value(jnp.concatenate(pieces, axis=0)), matrix, ((1,), (0,)))
        d = d.reshape(members, 2, lanes, d.shape[1])
        for ri in range(2):
            stage[ri, group * members : (group + 1) * members] = d[:, ri]
        cut = pl.ds(group * members, members)
        copies.append(pltpu.make_async_copy(stage.at[:, cut], out_ref.at[:, cut], sems.at[group]))
        copies[-1].start()
    for copy in copies:
        copy.wait()


def to_frequencies(y, matrix):
    components, lanes = y.shape[3], y.shape[5]
    shape = (2, components, lanes, matrix[0].shape[1])
    vmem = pl.BlockSpec(memory_space=pltpu.VMEM)
    return pl.pallas_call(
        frequency_kernel,
        in_specs=[vmem] * 3,
        out_specs=pl.BlockSpec(memory_space=pltpu.HBM),
        out_shape=jax.ShapeDtypeStruct(shape, jnp.float32),
        scratch_shapes=[pltpu.VMEM(shape, jnp.float32), pltpu.SemaphoreType.DMA((components // 2,))],
        compiler_params=pltpu.CompilerParams(vmem_limit_bytes=40 << 20),
        name="to_frequencies",
    )(y, *matrix)


def exchange(x):
    shape = x.shape
    flat = x.reshape(shape[0], -1, shape[-1])
    return lax.all_to_all(flat, "kb", split_axis=0, concat_axis=0, tiled=True).reshape(shape)


def local(green, pair_table, mirror_map):
    side = mirror_map.shape[1]
    plane = side * side
    lanes, count = green.shape[2], green.shape[3]
    devices = side * plane // lanes
    pairs = count // (2 * devices)
    padded = -(-pairs // ROWS) * ROWS
    strips = plane // 2 // lanes
    rows = time_rows(devices, pairs, padded)
    forward = [jnp.asarray(part) for part in split_constant(fermion_matrix(rows, count))]
    backward = [jnp.asarray(part) for part in split_constant(boson_matrix(rows, count))]

    def arrived(x):
        x = exchange(x[..., :pairs, :])
        x = jnp.pad(x, ((0, 0),) * 4 + ((0, padded - pairs), (0, 0)))
        x = x.reshape((side, 2, strips) + x.shape[1:])
        x = jnp.moveaxis(x, 2, -2)
        return x.reshape(x.shape[:-2] + (strips * lanes,))

    def returned(x):
        x = x[..., :pairs, :]
        x = x.reshape(x.shape[:-1] + (strips, lanes))
        x = jnp.moveaxis(x, -2, 2)
        x = exchange(x.reshape((devices,) + x.shape[3:]))
        return jnp.pad(x, ((0, 0),) * 4 + ((0, padded - pairs), (0, 0)))

    chi = middle(arrived(to_times(green, devices, padded, forward)), pair_table, mirror_map)
    return to_frequencies(returned(chi), backward)


def solution(mesh):
    placed = (P("set", None, "kb", None), P(), P("set", None))
    return jax.shard_map(
        local, mesh=mesh, in_specs=placed, out_specs=P("set", None, "kb", None), check_vma=False
    )
```

```python
import jax
import jax.numpy as jnp
import ml_dtypes
import numpy as np
from jax import lax
from jax.experimental import pallas as pl
from jax.experimental.pallas import tpu as pltpu
from jax.sharding import PartitionSpec as P

LANES = 128
ROWS = 8
GROUPS = 2


def split_constant(matrix):
    high = matrix.astype(np.float32).astype(ml_dtypes.bfloat16)
    low = (matrix - high.astype(np.float64)).astype(np.float32).astype(ml_dtypes.bfloat16)
    return high, low


def split_value(value):
    high = value.astype(jnp.bfloat16)
    low = (value - high.astype(jnp.float32)).astype(jnp.bfloat16)
    return high, low


def dot3(left, right, dims):
    def one(a, b):
        return lax.dot_general(a, b, (dims, ((), ())), preferred_element_type=jnp.float32)

    return one(left[0], right[0]) + (one(left[0], right[1]) + one(left[1], right[0]))


def time_rows(devices, pairs, padded):
    rows = np.full((devices, padded), -1, np.int64)
    rows[:, :pairs] = np.arange(devices * pairs).reshape(devices, pairs)
    return rows.reshape(-1)


def fermion_matrix(rows, count):
    n = np.arange(count, dtype=np.int64)
    angle = ((2 * n[None, :] - count + 1) * (2 * rows[:, None] + 1)) % (4 * count)
    angle = np.pi * angle / (2 * count)
    used = (rows >= 0)[:, None] * count**-0.5
    return np.concatenate([np.cos(angle) * used, np.sin(angle) * used], axis=0)


def boson_matrix(rows, count):
    v = np.arange(count, dtype=np.int64)
    angle = ((v[None, :] - count // 2) * (2 * rows[:, None] + 1)) % (2 * count)
    angle = np.pi * angle / count
    used = (rows >= 0)[:, None] * count**-0.5
    return np.concatenate([np.cos(angle) * used, np.sin(angle) * used], axis=0)


def plane_parts(side):
    p = np.arange(side * side, dtype=np.int64)
    angle = ((p[:, None] // side) * (p[None, :] // side) + (p[:, None] % side) * (p[None, :] % side)) % side
    angle = 2 * np.pi * angle / side
    scale = side**-1.5
    return np.cos(angle) * scale, np.sin(angle) * scale


def times_w4(re, im, power, sign):
    power = (power * sign) % 4
    if power == 0:
        return re, im
    if power == 1:
        return -im, re
    if power == 2:
        return -re, -im
    return im, -re


def dft4(values, sign):
    (r0, i0), (r1, i1), (r2, i2), (r3, i3) = values
    sr, si, dr, di = r0 + r2, i0 + i2, r0 - r2, i0 - i2
    tr, ti, er, ei = r1 + r3, i1 + i3, r1 - r3, i1 - i3
    if sign > 0:
        return [(sr + tr, si + ti), (dr - ei, di + er), (sr - tr, si - ti), (dr + ei, di - er)]
    return [(sr + tr, si + ti), (dr + ei, di - er), (sr - tr, si - ti), (dr - ei, di + er)]


def twiddle(value, power, sign, side):
    re, im = value
    if power % (side // 4) == 0:
        return times_w4(re, im, power // (side // 4), sign)
    angle = 2.0 * np.pi * power / side
    c, s = float(np.cos(angle)), float(sign * np.sin(angle))
    return re * c - im * s, re * s + im * c


def dft_line(values, sign):
    side = len(values)
    if side == 1:
        return values
    if side == 2:
        (r0, i0), (r1, i1) = values
        return [(r0 + r1, i0 + i1), (r0 - r1, i0 - i1)]
    if side == 4:
        return dft4(values, sign)
    inner = side // 4
    parts = [dft_line(values[b::4], sign) for b in range(4)]
    out = [None] * side
    for k1 in range(inner):
        column = [twiddle(parts[b][k1], b * k1, sign, side) for b in range(4)]
        for k2, value in enumerate(dft4(column, sign)):
            out[k1 + inner * k2] = value
    return out


def times_kernel(g_ref, mh_ref, ml_ref, out_ref):
    lanes = g_ref.shape[2]
    groups, _, _, _, rows, _ = out_ref.shape
    half = groups * rows
    g = jnp.concatenate([g_ref[0, 0], g_ref[1, 0]], axis=0)
    d = dot3((mh_ref[...], ml_ref[...]), split_value(g), ((1,), (1,)))
    c_re, c_im = d[:half, :lanes], d[:half, lanes:]
    s_re, s_im = d[half:, :lanes], d[half:, lanes:]
    for where, value in (
        ((0, 0), c_re + s_im),
        ((0, 1), c_im - s_re),
        ((1, 0), s_im - c_re),
        ((1, 1), -(c_im + s_re)),
    ):
        out_ref[:, where[0], where[1], 0] = value.reshape(groups, rows, lanes)


def to_times(green, devices, padded, matrix):
    _, entries, lanes, count = green.shape
    return pl.pallas_call(
        times_kernel,
        grid=(entries,),
        in_specs=[
            pl.BlockSpec((2, 1, lanes, count), lambda e: (0, e, 0, 0)),
            pl.BlockSpec(matrix[0].shape, lambda e: (0, 0)),
            pl.BlockSpec(matrix[1].shape, lambda e: (0, 0)),
        ],
        out_specs=pl.BlockSpec((devices, 2, 2, 1, padded, lanes), lambda e: (0, 0, 0, e, 0, 0)),
        out_shape=jax.ShapeDtypeStruct((devices, 2, 2, entries, padded, lanes), jnp.float32),
        compiler_params=pltpu.CompilerParams(vmem_limit_bytes=60 << 20),
        name="to_times",
    )(green, *matrix)


def fill_block(ref, cosine, sine):
    plane = cosine.shape[0]
    ref[:plane, :plane] = cosine.astype(jnp.bfloat16)
    ref[plane:, plane:] = cosine.astype(jnp.bfloat16)
    ref[:plane, plane:] = sine.astype(jnp.bfloat16)
    ref[plane:, :plane] = (-sine).astype(jnp.bfloat16)


def middle_kernel(
    table_ref, mirror_ref, index_ref, me_ref, x_ref, ch_ref, cl_ref, sh_ref, sl_ref, *refs
):
    outs, (forward, backward, mid, space, chi, stage, sems) = refs[:-7], refs[-7:]
    side, _, halves, _, entries, rows, lanes = x_ref.shape
    plane = 2 * lanes
    units, _, _, _, members, _, _ = stage.shape
    row = lax.broadcasted_iota(jnp.int32, (plane, plane), 0)
    pick = (row == index_ref[...]).astype(jnp.float32).astype(jnp.bfloat16)

    def dot(a, b):
        return jnp.dot(a, b, preferred_element_type=jnp.float32)

    for part, (c_ref, s_ref) in enumerate(((ch_ref, sh_ref), (cl_ref, sl_ref))):
        cosine, sine = c_ref[...].astype(jnp.float32), s_ref[...].astype(jnp.float32)
        fill_block(forward.at[0, part], cosine, sine)
        fill_block(backward.at[0, part], cosine, -sine)
        fill_block(forward.at[1, part], dot(c_ref[...], pick), dot(s_ref[...], pick))
        fill_block(backward.at[1, part], dot(pick, c_ref[...]), -dot(pick, s_ref[...]))

    for half in range(halves):
        pieces = [
            x_ref[:, h, half, ri].reshape(side * entries * rows, lanes) for ri in range(2) for h in range(2)
        ]
        value = split_value(jnp.concatenate(pieces, axis=1))
        d = dot3(value, (forward[half, 0], forward[half, 1]), ((1,), (0,)))
        for ri in range(2):
            mid[half, :, ri] = d[:, ri * plane : (ri + 1) * plane].reshape(side, entries, rows, plane)
    for half in range(halves):
        for e in range(entries):
            for block in range(2):
                cut = slice(block * lanes, (block + 1) * lanes)
                values = [(mid[half, x, 0, e, :, cut], mid[half, x, 1, e, :, cut]) for x in range(side)]
                for x, (re, im) in enumerate(dft_line(values, 1)):
                    space[half, x, 0, e, :, cut] = re
                    space[half, x, 1, e, :, cut] = im

    copies = []
    for unit in range(units):
        half, first = unit % halves, unit // halves * members
        for c in range(members):
            left, right = table_ref[first + c, 0], table_ref[first + c, 1]
            for block in range(2):
                cut = slice(block * lanes, (block + 1) * lanes)
                values = []
                for x in range(side):
                    other = mirror_ref[0, x]
                    a_re = space[half, x, 0, left, :, cut]
                    a_im = space[half, x, 1, left, :, cut]
                    b_re = space[1 - half, other, 0, right, :, cut]
                    b_im = space[1 - half, other, 1, right, :, cut]
                    values.append((a_re * b_re - a_im * b_im, a_re * b_im + a_im * b_re))
                for x, (re, im) in enumerate(dft_line(values, -1)):
                    chi[unit, 0, x, c, :, cut] = re
                    chi[unit, 1, x, c, :, cut] = im
        count = side * members * rows
        value = jnp.concatenate([chi[unit, ri].reshape(count, plane) for ri in range(2)], axis=1)
        d = dot3(split_value(value), (backward[half, 0], backward[half, 1]), ((1,), (0,)))
        for ri in range(2):
            for h in range(2):
                start = ri * plane + h * lanes
                stage[unit, :, h, ri] = d[:, start : start + lanes].reshape(side, members, rows, lanes)
        for slot, out_ref in enumerate(outs):
            target = me_ref[0] ^ slot
            piece = stage.at[unit, target // 2, target % 2]
            cut = out_ref.at[half, :, pl.ds(first, members)]
            copies.append(pltpu.make_async_copy(piece, cut, sems.at[unit, slot]))
            copies[-1].start()
    for copy in copies:
        copy.wait()


def middle(x, table, mirror_map):
    side, _, halves, _, entries, rows, lanes = x.shape
    plane = 2 * lanes
    components = table.shape[0]
    members = components // GROUPS
    units = halves * GROUPS
    index = (mirror_map[1][:, None] * side + mirror_map[2][None, :]).reshape(1, plane)
    cosine, sine = plane_parts(side)
    parts = [jnp.asarray(part) for part in split_constant(cosine) + split_constant(sine)]
    devices = 2 * side
    me = lax.axis_index("kb").astype(jnp.int32).reshape(1)
    smem = pl.BlockSpec(memory_space=pltpu.SMEM)
    vmem = pl.BlockSpec(memory_space=pltpu.VMEM)
    hbm = pl.BlockSpec(memory_space=pltpu.HBM)
    matrices = pltpu.VMEM((halves, 2, 2 * plane, 2 * plane), jnp.bfloat16)
    spatial = pltpu.VMEM((halves, side, 2, entries, rows, plane), jnp.float32)
    return pl.pallas_call(
        middle_kernel,
        in_specs=[smem, smem, vmem, smem] + [vmem] * 5,
        out_specs=[hbm] * devices,
        out_shape=[jax.ShapeDtypeStruct((halves, 2, components, rows, lanes), jnp.float32)] * devices,
        scratch_shapes=[
            matrices,
            matrices,
            spatial,
            spatial,
            pltpu.VMEM((units, 2, side, members, rows, plane), jnp.float32),
            pltpu.VMEM((units, side, 2, 2, members, rows, lanes), jnp.float32),
            pltpu.SemaphoreType.DMA((units, devices)),
        ],
        compiler_params=pltpu.CompilerParams(vmem_limit_bytes=48 << 20),
        name="middle",
    )(table, mirror_map, index, me, x, *parts)


def frequency_kernel(me_ref, mh_ref, ml_ref, *refs):
    pieces, (out_ref, y_ref, stage, in_sems, sems) = refs[:-5], refs[-5:]
    loads = [
        pltpu.make_async_copy(piece, y_ref.at[me_ref[0] ^ slot], in_sems.at[slot])
        for slot, piece in enumerate(pieces)
    ]
    for copy in loads:
        copy.start()
    for copy in loads:
        copy.wait()
    devices, _, _, components, rows, lanes = y_ref.shape
    count = devices * rows
    groups = sems.shape[0]
    members = components // groups
    matrix = (mh_ref[...], ml_ref[...])
    copies = []
    for group in range(groups):
        pieces = []
        for c in range(group * members, (group + 1) * members):
            part = [[y_ref[:, half, ri, c].reshape(count, lanes) for ri in range(2)] for half in range(2)]
            sums = [part[0][ri] + part[1][ri] for ri in range(2)]
            differences = [part[0][ri] - part[1][ri] for ri in range(2)]
            pieces.append(jnp.concatenate([sums[0], -differences[1]], axis=0).T)
            pieces.append(jnp.concatenate([sums[1], differences[0]], axis=0).T)
        d = dot3(split_value(jnp.concatenate(pieces, axis=0)), matrix, ((1,), (0,)))
        d = d.reshape(members, 2, lanes, d.shape[1])
        for ri in range(2):
            stage[ri, group * members : (group + 1) * members] = d[:, ri]
        cut = pl.ds(group * members, members)
        copies.append(pltpu.make_async_copy(stage.at[:, cut], out_ref.at[:, cut], sems.at[group]))
        copies[-1].start()
    for copy in copies:
        copy.wait()


def to_frequencies(pieces, matrix):
    _, _, components, rows, lanes = pieces[0].shape
    me = lax.axis_index("kb").astype(jnp.int32).reshape(1)
    smem = pl.BlockSpec(memory_space=pltpu.SMEM)
    hbm = pl.BlockSpec(memory_space=pltpu.HBM)
    shape = (2, components, lanes, matrix[0].shape[1])
    vmem = pl.BlockSpec(memory_space=pltpu.VMEM)
    return pl.pallas_call(
        frequency_kernel,
        in_specs=[smem, vmem, vmem] + [hbm] * len(pieces),
        out_specs=hbm,
        out_shape=jax.ShapeDtypeStruct(shape, jnp.float32),
        scratch_shapes=[
            pltpu.VMEM((len(pieces),) + pieces[0].shape, jnp.float32),
            pltpu.VMEM(shape, jnp.float32),
            pltpu.SemaphoreType.DMA((len(pieces),)),
            pltpu.SemaphoreType.DMA((components // 2,)),
        ],
        compiler_params=pltpu.CompilerParams(vmem_limit_bytes=40 << 20),
        name="to_frequencies",
    )(me, *matrix, *pieces)


def exchange(x):
    shape = x.shape
    flat = x.reshape(shape[0], -1, shape[-1])
    return lax.all_to_all(flat, "kb", split_axis=0, concat_axis=0, tiled=True).reshape(shape)


def swap(piece, slot, devices):
    if slot == 0:
        return piece
    return lax.ppermute(piece, "kb", [(device, device ^ slot) for device in range(devices)])


def local(green, pair_table, mirror_map):
    side = mirror_map.shape[1]
    plane = side * side
    lanes, count = green.shape[2], green.shape[3]
    devices = side * plane // lanes
    pairs = count // (2 * devices)
    padded = -(-pairs // ROWS) * ROWS
    strips = plane // 2 // lanes
    rows = time_rows(devices, pairs, padded)
    forward = [jnp.asarray(part) for part in split_constant(fermion_matrix(rows, count))]
    backward = [jnp.asarray(part) for part in split_constant(boson_matrix(rows, count))]

    def arrived(x):
        x = exchange(x[..., :pairs, :])
        x = jnp.pad(x, ((0, 0),) * 4 + ((0, padded - pairs), (0, 0)))
        x = x.reshape((side, 2, strips) + x.shape[1:])
        x = jnp.moveaxis(x, 2, -2)
        return x.reshape(x.shape[:-2] + (strips * lanes,))

    def returned(pieces):
        if lanes == LANES and pairs == padded:
            half = devices // 2
            order = [slot for near in range(half) for slot in (near + half, near)]
            moved = {slot: swap(pieces[slot], slot, devices) for slot in order}
            return [moved[slot] for slot in range(devices)]
        x = jnp.stack(pieces)[lax.axis_index("kb") ^ jnp.arange(2 * side)]
        x = x.reshape((side, 2) + x.shape[1:])[..., :pairs, :]
        x = x.reshape(x.shape[:-1] + (strips, lanes))
        x = jnp.moveaxis(x, -2, 2)
        x = exchange(x.reshape((devices,) + x.shape[3:]))
        x = jnp.pad(x, ((0, 0),) * 4 + ((0, padded - pairs), (0, 0)))
        return list(x[lax.axis_index("kb") ^ jnp.arange(devices)])

    pieces = middle(arrived(to_times(green, devices, padded, forward)), pair_table, mirror_map)
    return to_frequencies(returned(pieces), backward)


def solution(mesh):
    placed = (P("set", None, "kb", None), P(), P("set", None))
    return jax.shard_map(
        local, mesh=mesh, in_specs=placed, out_specs=P("set", None, "kb", None), check_vma=False
    )
```

```python
import functools
import math

import jax
import jax.numpy as jnp
import ml_dtypes
import numpy as np
from jax import lax
from jax.experimental import pallas as pl
from jax.experimental.pallas import tpu as pltpu
from jax.sharding import PartitionSpec as P

LANES = 128
ROWS = 8
GROUPS = 2


def split_constant(matrix):
    high = matrix.astype(np.float32).astype(ml_dtypes.bfloat16)
    low = (matrix - high.astype(np.float64)).astype(np.float32).astype(ml_dtypes.bfloat16)
    return high, low


def split_value(value):
    high = value.astype(jnp.bfloat16)
    low = (value - high.astype(jnp.float32)).astype(jnp.bfloat16)
    return high, low


def dot3(left, right, dims):
    (k_left,), (k_right,) = dims
    a = jnp.concatenate([left[0], left[0], left[1]], axis=k_left)
    b = jnp.concatenate([right[0], right[1], right[0]], axis=k_right)
    return lax.dot_general(a, b, (dims, ((), ())), preferred_element_type=jnp.float32)


def fermion_matrix(rows, count):
    n = np.arange(count, dtype=np.int64)
    angle = ((2 * n[None, :] - count + 1) * (2 * rows[:, None] + 1)) % (4 * count)
    angle = np.pi * angle / (2 * count)
    return np.concatenate([np.cos(angle), np.sin(angle)], axis=0) * count**-0.5


def boson_matrix(rows, count):
    v = np.arange(count, dtype=np.int64)
    angle = ((v[None, :] - count // 2) * (2 * rows[:, None] + 1)) % (2 * count)
    angle = np.pi * angle / count
    return np.concatenate([np.cos(angle), np.sin(angle)], axis=0) * count**-0.5


def plane_parts(side):
    p = np.arange(side * side, dtype=np.int64)
    angle = ((p[:, None] // side) * (p[None, :] // side) + (p[:, None] % side) * (p[None, :] % side)) % side
    angle = 2 * np.pi * angle / side
    scale = side**-1.5
    return np.cos(angle) * scale, np.sin(angle) * scale


def times_w4(re, im, power, sign):
    power = (power * sign) % 4
    if power == 0:
        return re, im
    if power == 1:
        return -im, re
    if power == 2:
        return -re, -im
    return im, -re


def dft4(values, sign):
    (r0, i0), (r1, i1), (r2, i2), (r3, i3) = values
    sr, si, dr, di = r0 + r2, i0 + i2, r0 - r2, i0 - i2
    tr, ti, er, ei = r1 + r3, i1 + i3, r1 - r3, i1 - i3
    if sign > 0:
        return [(sr + tr, si + ti), (dr - ei, di + er), (sr - tr, si - ti), (dr + ei, di - er)]
    return [(sr + tr, si + ti), (dr + ei, di - er), (sr - tr, si - ti), (dr - ei, di + er)]


def twiddle(value, power, sign, side):
    re, im = value
    if power % (side // 4) == 0:
        return times_w4(re, im, power // (side // 4), sign)
    angle = 2.0 * np.pi * power / side
    c, s = float(np.cos(angle)), float(sign * np.sin(angle))
    return re * c - im * s, re * s + im * c


def dft_line(values, sign):
    side = len(values)
    if side == 1:
        return values
    if side == 2:
        (r0, i0), (r1, i1) = values
        return [(r0 + r1, i0 + i1), (r0 - r1, i0 - i1)]
    if side == 4:
        return dft4(values, sign)
    inner = side // 4
    parts = [dft_line(values[b::4], sign) for b in range(4)]
    out = [None] * side
    for k1 in range(inner):
        column = [twiddle(parts[b][k1], b * k1, sign, side) for b in range(4)]
        for k2, value in enumerate(dft4(column, sign)):
            out[k1 + inner * k2] = value
    return out


def relative_rows(matrix_ref, me):
    parts, devices = matrix_ref.shape[:2]
    rows = [matrix_ref[part, slot ^ me] for part in range(parts) for slot in range(devices)]
    return jnp.concatenate(rows, axis=0)


def times_kernel(order, me_ref, g_ref, m_ref, *outs):
    _, entries, lanes, _ = g_ref.shape
    _, devices, rows, _ = m_ref.shape
    half = devices * rows
    matrix = split_value(relative_rows(m_ref, me_ref[0]))
    for e in range(entries):
        g = jnp.concatenate([g_ref[0, e], g_ref[1, e]], axis=0)
        d = dot3(matrix, split_value(g), ((1,), (1,)))
        c_re, c_im = d[:half, :lanes], d[:half, lanes:]
        s_re, s_im = d[half:, :lanes], d[half:, lanes:]
        for where, value in (
            ((0, 0), c_re + s_im),
            ((0, 1), c_im - s_re),
            ((1, 0), s_im - c_re),
            ((1, 1), -(c_im + s_re)),
        ):
            for out_ref, slot in zip(outs, order):
                out_ref[where[0], where[1], e] = value[slot * rows : (slot + 1) * rows]


def call_kernel(kernel, order, me, args, arg_specs, shape, scratch, limit, name):
    pieces = pl.pallas_call(
        kernel,
        in_specs=[pl.BlockSpec(memory_space=pltpu.SMEM)] + arg_specs,
        out_specs=[pl.BlockSpec(memory_space=pltpu.VMEM)] * len(order),
        out_shape=[jax.ShapeDtypeStruct(shape, jnp.float32)] * len(order),
        scratch_shapes=scratch,
        compiler_params=pltpu.CompilerParams(vmem_limit_bytes=limit << 20),
        name=name,
    )(me, *args)
    return dict(zip(order, pieces))


def to_times(green, matrix, me, order):
    _, entries, lanes, _ = green.shape
    shape = (2, 2, entries, matrix.shape[2], lanes)
    vmem = pl.BlockSpec(memory_space=pltpu.VMEM)
    kernel = functools.partial(times_kernel, order)
    return call_kernel(kernel, order, me, (green, matrix), [vmem] * 2, shape, [], 40, "to_times")


def fill_block(ref, cosine, sine):
    plane = cosine.shape[0]
    lanes = plane // 2
    for block in range(2):
        cut = slice(block * lanes, (block + 1) * lanes)
        re = slice(2 * block * lanes, (2 * block + 1) * lanes)
        im = slice((2 * block + 1) * lanes, (2 * block + 2) * lanes)
        ref[:plane, re] = cosine[:, cut].astype(jnp.bfloat16)
        ref[plane:, im] = cosine[:, cut].astype(jnp.bfloat16)
        ref[:plane, im] = sine[:, cut].astype(jnp.bfloat16)
        ref[plane:, re] = (-sine[:, cut]).astype(jnp.bfloat16)


def middle_kernel(order, me_ref, table_ref, mirror_ref, index_ref, ch_ref, cl_ref, sh_ref, sl_ref, *refs):
    count = len(order)
    pieces = dict(zip(order, refs[:count]))
    outs = dict(zip(order, refs[count : 2 * count]))
    forward, backward, mid, space, chi = refs[2 * count :]
    halves, _, side, _, entries, rows, lanes = space.shape
    plane = 2 * lanes
    units, _, _, members, _, _ = chi.shape
    line, core = me_ref[0] // 2, me_ref[0] % 2
    row = lax.broadcasted_iota(jnp.int32, (plane, plane), 0)
    pick = (row == index_ref[...]).astype(jnp.float32).astype(jnp.bfloat16)

    def dot(a, b):
        return jnp.dot(a, b, preferred_element_type=jnp.float32)

    def turned(value, axis):
        first = lax.slice_in_dim(value, 0, lanes, axis=axis)
        second = lax.slice_in_dim(value, lanes, plane, axis=axis)
        return jnp.where(core == 0, value, jnp.concatenate([second, first], axis=axis))

    for part, (c_ref, s_ref) in enumerate(((ch_ref, sh_ref), (cl_ref, sl_ref))):
        cosine, sine = c_ref[...].astype(jnp.float32), s_ref[...].astype(jnp.float32)
        fill_block(forward.at[0, part], turned(cosine, 0), turned(sine, 0))
        fill_block(backward.at[0, part], turned(cosine, 1), turned(-sine, 1))
        fill_block(
            forward.at[1, part], turned(dot(c_ref[...], pick), 0), turned(dot(s_ref[...], pick), 0)
        )
        fill_block(
            backward.at[1, part], turned(dot(pick, c_ref[...]), 1), turned(-dot(pick, s_ref[...]), 1)
        )

    def plane_dot(value, matrix, half, block):
        cut = slice(2 * block * lanes, 2 * (block + 1) * lanes)
        return dot3(value, (matrix[half, 0, :, cut], matrix[half, 1, :, cut]), ((1,), (0,)))

    def arrive(half):
        columns = []
        for ri in range(2):
            for h in range(2):
                rows_of = [pieces[2 * x + h][half, ri].reshape(entries * rows, lanes) for x in range(side)]
                columns.append(jnp.concatenate(rows_of, axis=0))
        return split_value(jnp.concatenate(columns, axis=1))

    def to_plane(value, half, block):
        d = plane_dot(value, forward, half, block)
        for ri in range(2):
            piece = d[:, ri * lanes : (ri + 1) * lanes]
            mid[half, block, ri] = piece.reshape(side, entries, rows, lanes)

    def along_line(half, block, e):
        values = [(mid[half, block, 0, x ^ line, e], mid[half, block, 1, x ^ line, e]) for x in range(side)]
        for x, (re, im) in enumerate(dft_line(values, 1)):
            space[half, block, x, 0, e] = re
            space[half, block, x, 1, e] = im

    def product(unit, block, c):
        half, first = unit % halves, unit // halves * members
        left, right = table_ref[first + c, 0], table_ref[first + c, 1]
        values = []
        for x in range(side):
            other = mirror_ref[0, x]
            a_re, a_im = space[half, block, x, 0, left], space[half, block, x, 1, left]
            b_re, b_im = space[1 - half, block, other, 0, right], space[1 - half, block, other, 1, right]
            values.append((a_re * b_re - a_im * b_im, a_re * b_im + a_im * b_re))
        cut = slice(block * lanes, (block + 1) * lanes)
        for x, (re, im) in enumerate(dft_line(values, -1)):
            chi[unit, 0, x ^ line, c, :, cut] = re
            chi[unit, 1, x ^ line, c, :, cut] = im

    def from_plane(unit, value, h):
        half, first = unit % halves, unit // halves * members
        d = plane_dot(value, backward, half, h)
        for ri in range(2):
            piece = d[:, ri * lanes : (ri + 1) * lanes].reshape(side, members, rows, lanes)
            for x in range(side):
                outs[2 * x + h][half, ri, first : first + members] = piece[x]

    def collect(unit):
        whole = (side * members * rows, plane)
        return split_value(jnp.concatenate([chi[unit, ri].reshape(whole) for ri in range(2)], axis=1))

    places = [(half, block) for half in range(halves) for block in range(2)]
    for step in range(len(places) + 1):
        if step < len(places):
            half, block = places[step]
            if block == 0:
                value = arrive(half)
            to_plane(value, half, block)
        if step > 0:
            for e in range(entries):
                along_line(*places[step - 1], e)

    for unit in range(units + 1):
        tasks = [(block, c) for block in range(2) for c in range(members)] if unit < units else []
        if unit > 0:
            value = collect(unit - 1)
        for h in range(2):
            if unit > 0:
                from_plane(unit - 1, value, h)
            for block, c in tasks[h * members : (h + 1) * members]:
                product(unit, block, c)


def middle(pieces, table, mirror_map, me, order):
    halves, _, entries, rows, lanes = pieces[0].shape
    plane = 2 * lanes
    side = len(order) // 2
    components = table.shape[0]
    members = components // GROUPS
    units = halves * GROUPS
    index = (mirror_map[1][:, None] * side + mirror_map[2][None, :]).reshape(1, plane)
    cosine, sine = plane_parts(side)
    parts = [jnp.asarray(part) for part in split_constant(cosine) + split_constant(sine)]
    smem = pl.BlockSpec(memory_space=pltpu.SMEM)
    vmem = pl.BlockSpec(memory_space=pltpu.VMEM)
    matrices = pltpu.VMEM((halves, 2, 2 * plane, 2 * plane), jnp.bfloat16)
    scratch = [
        matrices,
        matrices,
        pltpu.VMEM((halves, 2, 2, side, entries, rows, lanes), jnp.float32),
        pltpu.VMEM((halves, 2, side, 2, entries, rows, lanes), jnp.float32),
        pltpu.VMEM((units, 2, side, members, rows, plane), jnp.float32),
    ]
    args = (table, mirror_map, index, *parts) + tuple(pieces[slot] for slot in order)
    specs = [smem, smem, vmem] + [vmem] * (4 + len(order))
    shape = (halves, 2, components, rows, lanes)
    kernel = functools.partial(middle_kernel, order)
    return call_kernel(kernel, order, me, args, specs, shape, scratch, 40, "middle")


def frequency_kernel(order, me_ref, m_ref, *refs):
    pieces = dict(zip(order, refs[: len(order)]))
    out_ref, stage, sems = refs[len(order) :]
    components, lanes = stage.shape[1:3]
    groups = sems.shape[0]
    members = components // groups
    matrix = split_value(relative_rows(m_ref, me_ref[0]))
    copies = []
    for group in range(groups):
        values = []
        for c in range(group * members, (group + 1) * members):
            part = [
                [jnp.concatenate([pieces[slot][half, ri, c] for slot in range(len(order))], axis=0) for ri in range(2)]
                for half in range(2)
            ]
            sums = [part[0][ri] + part[1][ri] for ri in range(2)]
            differences = [part[0][ri] - part[1][ri] for ri in range(2)]
            values.append(jnp.concatenate([sums[0], -differences[1]], axis=0).T)
            values.append(jnp.concatenate([sums[1], differences[0]], axis=0).T)
        d = dot3(split_value(jnp.concatenate(values, axis=0)), matrix, ((1,), (0,)))
        d = d.reshape(members, 2, lanes, d.shape[1])
        for ri in range(2):
            stage[ri, group * members : (group + 1) * members] = d[:, ri]
        cut = pl.ds(group * members, members)
        copies.append(pltpu.make_async_copy(stage.at[:, cut], out_ref.at[:, cut], sems.at[group]))
        copies[-1].start()
    for copy in copies:
        copy.wait()


def to_frequencies(pieces, matrix, me, order):
    _, _, components, rows, lanes = pieces[0].shape
    shape = (2, components, lanes, matrix.shape[3])
    vmem = pl.BlockSpec(memory_space=pltpu.VMEM)
    return pl.pallas_call(
        functools.partial(frequency_kernel, order),
        in_specs=[pl.BlockSpec(memory_space=pltpu.SMEM)] + [vmem] * (1 + len(order)),
        out_specs=pl.BlockSpec(memory_space=pltpu.HBM),
        out_shape=jax.ShapeDtypeStruct(shape, jnp.float32),
        scratch_shapes=[pltpu.VMEM(shape, jnp.float32), pltpu.SemaphoreType.DMA((components // 2,))],
        compiler_params=pltpu.CompilerParams(vmem_limit_bytes=40 << 20),
        name="to_frequencies",
    )(me, matrix, *[pieces[slot] for slot in order])


def swap(pieces, order):
    moved = {}
    for slot in order:
        pairs = [(device, device ^ slot) for device in range(len(order))]
        moved[slot] = lax.ppermute(pieces[slot], "kb", pairs) if slot else pieces[slot]
    return moved


def slot_order(devices):
    half = devices // 2
    return [slot for near in range(half) for slot in (near + half, near)]


def trig_pair(angle_int, period, scale):
    angle = 2.0 * math.pi / period * angle_int.astype(jnp.float32)
    return (scale * jnp.cos(angle), scale * jnp.sin(angle))


def complex_combine(formula, cosine, sine, real_part, imag_part):
    first_term = jnp.einsum(formula, cosine, real_part + imag_part, precision=lax.Precision.HIGHEST)
    second_term = jnp.einsum(formula, cosine + sine, imag_part, precision=lax.Precision.HIGHEST)
    third_term = jnp.einsum(formula, sine - cosine, real_part, precision=lax.Precision.HIGHEST)
    return (first_term - second_term, first_term + third_term)


def forward_imaginary_time(tau_rows, frequency_count):
    freq_index = jnp.arange(frequency_count, dtype=jnp.int32)
    angle_int = (
        (2 * freq_index[None, :] - frequency_count + 1)
        * (2 * tau_rows[:, None] + 1)
        % (4 * frequency_count)
    )
    cosine, sine = trig_pair(angle_int, 4 * frequency_count, frequency_count ** (-0.5))
    return (cosine, -sine)


def tau_backward(tau_rows, frequency_count):
    freq_index = jnp.arange(frequency_count, dtype=jnp.int32)
    angle_int = (
        (freq_index[:, None] - frequency_count // 2)
        * (2 * tau_rows[None, :] + 1)
        % (2 * frequency_count)
    )
    return trig_pair(angle_int, 2 * frequency_count, frequency_count ** (-0.5))


def grid_transform(real_part, imag_part, grid_side, direction):
    shape = real_part.shape
    plane = jnp.arange(grid_side * grid_side, dtype=jnp.int32)
    upper = plane // grid_side
    lower = plane % grid_side
    plane_int = (upper[:, None] * upper[None, :] + lower[:, None] * lower[None, :]) % grid_side
    plane_cos, plane_sin = trig_pair(plane_int, grid_side, 1.0 / grid_side)
    line = jnp.arange(grid_side, dtype=jnp.int32)
    line_cos, line_sin = trig_pair(
        line[:, None] * line[None, :] % grid_side, grid_side, grid_side ** (-0.5)
    )
    real_part = real_part.reshape(shape[:-1] + (grid_side, grid_side * grid_side))
    imag_part = imag_part.reshape(shape[:-1] + (grid_side, grid_side * grid_side))
    real_part, imag_part = complex_combine(
        "pq,...xq->...xp", plane_cos, direction * plane_sin, real_part, imag_part
    )
    real_part, imag_part = complex_combine(
        "ax,...xp->...ap", line_cos, direction * line_sin, real_part, imag_part
    )
    return (real_part.reshape(shape), imag_part.reshape(shape))


def mirror_index(mirror_map, grid_side):
    index_x = mirror_map[0][:, None, None]
    index_y = mirror_map[1][None, :, None]
    index_z = mirror_map[2][None, None, :]
    return (index_x * grid_side * grid_side + index_y * grid_side + index_z).reshape(-1)


def bubble(gr_re, gr_im, mirror_re, mirror_im, pair_table, entries):
    entry_ids = jnp.arange(entries, dtype=jnp.int32)
    pick_left = (pair_table[:, 0][:, None] == entry_ids[None, :]).astype(jnp.float32)
    pick_right = (pair_table[:, 1][:, None] == entry_ids[None, :]).astype(jnp.float32)
    left_re = jnp.einsum("me,e...->m...", pick_left, gr_re, precision=lax.Precision.HIGHEST)
    left_im = jnp.einsum("me,e...->m...", pick_left, gr_im, precision=lax.Precision.HIGHEST)
    right_re = jnp.einsum("me,e...->m...", pick_right, mirror_re, precision=lax.Precision.HIGHEST)
    right_im = jnp.einsum("me,e...->m...", pick_right, mirror_im, precision=lax.Precision.HIGHEST)
    return (left_re * right_re - left_im * right_im, left_re * right_im + left_im * right_re)


def general(green_momentum_grid, pair_table, mirror_map):
    grid_side = mirror_map.shape[1]
    entries = green_momentum_grid.shape[1]
    frequency_count = green_momentum_grid.shape[3]
    position = jnp.arange(frequency_count, dtype=jnp.int32)
    fwd_cos, fwd_sin = forward_imaginary_time(position, frequency_count)
    tau_re, tau_im = complex_combine(
        "qa,fsa->fqs", fwd_cos, fwd_sin, green_momentum_grid[0], green_momentum_grid[1]
    )
    stacked = jnp.stack([tau_re, tau_im])

    def to_real_space(pieces):
        space_re, space_im = grid_transform(pieces[0], pieces[1], grid_side, 1.0)
        return jnp.stack([space_re, space_im])

    mirror_flat = mirror_index(mirror_map, grid_side)
    partner_rows = frequency_count - 1 - position
    reflected_cosine, reflected_sine = forward_imaginary_time(partner_rows, frequency_count)
    partner_real, partner_imaginary = complex_combine(
        "qa,fsa->fqs",
        reflected_cosine,
        reflected_sine,
        green_momentum_grid[0],
        green_momentum_grid[1],
    )
    other_stacked = jnp.stack([partner_real, partner_imaginary])
    pieces = (
        lax.all_to_all(stacked, "kb", split_axis=2, concat_axis=3, tiled=True),
        lax.all_to_all(other_stacked, "kb", split_axis=2, concat_axis=3, tiled=True),
    )
    in_cells = to_real_space(pieces[0])
    partner = to_real_space(pieces[1])
    mirrored = jnp.take(partner, mirror_flat, axis=3)
    chi_re, chi_im = bubble(in_cells[0], in_cells[1], mirrored[0], mirrored[1], pair_table, entries)
    chi_re, chi_im = grid_transform(chi_re, chi_im, grid_side, -1.0)
    momenta = jnp.stack([chi_re, chi_im])
    back_cos, back_sin = tau_backward(position, frequency_count)
    pieces = lax.all_to_all(momenta, "kb", split_axis=3, concat_axis=2, tiled=True)
    out_re, out_im = complex_combine("vj,ejk->ekv", back_cos, back_sin, pieces[0], pieces[1])
    return jnp.stack([out_re, out_im])


def local(green, pair_table, mirror_map):
    side = mirror_map.shape[1]
    plane = side * side
    lanes, count = green.shape[2], green.shape[3]
    devices = side * plane // lanes
    pairs = count // (2 * devices)
    if lanes != LANES or pairs != ROWS or 2 * lanes != plane:
        return general(green, pair_table, mirror_map)
    rows = np.arange(devices * pairs)
    shape = (2, devices, pairs, count)
    forward = jnp.asarray(fermion_matrix(rows, count).reshape(shape).astype(np.float32))
    backward = jnp.asarray(boson_matrix(rows, count).reshape(shape).astype(np.float32))
    order = slot_order(devices)
    me = lax.axis_index("kb").astype(jnp.int32).reshape(1)
    pieces = swap(to_times(green, forward, me, order), order)
    pieces = swap(middle(pieces, pair_table, mirror_map, me, order), order)
    return to_frequencies(pieces, backward, me, order)


def solution(mesh):
    placed = (P("set", None, "kb", None), P(), P("set", None))
    return jax.shard_map(
        local, mesh=mesh, in_specs=placed, out_specs=P("set", None, "kb", None), check_vma=False
    )
```

```python
import functools
import math

import jax
import jax.numpy as jnp
import ml_dtypes
import numpy as np
from jax import lax
from jax.experimental import pallas as pl
from jax.experimental.pallas import tpu as pltpu
from jax.sharding import PartitionSpec as P

LANES = 128
ROWS = 8
GROUPS = 2


def split_constant(matrix):
    high = matrix.astype(np.float32).astype(ml_dtypes.bfloat16)
    low = (matrix - high.astype(np.float64)).astype(np.float32).astype(ml_dtypes.bfloat16)
    return high, low


def split_value(value):
    high = value.astype(jnp.bfloat16)
    low = (value - high.astype(jnp.float32)).astype(jnp.bfloat16)
    return high, low


def dot3(left, right, dims):
    (k_left,), (k_right,) = dims
    a = jnp.concatenate([left[0], left[0], left[1]], axis=k_left)
    b = jnp.concatenate([right[0], right[1], right[0]], axis=k_right)
    return lax.dot_general(a, b, (dims, ((), ())), preferred_element_type=jnp.float32)


def fermion_matrix(rows, count):
    n = np.arange(count, dtype=np.int64)
    angle = ((2 * n[None, :] - count + 1) * (2 * rows[:, None] + 1)) % (4 * count)
    angle = np.pi * angle / (2 * count)
    return np.concatenate([np.cos(angle), np.sin(angle)], axis=0) * count**-0.5


def boson_matrix(rows, count):
    v = np.arange(count, dtype=np.int64)
    angle = ((v[None, :] - count // 2) * (2 * rows[:, None] + 1)) % (2 * count)
    angle = np.pi * angle / count
    return np.concatenate([np.cos(angle), np.sin(angle)], axis=0) * count**-0.5


def plane_parts(side):
    p = np.arange(side * side, dtype=np.int64)
    angle = ((p[:, None] // side) * (p[None, :] // side) + (p[:, None] % side) * (p[None, :] % side)) % side
    angle = 2 * np.pi * angle / side
    scale = side**-1.5
    return np.cos(angle) * scale, np.sin(angle) * scale


def times_w4(re, im, power, sign):
    power = (power * sign) % 4
    if power == 0:
        return re, im
    if power == 1:
        return -im, re
    if power == 2:
        return -re, -im
    return im, -re


def dft4(values, sign):
    (r0, i0), (r1, i1), (r2, i2), (r3, i3) = values
    sr, si, dr, di = r0 + r2, i0 + i2, r0 - r2, i0 - i2
    tr, ti, er, ei = r1 + r3, i1 + i3, r1 - r3, i1 - i3
    if sign > 0:
        return [(sr + tr, si + ti), (dr - ei, di + er), (sr - tr, si - ti), (dr + ei, di - er)]
    return [(sr + tr, si + ti), (dr + ei, di - er), (sr - tr, si - ti), (dr - ei, di + er)]


def twiddle(value, power, sign, side):
    re, im = value
    if power % (side // 4) == 0:
        return times_w4(re, im, power // (side // 4), sign)
    angle = 2.0 * np.pi * power / side
    c, s = float(np.cos(angle)), float(sign * np.sin(angle))
    return re * c - im * s, re * s + im * c


def dft_line(values, sign):
    side = len(values)
    if side == 1:
        return values
    if side == 2:
        (r0, i0), (r1, i1) = values
        return [(r0 + r1, i0 + i1), (r0 - r1, i0 - i1)]
    if side == 4:
        return dft4(values, sign)
    inner = side // 4
    parts = [dft_line(values[b::4], sign) for b in range(4)]
    out = [None] * side
    for k1 in range(inner):
        column = [twiddle(parts[b][k1], b * k1, sign, side) for b in range(4)]
        for k2, value in enumerate(dft4(column, sign)):
            out[k1 + inner * k2] = value
    return out


def place(refs, order, slot, me):
    if slot in order:
        return refs[1 + order.index(slot)], ()
    return refs[0], (slot ^ (me % refs[0].shape[0]),)


def relative_rows(matrix_ref, me):
    parts, devices = matrix_ref.shape[:2]
    rows = [matrix_ref[part, slot ^ me] for part in range(parts) for slot in range(devices)]
    return jnp.concatenate(rows, axis=0)


def times_kernel(order, me_ref, g_ref, m_ref, *outs):
    _, entries, lanes, _ = g_ref.shape
    _, devices, rows, _ = m_ref.shape
    half = devices * rows
    matrix = split_value(relative_rows(m_ref, me_ref[0]))
    for e in range(entries):
        g = jnp.concatenate([g_ref[0, e], g_ref[1, e]], axis=0)
        d = dot3(matrix, split_value(g), ((1,), (1,)))
        c_re, c_im = d[:half, :lanes], d[:half, lanes:]
        s_re, s_im = d[half:, :lanes], d[half:, lanes:]
        for where, value in (
            ((0, 0), c_re + s_im),
            ((0, 1), c_im - s_re),
            ((1, 0), s_im - c_re),
            ((1, 1), -(c_im + s_re)),
        ):
            for slot in range(devices):
                ref, at = place(outs, order, slot, me_ref[0])
                ref[at + (where[0], where[1], e)] = value[slot * rows : (slot + 1) * rows]


def call_kernel(kernel, near, order, me, args, arg_specs, shape, scratch, limit, name):
    return pl.pallas_call(
        kernel,
        in_specs=[pl.BlockSpec(memory_space=pltpu.SMEM)] + arg_specs,
        out_specs=[pl.BlockSpec(memory_space=pltpu.VMEM)] * (1 + len(order)),
        out_shape=[jax.ShapeDtypeStruct((near,) + shape, jnp.float32)]
        + [jax.ShapeDtypeStruct(shape, jnp.float32)] * len(order),
        scratch_shapes=scratch,
        compiler_params=pltpu.CompilerParams(vmem_limit_bytes=limit << 20),
        name=name,
    )(me, *args)


def to_times(green, matrix, me, order):
    _, entries, lanes, _ = green.shape
    shape = (2, 2, entries, matrix.shape[2], lanes)
    vmem = pl.BlockSpec(memory_space=pltpu.VMEM)
    kernel = functools.partial(times_kernel, order)
    near = matrix.shape[1] - len(order)
    return call_kernel(kernel, near, order, me, (green, matrix), [vmem] * 2, shape, [], 40, "to_times")


def fill_block(ref, cosine, sine):
    plane = cosine.shape[0]
    lanes = plane // 2
    for block in range(2):
        cut = slice(block * lanes, (block + 1) * lanes)
        re = slice(2 * block * lanes, (2 * block + 1) * lanes)
        im = slice((2 * block + 1) * lanes, (2 * block + 2) * lanes)
        ref[:plane, re] = cosine[:, cut].astype(jnp.bfloat16)
        ref[plane:, im] = cosine[:, cut].astype(jnp.bfloat16)
        ref[:plane, im] = sine[:, cut].astype(jnp.bfloat16)
        ref[plane:, re] = (-sine[:, cut]).astype(jnp.bfloat16)


def middle_kernel(order, me_ref, table_ref, mirror_ref, index_ref, ch_ref, cl_ref, sh_ref, sl_ref, *refs):
    count = 1 + len(order)
    pieces, outs = refs[:count], refs[count : 2 * count]
    forward, backward, mid, space, chi = refs[2 * count :]
    halves, _, side, _, entries, rows, lanes = space.shape
    plane = 2 * lanes
    units, _, _, members, _, _ = chi.shape
    line, core = me_ref[0] // 2, me_ref[0] % 2
    row = lax.broadcasted_iota(jnp.int32, (plane, plane), 0)
    pick = (row == index_ref[...]).astype(jnp.float32).astype(jnp.bfloat16)

    def dot(a, b):
        return jnp.dot(a, b, preferred_element_type=jnp.float32)

    def turned(value, axis):
        first = lax.slice_in_dim(value, 0, lanes, axis=axis)
        second = lax.slice_in_dim(value, lanes, plane, axis=axis)
        return jnp.where(core == 0, value, jnp.concatenate([second, first], axis=axis))

    for part, (c_ref, s_ref) in enumerate(((ch_ref, sh_ref), (cl_ref, sl_ref))):
        cosine, sine = c_ref[...].astype(jnp.float32), s_ref[...].astype(jnp.float32)
        fill_block(forward.at[0, part], turned(cosine, 0), turned(sine, 0))
        fill_block(backward.at[0, part], turned(cosine, 1), turned(-sine, 1))
        fill_block(
            forward.at[1, part], turned(dot(c_ref[...], pick), 0), turned(dot(s_ref[...], pick), 0)
        )
        fill_block(
            backward.at[1, part], turned(dot(pick, c_ref[...]), 1), turned(-dot(pick, s_ref[...]), 1)
        )

    def plane_dot(value, matrix, half, block):
        cut = slice(2 * block * lanes, 2 * (block + 1) * lanes)
        return dot3(value, (matrix[half, 0, :, cut], matrix[half, 1, :, cut]), ((1,), (0,)))

    def arrive(half):
        columns = []
        for ri in range(2):
            for h in range(2):
                rows_of = []
                for x in range(side):
                    ref, at = place(pieces, order, 2 * x + h, me_ref[0])
                    rows_of.append(ref[at + (half, ri)].reshape(entries * rows, lanes))
                columns.append(jnp.concatenate(rows_of, axis=0))
        return split_value(jnp.concatenate(columns, axis=1))

    def to_plane(value, half, block):
        d = plane_dot(value, forward, half, block)
        for ri in range(2):
            piece = d[:, ri * lanes : (ri + 1) * lanes]
            mid[half, block, ri] = piece.reshape(side, entries, rows, lanes)

    def along_line(half, block, e):
        values = [(mid[half, block, 0, x ^ line, e], mid[half, block, 1, x ^ line, e]) for x in range(side)]
        for x, (re, im) in enumerate(dft_line(values, 1)):
            space[half, block, x, 0, e] = re
            space[half, block, x, 1, e] = im

    def product(unit, block, c):
        half, first = unit % halves, unit // halves * members
        left, right = table_ref[first + c, 0], table_ref[first + c, 1]
        values = []
        for x in range(side):
            other = mirror_ref[0, x]
            a_re, a_im = space[half, block, x, 0, left], space[half, block, x, 1, left]
            b_re, b_im = space[1 - half, block, other, 0, right], space[1 - half, block, other, 1, right]
            values.append((a_re * b_re - a_im * b_im, a_re * b_im + a_im * b_re))
        cut = slice(block * lanes, (block + 1) * lanes)
        for x, (re, im) in enumerate(dft_line(values, -1)):
            chi[unit, 0, x ^ line, c, :, cut] = re
            chi[unit, 1, x ^ line, c, :, cut] = im

    def from_plane(unit, value, h):
        half, first = unit % halves, unit // halves * members
        d = plane_dot(value, backward, half, h)
        for ri in range(2):
            piece = d[:, ri * lanes : (ri + 1) * lanes].reshape(side, members, rows, lanes)
            for x in range(side):
                ref, at = place(outs, order, 2 * x + h, me_ref[0])
                ref[at + (half, ri, slice(first, first + members))] = piece[x]

    def collect(unit):
        whole = (side * members * rows, plane)
        return split_value(jnp.concatenate([chi[unit, ri].reshape(whole) for ri in range(2)], axis=1))

    places = [(half, block) for half in range(halves) for block in range(2)]
    for step in range(len(places) + 1):
        if step < len(places):
            half, block = places[step]
            if block == 0:
                value = arrive(half)
            to_plane(value, half, block)
        if step > 0:
            for e in range(entries):
                along_line(*places[step - 1], e)

    for unit in range(units + 1):
        tasks = [(block, c) for block in range(2) for c in range(members)] if unit < units else []
        if unit > 0:
            value = collect(unit - 1)
        for h in range(2):
            if unit > 0:
                from_plane(unit - 1, value, h)
            for block, c in tasks[h * members : (h + 1) * members]:
                product(unit, block, c)


def middle(pieces, table, mirror_map, me, order):
    near, halves, _, entries, rows, lanes = pieces[0].shape
    plane = 2 * lanes
    side = (near + len(order)) // 2
    components = table.shape[0]
    members = components // GROUPS
    units = halves * GROUPS
    index = (mirror_map[1][:, None] * side + mirror_map[2][None, :]).reshape(1, plane)
    cosine, sine = plane_parts(side)
    parts = [jnp.asarray(part) for part in split_constant(cosine) + split_constant(sine)]
    smem = pl.BlockSpec(memory_space=pltpu.SMEM)
    vmem = pl.BlockSpec(memory_space=pltpu.VMEM)
    matrices = pltpu.VMEM((halves, 2, 2 * plane, 2 * plane), jnp.bfloat16)
    scratch = [
        matrices,
        matrices,
        pltpu.VMEM((halves, 2, 2, side, entries, rows, lanes), jnp.float32),
        pltpu.VMEM((halves, 2, side, 2, entries, rows, lanes), jnp.float32),
        pltpu.VMEM((units, 2, side, members, rows, plane), jnp.float32),
    ]
    args = (table, mirror_map, index, *parts, *pieces)
    specs = [smem, smem, vmem] + [vmem] * (4 + len(pieces))
    shape = (halves, 2, components, rows, lanes)
    kernel = functools.partial(middle_kernel, order)
    return call_kernel(kernel, near, order, me, args, specs, shape, scratch, 40, "middle")


def frequency_kernel(order, me_ref, m_ref, *refs):
    pieces = refs[: 1 + len(order)]
    out_ref, stage, sems = refs[1 + len(order) :]
    devices = m_ref.shape[1]
    components, lanes = stage.shape[1:3]
    groups = sems.shape[0]
    members = components // groups
    matrix = split_value(relative_rows(m_ref, me_ref[0]))

    def gathered(half, ri, c):
        rows_of = []
        for slot in range(devices):
            ref, at = place(pieces, order, slot, me_ref[0])
            rows_of.append(ref[at + (half, ri, c)])
        return jnp.concatenate(rows_of, axis=0)

    copies = []
    for group in range(groups):
        values = []
        for c in range(group * members, (group + 1) * members):
            part = [[gathered(half, ri, c) for ri in range(2)] for half in range(2)]
            sums = [part[0][ri] + part[1][ri] for ri in range(2)]
            differences = [part[0][ri] - part[1][ri] for ri in range(2)]
            values.append(jnp.concatenate([sums[0], -differences[1]], axis=0).T)
            values.append(jnp.concatenate([sums[1], differences[0]], axis=0).T)
        d = dot3(split_value(jnp.concatenate(values, axis=0)), matrix, ((1,), (0,)))
        d = d.reshape(members, 2, lanes, d.shape[1])
        for ri in range(2):
            stage[ri, group * members : (group + 1) * members] = d[:, ri]
        cut = pl.ds(group * members, members)
        copies.append(pltpu.make_async_copy(stage.at[:, cut], out_ref.at[:, cut], sems.at[group]))
        copies[-1].start()
    for copy in copies:
        copy.wait()


def to_frequencies(pieces, matrix, me, order):
    components, rows, lanes = pieces[0].shape[3:]
    shape = (2, components, lanes, matrix.shape[3])
    vmem = pl.BlockSpec(memory_space=pltpu.VMEM)
    return pl.pallas_call(
        functools.partial(frequency_kernel, order),
        in_specs=[pl.BlockSpec(memory_space=pltpu.SMEM)] + [vmem] * (1 + len(pieces)),
        out_specs=pl.BlockSpec(memory_space=pltpu.HBM),
        out_shape=jax.ShapeDtypeStruct(shape, jnp.float32),
        scratch_shapes=[pltpu.VMEM(shape, jnp.float32), pltpu.SemaphoreType.DMA((components // 2,))],
        compiler_params=pltpu.CompilerParams(vmem_limit_bytes=40 << 20),
        name="to_frequencies",
    )(me, matrix, *pieces)


def swap(pieces, order, devices):
    near = pieces[0]
    size = near.shape[0]
    groups = [list(range(start, start + size)) for start in range(0, devices, size)]
    moved = []
    for piece, slot in zip(pieces[1:], order):
        pairs = [(device, device ^ slot) for device in range(devices)]
        moved.append(lax.ppermute(piece, "kb", pairs))
    flat = near.reshape(size, -1, near.shape[-1])
    flat = lax.all_to_all(flat, "kb", split_axis=0, concat_axis=0, tiled=True, axis_index_groups=groups)
    return [flat.reshape(near.shape)] + moved


def trig_pair(angle_int, period, scale):
    angle = 2.0 * math.pi / period * angle_int.astype(jnp.float32)
    return (scale * jnp.cos(angle), scale * jnp.sin(angle))


def complex_combine(formula, cosine, sine, real_part, imag_part):
    first_term = jnp.einsum(formula, cosine, real_part + imag_part, precision=lax.Precision.HIGHEST)
    second_term = jnp.einsum(formula, cosine + sine, imag_part, precision=lax.Precision.HIGHEST)
    third_term = jnp.einsum(formula, sine - cosine, real_part, precision=lax.Precision.HIGHEST)
    return (first_term - second_term, first_term + third_term)


def forward_imaginary_time(tau_rows, frequency_count):
    freq_index = jnp.arange(frequency_count, dtype=jnp.int32)
    angle_int = (
        (2 * freq_index[None, :] - frequency_count + 1)
        * (2 * tau_rows[:, None] + 1)
        % (4 * frequency_count)
    )
    cosine, sine = trig_pair(angle_int, 4 * frequency_count, frequency_count ** (-0.5))
    return (cosine, -sine)


def tau_backward(tau_rows, frequency_count):
    freq_index = jnp.arange(frequency_count, dtype=jnp.int32)
    angle_int = (
        (freq_index[:, None] - frequency_count // 2)
        * (2 * tau_rows[None, :] + 1)
        % (2 * frequency_count)
    )
    return trig_pair(angle_int, 2 * frequency_count, frequency_count ** (-0.5))


def grid_transform(real_part, imag_part, grid_side, direction):
    shape = real_part.shape
    plane = jnp.arange(grid_side * grid_side, dtype=jnp.int32)
    upper = plane // grid_side
    lower = plane % grid_side
    plane_int = (upper[:, None] * upper[None, :] + lower[:, None] * lower[None, :]) % grid_side
    plane_cos, plane_sin = trig_pair(plane_int, grid_side, 1.0 / grid_side)
    line = jnp.arange(grid_side, dtype=jnp.int32)
    line_cos, line_sin = trig_pair(
        line[:, None] * line[None, :] % grid_side, grid_side, grid_side ** (-0.5)
    )
    real_part = real_part.reshape(shape[:-1] + (grid_side, grid_side * grid_side))
    imag_part = imag_part.reshape(shape[:-1] + (grid_side, grid_side * grid_side))
    real_part, imag_part = complex_combine(
        "pq,...xq->...xp", plane_cos, direction * plane_sin, real_part, imag_part
    )
    real_part, imag_part = complex_combine(
        "ax,...xp->...ap", line_cos, direction * line_sin, real_part, imag_part
    )
    return (real_part.reshape(shape), imag_part.reshape(shape))


def mirror_index(mirror_map, grid_side):
    index_x = mirror_map[0][:, None, None]
    index_y = mirror_map[1][None, :, None]
    index_z = mirror_map[2][None, None, :]
    return (index_x * grid_side * grid_side + index_y * grid_side + index_z).reshape(-1)


def bubble(gr_re, gr_im, mirror_re, mirror_im, pair_table, entries):
    entry_ids = jnp.arange(entries, dtype=jnp.int32)
    pick_left = (pair_table[:, 0][:, None] == entry_ids[None, :]).astype(jnp.float32)
    pick_right = (pair_table[:, 1][:, None] == entry_ids[None, :]).astype(jnp.float32)
    left_re = jnp.einsum("me,e...->m...", pick_left, gr_re, precision=lax.Precision.HIGHEST)
    left_im = jnp.einsum("me,e...->m...", pick_left, gr_im, precision=lax.Precision.HIGHEST)
    right_re = jnp.einsum("me,e...->m...", pick_right, mirror_re, precision=lax.Precision.HIGHEST)
    right_im = jnp.einsum("me,e...->m...", pick_right, mirror_im, precision=lax.Precision.HIGHEST)
    return (left_re * right_re - left_im * right_im, left_re * right_im + left_im * right_re)


def general(green_momentum_grid, pair_table, mirror_map):
    grid_side = mirror_map.shape[1]
    entries = green_momentum_grid.shape[1]
    frequency_count = green_momentum_grid.shape[3]
    position = jnp.arange(frequency_count, dtype=jnp.int32)
    fwd_cos, fwd_sin = forward_imaginary_time(position, frequency_count)
    tau_re, tau_im = complex_combine(
        "qa,fsa->fqs", fwd_cos, fwd_sin, green_momentum_grid[0], green_momentum_grid[1]
    )
    stacked = jnp.stack([tau_re, tau_im])

    def to_real_space(pieces):
        space_re, space_im = grid_transform(pieces[0], pieces[1], grid_side, 1.0)
        return jnp.stack([space_re, space_im])

    mirror_flat = mirror_index(mirror_map, grid_side)
    partner_rows = frequency_count - 1 - position
    reflected_cosine, reflected_sine = forward_imaginary_time(partner_rows, frequency_count)
    partner_real, partner_imaginary = complex_combine(
        "qa,fsa->fqs",
        reflected_cosine,
        reflected_sine,
        green_momentum_grid[0],
        green_momentum_grid[1],
    )
    other_stacked = jnp.stack([partner_real, partner_imaginary])
    pieces = (
        lax.all_to_all(stacked, "kb", split_axis=2, concat_axis=3, tiled=True),
        lax.all_to_all(other_stacked, "kb", split_axis=2, concat_axis=3, tiled=True),
    )
    in_cells = to_real_space(pieces[0])
    partner = to_real_space(pieces[1])
    mirrored = jnp.take(partner, mirror_flat, axis=3)
    chi_re, chi_im = bubble(in_cells[0], in_cells[1], mirrored[0], mirrored[1], pair_table, entries)
    chi_re, chi_im = grid_transform(chi_re, chi_im, grid_side, -1.0)
    momenta = jnp.stack([chi_re, chi_im])
    back_cos, back_sin = tau_backward(position, frequency_count)
    pieces = lax.all_to_all(momenta, "kb", split_axis=3, concat_axis=2, tiled=True)
    out_re, out_im = complex_combine("vj,ejk->ekv", back_cos, back_sin, pieces[0], pieces[1])
    return jnp.stack([out_re, out_im])


def local(green, pair_table, mirror_map):
    side = mirror_map.shape[1]
    plane = side * side
    lanes, count = green.shape[2], green.shape[3]
    devices = side * plane // lanes
    pairs = count // (2 * devices)
    if lanes != LANES or pairs != ROWS or 2 * lanes != plane:
        return general(green, pair_table, mirror_map)
    rows = np.arange(devices * pairs)
    shape = (2, devices, pairs, count)
    forward = jnp.asarray(fermion_matrix(rows, count).reshape(shape).astype(np.float32))
    backward = jnp.asarray(boson_matrix(rows, count).reshape(shape).astype(np.float32))
    order = list(range(devices // 2, devices))
    me = lax.axis_index("kb").astype(jnp.int32).reshape(1)
    pieces = swap(to_times(green, forward, me, order), order, devices)
    pieces = swap(middle(pieces, pair_table, mirror_map, me, order), order, devices)
    return to_frequencies(pieces, backward, me, order)


def solution(mesh):
    placed = (P("set", None, "kb", None), P(), P("set", None))
    return jax.shard_map(
        local, mesh=mesh, in_specs=placed, out_specs=P("set", None, "kb", None), check_vma=False
    )
```

```python
import functools
import math

import jax
import jax.numpy as jnp
import ml_dtypes
import numpy as np
from jax import lax
from jax.experimental import pallas as pl
from jax.experimental.pallas import tpu as pltpu
from jax.sharding import PartitionSpec as P

LANES = 128
ROWS = 8
GROUPS = 2


def split_constant(matrix):
    high = matrix.astype(np.float32).astype(ml_dtypes.bfloat16)
    low = (matrix - high.astype(np.float64)).astype(np.float32).astype(ml_dtypes.bfloat16)
    return high, low


def split_value(value):
    high = value.astype(jnp.bfloat16)
    low = (value - high.astype(jnp.float32)).astype(jnp.bfloat16)
    return high, low


def dot3(left, right, dims):
    (k_left,), (k_right,) = dims
    a = jnp.concatenate([left[0], left[0], left[1]], axis=k_left)
    b = jnp.concatenate([right[0], right[1], right[0]], axis=k_right)
    return lax.dot_general(a, b, (dims, ((), ())), preferred_element_type=jnp.float32)


def fermion_matrix(rows, count):
    n = np.arange(count, dtype=np.int64)
    angle = ((2 * n[None, :] - count + 1) * (2 * rows[:, None] + 1)) % (4 * count)
    angle = np.pi * angle / (2 * count)
    return np.concatenate([np.cos(angle), np.sin(angle)], axis=0) * count**-0.5


def boson_matrix(rows, count):
    v = np.arange(count, dtype=np.int64)
    angle = ((v[None, :] - count // 2) * (2 * rows[:, None] + 1)) % (2 * count)
    angle = np.pi * angle / count
    return np.concatenate([np.cos(angle), np.sin(angle)], axis=0) * count**-0.5


def plane_parts(side):
    p = np.arange(side * side, dtype=np.int64)
    angle = ((p[:, None] // side) * (p[None, :] // side) + (p[:, None] % side) * (p[None, :] % side)) % side
    angle = 2 * np.pi * angle / side
    scale = side**-1.5
    return np.cos(angle) * scale, np.sin(angle) * scale


def times_w4(re, im, power, sign):
    power = (power * sign) % 4
    if power == 0:
        return re, im
    if power == 1:
        return -im, re
    if power == 2:
        return -re, -im
    return im, -re


def dft4(values, sign):
    (r0, i0), (r1, i1), (r2, i2), (r3, i3) = values
    sr, si, dr, di = r0 + r2, i0 + i2, r0 - r2, i0 - i2
    tr, ti, er, ei = r1 + r3, i1 + i3, r1 - r3, i1 - i3
    if sign > 0:
        return [(sr + tr, si + ti), (dr - ei, di + er), (sr - tr, si - ti), (dr + ei, di - er)]
    return [(sr + tr, si + ti), (dr + ei, di - er), (sr - tr, si - ti), (dr - ei, di + er)]


def twiddle(value, power, sign, side):
    re, im = value
    if power % (side // 4) == 0:
        return times_w4(re, im, power // (side // 4), sign)
    angle = 2.0 * np.pi * power / side
    c, s = float(np.cos(angle)), float(sign * np.sin(angle))
    return re * c - im * s, re * s + im * c


def dft_line(values, sign):
    side = len(values)
    if side == 1:
        return values
    if side == 2:
        (r0, i0), (r1, i1) = values
        return [(r0 + r1, i0 + i1), (r0 - r1, i0 - i1)]
    if side == 4:
        return dft4(values, sign)
    inner = side // 4
    parts = [dft_line(values[b::4], sign) for b in range(4)]
    out = [None] * side
    for k1 in range(inner):
        column = [twiddle(parts[b][k1], b * k1, sign, side) for b in range(4)]
        for k2, value in enumerate(dft4(column, sign)):
            out[k1 + inner * k2] = value
    return out


def half_line(values, sign, parity):
    side = len(values)
    inner = side // 4
    parts = [dft_line(values[b::4], sign) for b in range(4)]
    out = [None] * (side // 2)
    for k1 in range(inner):
        column = [twiddle(parts[b][k1], b * k1, sign, side) for b in range(4)]
        column = [(re * parity, im * parity) if b % 2 else (re, im) for b, (re, im) in enumerate(column)]
        for k2, value in enumerate(dft4(column, sign)[:2]):
            out[k1 + inner * k2] = value
    return out


def times_kernel(g_hbm, m_hbm, out_ref, g_ref, m_ref, stage, in_sems, m_sem, out_sems):
    entries, lanes = g_ref.shape[1:3]
    near, _, _, _, rows, _ = stage.shape
    half = near * rows
    load = pltpu.make_async_copy(m_hbm, m_ref, m_sem)
    pieces = [
        pltpu.make_async_copy(g_hbm.at[:, pl.ds(e, 1)], g_ref.at[:, pl.ds(e, 1)], in_sems.at[e])
        for e in range(entries)
    ]
    for copy in [load] + pieces:
        copy.start()
    load.wait()
    matrix = split_value(m_ref[...])
    copies = []
    for e in range(entries):
        pieces[e].wait()
        g = jnp.concatenate([g_ref[0, e], g_ref[1, e]], axis=0)
        d = dot3(matrix, split_value(g), ((1,), (1,)))
        c_re, c_im = d[:half, :lanes], d[:half, lanes:]
        s_re, s_im = d[half:, :lanes], d[half:, lanes:]
        for where, value in (
            ((0, 0), c_re + s_im),
            ((0, 1), c_im - s_re),
            ((1, 0), s_im - c_re),
            ((1, 1), -(c_im + s_re)),
        ):
            stage[:, where[0], where[1], e] = value.reshape(near, rows, lanes)
        cut = pl.ds(e, 1)
        for side in range(2):
            target = out_ref.at[pl.ds(side * near, near), :, :, cut]
            copies.append(pltpu.make_async_copy(stage.at[:, :, :, cut], target, out_sems.at[e, side]))
            copies[-1].start()
    for copy in copies:
        copy.wait()


def to_times(green, matrix, near):
    _, entries, lanes, _ = green.shape
    shape = (near, 2, 2, entries, ROWS, lanes)
    hbm = pl.BlockSpec(memory_space=pltpu.HBM)
    return pl.pallas_call(
        times_kernel,
        in_specs=[hbm, hbm],
        out_specs=hbm,
        out_shape=jax.ShapeDtypeStruct((2 * near,) + shape[1:], jnp.float32),
        scratch_shapes=[
            pltpu.VMEM(green.shape, jnp.float32),
            pltpu.VMEM(matrix.shape, jnp.float32),
            pltpu.VMEM(shape, jnp.float32),
            pltpu.SemaphoreType.DMA((entries,)),
            pltpu.SemaphoreType.DMA,
            pltpu.SemaphoreType.DMA((entries, 2)),
        ],
        compiler_params=pltpu.CompilerParams(vmem_limit_bytes=60 << 20),
        name="to_times",
    )(green, matrix)


def fill_block(ref, cosine, sine):
    plane = cosine.shape[0]
    lanes = plane // 2
    for block in range(2):
        cut = slice(block * lanes, (block + 1) * lanes)
        re = slice(2 * block * lanes, (2 * block + 1) * lanes)
        im = slice((2 * block + 1) * lanes, (2 * block + 2) * lanes)
        ref[:plane, re] = cosine[:, cut].astype(jnp.bfloat16)
        ref[plane:, im] = cosine[:, cut].astype(jnp.bfloat16)
        ref[:plane, im] = sine[:, cut].astype(jnp.bfloat16)
        ref[plane:, re] = (-sine[:, cut]).astype(jnp.bfloat16)


def middle_kernel(me_ref, table_ref, mirror_ref, index_ref, ch_ref, cl_ref, sh_ref, sl_ref, x_ref, *refs):
    outs, (forward, backward, mid, space, chi) = refs[:-5], refs[-5:]
    halves, _, side, _, entries, rows, lanes = space.shape
    plane = 2 * lanes
    units, _, kept, members, _, _ = chi.shape
    me, near = me_ref[0], len(outs)
    core, line = me % 2, me // 2 % kept
    parity = (1 - 2 * (me // near)).astype(jnp.float32)
    row = lax.broadcasted_iota(jnp.int32, (plane, plane), 0)
    pick = (row == index_ref[...]).astype(jnp.float32).astype(jnp.bfloat16)

    def dot(a, b):
        return jnp.dot(a, b, preferred_element_type=jnp.float32)

    def turned(value):
        return jnp.where(core == 0, value, jnp.concatenate([value[:, lanes:], value[:, :lanes]], axis=1))

    for part, (c_ref, s_ref) in enumerate(((ch_ref, sh_ref), (cl_ref, sl_ref))):
        cosine, sine = c_ref[...].astype(jnp.float32), s_ref[...].astype(jnp.float32)
        fill_block(forward.at[0, part], cosine, sine)
        fill_block(backward.at[0, part], turned(cosine), turned(-sine))
        fill_block(forward.at[1, part], dot(c_ref[...], pick), dot(s_ref[...], pick))
        fill_block(backward.at[1, part], turned(dot(pick, c_ref[...])), turned(-dot(pick, s_ref[...])))

    def plane_dot(value, matrix, half, block):
        cut = slice(2 * block * lanes, 2 * (block + 1) * lanes)
        return dot3(value, (matrix[half, 0, :, cut], matrix[half, 1, :, cut]), ((1,), (0,)))

    def arrive(half):
        columns = [
            x_ref[:, h, half, ri].reshape(side * entries * rows, lanes) for ri in range(2) for h in range(2)
        ]
        return split_value(jnp.concatenate(columns, axis=1))

    def to_plane(value, half, block):
        d = plane_dot(value, forward, half, block)
        for ri in range(2):
            piece = d[:, ri * lanes : (ri + 1) * lanes]
            mid[half, block, ri] = piece.reshape(side, entries, rows, lanes)

    def along_line(half, block, e):
        values = [(mid[half, block, 0, x, e], mid[half, block, 1, x, e]) for x in range(side)]
        for x, (re, im) in enumerate(dft_line(values, 1)):
            space[half, block, x, 0, e] = re
            space[half, block, x, 1, e] = im

    def product(unit, block, c):
        half, first = unit % halves, unit // halves * members
        left, right = table_ref[first + c, 0], table_ref[first + c, 1]
        values = []
        for x in range(side):
            other = mirror_ref[0, x]
            a_re, a_im = space[half, block, x, 0, left], space[half, block, x, 1, left]
            b_re, b_im = space[1 - half, block, other, 0, right], space[1 - half, block, other, 1, right]
            values.append((a_re * b_re - a_im * b_im, a_re * b_im + a_im * b_re))
        cut = slice(block * lanes, (block + 1) * lanes)
        for x, (re, im) in enumerate(half_line(values, -1, parity)):
            chi[unit, 0, x ^ line, c, :, cut] = re
            chi[unit, 1, x ^ line, c, :, cut] = im

    def from_plane(unit, value, h):
        half, first = unit % halves, unit // halves * members
        d = plane_dot(value, backward, half, h)
        for ri in range(2):
            piece = d[:, ri * lanes : (ri + 1) * lanes].reshape(kept, members, rows, lanes)
            for x in range(kept):
                outs[2 * x + h][half, ri, first : first + members] = piece[x]

    def collect(unit):
        whole = (kept * members * rows, plane)
        return split_value(jnp.concatenate([chi[unit, ri].reshape(whole) for ri in range(2)], axis=1))

    places = [(half, block) for half in range(halves) for block in range(2)]
    for step in range(len(places) + 1):
        if step < len(places):
            half, block = places[step]
            if block == 0:
                value = arrive(half)
            to_plane(value, half, block)
        if step > 0:
            for e in range(entries):
                along_line(*places[step - 1], e)

    for unit in range(units + 1):
        tasks = [(block, c) for block in range(2) for c in range(members)] if unit < units else []
        if unit > 0:
            value = collect(unit - 1)
        for h in range(2):
            if unit > 0:
                from_plane(unit - 1, value, h)
            for block, c in tasks[h * members : (h + 1) * members]:
                product(unit, block, c)


def middle(x, table, mirror_map, me, near):
    devices, halves, _, entries, rows, lanes = x.shape
    plane = 2 * lanes
    side = devices // 2
    components = table.shape[0]
    members = components // GROUPS
    units = halves * GROUPS
    index = (mirror_map[1][:, None] * side + mirror_map[2][None, :]).reshape(1, plane)
    cosine, sine = plane_parts(side)
    parts = [jnp.asarray(part) for part in split_constant(cosine) + split_constant(sine)]
    smem = pl.BlockSpec(memory_space=pltpu.SMEM)
    vmem = pl.BlockSpec(memory_space=pltpu.VMEM)
    matrices = pltpu.VMEM((halves, 2, 2 * plane, 2 * plane), jnp.bfloat16)
    return pl.pallas_call(
        middle_kernel,
        in_specs=[smem, smem, smem] + [vmem] * 6,
        out_specs=[vmem] * near,
        out_shape=[jax.ShapeDtypeStruct((halves, 2, components, rows, lanes), jnp.float32)] * near,
        scratch_shapes=[
            matrices,
            matrices,
            pltpu.VMEM((halves, 2, 2, side, entries, rows, lanes), jnp.float32),
            pltpu.VMEM((halves, 2, side, 2, entries, rows, lanes), jnp.float32),
            pltpu.VMEM((units, 2, near // 2, members, rows, plane), jnp.float32),
        ],
        compiler_params=pltpu.CompilerParams(vmem_limit_bytes=28 << 20),
        name="middle",
    )(me, table, mirror_map, index, *parts, x.reshape((side, 2) + x.shape[1:]))


def frequency_kernel(near, me_ref, m_ref, *refs):
    pieces, (out_ref, stage, sems) = refs[:-3], refs[-3:]
    components, lanes = stage.shape[1:3]
    groups = sems.shape[0]
    members = components // groups
    sets = len(pieces) // near
    me = me_ref[0] % near
    rows = [
        m_ref[part, some * near + (slot ^ me)] for part in range(2) for some in range(sets) for slot in range(near)
    ]
    matrix = split_value(jnp.concatenate(rows, axis=0))

    def gathered(half, ri, c):
        return jnp.concatenate([piece[half, ri, c] for piece in pieces], axis=0)

    copies = []
    for group in range(groups):
        values = []
        for c in range(group * members, (group + 1) * members):
            part = [[gathered(half, ri, c) for ri in range(2)] for half in range(2)]
            sums = [part[0][ri] + part[1][ri] for ri in range(2)]
            differences = [part[0][ri] - part[1][ri] for ri in range(2)]
            values.append(jnp.concatenate([sums[0], -differences[1]], axis=0).T)
            values.append(jnp.concatenate([sums[1], differences[0]], axis=0).T)
        d = dot3(split_value(jnp.concatenate(values, axis=0)), matrix, ((1,), (0,)))
        d = d.reshape(members, 2, lanes, d.shape[1])
        for ri in range(2):
            stage[ri, group * members : (group + 1) * members] = d[:, ri]
        cut = pl.ds(group * members, members)
        copies.append(pltpu.make_async_copy(stage.at[:, cut], out_ref.at[:, cut], sems.at[group]))
        copies[-1].start()
    for copy in copies:
        copy.wait()


def to_frequencies(pieces, matrix, me, near):
    components, rows, lanes = pieces[0].shape[2:]
    shape = (2, components, lanes, matrix.shape[3])
    vmem = pl.BlockSpec(memory_space=pltpu.VMEM)
    return pl.pallas_call(
        functools.partial(frequency_kernel, near),
        in_specs=[pl.BlockSpec(memory_space=pltpu.SMEM)] + [vmem] * (1 + len(pieces)),
        out_specs=pl.BlockSpec(memory_space=pltpu.HBM),
        out_shape=jax.ShapeDtypeStruct(shape, jnp.float32),
        scratch_shapes=[pltpu.VMEM(shape, jnp.float32), pltpu.SemaphoreType.DMA((components // 2,))],
        compiler_params=pltpu.CompilerParams(vmem_limit_bytes=28 << 20),
        name="to_frequencies",
    )(me, matrix, *pieces)


def exchange(x):
    flat = x.reshape(x.shape[0], -1, x.shape[-1])
    return lax.all_to_all(flat, "kb", split_axis=0, concat_axis=0, tiled=True).reshape(x.shape)


def swap(pieces, devices):
    moved = [pieces[0]]
    for slot in range(1, len(pieces)):
        pairs = [(device, device ^ slot) for device in range(devices)]
        moved.append(lax.ppermute(pieces[slot], "kb", pairs))
    return moved


def trig_pair(angle_int, period, scale):
    angle = 2.0 * math.pi / period * angle_int.astype(jnp.float32)
    return (scale * jnp.cos(angle), scale * jnp.sin(angle))


def complex_combine(formula, cosine, sine, real_part, imag_part):
    first_term = jnp.einsum(formula, cosine, real_part + imag_part, precision=lax.Precision.HIGHEST)
    second_term = jnp.einsum(formula, cosine + sine, imag_part, precision=lax.Precision.HIGHEST)
    third_term = jnp.einsum(formula, sine - cosine, real_part, precision=lax.Precision.HIGHEST)
    return (first_term - second_term, first_term + third_term)


def forward_imaginary_time(tau_rows, frequency_count):
    freq_index = jnp.arange(frequency_count, dtype=jnp.int32)
    angle_int = (
        (2 * freq_index[None, :] - frequency_count + 1)
        * (2 * tau_rows[:, None] + 1)
        % (4 * frequency_count)
    )
    cosine, sine = trig_pair(angle_int, 4 * frequency_count, frequency_count ** (-0.5))
    return (cosine, -sine)


def tau_backward(tau_rows, frequency_count):
    freq_index = jnp.arange(frequency_count, dtype=jnp.int32)
    angle_int = (
        (freq_index[:, None] - frequency_count // 2)
        * (2 * tau_rows[None, :] + 1)
        % (2 * frequency_count)
    )
    return trig_pair(angle_int, 2 * frequency_count, frequency_count ** (-0.5))


def grid_transform(real_part, imag_part, grid_side, direction):
    shape = real_part.shape
    plane = jnp.arange(grid_side * grid_side, dtype=jnp.int32)
    upper = plane // grid_side
    lower = plane % grid_side
    plane_int = (upper[:, None] * upper[None, :] + lower[:, None] * lower[None, :]) % grid_side
    plane_cos, plane_sin = trig_pair(plane_int, grid_side, 1.0 / grid_side)
    line = jnp.arange(grid_side, dtype=jnp.int32)
    line_cos, line_sin = trig_pair(
        line[:, None] * line[None, :] % grid_side, grid_side, grid_side ** (-0.5)
    )
    real_part = real_part.reshape(shape[:-1] + (grid_side, grid_side * grid_side))
    imag_part = imag_part.reshape(shape[:-1] + (grid_side, grid_side * grid_side))
    real_part, imag_part = complex_combine(
        "pq,...xq->...xp", plane_cos, direction * plane_sin, real_part, imag_part
    )
    real_part, imag_part = complex_combine(
        "ax,...xp->...ap", line_cos, direction * line_sin, real_part, imag_part
    )
    return (real_part.reshape(shape), imag_part.reshape(shape))


def mirror_index(mirror_map, grid_side):
    index_x = mirror_map[0][:, None, None]
    index_y = mirror_map[1][None, :, None]
    index_z = mirror_map[2][None, None, :]
    return (index_x * grid_side * grid_side + index_y * grid_side + index_z).reshape(-1)


def bubble(gr_re, gr_im, mirror_re, mirror_im, pair_table, entries):
    entry_ids = jnp.arange(entries, dtype=jnp.int32)
    pick_left = (pair_table[:, 0][:, None] == entry_ids[None, :]).astype(jnp.float32)
    pick_right = (pair_table[:, 1][:, None] == entry_ids[None, :]).astype(jnp.float32)
    left_re = jnp.einsum("me,e...->m...", pick_left, gr_re, precision=lax.Precision.HIGHEST)
    left_im = jnp.einsum("me,e...->m...", pick_left, gr_im, precision=lax.Precision.HIGHEST)
    right_re = jnp.einsum("me,e...->m...", pick_right, mirror_re, precision=lax.Precision.HIGHEST)
    right_im = jnp.einsum("me,e...->m...", pick_right, mirror_im, precision=lax.Precision.HIGHEST)
    return (left_re * right_re - left_im * right_im, left_re * right_im + left_im * right_re)


def general(green_momentum_grid, pair_table, mirror_map):
    grid_side = mirror_map.shape[1]
    entries = green_momentum_grid.shape[1]
    frequency_count = green_momentum_grid.shape[3]
    position = jnp.arange(frequency_count, dtype=jnp.int32)
    fwd_cos, fwd_sin = forward_imaginary_time(position, frequency_count)
    tau_re, tau_im = complex_combine(
        "qa,fsa->fqs", fwd_cos, fwd_sin, green_momentum_grid[0], green_momentum_grid[1]
    )
    stacked = jnp.stack([tau_re, tau_im])

    def to_real_space(pieces):
        space_re, space_im = grid_transform(pieces[0], pieces[1], grid_side, 1.0)
        return jnp.stack([space_re, space_im])

    mirror_flat = mirror_index(mirror_map, grid_side)
    partner_rows = frequency_count - 1 - position
    reflected_cosine, reflected_sine = forward_imaginary_time(partner_rows, frequency_count)
    partner_real, partner_imaginary = complex_combine(
        "qa,fsa->fqs",
        reflected_cosine,
        reflected_sine,
        green_momentum_grid[0],
        green_momentum_grid[1],
    )
    other_stacked = jnp.stack([partner_real, partner_imaginary])
    pieces = (
        lax.all_to_all(stacked, "kb", split_axis=2, concat_axis=3, tiled=True),
        lax.all_to_all(other_stacked, "kb", split_axis=2, concat_axis=3, tiled=True),
    )
    in_cells = to_real_space(pieces[0])
    partner = to_real_space(pieces[1])
    mirrored = jnp.take(partner, mirror_flat, axis=3)
    chi_re, chi_im = bubble(in_cells[0], in_cells[1], mirrored[0], mirrored[1], pair_table, entries)
    chi_re, chi_im = grid_transform(chi_re, chi_im, grid_side, -1.0)
    momenta = jnp.stack([chi_re, chi_im])
    back_cos, back_sin = tau_backward(position, frequency_count)
    pieces = lax.all_to_all(momenta, "kb", split_axis=3, concat_axis=2, tiled=True)
    out_re, out_im = complex_combine("vj,ejk->ekv", back_cos, back_sin, pieces[0], pieces[1])
    return jnp.stack([out_re, out_im])


def local(green, pair_table, mirror_map):
    side = mirror_map.shape[1]
    plane = side * side
    lanes, count = green.shape[2], green.shape[3]
    devices = side * plane // lanes
    near = devices // 2
    sets = count // (2 * near * ROWS)
    if lanes != LANES or 2 * lanes != plane or sets * 2 * near * ROWS != count:
        return general(green, pair_table, mirror_map)
    rows = np.arange(count // 2)
    fermion = fermion_matrix(rows, count).reshape(2, sets, near * ROWS, count).swapaxes(0, 1)
    fermion = fermion.reshape(sets, 2 * near * ROWS, count).astype(np.float32)
    boson = boson_matrix(rows, count).reshape(2, sets * near, ROWS, count).astype(np.float32)
    me = lax.axis_index("kb").astype(jnp.int32).reshape(1)
    sent = []
    for some in range(sets):
        if sent:
            green, sent[-1] = lax.optimization_barrier((green, sent[-1]))
        sent.append(to_times(green, jnp.asarray(fermion[some]), near))
    returned = []
    for some in range(sets):
        x, returned, sent[some + 1 :] = lax.optimization_barrier((exchange(sent[some]), returned, sent[some + 1 :]))
        returned = returned + swap(middle(x, pair_table, mirror_map, me, near), devices)
    return to_frequencies(returned, jnp.asarray(boson), me, near)


def solution(mesh):
    placed = (P("set", None, "kb", None), P(), P("set", None))
    return jax.shard_map(
        local, mesh=mesh, in_specs=placed, out_specs=P("set", None, "kb", None), check_vma=False
    )
```

```python
import functools
import math

import jax
import jax.numpy as jnp
import ml_dtypes
import numpy as np
from jax import lax
from jax.experimental import pallas as pl
from jax.experimental.pallas import tpu as pltpu
from jax.sharding import PartitionSpec as P

LANES = 128
ROWS = 8
GROUPS = 2


def split_constant(matrix):
    high = matrix.astype(np.float32).astype(ml_dtypes.bfloat16)
    low = (matrix - high.astype(np.float64)).astype(np.float32).astype(ml_dtypes.bfloat16)
    return high, low


def split_value(value):
    high = value.astype(jnp.bfloat16)
    low = (value - high.astype(jnp.float32)).astype(jnp.bfloat16)
    return high, low


def dot3(left, right, dims):
    (k_left,), (k_right,) = dims
    a = jnp.concatenate([left[0], left[0], left[1]], axis=k_left)
    b = jnp.concatenate([right[0], right[1], right[0]], axis=k_right)
    return lax.dot_general(a, b, (dims, ((), ())), preferred_element_type=jnp.float32)


def fermion_matrix(rows, count):
    n = np.arange(count, dtype=np.int64)
    angle = ((2 * n[None, :] - count + 1) * (2 * rows[:, None] + 1)) % (4 * count)
    angle = np.pi * angle / (2 * count)
    return np.concatenate([np.cos(angle), np.sin(angle)], axis=0) * count**-0.5


def boson_matrix(rows, count):
    v = np.arange(count, dtype=np.int64)
    angle = ((v[None, :] - count // 2) * (2 * rows[:, None] + 1)) % (2 * count)
    angle = np.pi * angle / count
    return np.concatenate([np.cos(angle), np.sin(angle)], axis=0) * count**-0.5


def plane_parts(side):
    p = np.arange(side * side, dtype=np.int64)
    angle = ((p[:, None] // side) * (p[None, :] // side) + (p[:, None] % side) * (p[None, :] % side)) % side
    angle = 2 * np.pi * angle / side
    scale = side**-1.5
    return np.cos(angle) * scale, np.sin(angle) * scale


def times_w4(re, im, power, sign):
    power = (power * sign) % 4
    if power == 0:
        return re, im
    if power == 1:
        return -im, re
    if power == 2:
        return -re, -im
    return im, -re


def dft4(values, sign):
    (r0, i0), (r1, i1), (r2, i2), (r3, i3) = values
    sr, si, dr, di = r0 + r2, i0 + i2, r0 - r2, i0 - i2
    tr, ti, er, ei = r1 + r3, i1 + i3, r1 - r3, i1 - i3
    if sign > 0:
        return [(sr + tr, si + ti), (dr - ei, di + er), (sr - tr, si - ti), (dr + ei, di - er)]
    return [(sr + tr, si + ti), (dr + ei, di - er), (sr - tr, si - ti), (dr - ei, di + er)]


def twiddle(value, power, sign, side):
    re, im = value
    if power % (side // 4) == 0:
        return times_w4(re, im, power // (side // 4), sign)
    angle = 2.0 * np.pi * power / side
    c, s = float(np.cos(angle)), float(sign * np.sin(angle))
    return re * c - im * s, re * s + im * c


def dft_line(values, sign):
    side = len(values)
    if side == 1:
        return values
    if side == 2:
        (r0, i0), (r1, i1) = values
        return [(r0 + r1, i0 + i1), (r0 - r1, i0 - i1)]
    if side == 4:
        return dft4(values, sign)
    inner = side // 4
    parts = [dft_line(values[b::4], sign) for b in range(4)]
    out = [None] * side
    for k1 in range(inner):
        column = [twiddle(parts[b][k1], b * k1, sign, side) for b in range(4)]
        for k2, value in enumerate(dft4(column, sign)):
            out[k1 + inner * k2] = value
    return out


def half_line(values, sign, parity):
    side = len(values)
    inner = side // 4
    parts = [dft_line(values[b::4], sign) for b in range(4)]
    out = [None] * (side // 2)
    for k1 in range(inner):
        column = [twiddle(parts[b][k1], b * k1, sign, side) for b in range(4)]
        column = [(re * parity, im * parity) if b % 2 else (re, im) for b, (re, im) in enumerate(column)]
        for k2, value in enumerate(dft4(column, sign)[:2]):
            out[k1 + inner * k2] = value
    return out


def load_inputs(g_hbm, m_hbm, g_ref, m_ref, in_sems, m_sem):
    load = pltpu.make_async_copy(m_hbm, m_ref, m_sem)
    pieces = [
        pltpu.make_async_copy(g_hbm.at[:, pl.ds(e, 1)], g_ref.at[:, pl.ds(e, 1)], in_sems.at[e])
        for e in range(g_ref.shape[1])
    ]
    for copy in [load] + pieces:
        copy.start()
    load.wait()
    return pieces


def sums_of(matrix, g_ref, e):
    lanes = g_ref.shape[2]
    g = jnp.concatenate([g_ref[0, e], g_ref[1, e]], axis=0)
    d = dot3(matrix, split_value(g), ((1,), (1,)))
    half = d.shape[0] // 2
    return d[:half, :lanes], d[:half, lanes:], d[half:, :lanes], d[half:, lanes:]


def both_times_kernel(g_hbm, m_hbm, out_ref, g_ref, m_ref, stage, in_sems, m_sem, out_sems):
    entries, lanes = g_ref.shape[1:3]
    near, _, _, _, rows, _ = stage.shape
    pieces = load_inputs(g_hbm, m_hbm, g_ref, m_ref, in_sems, m_sem)
    matrix = split_value(m_ref[...])
    copies = []
    for e in range(entries):
        pieces[e].wait()
        c_re, c_im, s_re, s_im = sums_of(matrix, g_ref, e)
        for where, value in (
            ((0, 0), c_re + s_im),
            ((0, 1), c_im - s_re),
            ((1, 0), s_im - c_re),
            ((1, 1), -(c_im + s_re)),
        ):
            stage[:, where[0], where[1], e] = value.reshape(near, rows, lanes)
        cut = pl.ds(e, 1)
        for side in range(2):
            target = out_ref.at[pl.ds(side * near, near), :, :, cut]
            copies.append(pltpu.make_async_copy(stage.at[:, :, :, cut], target, out_sems.at[e, side]))
            copies[-1].start()
    for copy in copies:
        copy.wait()


def one_times_kernel(g_hbm, m_hbm, out_ref, g_ref, m_ref, stage, in_sems, m_sem, out_sems):
    entries, lanes = g_ref.shape[1:3]
    devices, _, _, rows, _ = stage.shape
    pieces = load_inputs(g_hbm, m_hbm, g_ref, m_ref, in_sems, m_sem)
    matrix = split_value(m_ref[...])
    copies = []
    for e in range(entries):
        pieces[e].wait()
        c_re, c_im, s_re, s_im = sums_of(matrix, g_ref, e)
        stage[:, 0, e] = (c_re + s_im).reshape(devices, rows, lanes)
        stage[:, 1, e] = (c_im - s_re).reshape(devices, rows, lanes)
        cut = pl.ds(e, 1)
        copies.append(pltpu.make_async_copy(stage.at[:, :, cut], out_ref.at[:, :, cut], out_sems.at[e, 0]))
        copies[-1].start()
    for copy in copies:
        copy.wait()


def to_times(kernel, green, matrix, shape, targets, name):
    entries = green.shape[1]
    hbm = pl.BlockSpec(memory_space=pltpu.HBM)
    return pl.pallas_call(
        kernel,
        in_specs=[hbm, hbm],
        out_specs=hbm,
        out_shape=jax.ShapeDtypeStruct((targets,) + shape[1:], jnp.float32),
        scratch_shapes=[
            pltpu.VMEM(green.shape, jnp.float32),
            pltpu.VMEM(matrix.shape, jnp.float32),
            pltpu.VMEM(shape, jnp.float32),
            pltpu.SemaphoreType.DMA((entries,)),
            pltpu.SemaphoreType.DMA,
            pltpu.SemaphoreType.DMA((entries, 2)),
        ],
        compiler_params=pltpu.CompilerParams(vmem_limit_bytes=60 << 20),
        name=name,
    )(green, matrix)


def fill_block(ref, cosine, sine):
    plane = cosine.shape[0]
    lanes = plane // 2
    for block in range(2):
        cut = slice(block * lanes, (block + 1) * lanes)
        re = slice(2 * block * lanes, (2 * block + 1) * lanes)
        im = slice((2 * block + 1) * lanes, (2 * block + 2) * lanes)
        ref[:plane, re] = cosine[:, cut].astype(jnp.bfloat16)
        ref[plane:, im] = cosine[:, cut].astype(jnp.bfloat16)
        ref[:plane, im] = sine[:, cut].astype(jnp.bfloat16)
        ref[plane:, re] = (-sine[:, cut]).astype(jnp.bfloat16)


def fill_matrices(index_ref, parts, forward, backward, turned):
    plane = parts[0].shape[0]
    row = lax.broadcasted_iota(jnp.int32, (plane, plane), 0)
    pick = (row == index_ref[...]).astype(jnp.float32).astype(jnp.bfloat16)

    def dot(a, b):
        return jnp.dot(a, b, preferred_element_type=jnp.float32)

    for part in range(2):
        c_ref, s_ref = parts[part], parts[2 + part]
        cosine, sine = c_ref[...].astype(jnp.float32), s_ref[...].astype(jnp.float32)
        fill_block(forward.at[0, part], cosine, sine)
        fill_block(backward.at[0, part], turned(cosine), turned(-sine))
        fill_block(forward.at[1, part], dot(c_ref[...], pick), dot(s_ref[...], pick))
        fill_block(backward.at[1, part], turned(dot(pick, c_ref[...])), turned(-dot(pick, s_ref[...])))


def plane_dot(value, matrix, half, block):
    width = matrix.shape[3] // 2
    cut = slice(block * width, (block + 1) * width)
    return dot3(value, (matrix[half, 0, :, cut], matrix[half, 1, :, cut]), ((1,), (0,)))


def one_middle_kernel(table_ref, mirror_ref, index_ref, ch_ref, cl_ref, sh_ref, sl_ref, x_ref, out_ref, *refs):
    forward, backward, mid, space, other_space, chi = refs
    _, side, _, entries, rows, lanes = space.shape
    plane = 2 * lanes
    groups, _, _, members, _, _ = chi.shape
    fill_matrices(index_ref, (ch_ref, cl_ref, sh_ref, sl_ref), forward, backward, lambda value: value)

    def select_dot(value, matrix, block):
        shape = (value[0].shape[0] // rows, rows, plane)
        first, second = (plane_dot(value, matrix, half, block).reshape(shape) for half in range(2))
        upper = lax.broadcasted_iota(jnp.int32, shape, 1) < rows // 2
        return jnp.where(upper, first, second)

    columns = [x_ref[:, h, ri].reshape(side * entries * rows, lanes) for ri in range(2) for h in range(2)]
    value = split_value(jnp.concatenate(columns, axis=1))
    for block in range(2):
        d = select_dot(value, forward, block)
        for ri in range(2):
            piece = d[:, :, ri * lanes : (ri + 1) * lanes]
            mid[block, ri] = piece.reshape(side, entries, rows, lanes)
    for block in range(2):
        for e in range(entries):
            values = [(mid[block, 0, x, e], mid[block, 1, x, e]) for x in range(side)]
            for x, parts in enumerate(dft_line(values, 1)):
                for ri in range(2):
                    space[block, x, ri, e] = parts[ri]
                    other_space[block, x, ri, e] = pltpu.roll(parts[ri], rows // 2, 0)

    for group in range(groups):
        for c in range(members):
            left, right = table_ref[group * members + c, 0], table_ref[group * members + c, 1]
            for block in range(2):
                values = []
                for x in range(side):
                    other = mirror_ref[0, x]
                    a_re, a_im = space[block, x, 0, left], space[block, x, 1, left]
                    b_re, b_im = other_space[block, other, 0, right], other_space[block, other, 1, right]
                    values.append((a_re * b_re - a_im * b_im, a_re * b_im + a_im * b_re))
                cut = slice(block * lanes, (block + 1) * lanes)
                for x, parts in enumerate(dft_line(values, -1)):
                    for ri in range(2):
                        chi[group, ri, x, c, :, cut] = parts[ri]
        whole = (side * members * rows, plane)
        value = split_value(jnp.concatenate([chi[group, ri].reshape(whole) for ri in range(2)], axis=1))
        for h in range(2):
            d = select_dot(value, backward, h)
            for ri in range(2):
                piece = d[:, :, ri * lanes : (ri + 1) * lanes].reshape(side, members, rows, lanes)
                out_ref[:, h, ri, group * members : (group + 1) * members] = piece


def both_middle_kernel(me_ref, table_ref, mirror_ref, index_ref, ch_ref, cl_ref, sh_ref, sl_ref, x_ref, *refs):
    outs, (forward, backward, mid, space, chi) = refs[:-5], refs[-5:]
    halves, _, side, _, entries, rows, lanes = space.shape
    plane = 2 * lanes
    units, _, kept, members, _, _ = chi.shape
    me, near = me_ref[0], len(outs)
    core, line = me % 2, me // 2 % kept
    parity = (1 - 2 * (me // near)).astype(jnp.float32)

    def turned(value):
        return jnp.where(core == 0, value, jnp.concatenate([value[:, lanes:], value[:, :lanes]], axis=1))

    fill_matrices(index_ref, (ch_ref, cl_ref, sh_ref, sl_ref), forward, backward, turned)

    def arrive(half):
        columns = [
            x_ref[:, h, half, ri].reshape(side * entries * rows, lanes) for ri in range(2) for h in range(2)
        ]
        return split_value(jnp.concatenate(columns, axis=1))

    def to_plane(value, half, block):
        d = plane_dot(value, forward, half, block)
        for ri in range(2):
            piece = d[:, ri * lanes : (ri + 1) * lanes]
            mid[half, block, ri] = piece.reshape(side, entries, rows, lanes)

    def along_line(half, block, e):
        values = [(mid[half, block, 0, x, e], mid[half, block, 1, x, e]) for x in range(side)]
        for x, (re, im) in enumerate(dft_line(values, 1)):
            space[half, block, x, 0, e] = re
            space[half, block, x, 1, e] = im

    def product(unit, block, c):
        half, first = unit % halves, unit // halves * members
        left, right = table_ref[first + c, 0], table_ref[first + c, 1]
        values = []
        for x in range(side):
            other = mirror_ref[0, x]
            a_re, a_im = space[half, block, x, 0, left], space[half, block, x, 1, left]
            b_re, b_im = space[1 - half, block, other, 0, right], space[1 - half, block, other, 1, right]
            values.append((a_re * b_re - a_im * b_im, a_re * b_im + a_im * b_re))
        cut = slice(block * lanes, (block + 1) * lanes)
        for x, (re, im) in enumerate(half_line(values, -1, parity)):
            chi[unit, 0, x ^ line, c, :, cut] = re
            chi[unit, 1, x ^ line, c, :, cut] = im

    def from_plane(unit, value, h):
        half, first = unit % halves, unit // halves * members
        d = plane_dot(value, backward, half, h)
        for ri in range(2):
            piece = d[:, ri * lanes : (ri + 1) * lanes].reshape(kept, members, rows, lanes)
            for x in range(kept):
                outs[2 * x + h][half, ri, first : first + members] = piece[x]

    def collect(unit):
        whole = (kept * members * rows, plane)
        return split_value(jnp.concatenate([chi[unit, ri].reshape(whole) for ri in range(2)], axis=1))

    places = [(half, block) for half in range(halves) for block in range(2)]
    for step in range(len(places) + 1):
        if step < len(places):
            half, block = places[step]
            if block == 0:
                value = arrive(half)
            to_plane(value, half, block)
        if step > 0:
            for e in range(entries):
                along_line(*places[step - 1], e)

    for unit in range(units + 1):
        tasks = [(block, c) for block in range(2) for c in range(members)] if unit < units else []
        if unit > 0:
            value = collect(unit - 1)
        for h in range(2):
            if unit > 0:
                from_plane(unit - 1, value, h)
            for block, c in tasks[h * members : (h + 1) * members]:
                product(unit, block, c)


def middle_inputs(table, mirror_map, x):
    side, plane = x.shape[0] // 2, 2 * x.shape[-1]
    index = (mirror_map[1][:, None] * side + mirror_map[2][None, :]).reshape(1, plane)
    cosine, sine = plane_parts(side)
    parts = [jnp.asarray(part) for part in split_constant(cosine) + split_constant(sine)]
    smem = pl.BlockSpec(memory_space=pltpu.SMEM)
    vmem = pl.BlockSpec(memory_space=pltpu.VMEM)
    args = (table, mirror_map, index, *parts, x.reshape((side, 2) + x.shape[1:]))
    return args, [smem, smem] + [vmem] * 6, pltpu.VMEM((2, 2, 2 * plane, 2 * plane), jnp.bfloat16)


def one_middle(x, table, mirror_map):
    devices, _, entries, rows, lanes = x.shape
    side, components = devices // 2, table.shape[0]
    args, specs, matrices = middle_inputs(table, mirror_map, x)
    spatial = pltpu.VMEM((2, side, 2, entries, rows, lanes), jnp.float32)
    shape = (side, 2, 2, components, rows, lanes)
    out = pl.pallas_call(
        one_middle_kernel,
        in_specs=specs,
        out_specs=pl.BlockSpec(memory_space=pltpu.VMEM),
        out_shape=jax.ShapeDtypeStruct(shape, jnp.float32),
        scratch_shapes=[
            matrices,
            matrices,
            pltpu.VMEM((2, 2, side, entries, rows, lanes), jnp.float32),
            spatial,
            spatial,
            pltpu.VMEM((GROUPS, 2, side, components // GROUPS, rows, 2 * lanes), jnp.float32),
        ],
        compiler_params=pltpu.CompilerParams(vmem_limit_bytes=28 << 20),
        name="one_middle",
    )(*args)
    return out.reshape((devices,) + shape[2:])


def both_middle(x, table, mirror_map, me, near):
    devices, halves, _, entries, rows, lanes = x.shape
    side, components = devices // 2, table.shape[0]
    args, specs, matrices = middle_inputs(table, mirror_map, x)
    members = components // GROUPS
    return pl.pallas_call(
        both_middle_kernel,
        in_specs=[pl.BlockSpec(memory_space=pltpu.SMEM)] + specs,
        out_specs=[pl.BlockSpec(memory_space=pltpu.VMEM)] * near,
        out_shape=[jax.ShapeDtypeStruct((halves, 2, components, rows, lanes), jnp.float32)] * near,
        scratch_shapes=[
            matrices,
            matrices,
            pltpu.VMEM((halves, 2, 2, side, entries, rows, lanes), jnp.float32),
            pltpu.VMEM((halves, 2, side, 2, entries, rows, lanes), jnp.float32),
            pltpu.VMEM((halves * GROUPS, 2, near // 2, members, rows, 2 * lanes), jnp.float32),
        ],
        compiler_params=pltpu.CompilerParams(vmem_limit_bytes=28 << 20),
        name="both_middle",
    )(me, *args)


def frequency_kernel(me_ref, both_ref, one_ref, y_ref, *refs):
    pieces, (out_ref, stage, sems) = refs[:-3], refs[-3:]
    near = len(pieces)
    devices, _, components, rows, lanes = y_ref.shape
    groups = sems.shape[0]
    members = components // groups
    me = me_ref[0] % near
    both = [both_ref[part, slot ^ me] for part in range(2) for slot in range(near)]
    matrix = split_value(jnp.concatenate(both + [one_ref[...]], axis=0))
    upper_rows = lax.broadcasted_iota(jnp.int32, (devices, rows, lanes), 1) < rows // 2

    def gathered(half, ri, c):
        return jnp.concatenate([piece[half, ri, c] for piece in pieces], axis=0)

    copies = []
    for group in range(groups):
        values = []
        for c in range(group * members, (group + 1) * members):
            part = [[gathered(half, ri, c) for ri in range(2)] for half in range(2)]
            sums = [part[0][ri] + part[1][ri] for ri in range(2)]
            differences = [part[0][ri] - part[1][ri] for ri in range(2)]
            folded = []
            for ri in range(2):
                tile = y_ref[:, ri, c]
                turned = pltpu.roll(tile, rows // 2, 1)
                folded.append((tile + turned, turned - tile))
            first = jnp.where(upper_rows, folded[0][0], -folded[1][1]).reshape(devices * rows, lanes)
            second = jnp.where(upper_rows, folded[1][0], folded[0][1]).reshape(devices * rows, lanes)
            values.append(jnp.concatenate([sums[0], -differences[1], first], axis=0).T)
            values.append(jnp.concatenate([sums[1], differences[0], second], axis=0).T)
        d = dot3(split_value(jnp.concatenate(values, axis=0)), matrix, ((1,), (0,)))
        d = d.reshape(members, 2, lanes, d.shape[1])
        for ri in range(2):
            stage[ri, group * members : (group + 1) * members] = d[:, ri]
        cut = pl.ds(group * members, members)
        copies.append(pltpu.make_async_copy(stage.at[:, cut], out_ref.at[:, cut], sems.at[group]))
        copies[-1].start()
    for copy in copies:
        copy.wait()


def to_frequencies(y, pieces, both, one, me):
    _, _, components, _, lanes = y.shape
    shape = (2, components, lanes, one.shape[1])
    vmem = pl.BlockSpec(memory_space=pltpu.VMEM)
    return pl.pallas_call(
        frequency_kernel,
        in_specs=[pl.BlockSpec(memory_space=pltpu.SMEM)] + [vmem] * (3 + len(pieces)),
        out_specs=pl.BlockSpec(memory_space=pltpu.HBM),
        out_shape=jax.ShapeDtypeStruct(shape, jnp.float32),
        scratch_shapes=[pltpu.VMEM(shape, jnp.float32), pltpu.SemaphoreType.DMA((components // 2,))],
        compiler_params=pltpu.CompilerParams(vmem_limit_bytes=28 << 20),
        name="to_frequencies",
    )(me, both, one, y, *pieces)


def exchange(x):
    flat = x.reshape(x.shape[0], -1, x.shape[-1])
    return lax.all_to_all(flat, "kb", split_axis=0, concat_axis=0, tiled=True).reshape(x.shape)


def swap(pieces, devices):
    moved = [pieces[0]]
    for slot in range(1, len(pieces)):
        pairs = [(device, device ^ slot) for device in range(devices)]
        moved.append(lax.ppermute(pieces[slot], "kb", pairs))
    return moved


def trig_pair(angle_int, period, scale):
    angle = 2.0 * math.pi / period * angle_int.astype(jnp.float32)
    return (scale * jnp.cos(angle), scale * jnp.sin(angle))


def complex_combine(formula, cosine, sine, real_part, imag_part):
    first_term = jnp.einsum(formula, cosine, real_part + imag_part, precision=lax.Precision.HIGHEST)
    second_term = jnp.einsum(formula, cosine + sine, imag_part, precision=lax.Precision.HIGHEST)
    third_term = jnp.einsum(formula, sine - cosine, real_part, precision=lax.Precision.HIGHEST)
    return (first_term - second_term, first_term + third_term)


def forward_imaginary_time(tau_rows, frequency_count):
    freq_index = jnp.arange(frequency_count, dtype=jnp.int32)
    angle_int = (
        (2 * freq_index[None, :] - frequency_count + 1)
        * (2 * tau_rows[:, None] + 1)
        % (4 * frequency_count)
    )
    cosine, sine = trig_pair(angle_int, 4 * frequency_count, frequency_count ** (-0.5))
    return (cosine, -sine)


def tau_backward(tau_rows, frequency_count):
    freq_index = jnp.arange(frequency_count, dtype=jnp.int32)
    angle_int = (
        (freq_index[:, None] - frequency_count // 2)
        * (2 * tau_rows[None, :] + 1)
        % (2 * frequency_count)
    )
    return trig_pair(angle_int, 2 * frequency_count, frequency_count ** (-0.5))


def grid_transform(real_part, imag_part, grid_side, direction):
    shape = real_part.shape
    plane = jnp.arange(grid_side * grid_side, dtype=jnp.int32)
    upper = plane // grid_side
    lower = plane % grid_side
    plane_int = (upper[:, None] * upper[None, :] + lower[:, None] * lower[None, :]) % grid_side
    plane_cos, plane_sin = trig_pair(plane_int, grid_side, 1.0 / grid_side)
    line = jnp.arange(grid_side, dtype=jnp.int32)
    line_cos, line_sin = trig_pair(
        line[:, None] * line[None, :] % grid_side, grid_side, grid_side ** (-0.5)
    )
    real_part = real_part.reshape(shape[:-1] + (grid_side, grid_side * grid_side))
    imag_part = imag_part.reshape(shape[:-1] + (grid_side, grid_side * grid_side))
    real_part, imag_part = complex_combine(
        "pq,...xq->...xp", plane_cos, direction * plane_sin, real_part, imag_part
    )
    real_part, imag_part = complex_combine(
        "ax,...xp->...ap", line_cos, direction * line_sin, real_part, imag_part
    )
    return (real_part.reshape(shape), imag_part.reshape(shape))


def mirror_index(mirror_map, grid_side):
    index_x = mirror_map[0][:, None, None]
    index_y = mirror_map[1][None, :, None]
    index_z = mirror_map[2][None, None, :]
    return (index_x * grid_side * grid_side + index_y * grid_side + index_z).reshape(-1)


def bubble(gr_re, gr_im, mirror_re, mirror_im, pair_table, entries):
    entry_ids = jnp.arange(entries, dtype=jnp.int32)
    pick_left = (pair_table[:, 0][:, None] == entry_ids[None, :]).astype(jnp.float32)
    pick_right = (pair_table[:, 1][:, None] == entry_ids[None, :]).astype(jnp.float32)
    left_re = jnp.einsum("me,e...->m...", pick_left, gr_re, precision=lax.Precision.HIGHEST)
    left_im = jnp.einsum("me,e...->m...", pick_left, gr_im, precision=lax.Precision.HIGHEST)
    right_re = jnp.einsum("me,e...->m...", pick_right, mirror_re, precision=lax.Precision.HIGHEST)
    right_im = jnp.einsum("me,e...->m...", pick_right, mirror_im, precision=lax.Precision.HIGHEST)
    return (left_re * right_re - left_im * right_im, left_re * right_im + left_im * right_re)


def general(green_momentum_grid, pair_table, mirror_map):
    grid_side = mirror_map.shape[1]
    entries = green_momentum_grid.shape[1]
    frequency_count = green_momentum_grid.shape[3]
    position = jnp.arange(frequency_count, dtype=jnp.int32)
    fwd_cos, fwd_sin = forward_imaginary_time(position, frequency_count)
    tau_re, tau_im = complex_combine(
        "qa,fsa->fqs", fwd_cos, fwd_sin, green_momentum_grid[0], green_momentum_grid[1]
    )
    stacked = jnp.stack([tau_re, tau_im])

    def to_real_space(pieces):
        space_re, space_im = grid_transform(pieces[0], pieces[1], grid_side, 1.0)
        return jnp.stack([space_re, space_im])

    mirror_flat = mirror_index(mirror_map, grid_side)
    partner_rows = frequency_count - 1 - position
    reflected_cosine, reflected_sine = forward_imaginary_time(partner_rows, frequency_count)
    partner_real, partner_imaginary = complex_combine(
        "qa,fsa->fqs",
        reflected_cosine,
        reflected_sine,
        green_momentum_grid[0],
        green_momentum_grid[1],
    )
    other_stacked = jnp.stack([partner_real, partner_imaginary])
    pieces = (
        lax.all_to_all(stacked, "kb", split_axis=2, concat_axis=3, tiled=True),
        lax.all_to_all(other_stacked, "kb", split_axis=2, concat_axis=3, tiled=True),
    )
    in_cells = to_real_space(pieces[0])
    partner = to_real_space(pieces[1])
    mirrored = jnp.take(partner, mirror_flat, axis=3)
    chi_re, chi_im = bubble(in_cells[0], in_cells[1], mirrored[0], mirrored[1], pair_table, entries)
    chi_re, chi_im = grid_transform(chi_re, chi_im, grid_side, -1.0)
    momenta = jnp.stack([chi_re, chi_im])
    back_cos, back_sin = tau_backward(position, frequency_count)
    pieces = lax.all_to_all(momenta, "kb", split_axis=3, concat_axis=2, tiled=True)
    out_re, out_im = complex_combine("vj,ejk->ekv", back_cos, back_sin, pieces[0], pieces[1])
    return jnp.stack([out_re, out_im])


def local(green, pair_table, mirror_map):
    side = mirror_map.shape[1]
    plane = side * side
    lanes, count = green.shape[2], green.shape[3]
    devices = side * plane // lanes
    near = devices // 2
    half = ROWS // 2
    shared = near * ROWS
    if lanes != LANES or 2 * lanes != plane or 2 * (shared + devices * half) != count:
        return general(green, pair_table, mirror_map)
    me = lax.axis_index("kb").astype(jnp.int32).reshape(1)
    entries = green.shape[1]

    rows = np.arange(shared)
    both_fermion = fermion_matrix(rows, count).astype(np.float32)
    both_boson = boson_matrix(rows, count).reshape(2, near, ROWS, count).astype(np.float32)
    rows = shared + np.arange(devices * half).reshape(devices, half)
    times = np.concatenate([rows, count - 1 - rows], axis=1).reshape(-1)
    one_fermion = fermion_matrix(times, count).astype(np.float32)
    one_boson = boson_matrix(rows.reshape(-1), count).reshape(2, devices, half, count).swapaxes(0, 1)
    one_boson = one_boson.reshape(devices * ROWS, count).astype(np.float32)

    shape = (devices, 2, entries, ROWS, lanes)
    one = to_times(one_times_kernel, green, jnp.asarray(one_fermion), shape, devices, "one_times")
    green, one = lax.optimization_barrier((green, one))
    shape = (near, 2, 2, entries, ROWS, lanes)
    both = to_times(both_times_kernel, green, jnp.asarray(both_fermion), shape, devices, "both_times")
    one, both = lax.optimization_barrier((exchange(one), both))
    one, both = lax.optimization_barrier((one_middle(one, pair_table, mirror_map), exchange(both)))
    pieces = swap(both_middle(both, pair_table, mirror_map, me, near), devices)
    return to_frequencies(exchange(one), pieces, jnp.asarray(both_boson), jnp.asarray(one_boson), me)


def solution(mesh):
    placed = (P("set", None, "kb", None), P(), P("set", None))
    return jax.shard_map(
        local, mesh=mesh, in_specs=placed, out_specs=P("set", None, "kb", None), check_vma=False
    )
```

```python
import functools
import math

import jax
import jax.numpy as jnp
import ml_dtypes
import numpy as np
from jax import lax
from jax.experimental import pallas as pl
from jax.experimental.pallas import tpu as pltpu
from jax.sharding import PartitionSpec as P

LANES = 128
ROWS = 8
GROUPS = 2


def split_constant(matrix):
    high = matrix.astype(np.float32).astype(ml_dtypes.bfloat16)
    low = (matrix - high.astype(np.float64)).astype(np.float32).astype(ml_dtypes.bfloat16)
    return high, low


def split_value(value):
    high = value.astype(jnp.bfloat16)
    low = (value - high.astype(jnp.float32)).astype(jnp.bfloat16)
    return high, low


def dot3(left, right, dims):
    (k_left,), (k_right,) = dims
    a = jnp.concatenate([left[0], left[0], left[1]], axis=k_left)
    b = jnp.concatenate([right[0], right[1], right[0]], axis=k_right)
    return lax.dot_general(a, b, (dims, ((), ())), preferred_element_type=jnp.float32)


def fermion_matrix(rows, count):
    n = np.arange(count, dtype=np.int64)
    angle = ((2 * n[None, :] - count + 1) * (2 * rows[:, None] + 1)) % (4 * count)
    angle = np.pi * angle / (2 * count)
    return np.concatenate([np.cos(angle), np.sin(angle)], axis=0) * count**-0.5


def boson_matrix(rows, count):
    v = np.arange(count, dtype=np.int64)
    angle = ((v[None, :] - count // 2) * (2 * rows[:, None] + 1)) % (2 * count)
    angle = np.pi * angle / count
    return np.concatenate([np.cos(angle), np.sin(angle)], axis=0) * count**-0.5


def plane_parts(side):
    p = np.arange(side * side, dtype=np.int64)
    angle = ((p[:, None] // side) * (p[None, :] // side) + (p[:, None] % side) * (p[None, :] % side)) % side
    angle = 2 * np.pi * angle / side
    scale = side**-1.5
    return np.cos(angle) * scale, np.sin(angle) * scale


def times_w4(re, im, power, sign):
    power = (power * sign) % 4
    if power == 0:
        return re, im
    if power == 1:
        return -im, re
    if power == 2:
        return -re, -im
    return im, -re


def dft4(values, sign):
    (r0, i0), (r1, i1), (r2, i2), (r3, i3) = values
    sr, si, dr, di = r0 + r2, i0 + i2, r0 - r2, i0 - i2
    tr, ti, er, ei = r1 + r3, i1 + i3, r1 - r3, i1 - i3
    if sign > 0:
        return [(sr + tr, si + ti), (dr - ei, di + er), (sr - tr, si - ti), (dr + ei, di - er)]
    return [(sr + tr, si + ti), (dr + ei, di - er), (sr - tr, si - ti), (dr - ei, di + er)]


def twiddle(value, power, sign, side):
    re, im = value
    if power % (side // 4) == 0:
        return times_w4(re, im, power // (side // 4), sign)
    angle = 2.0 * np.pi * power / side
    c, s = float(np.cos(angle)), float(sign * np.sin(angle))
    return re * c - im * s, re * s + im * c


def dft_line(values, sign):
    side = len(values)
    if side == 1:
        return values
    if side == 2:
        (r0, i0), (r1, i1) = values
        return [(r0 + r1, i0 + i1), (r0 - r1, i0 - i1)]
    if side == 4:
        return dft4(values, sign)
    inner = side // 4
    parts = [dft_line(values[b::4], sign) for b in range(4)]
    out = [None] * side
    for k1 in range(inner):
        column = [twiddle(parts[b][k1], b * k1, sign, side) for b in range(4)]
        for k2, value in enumerate(dft4(column, sign)):
            out[k1 + inner * k2] = value
    return out


def half_line(values, sign, parity):
    side = len(values)
    inner = side // 4
    parts = [dft_line(values[b::4], sign) for b in range(4)]
    out = [None] * (side // 2)
    for k1 in range(inner):
        column = [twiddle(parts[b][k1], b * k1, sign, side) for b in range(4)]
        column = [(re * parity, im * parity) if b % 2 else (re, im) for b, (re, im) in enumerate(column)]
        for k2, value in enumerate(dft4(column, sign)[:2]):
            out[k1 + inner * k2] = value
    return out


def load_inputs(g_hbm, m_hbm, g_ref, m_ref, in_sems, m_sem):
    load = pltpu.make_async_copy(m_hbm, m_ref, m_sem)
    pieces = [
        pltpu.make_async_copy(g_hbm.at[:, pl.ds(e, 1)], g_ref.at[:, pl.ds(e, 1)], in_sems.at[e])
        for e in range(g_ref.shape[1])
    ]
    for copy in [load] + pieces:
        copy.start()
    load.wait()
    return pieces


def sums_of(matrix, g_ref, e):
    lanes = g_ref.shape[2]
    g = jnp.concatenate([g_ref[0, e], g_ref[1, e]], axis=0)
    d = dot3(matrix, split_value(g), ((1,), (1,)))
    half = d.shape[0] // 2
    return d[:half, :lanes], d[:half, lanes:], d[half:, :lanes], d[half:, lanes:]


def both_times_kernel(g_hbm, m_hbm, out_ref, g_ref, m_ref, stage, in_sems, m_sem, out_sems):
    entries, lanes = g_ref.shape[1:3]
    near, _, _, _, rows, _ = stage.shape
    pieces = load_inputs(g_hbm, m_hbm, g_ref, m_ref, in_sems, m_sem)
    matrix = split_value(m_ref[...])
    copies = []
    for e in range(entries):
        pieces[e].wait()
        c_re, c_im, s_re, s_im = sums_of(matrix, g_ref, e)
        for where, value in (
            ((0, 0), c_re + s_im),
            ((0, 1), c_im - s_re),
            ((1, 0), s_im - c_re),
            ((1, 1), -(c_im + s_re)),
        ):
            stage[:, where[0], where[1], e] = value.reshape(near, rows, lanes)
        cut = pl.ds(e, 1)
        for side in range(2):
            target = out_ref.at[pl.ds(side * near, near), :, :, cut]
            copies.append(pltpu.make_async_copy(stage.at[:, :, :, cut], target, out_sems.at[e, side]))
            copies[-1].start()
    for copy in copies:
        copy.wait()


def one_times_kernel(g_hbm, m_hbm, out_ref, g_ref, m_ref, stage, in_sems, m_sem, out_sems):
    entries, lanes = g_ref.shape[1:3]
    devices, _, _, rows, _ = stage.shape
    pieces = load_inputs(g_hbm, m_hbm, g_ref, m_ref, in_sems, m_sem)
    matrix = split_value(m_ref[...])
    copies = []
    for e in range(entries):
        pieces[e].wait()
        c_re, c_im, s_re, s_im = sums_of(matrix, g_ref, e)
        stage[:, 0, e] = (c_re + s_im).reshape(devices, rows, lanes)
        stage[:, 1, e] = (c_im - s_re).reshape(devices, rows, lanes)
        cut = pl.ds(e, 1)
        copies.append(pltpu.make_async_copy(stage.at[:, :, cut], out_ref.at[:, :, cut], out_sems.at[e, 0]))
        copies[-1].start()
    for copy in copies:
        copy.wait()


def to_times(kernel, green, matrix, shape, targets, name):
    entries = green.shape[1]
    hbm = pl.BlockSpec(memory_space=pltpu.HBM)
    return pl.pallas_call(
        kernel,
        in_specs=[hbm, hbm],
        out_specs=hbm,
        out_shape=jax.ShapeDtypeStruct((targets,) + shape[1:], jnp.float32),
        scratch_shapes=[
            pltpu.VMEM(green.shape, jnp.float32),
            pltpu.VMEM(matrix.shape, jnp.float32),
            pltpu.VMEM(shape, jnp.float32),
            pltpu.SemaphoreType.DMA((entries,)),
            pltpu.SemaphoreType.DMA,
            pltpu.SemaphoreType.DMA((entries, 2)),
        ],
        compiler_params=pltpu.CompilerParams(vmem_limit_bytes=60 << 20),
        name=name,
    )(green, matrix)


def fill_block(ref, cosine, sine):
    plane = cosine.shape[0]
    lanes = plane // 2
    for block in range(2):
        cut = slice(block * lanes, (block + 1) * lanes)
        re = slice(2 * block * lanes, (2 * block + 1) * lanes)
        im = slice((2 * block + 1) * lanes, (2 * block + 2) * lanes)
        ref[:plane, re] = cosine[:, cut].astype(jnp.bfloat16)
        ref[plane:, im] = cosine[:, cut].astype(jnp.bfloat16)
        ref[:plane, im] = sine[:, cut].astype(jnp.bfloat16)
        ref[plane:, re] = (-sine[:, cut]).astype(jnp.bfloat16)


def fill_matrices(index_ref, parts, forward, backward, turned):
    plane = parts[0].shape[0]
    row = lax.broadcasted_iota(jnp.int32, (plane, plane), 0)
    pick = (row == index_ref[...]).astype(jnp.float32).astype(jnp.bfloat16)

    def dot(a, b):
        return jnp.dot(a, b, preferred_element_type=jnp.float32)

    for part in range(2):
        c_ref, s_ref = parts[part], parts[2 + part]
        cosine, sine = c_ref[...].astype(jnp.float32), s_ref[...].astype(jnp.float32)
        fill_block(forward.at[0, part], cosine, sine)
        fill_block(backward.at[0, part], turned(cosine), turned(-sine))
        fill_block(forward.at[1, part], dot(c_ref[...], pick), dot(s_ref[...], pick))
        fill_block(backward.at[1, part], turned(dot(pick, c_ref[...])), turned(-dot(pick, s_ref[...])))


def plane_dot(value, matrix, half, block):
    width = matrix.shape[3] // 2
    cut = slice(block * width, (block + 1) * width)
    return dot3(value, (matrix[half, 0, :, cut], matrix[half, 1, :, cut]), ((1,), (0,)))


def one_middle_kernel(table_ref, mirror_ref, index_ref, ch_ref, cl_ref, sh_ref, sl_ref, x_ref, out_ref, *refs):
    forward, backward, mid, space, other_space, chi, stage, sems = refs
    _, side, _, entries, rows, lanes = space.shape
    plane = 2 * lanes
    groups, _, _, members, _, _ = chi.shape
    fill_matrices(index_ref, (ch_ref, cl_ref, sh_ref, sl_ref), forward, backward, lambda value: value)

    def select_dot(value, matrix, block):
        shape = (value[0].shape[0] // rows, rows, plane)
        first, second = (plane_dot(value, matrix, half, block).reshape(shape) for half in range(2))
        upper = lax.broadcasted_iota(jnp.int32, shape, 1) < rows // 2
        return jnp.where(upper, first, second)

    columns = [x_ref[:, h, ri].reshape(side * entries * rows, lanes) for ri in range(2) for h in range(2)]
    value = split_value(jnp.concatenate(columns, axis=1))
    for block in range(2):
        d = select_dot(value, forward, block)
        for ri in range(2):
            piece = d[:, :, ri * lanes : (ri + 1) * lanes]
            mid[block, ri] = piece.reshape(side, entries, rows, lanes)
    for block in range(2):
        for e in range(entries):
            values = [(mid[block, 0, x, e], mid[block, 1, x, e]) for x in range(side)]
            for x, parts in enumerate(dft_line(values, 1)):
                for ri in range(2):
                    space[block, x, ri, e] = parts[ri]
                    other_space[block, x, ri, e] = pltpu.roll(parts[ri], rows // 2, 0)

    copies = []
    for group in range(groups):
        for c in range(members):
            left, right = table_ref[group * members + c, 0], table_ref[group * members + c, 1]
            for block in range(2):
                values = []
                for x in range(side):
                    other = mirror_ref[0, x]
                    a_re, a_im = space[block, x, 0, left], space[block, x, 1, left]
                    b_re, b_im = other_space[block, other, 0, right], other_space[block, other, 1, right]
                    values.append((a_re * b_re - a_im * b_im, a_re * b_im + a_im * b_re))
                cut = slice(block * lanes, (block + 1) * lanes)
                for x, parts in enumerate(dft_line(values, -1)):
                    for ri in range(2):
                        chi[group, ri, x, c, :, cut] = parts[ri]
        whole = (side * members * rows, plane)
        value = split_value(jnp.concatenate([chi[group, ri].reshape(whole) for ri in range(2)], axis=1))
        for h in range(2):
            d = select_dot(value, backward, h)
            for ri in range(2):
                piece = d[:, :, ri * lanes : (ri + 1) * lanes].reshape(side, members, rows, lanes)
                stage[group, :, h, ri] = piece
        target = out_ref.at[:, :, :, pl.ds(group * members, members)]
        copies.append(pltpu.make_async_copy(stage.at[group], target, sems.at[group]))
        copies[-1].start()
    for copy in copies:
        copy.wait()


def both_middle_kernel(me_ref, table_ref, mirror_ref, index_ref, ch_ref, cl_ref, sh_ref, sl_ref, x_ref, *refs):
    outs, (forward, backward, mid, space, chi) = refs[:-5], refs[-5:]
    halves, _, side, _, entries, rows, lanes = space.shape
    plane = 2 * lanes
    units, _, kept, members, _, _ = chi.shape
    me, near = me_ref[0], len(outs)
    core, line = me % 2, me // 2 % kept
    parity = (1 - 2 * (me // near)).astype(jnp.float32)

    def turned(value):
        return jnp.where(core == 0, value, jnp.concatenate([value[:, lanes:], value[:, :lanes]], axis=1))

    fill_matrices(index_ref, (ch_ref, cl_ref, sh_ref, sl_ref), forward, backward, turned)

    def arrive(half):
        columns = [
            x_ref[:, h, half, ri].reshape(side * entries * rows, lanes) for ri in range(2) for h in range(2)
        ]
        return split_value(jnp.concatenate(columns, axis=1))

    def to_plane(value, half, block):
        d = plane_dot(value, forward, half, block)
        for ri in range(2):
            piece = d[:, ri * lanes : (ri + 1) * lanes]
            mid[half, block, ri] = piece.reshape(side, entries, rows, lanes)

    def along_line(half, block, e):
        values = [(mid[half, block, 0, x, e], mid[half, block, 1, x, e]) for x in range(side)]
        for x, (re, im) in enumerate(dft_line(values, 1)):
            space[half, block, x, 0, e] = re
            space[half, block, x, 1, e] = im

    def product(unit, block, c):
        half, first = unit % halves, unit // halves * members
        left, right = table_ref[first + c, 0], table_ref[first + c, 1]
        values = []
        for x in range(side):
            other = mirror_ref[0, x]
            a_re, a_im = space[half, block, x, 0, left], space[half, block, x, 1, left]
            b_re, b_im = space[1 - half, block, other, 0, right], space[1 - half, block, other, 1, right]
            values.append((a_re * b_re - a_im * b_im, a_re * b_im + a_im * b_re))
        cut = slice(block * lanes, (block + 1) * lanes)
        for x, (re, im) in enumerate(half_line(values, -1, parity)):
            chi[unit, 0, x ^ line, c, :, cut] = re
            chi[unit, 1, x ^ line, c, :, cut] = im

    def from_plane(unit, value, h):
        half, first = unit % halves, unit // halves * members
        d = plane_dot(value, backward, half, h)
        for ri in range(2):
            piece = d[:, ri * lanes : (ri + 1) * lanes].reshape(kept, members, rows, lanes)
            for x in range(kept):
                outs[2 * x + h][half, ri, first : first + members] = piece[x]

    def collect(unit):
        whole = (kept * members * rows, plane)
        return split_value(jnp.concatenate([chi[unit, ri].reshape(whole) for ri in range(2)], axis=1))

    places = [(half, block) for half in range(halves) for block in range(2)]
    for step in range(len(places) + 1):
        if step < len(places):
            half, block = places[step]
            if block == 0:
                value = arrive(half)
            to_plane(value, half, block)
        if step > 0:
            for e in range(entries):
                along_line(*places[step - 1], e)

    for unit in range(units + 1):
        tasks = [(block, c) for block in range(2) for c in range(members)] if unit < units else []
        if unit > 0:
            value = collect(unit - 1)
        for h in range(2):
            if unit > 0:
                from_plane(unit - 1, value, h)
            for block, c in tasks[h * members : (h + 1) * members]:
                product(unit, block, c)


def middle_inputs(table, mirror_map, x):
    side, plane = x.shape[0] // 2, 2 * x.shape[-1]
    index = (mirror_map[1][:, None] * side + mirror_map[2][None, :]).reshape(1, plane)
    cosine, sine = plane_parts(side)
    parts = [jnp.asarray(part) for part in split_constant(cosine) + split_constant(sine)]
    smem = pl.BlockSpec(memory_space=pltpu.SMEM)
    vmem = pl.BlockSpec(memory_space=pltpu.VMEM)
    args = (table, mirror_map, index, *parts, x.reshape((side, 2) + x.shape[1:]))
    return args, [smem, smem] + [vmem] * 6, pltpu.VMEM((2, 2, 2 * plane, 2 * plane), jnp.bfloat16)


def one_middle(x, table, mirror_map):
    devices, _, entries, rows, lanes = x.shape
    side, components = devices // 2, table.shape[0]
    args, specs, matrices = middle_inputs(table, mirror_map, x)
    spatial = pltpu.VMEM((2, side, 2, entries, rows, lanes), jnp.float32)
    shape = (side, 2, 2, components, rows, lanes)
    out = pl.pallas_call(
        one_middle_kernel,
        in_specs=specs,
        out_specs=pl.BlockSpec(memory_space=pltpu.HBM),
        out_shape=jax.ShapeDtypeStruct(shape, jnp.float32),
        scratch_shapes=[
            matrices,
            matrices,
            pltpu.VMEM((2, 2, side, entries, rows, lanes), jnp.float32),
            spatial,
            spatial,
            pltpu.VMEM((GROUPS, 2, side, components // GROUPS, rows, 2 * lanes), jnp.float32),
            pltpu.VMEM((GROUPS, side, 2, 2, components // GROUPS, rows, lanes), jnp.float32),
            pltpu.SemaphoreType.DMA((GROUPS,)),
        ],
        compiler_params=pltpu.CompilerParams(vmem_limit_bytes=61 << 20),
        name="one_middle",
    )(*args)
    return out.reshape((devices,) + shape[2:])


def both_middle(x, table, mirror_map, me, near):
    devices, halves, _, entries, rows, lanes = x.shape
    side, components = devices // 2, table.shape[0]
    args, specs, matrices = middle_inputs(table, mirror_map, x)
    members = components // GROUPS
    return pl.pallas_call(
        both_middle_kernel,
        in_specs=[pl.BlockSpec(memory_space=pltpu.SMEM)] + specs,
        out_specs=[pl.BlockSpec(memory_space=pltpu.VMEM)] * near,
        out_shape=[jax.ShapeDtypeStruct((halves, 2, components, rows, lanes), jnp.float32)] * near,
        scratch_shapes=[
            matrices,
            matrices,
            pltpu.VMEM((halves, 2, 2, side, entries, rows, lanes), jnp.float32),
            pltpu.VMEM((halves, 2, side, 2, entries, rows, lanes), jnp.float32),
            pltpu.VMEM((halves * GROUPS, 2, near // 2, members, rows, 2 * lanes), jnp.float32),
        ],
        compiler_params=pltpu.CompilerParams(vmem_limit_bytes=60 << 20),
        name="both_middle",
    )(me, *args)


def both_frequency_kernel(me_ref, m_ref, *refs):
    pieces, (out_ref, stage, sems) = refs[:-3], refs[-3:]
    near = len(pieces)
    components, lanes = stage.shape[1:3]
    groups = sems.shape[0]
    members = components // groups
    me = me_ref[0] % near
    matrix = split_value(jnp.concatenate([m_ref[part, slot ^ me] for part in range(2) for slot in range(near)], axis=0))

    def gathered(half, ri, c):
        return jnp.concatenate([piece[half, ri, c] for piece in pieces], axis=0)

    copies = []
    for group in range(groups):
        values = []
        for c in range(group * members, (group + 1) * members):
            part = [[gathered(half, ri, c) for ri in range(2)] for half in range(2)]
            sums = [part[0][ri] + part[1][ri] for ri in range(2)]
            differences = [part[0][ri] - part[1][ri] for ri in range(2)]
            values.append(jnp.concatenate([sums[0], -differences[1]], axis=0).T)
            values.append(jnp.concatenate([sums[1], differences[0]], axis=0).T)
        d = dot3(split_value(jnp.concatenate(values, axis=0)), matrix, ((1,), (0,)))
        d = d.reshape(members, 2, lanes, d.shape[1])
        for ri in range(2):
            stage[ri, group * members : (group + 1) * members] = d[:, ri]
        cut = pl.ds(group * members, members)
        copies.append(pltpu.make_async_copy(stage.at[:, cut], out_ref.at[:, cut], sems.at[group]))
        copies[-1].start()
    for copy in copies:
        copy.wait()


def both_frequencies(pieces, matrix, me):
    _, _, components, _, lanes = pieces[0].shape
    shape = (2, components, lanes, matrix.shape[3])
    vmem = pl.BlockSpec(memory_space=pltpu.VMEM)
    return pl.pallas_call(
        both_frequency_kernel,
        in_specs=[pl.BlockSpec(memory_space=pltpu.SMEM)] + [vmem] * (1 + len(pieces)),
        out_specs=pl.BlockSpec(memory_space=pltpu.HBM),
        out_shape=jax.ShapeDtypeStruct(shape, jnp.float32),
        scratch_shapes=[pltpu.VMEM(shape, jnp.float32), pltpu.SemaphoreType.DMA((components // 2,))],
        compiler_params=pltpu.CompilerParams(vmem_limit_bytes=60 << 20),
        name="both_frequencies",
    )(me, matrix, *pieces)


def one_frequency_kernel(y_ref, m_ref, earlier_hbm, out_ref, earlier, stage, in_sems, sems):
    devices, _, components, rows, lanes = y_ref.shape
    groups = sems.shape[0]
    members = components // groups
    cuts = [pl.ds(group * members, members) for group in range(groups)]
    loads = [
        pltpu.make_async_copy(earlier_hbm.at[:, cut], earlier.at[:, cut], in_sems.at[group])
        for group, cut in enumerate(cuts)
    ]
    for copy in loads:
        copy.start()
    matrix = split_value(m_ref[...])
    upper_rows = lax.broadcasted_iota(jnp.int32, (devices, rows, lanes), 1) < rows // 2
    copies = []
    for group, cut in enumerate(cuts):
        values = []
        for c in range(group * members, (group + 1) * members):
            folded = []
            for ri in range(2):
                tile = y_ref[:, ri, c]
                turned = pltpu.roll(tile, rows // 2, 1)
                folded.append((tile + turned, turned - tile))
            first = jnp.where(upper_rows, folded[0][0], -folded[1][1])
            second = jnp.where(upper_rows, folded[1][0], folded[0][1])
            values.append(first.reshape(devices * rows, lanes).T)
            values.append(second.reshape(devices * rows, lanes).T)
        d = dot3(split_value(jnp.concatenate(values, axis=0)), matrix, ((1,), (0,)))
        d = d.reshape(members, 2, lanes, d.shape[1])
        loads[group].wait()
        for ri in range(2):
            own = slice(group * members, (group + 1) * members)
            stage[ri, own] = earlier[ri, own] + d[:, ri]
        copies.append(pltpu.make_async_copy(stage.at[:, cut], out_ref.at[:, cut], sems.at[group]))
        copies[-1].start()
    for copy in copies:
        copy.wait()


def one_frequencies(y, matrix, earlier):
    vmem = pl.BlockSpec(memory_space=pltpu.VMEM)
    hbm = pl.BlockSpec(memory_space=pltpu.HBM)
    groups = earlier.shape[1] // 2
    return pl.pallas_call(
        one_frequency_kernel,
        in_specs=[vmem, vmem, hbm],
        out_specs=hbm,
        out_shape=jax.ShapeDtypeStruct(earlier.shape, jnp.float32),
        scratch_shapes=[
            pltpu.VMEM(earlier.shape, jnp.float32),
            pltpu.VMEM(earlier.shape, jnp.float32),
            pltpu.SemaphoreType.DMA((groups,)),
            pltpu.SemaphoreType.DMA((groups,)),
        ],
        compiler_params=pltpu.CompilerParams(vmem_limit_bytes=60 << 20),
        name="one_frequencies",
    )(y, matrix, earlier)


def exchange(x):
    flat = x.reshape(x.shape[0], -1, x.shape[-1])
    return lax.all_to_all(flat, "kb", split_axis=0, concat_axis=0, tiled=True).reshape(x.shape)


def swap(pieces, devices):
    moved = [pieces[0]]
    for slot in range(1, len(pieces)):
        pairs = [(device, device ^ slot) for device in range(devices)]
        moved.append(lax.ppermute(pieces[slot], "kb", pairs))
    return moved


def trig_pair(angle_int, period, scale):
    angle = 2.0 * math.pi / period * angle_int.astype(jnp.float32)
    return (scale * jnp.cos(angle), scale * jnp.sin(angle))


def complex_combine(formula, cosine, sine, real_part, imag_part):
    first_term = jnp.einsum(formula, cosine, real_part + imag_part, precision=lax.Precision.HIGHEST)
    second_term = jnp.einsum(formula, cosine + sine, imag_part, precision=lax.Precision.HIGHEST)
    third_term = jnp.einsum(formula, sine - cosine, real_part, precision=lax.Precision.HIGHEST)
    return (first_term - second_term, first_term + third_term)


def forward_imaginary_time(tau_rows, frequency_count):
    freq_index = jnp.arange(frequency_count, dtype=jnp.int32)
    angle_int = (
        (2 * freq_index[None, :] - frequency_count + 1)
        * (2 * tau_rows[:, None] + 1)
        % (4 * frequency_count)
    )
    cosine, sine = trig_pair(angle_int, 4 * frequency_count, frequency_count ** (-0.5))
    return (cosine, -sine)


def tau_backward(tau_rows, frequency_count):
    freq_index = jnp.arange(frequency_count, dtype=jnp.int32)
    angle_int = (
        (freq_index[:, None] - frequency_count // 2)
        * (2 * tau_rows[None, :] + 1)
        % (2 * frequency_count)
    )
    return trig_pair(angle_int, 2 * frequency_count, frequency_count ** (-0.5))


def grid_transform(real_part, imag_part, grid_side, direction):
    shape = real_part.shape
    plane = jnp.arange(grid_side * grid_side, dtype=jnp.int32)
    upper = plane // grid_side
    lower = plane % grid_side
    plane_int = (upper[:, None] * upper[None, :] + lower[:, None] * lower[None, :]) % grid_side
    plane_cos, plane_sin = trig_pair(plane_int, grid_side, 1.0 / grid_side)
    line = jnp.arange(grid_side, dtype=jnp.int32)
    line_cos, line_sin = trig_pair(
        line[:, None] * line[None, :] % grid_side, grid_side, grid_side ** (-0.5)
    )
    real_part = real_part.reshape(shape[:-1] + (grid_side, grid_side * grid_side))
    imag_part = imag_part.reshape(shape[:-1] + (grid_side, grid_side * grid_side))
    real_part, imag_part = complex_combine(
        "pq,...xq->...xp", plane_cos, direction * plane_sin, real_part, imag_part
    )
    real_part, imag_part = complex_combine(
        "ax,...xp->...ap", line_cos, direction * line_sin, real_part, imag_part
    )
    return (real_part.reshape(shape), imag_part.reshape(shape))


def mirror_index(mirror_map, grid_side):
    index_x = mirror_map[0][:, None, None]
    index_y = mirror_map[1][None, :, None]
    index_z = mirror_map[2][None, None, :]
    return (index_x * grid_side * grid_side + index_y * grid_side + index_z).reshape(-1)


def bubble(gr_re, gr_im, mirror_re, mirror_im, pair_table, entries):
    entry_ids = jnp.arange(entries, dtype=jnp.int32)
    pick_left = (pair_table[:, 0][:, None] == entry_ids[None, :]).astype(jnp.float32)
    pick_right = (pair_table[:, 1][:, None] == entry_ids[None, :]).astype(jnp.float32)
    left_re = jnp.einsum("me,e...->m...", pick_left, gr_re, precision=lax.Precision.HIGHEST)
    left_im = jnp.einsum("me,e...->m...", pick_left, gr_im, precision=lax.Precision.HIGHEST)
    right_re = jnp.einsum("me,e...->m...", pick_right, mirror_re, precision=lax.Precision.HIGHEST)
    right_im = jnp.einsum("me,e...->m...", pick_right, mirror_im, precision=lax.Precision.HIGHEST)
    return (left_re * right_re - left_im * right_im, left_re * right_im + left_im * right_re)


def general(green_momentum_grid, pair_table, mirror_map):
    grid_side = mirror_map.shape[1]
    entries = green_momentum_grid.shape[1]
    frequency_count = green_momentum_grid.shape[3]
    position = jnp.arange(frequency_count, dtype=jnp.int32)
    fwd_cos, fwd_sin = forward_imaginary_time(position, frequency_count)
    tau_re, tau_im = complex_combine(
        "qa,fsa->fqs", fwd_cos, fwd_sin, green_momentum_grid[0], green_momentum_grid[1]
    )
    stacked = jnp.stack([tau_re, tau_im])

    def to_real_space(pieces):
        space_re, space_im = grid_transform(pieces[0], pieces[1], grid_side, 1.0)
        return jnp.stack([space_re, space_im])

    mirror_flat = mirror_index(mirror_map, grid_side)
    partner_rows = frequency_count - 1 - position
    reflected_cosine, reflected_sine = forward_imaginary_time(partner_rows, frequency_count)
    partner_real, partner_imaginary = complex_combine(
        "qa,fsa->fqs",
        reflected_cosine,
        reflected_sine,
        green_momentum_grid[0],
        green_momentum_grid[1],
    )
    other_stacked = jnp.stack([partner_real, partner_imaginary])
    pieces = (
        lax.all_to_all(stacked, "kb", split_axis=2, concat_axis=3, tiled=True),
        lax.all_to_all(other_stacked, "kb", split_axis=2, concat_axis=3, tiled=True),
    )
    in_cells = to_real_space(pieces[0])
    partner = to_real_space(pieces[1])
    mirrored = jnp.take(partner, mirror_flat, axis=3)
    chi_re, chi_im = bubble(in_cells[0], in_cells[1], mirrored[0], mirrored[1], pair_table, entries)
    chi_re, chi_im = grid_transform(chi_re, chi_im, grid_side, -1.0)
    momenta = jnp.stack([chi_re, chi_im])
    back_cos, back_sin = tau_backward(position, frequency_count)
    pieces = lax.all_to_all(momenta, "kb", split_axis=3, concat_axis=2, tiled=True)
    out_re, out_im = complex_combine("vj,ejk->ekv", back_cos, back_sin, pieces[0], pieces[1])
    return jnp.stack([out_re, out_im])


def local(green, pair_table, mirror_map):
    side = mirror_map.shape[1]
    plane = side * side
    lanes, count = green.shape[2], green.shape[3]
    devices = side * plane // lanes
    near = devices // 2
    half = ROWS // 2
    shared = near * ROWS
    if lanes != LANES or 2 * lanes != plane or 2 * (shared + devices * half) != count:
        return general(green, pair_table, mirror_map)
    me = lax.axis_index("kb").astype(jnp.int32).reshape(1)
    entries = green.shape[1]

    rows = np.arange(shared)
    both_fermion = fermion_matrix(rows, count).astype(np.float32)
    both_boson = boson_matrix(rows, count).reshape(2, near, ROWS, count).astype(np.float32)
    rows = shared + np.arange(devices * half).reshape(devices, half)
    times = np.concatenate([rows, count - 1 - rows], axis=1).reshape(-1)
    one_fermion = fermion_matrix(times, count).astype(np.float32)
    one_boson = boson_matrix(rows.reshape(-1), count).reshape(2, devices, half, count).swapaxes(0, 1)
    one_boson = one_boson.reshape(devices * ROWS, count).astype(np.float32)

    shape = (near, 2, 2, entries, ROWS, lanes)
    both = to_times(both_times_kernel, green, jnp.asarray(both_fermion), shape, devices, "both_times")
    green, both = lax.optimization_barrier((green, both))
    shape = (devices, 2, entries, ROWS, lanes)
    one = to_times(one_times_kernel, green, jnp.asarray(one_fermion), shape, devices, "one_times")
    both, one = lax.optimization_barrier((exchange(both), one))
    pieces = list(both_middle(both, pair_table, mirror_map, me, near))
    one, pieces[0] = lax.optimization_barrier((exchange(one), pieces[0]))
    one = exchange(one_middle(one, pair_table, mirror_map))
    earlier = both_frequencies(swap(pieces, devices), jnp.asarray(both_boson), me)
    return one_frequencies(one, jnp.asarray(one_boson), earlier)


def solution(mesh):
    placed = (P("set", None, "kb", None), P(), P("set", None))
    return jax.shard_map(
        local, mesh=mesh, in_specs=placed, out_specs=P("set", None, "kb", None), check_vma=False
    )
```

```python
import functools
import math

import jax
import jax.numpy as jnp
import ml_dtypes
import numpy as np
from jax import lax
from jax.experimental import pallas as pl
from jax.experimental.pallas import tpu as pltpu
from jax.sharding import PartitionSpec as P

LANES = 128
ROWS = 8
GROUPS = 2


def split_constant(matrix):
    high = matrix.astype(np.float32).astype(ml_dtypes.bfloat16)
    low = (matrix - high.astype(np.float64)).astype(np.float32).astype(ml_dtypes.bfloat16)
    return high, low


def split_value(value):
    high = value.astype(jnp.bfloat16)
    low = (value - high.astype(jnp.float32)).astype(jnp.bfloat16)
    return high, low


def dot3(left, right, dims):
    (k_left,), (k_right,) = dims
    a = jnp.concatenate([left[0], left[0], left[1]], axis=k_left)
    b = jnp.concatenate([right[0], right[1], right[0]], axis=k_right)
    return lax.dot_general(a, b, (dims, ((), ())), preferred_element_type=jnp.float32)


def fermion_matrix(rows, count):
    n = np.arange(count, dtype=np.int64)
    angle = ((2 * n[None, :] - count + 1) * (2 * rows[:, None] + 1)) % (4 * count)
    angle = np.pi * angle / (2 * count)
    return np.concatenate([np.cos(angle), np.sin(angle)], axis=0) * count**-0.5


def boson_matrix(rows, count):
    v = np.arange(count, dtype=np.int64)
    angle = ((v[None, :] - count // 2) * (2 * rows[:, None] + 1)) % (2 * count)
    angle = np.pi * angle / count
    return np.concatenate([np.cos(angle), np.sin(angle)], axis=0) * count**-0.5


def plane_parts(side):
    p = np.arange(side * side, dtype=np.int64)
    angle = ((p[:, None] // side) * (p[None, :] // side) + (p[:, None] % side) * (p[None, :] % side)) % side
    angle = 2 * np.pi * angle / side
    scale = side**-1.5
    return np.cos(angle) * scale, np.sin(angle) * scale


def times_w4(re, im, power, sign):
    power = (power * sign) % 4
    if power == 0:
        return re, im
    if power == 1:
        return -im, re
    if power == 2:
        return -re, -im
    return im, -re


def dft4(values, sign):
    (r0, i0), (r1, i1), (r2, i2), (r3, i3) = values
    sr, si, dr, di = r0 + r2, i0 + i2, r0 - r2, i0 - i2
    tr, ti, er, ei = r1 + r3, i1 + i3, r1 - r3, i1 - i3
    if sign > 0:
        return [(sr + tr, si + ti), (dr - ei, di + er), (sr - tr, si - ti), (dr + ei, di - er)]
    return [(sr + tr, si + ti), (dr + ei, di - er), (sr - tr, si - ti), (dr - ei, di + er)]


def twiddle(value, power, sign, side):
    re, im = value
    if power % (side // 4) == 0:
        return times_w4(re, im, power // (side // 4), sign)
    angle = 2.0 * np.pi * power / side
    c, s = float(np.cos(angle)), float(sign * np.sin(angle))
    return re * c - im * s, re * s + im * c


def dft_line(values, sign):
    side = len(values)
    if side == 1:
        return values
    if side == 2:
        (r0, i0), (r1, i1) = values
        return [(r0 + r1, i0 + i1), (r0 - r1, i0 - i1)]
    if side == 4:
        return dft4(values, sign)
    inner = side // 4
    parts = [dft_line(values[b::4], sign) for b in range(4)]
    out = [None] * side
    for k1 in range(inner):
        column = [twiddle(parts[b][k1], b * k1, sign, side) for b in range(4)]
        for k2, value in enumerate(dft4(column, sign)):
            out[k1 + inner * k2] = value
    return out


def half_line(values, sign, parity):
    side = len(values)
    inner = side // 4
    parts = [dft_line(values[b::4], sign) for b in range(4)]
    out = [None] * (side // 2)
    for k1 in range(inner):
        column = [twiddle(parts[b][k1], b * k1, sign, side) for b in range(4)]
        column = [(re * parity, im * parity) if b % 2 else (re, im) for b, (re, im) in enumerate(column)]
        for k2, value in enumerate(dft4(column, sign)[:2]):
            out[k1 + inner * k2] = value
    return out


def load_inputs(g_hbm, m_hbm, g_ref, m_ref, in_sems, m_sem):
    load = pltpu.make_async_copy(m_hbm, m_ref, m_sem)
    pieces = [
        pltpu.make_async_copy(g_hbm.at[:, pl.ds(e, 1)], g_ref.at[:, pl.ds(e, 1)], in_sems.at[e])
        for e in range(g_ref.shape[1])
    ]
    for copy in [load] + pieces:
        copy.start()
    load.wait()
    return pieces


def sums_of(matrix, g_ref, e):
    lanes = g_ref.shape[2]
    g = jnp.concatenate([g_ref[0, e], g_ref[1, e]], axis=0)
    d = dot3(matrix, split_value(g), ((1,), (1,)))
    half = d.shape[0] // 2
    return d[:half, :lanes], d[:half, lanes:], d[half:, :lanes], d[half:, lanes:]


def both_times_kernel(g_hbm, m_hbm, out_ref, g_ref, m_ref, stage, in_sems, m_sem, out_sems):
    entries, lanes = g_ref.shape[1:3]
    near, _, _, _, rows, _ = stage.shape
    pieces = load_inputs(g_hbm, m_hbm, g_ref, m_ref, in_sems, m_sem)
    matrix = split_value(m_ref[...])
    copies = []
    for e in range(entries):
        pieces[e].wait()
        c_re, c_im, s_re, s_im = sums_of(matrix, g_ref, e)
        for where, value in (
            ((0, 0), c_re + s_im),
            ((0, 1), c_im - s_re),
            ((1, 0), s_im - c_re),
            ((1, 1), -(c_im + s_re)),
        ):
            stage[:, where[0], where[1], e] = value.reshape(near, rows, lanes)
        cut = pl.ds(e, 1)
        for side in range(2):
            target = out_ref.at[pl.ds(side * near, near), :, :, cut]
            copies.append(pltpu.make_async_copy(stage.at[:, :, :, cut], target, out_sems.at[e, side]))
            copies[-1].start()
    for copy in copies:
        copy.wait()


def one_times_kernel(g_hbm, m_hbm, out_ref, g_ref, m_ref, stage, in_sems, m_sem, out_sems):
    entries, lanes = g_ref.shape[1:3]
    devices, _, _, rows, _ = stage.shape
    pieces = load_inputs(g_hbm, m_hbm, g_ref, m_ref, in_sems, m_sem)
    matrix = split_value(m_ref[...])
    copies = []
    for e in range(entries):
        pieces[e].wait()
        c_re, c_im, s_re, s_im = sums_of(matrix, g_ref, e)
        stage[:, 0, e] = (c_re + s_im).reshape(devices, rows, lanes)
        stage[:, 1, e] = (c_im - s_re).reshape(devices, rows, lanes)
        cut = pl.ds(e, 1)
        copies.append(pltpu.make_async_copy(stage.at[:, :, cut], out_ref.at[:, :, cut], out_sems.at[e, 0]))
        copies[-1].start()
    for copy in copies:
        copy.wait()


def to_times(kernel, green, matrix, shape, targets, name):
    entries = green.shape[1]
    hbm = pl.BlockSpec(memory_space=pltpu.HBM)
    return pl.pallas_call(
        kernel,
        in_specs=[hbm, hbm],
        out_specs=hbm,
        out_shape=jax.ShapeDtypeStruct((targets,) + shape[1:], jnp.float32),
        scratch_shapes=[
            pltpu.VMEM(green.shape, jnp.float32),
            pltpu.VMEM(matrix.shape, jnp.float32),
            pltpu.VMEM(shape, jnp.float32),
            pltpu.SemaphoreType.DMA((entries,)),
            pltpu.SemaphoreType.DMA,
            pltpu.SemaphoreType.DMA((entries, 2)),
        ],
        compiler_params=pltpu.CompilerParams(vmem_limit_bytes=60 << 20),
        name=name,
    )(green, matrix)


def fill_block(ref, cosine, sine):
    plane = cosine.shape[0]
    lanes = plane // 2
    for block in range(2):
        cut = slice(block * lanes, (block + 1) * lanes)
        re = slice(2 * block * lanes, (2 * block + 1) * lanes)
        im = slice((2 * block + 1) * lanes, (2 * block + 2) * lanes)
        ref[:plane, re] = cosine[:, cut].astype(jnp.bfloat16)
        ref[plane:, im] = cosine[:, cut].astype(jnp.bfloat16)
        ref[:plane, im] = sine[:, cut].astype(jnp.bfloat16)
        ref[plane:, re] = (-sine[:, cut]).astype(jnp.bfloat16)


def fill_matrices(index_ref, parts, forward, backward, turned):
    plane = parts[0].shape[0]
    row = lax.broadcasted_iota(jnp.int32, (plane, plane), 0)
    pick = (row == index_ref[...]).astype(jnp.float32).astype(jnp.bfloat16)

    def dot(a, b):
        return jnp.dot(a, b, preferred_element_type=jnp.float32)

    for part in range(2):
        c_ref, s_ref = parts[part], parts[2 + part]
        cosine, sine = c_ref[...].astype(jnp.float32), s_ref[...].astype(jnp.float32)
        fill_block(forward.at[0, part], cosine, sine)
        fill_block(backward.at[0, part], turned(cosine), turned(-sine))
        fill_block(forward.at[1, part], dot(c_ref[...], pick), dot(s_ref[...], pick))
        fill_block(backward.at[1, part], turned(dot(pick, c_ref[...])), turned(-dot(pick, s_ref[...])))


def plane_dot(value, matrix, half, block):
    width = matrix.shape[3] // 2
    cut = slice(block * width, (block + 1) * width)
    return dot3(value, (matrix[half, 0, :, cut], matrix[half, 1, :, cut]), ((1,), (0,)))


def one_middle_kernel(table_ref, mirror_ref, index_ref, ch_ref, cl_ref, sh_ref, sl_ref, x_ref, out_ref, *refs):
    forward, backward, mid, space, other_space, chi, stage, sems = refs
    _, side, _, entries, rows, lanes = space.shape
    plane = 2 * lanes
    groups, _, _, members, _, _ = chi.shape
    fill_matrices(index_ref, (ch_ref, cl_ref, sh_ref, sl_ref), forward, backward, lambda value: value)

    def paired(first, second):
        upper = lax.broadcasted_iota(jnp.int32, first.shape, 1) < rows // 2
        turned = [pltpu.roll(part, rows // 2, 1) for part in (first, second)]
        return jnp.where(upper, first, turned[1]), jnp.where(upper, turned[0], second)

    def halves_of(columns):
        value = jnp.concatenate(columns, axis=1)
        count, width = value.shape
        value = value.reshape(count // (2 * rows), 2, rows, width)
        parts = paired(value[:, 0], value[:, 1])
        return [split_value(part.reshape(count // 2, width)) for part in parts]

    def halves_dot(parts, matrix, block):
        shape = (parts[0][0].shape[0] // rows, rows, plane)
        d = paired(*(plane_dot(parts[half], matrix, half, block).reshape(shape) for half in range(2)))
        return jnp.concatenate([part.reshape(shape[0], 1, rows, plane) for part in d], axis=1)

    parts = halves_of([x_ref[:, h, ri].reshape(side * entries * rows, lanes) for ri in range(2) for h in range(2)])
    for block in range(2):
        d = halves_dot(parts, forward, block)
        for ri in range(2):
            piece = d[:, :, :, ri * lanes : (ri + 1) * lanes]
            mid[block, ri] = piece.reshape(side, entries, rows, lanes)
    for block in range(2):
        for e in range(entries):
            values = [(mid[block, 0, x, e], mid[block, 1, x, e]) for x in range(side)]
            for x, parts in enumerate(dft_line(values, 1)):
                for ri in range(2):
                    space[block, x, ri, e] = parts[ri]
                    other_space[block, x, ri, e] = pltpu.roll(parts[ri], rows // 2, 0)

    copies = []
    for group in range(groups):
        for c in range(members):
            left, right = table_ref[group * members + c, 0], table_ref[group * members + c, 1]
            for block in range(2):
                values = []
                for x in range(side):
                    other = mirror_ref[0, x]
                    a_re, a_im = space[block, x, 0, left], space[block, x, 1, left]
                    b_re, b_im = other_space[block, other, 0, right], other_space[block, other, 1, right]
                    values.append((a_re * b_re - a_im * b_im, a_re * b_im + a_im * b_re))
                cut = slice(block * lanes, (block + 1) * lanes)
                for x, parts in enumerate(dft_line(values, -1)):
                    for ri in range(2):
                        chi[group, ri, x, c, :, cut] = parts[ri]
        whole = (side * members * rows, plane)
        parts = halves_of([chi[group, ri].reshape(whole) for ri in range(2)])
        for h in range(2):
            d = halves_dot(parts, backward, h)
            for ri in range(2):
                piece = d[:, :, :, ri * lanes : (ri + 1) * lanes].reshape(side, members, rows, lanes)
                stage[group, :, h, ri] = piece
        target = out_ref.at[:, :, :, pl.ds(group * members, members)]
        copies.append(pltpu.make_async_copy(stage.at[group], target, sems.at[group]))
        copies[-1].start()
    for copy in copies:
        copy.wait()


def both_middle_kernel(me_ref, table_ref, mirror_ref, index_ref, ch_ref, cl_ref, sh_ref, sl_ref, x_ref, *refs):
    outs, (forward, backward, mid, space, chi) = refs[:-5], refs[-5:]
    halves, _, side, _, entries, rows, lanes = space.shape
    plane = 2 * lanes
    units, _, kept, members, _, _ = chi.shape
    me, near = me_ref[0], len(outs)
    core, line = me % 2, me // 2 % kept
    parity = (1 - 2 * (me // near)).astype(jnp.float32)

    def turned(value):
        return jnp.where(core == 0, value, jnp.concatenate([value[:, lanes:], value[:, :lanes]], axis=1))

    fill_matrices(index_ref, (ch_ref, cl_ref, sh_ref, sl_ref), forward, backward, turned)

    def arrive(half):
        columns = [
            x_ref[:, h, half, ri].reshape(side * entries * rows, lanes) for ri in range(2) for h in range(2)
        ]
        return split_value(jnp.concatenate(columns, axis=1))

    def to_plane(value, half, block):
        d = plane_dot(value, forward, half, block)
        for ri in range(2):
            piece = d[:, ri * lanes : (ri + 1) * lanes]
            mid[half, block, ri] = piece.reshape(side, entries, rows, lanes)

    def along_line(half, block, e):
        values = [(mid[half, block, 0, x, e], mid[half, block, 1, x, e]) for x in range(side)]
        for x, (re, im) in enumerate(dft_line(values, 1)):
            space[half, block, x, 0, e] = re
            space[half, block, x, 1, e] = im

    def product(unit, block, c):
        half, first = unit % halves, unit // halves * members
        left, right = table_ref[first + c, 0], table_ref[first + c, 1]
        values = []
        for x in range(side):
            other = mirror_ref[0, x]
            a_re, a_im = space[half, block, x, 0, left], space[half, block, x, 1, left]
            b_re, b_im = space[1 - half, block, other, 0, right], space[1 - half, block, other, 1, right]
            values.append((a_re * b_re - a_im * b_im, a_re * b_im + a_im * b_re))
        cut = slice(block * lanes, (block + 1) * lanes)
        for x, (re, im) in enumerate(half_line(values, -1, parity)):
            chi[unit, 0, x ^ line, c, :, cut] = re
            chi[unit, 1, x ^ line, c, :, cut] = im

    def from_plane(unit, value, h):
        half, first = unit % halves, unit // halves * members
        d = plane_dot(value, backward, half, h)
        for ri in range(2):
            piece = d[:, ri * lanes : (ri + 1) * lanes].reshape(kept, members, rows, lanes)
            for x in range(kept):
                outs[2 * x + h][half, ri, first : first + members] = piece[x]

    def collect(unit):
        whole = (kept * members * rows, plane)
        return split_value(jnp.concatenate([chi[unit, ri].reshape(whole) for ri in range(2)], axis=1))

    places = [(half, block) for half in range(halves) for block in range(2)]
    for step in range(len(places) + 1):
        if step < len(places):
            half, block = places[step]
            if block == 0:
                value = arrive(half)
            to_plane(value, half, block)
        if step > 0:
            for e in range(entries):
                along_line(*places[step - 1], e)

    for unit in range(units + 1):
        tasks = [(block, c) for block in range(2) for c in range(members)] if unit < units else []
        if unit > 0:
            value = collect(unit - 1)
        for h in range(2):
            if unit > 0:
                from_plane(unit - 1, value, h)
            for block, c in tasks[h * members : (h + 1) * members]:
                product(unit, block, c)


def middle_inputs(table, mirror_map, x):
    side, plane = x.shape[0] // 2, 2 * x.shape[-1]
    index = (mirror_map[1][:, None] * side + mirror_map[2][None, :]).reshape(1, plane)
    cosine, sine = plane_parts(side)
    parts = [jnp.asarray(part) for part in split_constant(cosine) + split_constant(sine)]
    smem = pl.BlockSpec(memory_space=pltpu.SMEM)
    vmem = pl.BlockSpec(memory_space=pltpu.VMEM)
    args = (table, mirror_map, index, *parts, x.reshape((side, 2) + x.shape[1:]))
    return args, [smem, smem] + [vmem] * 6, pltpu.VMEM((2, 2, 2 * plane, 2 * plane), jnp.bfloat16)


def one_middle(x, table, mirror_map):
    devices, _, entries, rows, lanes = x.shape
    side, components = devices // 2, table.shape[0]
    args, specs, matrices = middle_inputs(table, mirror_map, x)
    spatial = pltpu.VMEM((2, side, 2, entries, rows, lanes), jnp.float32)
    shape = (side, 2, 2, components, rows, lanes)
    out = pl.pallas_call(
        one_middle_kernel,
        in_specs=specs,
        out_specs=pl.BlockSpec(memory_space=pltpu.HBM),
        out_shape=jax.ShapeDtypeStruct(shape, jnp.float32),
        scratch_shapes=[
            matrices,
            matrices,
            pltpu.VMEM((2, 2, side, entries, rows, lanes), jnp.float32),
            spatial,
            spatial,
            pltpu.VMEM((GROUPS, 2, side, components // GROUPS, rows, 2 * lanes), jnp.float32),
            pltpu.VMEM((GROUPS, side, 2, 2, components // GROUPS, rows, lanes), jnp.float32),
            pltpu.SemaphoreType.DMA((GROUPS,)),
        ],
        compiler_params=pltpu.CompilerParams(vmem_limit_bytes=44 << 20),
        name="one_middle",
    )(*args)
    return out.reshape((devices,) + shape[2:])


def both_middle(x, table, mirror_map, me, near):
    devices, halves, _, entries, rows, lanes = x.shape
    side, components = devices // 2, table.shape[0]
    args, specs, matrices = middle_inputs(table, mirror_map, x)
    members = components // GROUPS
    return pl.pallas_call(
        both_middle_kernel,
        in_specs=[pl.BlockSpec(memory_space=pltpu.SMEM)] + specs,
        out_specs=[pl.BlockSpec(memory_space=pltpu.VMEM)] * near,
        out_shape=[jax.ShapeDtypeStruct((halves, 2, components, rows, lanes), jnp.float32)] * near,
        scratch_shapes=[
            matrices,
            matrices,
            pltpu.VMEM((halves, 2, 2, side, entries, rows, lanes), jnp.float32),
            pltpu.VMEM((halves, 2, side, 2, entries, rows, lanes), jnp.float32),
            pltpu.VMEM((halves * GROUPS, 2, near // 2, members, rows, 2 * lanes), jnp.float32),
        ],
        compiler_params=pltpu.CompilerParams(vmem_limit_bytes=60 << 20),
        name="both_middle",
    )(me, *args)


def both_frequency_kernel(me_ref, m_ref, *refs):
    pieces, (out_ref, stage, sems) = refs[:-3], refs[-3:]
    near = len(pieces)
    components, lanes = stage.shape[1:3]
    groups = sems.shape[0]
    members = components // groups
    me = me_ref[0] % near
    matrix = split_value(jnp.concatenate([m_ref[part, slot ^ me] for part in range(2) for slot in range(near)], axis=0))

    def gathered(half, ri, c):
        return jnp.concatenate([piece[half, ri, c] for piece in pieces], axis=0)

    copies = []
    for group in range(groups):
        values = []
        for c in range(group * members, (group + 1) * members):
            part = [[gathered(half, ri, c) for ri in range(2)] for half in range(2)]
            sums = [part[0][ri] + part[1][ri] for ri in range(2)]
            differences = [part[0][ri] - part[1][ri] for ri in range(2)]
            values.append(jnp.concatenate([sums[0], -differences[1]], axis=0).T)
            values.append(jnp.concatenate([sums[1], differences[0]], axis=0).T)
        d = dot3(split_value(jnp.concatenate(values, axis=0)), matrix, ((1,), (0,)))
        d = d.reshape(members, 2, lanes, d.shape[1])
        for ri in range(2):
            stage[ri, group * members : (group + 1) * members] = d[:, ri]
        cut = pl.ds(group * members, members)
        copies.append(pltpu.make_async_copy(stage.at[:, cut], out_ref.at[:, cut], sems.at[group]))
        copies[-1].start()
    for copy in copies:
        copy.wait()


def both_frequencies(pieces, matrix, me):
    _, _, components, _, lanes = pieces[0].shape
    shape = (2, components, lanes, matrix.shape[3])
    vmem = pl.BlockSpec(memory_space=pltpu.VMEM)
    return pl.pallas_call(
        both_frequency_kernel,
        in_specs=[pl.BlockSpec(memory_space=pltpu.SMEM)] + [vmem] * (1 + len(pieces)),
        out_specs=pl.BlockSpec(memory_space=pltpu.HBM),
        out_shape=jax.ShapeDtypeStruct(shape, jnp.float32),
        scratch_shapes=[pltpu.VMEM(shape, jnp.float32), pltpu.SemaphoreType.DMA((components // 2,))],
        compiler_params=pltpu.CompilerParams(vmem_limit_bytes=60 << 20),
        name="both_frequencies",
    )(me, matrix, *pieces)


def one_frequency_kernel(y_ref, m_ref, earlier_hbm, out_ref, earlier, stage, in_sems, sems):
    devices, _, components, rows, lanes = y_ref.shape
    groups = sems.shape[0]
    members = components // groups
    cuts = [pl.ds(group * members, members) for group in range(groups)]
    loads = [
        pltpu.make_async_copy(earlier_hbm.at[:, cut], earlier.at[:, cut], in_sems.at[group])
        for group, cut in enumerate(cuts)
    ]
    for copy in loads:
        copy.start()
    matrix = split_value(m_ref[...])
    upper_rows = lax.broadcasted_iota(jnp.int32, (devices, rows, lanes), 1) < rows // 2
    copies = []
    for group, cut in enumerate(cuts):
        values = []
        for c in range(group * members, (group + 1) * members):
            folded = []
            for ri in range(2):
                tile = y_ref[:, ri, c]
                turned = pltpu.roll(tile, rows // 2, 1)
                folded.append((tile + turned, turned - tile))
            first = jnp.where(upper_rows, folded[0][0], -folded[1][1])
            second = jnp.where(upper_rows, folded[1][0], folded[0][1])
            values.append(first.reshape(devices * rows, lanes).T)
            values.append(second.reshape(devices * rows, lanes).T)
        d = dot3(split_value(jnp.concatenate(values, axis=0)), matrix, ((1,), (0,)))
        d = d.reshape(members, 2, lanes, d.shape[1])
        loads[group].wait()
        for ri in range(2):
            own = slice(group * members, (group + 1) * members)
            stage[ri, own] = earlier[ri, own] + d[:, ri]
        copies.append(pltpu.make_async_copy(stage.at[:, cut], out_ref.at[:, cut], sems.at[group]))
        copies[-1].start()
    for copy in copies:
        copy.wait()


def one_frequencies(y, matrix, earlier):
    vmem = pl.BlockSpec(memory_space=pltpu.VMEM)
    hbm = pl.BlockSpec(memory_space=pltpu.HBM)
    groups = earlier.shape[1] // 2
    return pl.pallas_call(
        one_frequency_kernel,
        in_specs=[vmem, vmem, hbm],
        out_specs=hbm,
        out_shape=jax.ShapeDtypeStruct(earlier.shape, jnp.float32),
        scratch_shapes=[
            pltpu.VMEM(earlier.shape, jnp.float32),
            pltpu.VMEM(earlier.shape, jnp.float32),
            pltpu.SemaphoreType.DMA((groups,)),
            pltpu.SemaphoreType.DMA((groups,)),
        ],
        compiler_params=pltpu.CompilerParams(vmem_limit_bytes=60 << 20),
        name="one_frequencies",
    )(y, matrix, earlier)


def exchange(x):
    flat = x.reshape(x.shape[0], -1, x.shape[-1])
    return lax.all_to_all(flat, "kb", split_axis=0, concat_axis=0, tiled=True).reshape(x.shape)


def swap(piece, slot, devices):
    if slot == 0:
        return piece
    return lax.ppermute(piece, "kb", [(device, device ^ slot) for device in range(devices)])


def trig_pair(angle_int, period, scale):
    angle = 2.0 * math.pi / period * angle_int.astype(jnp.float32)
    return (scale * jnp.cos(angle), scale * jnp.sin(angle))


def complex_combine(formula, cosine, sine, real_part, imag_part):
    first_term = jnp.einsum(formula, cosine, real_part + imag_part, precision=lax.Precision.HIGHEST)
    second_term = jnp.einsum(formula, cosine + sine, imag_part, precision=lax.Precision.HIGHEST)
    third_term = jnp.einsum(formula, sine - cosine, real_part, precision=lax.Precision.HIGHEST)
    return (first_term - second_term, first_term + third_term)


def forward_imaginary_time(tau_rows, frequency_count):
    freq_index = jnp.arange(frequency_count, dtype=jnp.int32)
    angle_int = (
        (2 * freq_index[None, :] - frequency_count + 1)
        * (2 * tau_rows[:, None] + 1)
        % (4 * frequency_count)
    )
    cosine, sine = trig_pair(angle_int, 4 * frequency_count, frequency_count ** (-0.5))
    return (cosine, -sine)


def tau_backward(tau_rows, frequency_count):
    freq_index = jnp.arange(frequency_count, dtype=jnp.int32)
    angle_int = (
        (freq_index[:, None] - frequency_count // 2)
        * (2 * tau_rows[None, :] + 1)
        % (2 * frequency_count)
    )
    return trig_pair(angle_int, 2 * frequency_count, frequency_count ** (-0.5))


def grid_transform(real_part, imag_part, grid_side, direction):
    shape = real_part.shape
    plane = jnp.arange(grid_side * grid_side, dtype=jnp.int32)
    upper = plane // grid_side
    lower = plane % grid_side
    plane_int = (upper[:, None] * upper[None, :] + lower[:, None] * lower[None, :]) % grid_side
    plane_cos, plane_sin = trig_pair(plane_int, grid_side, 1.0 / grid_side)
    line = jnp.arange(grid_side, dtype=jnp.int32)
    line_cos, line_sin = trig_pair(
        line[:, None] * line[None, :] % grid_side, grid_side, grid_side ** (-0.5)
    )
    real_part = real_part.reshape(shape[:-1] + (grid_side, grid_side * grid_side))
    imag_part = imag_part.reshape(shape[:-1] + (grid_side, grid_side * grid_side))
    real_part, imag_part = complex_combine(
        "pq,...xq->...xp", plane_cos, direction * plane_sin, real_part, imag_part
    )
    real_part, imag_part = complex_combine(
        "ax,...xp->...ap", line_cos, direction * line_sin, real_part, imag_part
    )
    return (real_part.reshape(shape), imag_part.reshape(shape))


def mirror_index(mirror_map, grid_side):
    index_x = mirror_map[0][:, None, None]
    index_y = mirror_map[1][None, :, None]
    index_z = mirror_map[2][None, None, :]
    return (index_x * grid_side * grid_side + index_y * grid_side + index_z).reshape(-1)


def bubble(gr_re, gr_im, mirror_re, mirror_im, pair_table, entries):
    entry_ids = jnp.arange(entries, dtype=jnp.int32)
    pick_left = (pair_table[:, 0][:, None] == entry_ids[None, :]).astype(jnp.float32)
    pick_right = (pair_table[:, 1][:, None] == entry_ids[None, :]).astype(jnp.float32)
    left_re = jnp.einsum("me,e...->m...", pick_left, gr_re, precision=lax.Precision.HIGHEST)
    left_im = jnp.einsum("me,e...->m...", pick_left, gr_im, precision=lax.Precision.HIGHEST)
    right_re = jnp.einsum("me,e...->m...", pick_right, mirror_re, precision=lax.Precision.HIGHEST)
    right_im = jnp.einsum("me,e...->m...", pick_right, mirror_im, precision=lax.Precision.HIGHEST)
    return (left_re * right_re - left_im * right_im, left_re * right_im + left_im * right_re)


def general(green_momentum_grid, pair_table, mirror_map):
    grid_side = mirror_map.shape[1]
    entries = green_momentum_grid.shape[1]
    frequency_count = green_momentum_grid.shape[3]
    position = jnp.arange(frequency_count, dtype=jnp.int32)
    fwd_cos, fwd_sin = forward_imaginary_time(position, frequency_count)
    tau_re, tau_im = complex_combine(
        "qa,fsa->fqs", fwd_cos, fwd_sin, green_momentum_grid[0], green_momentum_grid[1]
    )
    stacked = jnp.stack([tau_re, tau_im])

    def to_real_space(pieces):
        space_re, space_im = grid_transform(pieces[0], pieces[1], grid_side, 1.0)
        return jnp.stack([space_re, space_im])

    mirror_flat = mirror_index(mirror_map, grid_side)
    partner_rows = frequency_count - 1 - position
    reflected_cosine, reflected_sine = forward_imaginary_time(partner_rows, frequency_count)
    partner_real, partner_imaginary = complex_combine(
        "qa,fsa->fqs",
        reflected_cosine,
        reflected_sine,
        green_momentum_grid[0],
        green_momentum_grid[1],
    )
    other_stacked = jnp.stack([partner_real, partner_imaginary])
    pieces = (
        lax.all_to_all(stacked, "kb", split_axis=2, concat_axis=3, tiled=True),
        lax.all_to_all(other_stacked, "kb", split_axis=2, concat_axis=3, tiled=True),
    )
    in_cells = to_real_space(pieces[0])
    partner = to_real_space(pieces[1])
    mirrored = jnp.take(partner, mirror_flat, axis=3)
    chi_re, chi_im = bubble(in_cells[0], in_cells[1], mirrored[0], mirrored[1], pair_table, entries)
    chi_re, chi_im = grid_transform(chi_re, chi_im, grid_side, -1.0)
    momenta = jnp.stack([chi_re, chi_im])
    back_cos, back_sin = tau_backward(position, frequency_count)
    pieces = lax.all_to_all(momenta, "kb", split_axis=3, concat_axis=2, tiled=True)
    out_re, out_im = complex_combine("vj,ejk->ekv", back_cos, back_sin, pieces[0], pieces[1])
    return jnp.stack([out_re, out_im])


def local(green, pair_table, mirror_map):
    side = mirror_map.shape[1]
    plane = side * side
    lanes, count = green.shape[2], green.shape[3]
    devices = side * plane // lanes
    near = devices // 2
    half = ROWS // 2
    shared = near * ROWS
    if lanes != LANES or 2 * lanes != plane or 2 * (shared + devices * half) != count:
        return general(green, pair_table, mirror_map)
    me = lax.axis_index("kb").astype(jnp.int32).reshape(1)
    entries = green.shape[1]

    rows = np.arange(shared)
    both_fermion = fermion_matrix(rows, count).astype(np.float32)
    both_boson = boson_matrix(rows, count).reshape(2, near, ROWS, count).astype(np.float32)
    rows = shared + np.arange(devices * half).reshape(devices, half)
    times = np.concatenate([rows, count - 1 - rows], axis=1).reshape(-1)
    one_fermion = fermion_matrix(times, count).astype(np.float32)
    one_boson = boson_matrix(rows.reshape(-1), count).reshape(2, devices, half, count).swapaxes(0, 1)
    one_boson = one_boson.reshape(devices * ROWS, count).astype(np.float32)

    shape = (near, 2, 2, entries, ROWS, lanes)
    both = to_times(both_times_kernel, green, jnp.asarray(both_fermion), shape, devices, "both_times")
    green, both = lax.optimization_barrier((green, both))
    shape = (devices, 2, entries, ROWS, lanes)
    one = to_times(one_times_kernel, green, jnp.asarray(one_fermion), shape, devices, "one_times")
    both, one = lax.optimization_barrier((exchange(both), one))
    pieces = both_middle(both, pair_table, mirror_map, me, near)
    early = [swap(piece, slot, devices) for slot, piece in enumerate(pieces[: near // 2 + 1])]
    one, early = lax.optimization_barrier((exchange(one), early))
    one = exchange(one_middle(one, pair_table, mirror_map))
    late = [swap(pieces[slot], slot, devices) for slot in range(len(early), near)]
    earlier = both_frequencies(early + late, jnp.asarray(both_boson), me)
    return one_frequencies(one, jnp.asarray(one_boson), earlier)


def solution(mesh):
    placed = (P("set", None, "kb", None), P(), P("set", None))
    return jax.shard_map(
        local, mesh=mesh, in_specs=placed, out_specs=P("set", None, "kb", None), check_vma=False
    )
```

```python
import functools
import math

import jax
import jax.numpy as jnp
import ml_dtypes
import numpy as np
from jax import lax
from jax.experimental import pallas as pl
from jax.experimental.pallas import tpu as pltpu
from jax.sharding import PartitionSpec as P

LANES = 128
ROWS = 8
GROUPS = 2


def split_constant(matrix):
    high = matrix.astype(np.float32).astype(ml_dtypes.bfloat16)
    low = (matrix - high.astype(np.float64)).astype(np.float32).astype(ml_dtypes.bfloat16)
    return high, low


def split_value(value):
    high = value.astype(jnp.bfloat16)
    low = (value - high.astype(jnp.float32)).astype(jnp.bfloat16)
    return high, low


def dot3(left, right, dims):
    (k_left,), (k_right,) = dims
    a = jnp.concatenate([left[0], left[0], left[1]], axis=k_left)
    b = jnp.concatenate([right[0], right[1], right[0]], axis=k_right)
    return lax.dot_general(a, b, (dims, ((), ())), preferred_element_type=jnp.float32)


def fermion_matrix(rows, count):
    n = np.arange(count, dtype=np.int64)
    angle = ((2 * n[None, :] - count + 1) * (2 * rows[:, None] + 1)) % (4 * count)
    angle = np.pi * angle / (2 * count)
    return np.concatenate([np.cos(angle), np.sin(angle)], axis=0) * count**-0.5


def boson_matrix(rows, count):
    v = np.arange(count, dtype=np.int64)
    angle = ((v[None, :] - count // 2) * (2 * rows[:, None] + 1)) % (2 * count)
    angle = np.pi * angle / count
    return np.concatenate([np.cos(angle), np.sin(angle)], axis=0) * count**-0.5


def plane_parts(side):
    p = np.arange(side * side, dtype=np.int64)
    angle = ((p[:, None] // side) * (p[None, :] // side) + (p[:, None] % side) * (p[None, :] % side)) % side
    angle = 2 * np.pi * angle / side
    scale = side**-1.5
    return np.cos(angle) * scale, np.sin(angle) * scale


def times_w4(re, im, power, sign):
    power = (power * sign) % 4
    if power == 0:
        return re, im
    if power == 1:
        return -im, re
    if power == 2:
        return -re, -im
    return im, -re


def dft4(values, sign):
    (r0, i0), (r1, i1), (r2, i2), (r3, i3) = values
    sr, si, dr, di = r0 + r2, i0 + i2, r0 - r2, i0 - i2
    tr, ti, er, ei = r1 + r3, i1 + i3, r1 - r3, i1 - i3
    if sign > 0:
        return [(sr + tr, si + ti), (dr - ei, di + er), (sr - tr, si - ti), (dr + ei, di - er)]
    return [(sr + tr, si + ti), (dr + ei, di - er), (sr - tr, si - ti), (dr - ei, di + er)]


def twiddle(value, power, sign, side):
    re, im = value
    if power % (side // 4) == 0:
        return times_w4(re, im, power // (side // 4), sign)
    angle = 2.0 * np.pi * power / side
    c, s = float(np.cos(angle)), float(sign * np.sin(angle))
    return re * c - im * s, re * s + im * c


def dft_line(values, sign):
    side = len(values)
    if side == 1:
        return values
    if side == 2:
        (r0, i0), (r1, i1) = values
        return [(r0 + r1, i0 + i1), (r0 - r1, i0 - i1)]
    if side == 4:
        return dft4(values, sign)
    inner = side // 4
    parts = [dft_line(values[b::4], sign) for b in range(4)]
    out = [None] * side
    for k1 in range(inner):
        column = [twiddle(parts[b][k1], b * k1, sign, side) for b in range(4)]
        for k2, value in enumerate(dft4(column, sign)):
            out[k1 + inner * k2] = value
    return out


def half_line(values, sign, parity):
    side = len(values)
    inner = side // 4
    parts = [dft_line(values[b::4], sign) for b in range(4)]
    out = [None] * (side // 2)
    for k1 in range(inner):
        column = [twiddle(parts[b][k1], b * k1, sign, side) for b in range(4)]
        column = [(re * parity, im * parity) if b % 2 else (re, im) for b, (re, im) in enumerate(column)]
        for k2, value in enumerate(dft4(column, sign)[:2]):
            out[k1 + inner * k2] = value
    return out


def load_inputs(g_hbm, m_hbm, g_ref, m_ref, in_sems, m_sem):
    load = pltpu.make_async_copy(m_hbm, m_ref, m_sem)
    pieces = [
        pltpu.make_async_copy(g_hbm.at[:, pl.ds(e, 1)], g_ref.at[:, pl.ds(e, 1)], in_sems.at[e])
        for e in range(g_ref.shape[1])
    ]
    for copy in [load] + pieces:
        copy.start()
    load.wait()
    return pieces


def sums_of(matrix, g_ref, e):
    lanes = g_ref.shape[2]
    g = jnp.concatenate([g_ref[0, e], g_ref[1, e]], axis=0)
    d = dot3(matrix, split_value(g), ((1,), (1,)))
    half = d.shape[0] // 2
    return d[:half, :lanes], d[:half, lanes:], d[half:, :lanes], d[half:, lanes:]


def both_times_kernel(g_hbm, m_hbm, out_ref, g_ref, m_ref, stage, in_sems, m_sem, out_sems):
    entries, lanes = g_ref.shape[1:3]
    near, _, _, _, rows, _ = stage.shape
    pieces = load_inputs(g_hbm, m_hbm, g_ref, m_ref, in_sems, m_sem)
    matrix = split_value(m_ref[...])
    copies = []
    for e in range(entries):
        pieces[e].wait()
        c_re, c_im, s_re, s_im = sums_of(matrix, g_ref, e)
        for where, value in (
            ((0, 0), c_re + s_im),
            ((0, 1), c_im - s_re),
            ((1, 0), s_im - c_re),
            ((1, 1), -(c_im + s_re)),
        ):
            stage[:, where[0], where[1], e] = value.reshape(near, rows, lanes)
        cut = pl.ds(e, 1)
        for side in range(2):
            target = out_ref.at[pl.ds(side * near, near), :, :, cut]
            copies.append(pltpu.make_async_copy(stage.at[:, :, :, cut], target, out_sems.at[e, side]))
            copies[-1].start()
    for copy in copies:
        copy.wait()


def one_times_kernel(g_hbm, m_hbm, out_ref, g_ref, m_ref, stage, in_sems, m_sem, out_sems):
    entries, lanes = g_ref.shape[1:3]
    devices, _, _, rows, _ = stage.shape
    pieces = load_inputs(g_hbm, m_hbm, g_ref, m_ref, in_sems, m_sem)
    matrix = split_value(m_ref[...])
    copies = []
    for e in range(entries):
        pieces[e].wait()
        c_re, c_im, s_re, s_im = sums_of(matrix, g_ref, e)
        stage[:, 0, e] = (c_re + s_im).reshape(devices, rows, lanes)
        stage[:, 1, e] = (c_im - s_re).reshape(devices, rows, lanes)
        cut = pl.ds(e, 1)
        copies.append(pltpu.make_async_copy(stage.at[:, :, cut], out_ref.at[:, :, cut], out_sems.at[e, 0]))
        copies[-1].start()
    for copy in copies:
        copy.wait()


def to_times(kernel, green, matrix, shape, targets, name):
    entries = green.shape[1]
    hbm = pl.BlockSpec(memory_space=pltpu.HBM)
    return pl.pallas_call(
        kernel,
        in_specs=[hbm, hbm],
        out_specs=hbm,
        out_shape=jax.ShapeDtypeStruct((targets,) + shape[1:], jnp.float32),
        scratch_shapes=[
            pltpu.VMEM(green.shape, jnp.float32),
            pltpu.VMEM(matrix.shape, jnp.float32),
            pltpu.VMEM(shape, jnp.float32),
            pltpu.SemaphoreType.DMA((entries,)),
            pltpu.SemaphoreType.DMA,
            pltpu.SemaphoreType.DMA((entries, 2)),
        ],
        compiler_params=pltpu.CompilerParams(vmem_limit_bytes=60 << 20),
        name=name,
    )(green, matrix)


def fill_block(ref, cosine, sine):
    plane = cosine.shape[0]
    lanes = plane // 2
    for block in range(2):
        cut = slice(block * lanes, (block + 1) * lanes)
        re = slice(2 * block * lanes, (2 * block + 1) * lanes)
        im = slice((2 * block + 1) * lanes, (2 * block + 2) * lanes)
        ref[:plane, re] = cosine[:, cut].astype(jnp.bfloat16)
        ref[plane:, im] = cosine[:, cut].astype(jnp.bfloat16)
        ref[:plane, im] = sine[:, cut].astype(jnp.bfloat16)
        ref[plane:, re] = (-sine[:, cut]).astype(jnp.bfloat16)


def fill_matrices(mirror_ref, parts, forward, backward, turned):
    plane = parts[0].shape[0]
    side = mirror_ref.shape[1]
    row = lax.broadcasted_iota(jnp.int32, (plane, plane), 0)
    column = lax.broadcasted_iota(jnp.int32, (plane, plane), 1)
    upper = (mirror_ref[1, 0] - column // side) & (side - 1)
    lower = (mirror_ref[2, 0] - column % side) & (side - 1)
    pick = (row == upper * side + lower).astype(jnp.float32).astype(jnp.bfloat16)

    def dot(a, b):
        return jnp.dot(a, b, preferred_element_type=jnp.float32)

    for part in range(2):
        c_ref, s_ref = parts[part], parts[2 + part]
        cosine, sine = c_ref[...].astype(jnp.float32), s_ref[...].astype(jnp.float32)
        fill_block(forward.at[0, part], cosine, sine)
        fill_block(backward.at[0, part], turned(cosine), turned(-sine))
        fill_block(forward.at[1, part], dot(c_ref[...], pick), dot(s_ref[...], pick))
        fill_block(backward.at[1, part], turned(dot(pick, c_ref[...])), turned(-dot(pick, s_ref[...])))


def plane_dot(value, matrix, half, block):
    width = matrix.shape[3] // 2
    cut = slice(block * width, (block + 1) * width)
    return dot3(value, (matrix[half, 0, :, cut], matrix[half, 1, :, cut]), ((1,), (0,)))


def one_middle_kernel(table_ref, mirror_ref, ch_ref, cl_ref, sh_ref, sl_ref, x_ref, out_ref, *refs):
    forward, backward, mid, space, other_space, chi, stage, sems = refs
    _, side, _, entries, rows, lanes = space.shape
    plane = 2 * lanes
    groups, _, _, members, _, _ = chi.shape
    fill_matrices(mirror_ref, (ch_ref, cl_ref, sh_ref, sl_ref), forward, backward, lambda value: value)

    def paired(first, second):
        upper = lax.broadcasted_iota(jnp.int32, first.shape, 1) < rows // 2
        turned = [pltpu.roll(part, rows // 2, 1) for part in (first, second)]
        return jnp.where(upper, first, turned[1]), jnp.where(upper, turned[0], second)

    def halves_of(columns):
        value = jnp.concatenate(columns, axis=1)
        count, width = value.shape
        value = value.reshape(count // (2 * rows), 2, rows, width)
        parts = paired(value[:, 0], value[:, 1])
        return [split_value(part.reshape(count // 2, width)) for part in parts]

    def halves_dot(parts, matrix, block):
        shape = (parts[0][0].shape[0] // rows, rows, plane)
        d = paired(*(plane_dot(parts[half], matrix, half, block).reshape(shape) for half in range(2)))
        return jnp.concatenate([part.reshape(shape[0], 1, rows, plane) for part in d], axis=1)

    parts = halves_of([x_ref[:, h, ri].reshape(side * entries * rows, lanes) for ri in range(2) for h in range(2)])
    for block in range(2):
        d = halves_dot(parts, forward, block)
        for ri in range(2):
            piece = d[:, :, :, ri * lanes : (ri + 1) * lanes]
            mid[block, ri] = piece.reshape(side, entries, rows, lanes)
    for block in range(2):
        for e in range(entries):
            values = [(mid[block, 0, x, e], mid[block, 1, x, e]) for x in range(side)]
            for x, parts in enumerate(dft_line(values, 1)):
                for ri in range(2):
                    space[block, x, ri, e] = parts[ri]
                    other_space[block, x, ri, e] = pltpu.roll(parts[ri], rows // 2, 0)

    copies = []
    for group in range(groups):
        for c in range(members):
            left, right = table_ref[0, group * members + c], table_ref[1, group * members + c]
            for block in range(2):
                values = []
                for x in range(side):
                    other = mirror_ref[0, x]
                    a_re, a_im = space[block, x, 0, left], space[block, x, 1, left]
                    b_re, b_im = other_space[block, other, 0, right], other_space[block, other, 1, right]
                    values.append((a_re * b_re - a_im * b_im, a_re * b_im + a_im * b_re))
                cut = slice(block * lanes, (block + 1) * lanes)
                for x, parts in enumerate(dft_line(values, -1)):
                    for ri in range(2):
                        chi[group, ri, x, c, :, cut] = parts[ri]
        whole = (side * members * rows, plane)
        parts = halves_of([chi[group, ri].reshape(whole) for ri in range(2)])
        for h in range(2):
            d = halves_dot(parts, backward, h)
            for ri in range(2):
                piece = d[:, :, :, ri * lanes : (ri + 1) * lanes].reshape(side, members, rows, lanes)
                stage[group, :, h, ri] = piece
        target = out_ref.at[:, :, :, pl.ds(group * members, members)]
        copies.append(pltpu.make_async_copy(stage.at[group], target, sems.at[group]))
        copies[-1].start()
    for copy in copies:
        copy.wait()


def both_middle_kernel(me_ref, table_ref, mirror_ref, ch_ref, cl_ref, sh_ref, sl_ref, x_ref, *refs):
    outs, (forward, backward, mid, space, chi) = refs[:-5], refs[-5:]
    halves, _, side, _, entries, rows, lanes = space.shape
    plane = 2 * lanes
    units, _, kept, members, _, _ = chi.shape
    me, near = me_ref[0], len(outs)
    core, line = me % 2, me // 2 % kept
    parity = (1 - 2 * (me // near)).astype(jnp.float32)

    def turned(value):
        return jnp.where(core == 0, value, jnp.concatenate([value[:, lanes:], value[:, :lanes]], axis=1))

    fill_matrices(mirror_ref, (ch_ref, cl_ref, sh_ref, sl_ref), forward, backward, turned)

    def arrive(half):
        columns = [
            x_ref[:, h, half, ri].reshape(side * entries * rows, lanes) for ri in range(2) for h in range(2)
        ]
        return split_value(jnp.concatenate(columns, axis=1))

    def to_plane(value, half, block):
        d = plane_dot(value, forward, half, block)
        for ri in range(2):
            piece = d[:, ri * lanes : (ri + 1) * lanes]
            mid[half, block, ri] = piece.reshape(side, entries, rows, lanes)

    def along_line(half, block, e):
        values = [(mid[half, block, 0, x, e], mid[half, block, 1, x, e]) for x in range(side)]
        for x, (re, im) in enumerate(dft_line(values, 1)):
            space[half, block, x, 0, e] = re
            space[half, block, x, 1, e] = im

    def product(unit, block, c):
        half, first = unit % halves, unit // halves * members
        left, right = table_ref[0, first + c], table_ref[1, first + c]
        values = []
        for x in range(side):
            other = mirror_ref[0, x]
            a_re, a_im = space[half, block, x, 0, left], space[half, block, x, 1, left]
            b_re, b_im = space[1 - half, block, other, 0, right], space[1 - half, block, other, 1, right]
            values.append((a_re * b_re - a_im * b_im, a_re * b_im + a_im * b_re))
        cut = slice(block * lanes, (block + 1) * lanes)
        for x, (re, im) in enumerate(half_line(values, -1, parity)):
            chi[unit, 0, x ^ line, c, :, cut] = re
            chi[unit, 1, x ^ line, c, :, cut] = im

    def from_plane(unit, value, h):
        half, first = unit % halves, unit // halves * members
        d = plane_dot(value, backward, half, h)
        for ri in range(2):
            piece = d[:, ri * lanes : (ri + 1) * lanes].reshape(kept, members, rows, lanes)
            for x in range(kept):
                outs[2 * x + h][half, ri, first : first + members] = piece[x]

    def collect(unit):
        whole = (kept * members * rows, plane)
        return split_value(jnp.concatenate([chi[unit, ri].reshape(whole) for ri in range(2)], axis=1))

    places = [(half, block) for half in range(halves) for block in range(2)]
    for step in range(len(places) + 1):
        if step < len(places):
            half, block = places[step]
            if block == 0:
                value = arrive(half)
            to_plane(value, half, block)
        if step > 0:
            for e in range(entries):
                along_line(*places[step - 1], e)

    for unit in range(units + 1):
        tasks = [(block, c) for block in range(2) for c in range(members)] if unit < units else []
        if unit > 0:
            value = collect(unit - 1)
        for h in range(2):
            if unit > 0:
                from_plane(unit - 1, value, h)
            for block, c in tasks[h * members : (h + 1) * members]:
                product(unit, block, c)


def middle_inputs(table, mirror_map, x):
    side, plane = x.shape[0] // 2, 2 * x.shape[-1]
    cosine, sine = plane_parts(side)
    parts = [jnp.asarray(part) for part in split_constant(cosine) + split_constant(sine)]
    smem = pl.BlockSpec(memory_space=pltpu.SMEM)
    vmem = pl.BlockSpec(memory_space=pltpu.VMEM)
    args = (table.T, mirror_map, *parts, x.reshape((side, 2) + x.shape[1:]))
    return args, [smem, smem] + [vmem] * 5, pltpu.VMEM((2, 2, 2 * plane, 2 * plane), jnp.bfloat16)


def one_middle(x, table, mirror_map):
    devices, _, entries, rows, lanes = x.shape
    side, components = devices // 2, table.shape[0]
    args, specs, matrices = middle_inputs(table, mirror_map, x)
    spatial = pltpu.VMEM((2, side, 2, entries, rows, lanes), jnp.float32)
    shape = (side, 2, 2, components, rows, lanes)
    out = pl.pallas_call(
        one_middle_kernel,
        in_specs=specs,
        out_specs=pl.BlockSpec(memory_space=pltpu.HBM),
        out_shape=jax.ShapeDtypeStruct(shape, jnp.float32),
        scratch_shapes=[
            matrices,
            matrices,
            pltpu.VMEM((2, 2, side, entries, rows, lanes), jnp.float32),
            spatial,
            spatial,
            pltpu.VMEM((GROUPS, 2, side, components // GROUPS, rows, 2 * lanes), jnp.float32),
            pltpu.VMEM((GROUPS, side, 2, 2, components // GROUPS, rows, lanes), jnp.float32),
            pltpu.SemaphoreType.DMA((GROUPS,)),
        ],
        compiler_params=pltpu.CompilerParams(vmem_limit_bytes=44 << 20),
        name="one_middle",
    )(*args)
    return out.reshape((devices,) + shape[2:])


def both_middle(x, table, mirror_map, me, near):
    devices, halves, _, entries, rows, lanes = x.shape
    side, components = devices // 2, table.shape[0]
    args, specs, matrices = middle_inputs(table, mirror_map, x)
    members = components // GROUPS
    return pl.pallas_call(
        both_middle_kernel,
        in_specs=[pl.BlockSpec(memory_space=pltpu.SMEM)] + specs,
        out_specs=[pl.BlockSpec(memory_space=pltpu.VMEM)] * near,
        out_shape=[jax.ShapeDtypeStruct((halves, 2, components, rows, lanes), jnp.float32)] * near,
        scratch_shapes=[
            matrices,
            matrices,
            pltpu.VMEM((halves, 2, 2, side, entries, rows, lanes), jnp.float32),
            pltpu.VMEM((halves, 2, side, 2, entries, rows, lanes), jnp.float32),
            pltpu.VMEM((halves * GROUPS, 2, near // 2, members, rows, 2 * lanes), jnp.float32),
        ],
        compiler_params=pltpu.CompilerParams(vmem_limit_bytes=60 << 20),
        name="both_middle",
    )(me, *args)


def frequency_kernel(me_ref, both_ref, one_ref, y_ref, *refs):
    pieces, (out_ref, held, stage, in_sems, sems) = refs[:-5], refs[-5:]
    near = len(pieces)
    devices, _, components, rows, lanes = y_ref.shape
    groups = sems.shape[0]
    members = components // groups
    loads = [pltpu.make_async_copy(piece, held.at[slot], in_sems.at[slot]) for slot, piece in enumerate(pieces)]
    for copy in loads:
        copy.start()
    me = me_ref[0] % near
    both = [both_ref[part, slot ^ me] for part in range(2) for slot in range(near)]
    matrix = split_value(jnp.concatenate(both + [one_ref[...]], axis=0))
    upper_rows = lax.broadcasted_iota(jnp.int32, (devices, rows, lanes), 1) < rows // 2
    for copy in loads:
        copy.wait()

    copies = []
    for group in range(groups):
        values = []
        for c in range(group * members, (group + 1) * members):
            part = [[held[:, half, ri, c].reshape(near * rows, lanes) for ri in range(2)] for half in range(2)]
            sums = [part[0][ri] + part[1][ri] for ri in range(2)]
            differences = [part[0][ri] - part[1][ri] for ri in range(2)]
            folded = []
            for ri in range(2):
                tile = y_ref[:, ri, c]
                turned = pltpu.roll(tile, rows // 2, 1)
                folded.append((tile + turned, turned - tile))
            first = jnp.where(upper_rows, folded[0][0], -folded[1][1]).reshape(devices * rows, lanes)
            second = jnp.where(upper_rows, folded[1][0], folded[0][1]).reshape(devices * rows, lanes)
            values.append(jnp.concatenate([sums[0], -differences[1], first], axis=0).T)
            values.append(jnp.concatenate([sums[1], differences[0], second], axis=0).T)
        d = dot3(split_value(jnp.concatenate(values, axis=0)), matrix, ((1,), (0,)))
        d = d.reshape(members, 2, lanes, d.shape[1])
        for ri in range(2):
            stage[ri, group * members : (group + 1) * members] = d[:, ri]
        cut = pl.ds(group * members, members)
        copies.append(pltpu.make_async_copy(stage.at[:, cut], out_ref.at[:, cut], sems.at[group]))
        copies[-1].start()
    for copy in copies:
        copy.wait()


def to_frequencies(y, pieces, both, one, me):
    _, _, components, _, lanes = y.shape
    shape = (2, components, lanes, one.shape[1])
    vmem = pl.BlockSpec(memory_space=pltpu.VMEM)
    hbm = pl.BlockSpec(memory_space=pltpu.HBM)
    return pl.pallas_call(
        frequency_kernel,
        in_specs=[pl.BlockSpec(memory_space=pltpu.SMEM)] + [vmem] * 3 + [hbm] * len(pieces),
        out_specs=hbm,
        out_shape=jax.ShapeDtypeStruct(shape, jnp.float32),
        scratch_shapes=[
            pltpu.VMEM((len(pieces),) + pieces[0].shape, jnp.float32),
            pltpu.VMEM(shape, jnp.float32),
            pltpu.SemaphoreType.DMA((len(pieces),)),
            pltpu.SemaphoreType.DMA((components // 2,)),
        ],
        compiler_params=pltpu.CompilerParams(vmem_limit_bytes=60 << 20),
        name="to_frequencies",
    )(me, both, one, y, *pieces)


def exchange(x):
    flat = x.reshape(x.shape[0], -1, x.shape[-1])
    return lax.all_to_all(flat, "kb", split_axis=0, concat_axis=0, tiled=True).reshape(x.shape)


def swap(piece, slot, devices):
    if slot == 0:
        return piece
    return lax.ppermute(piece, "kb", [(device, device ^ slot) for device in range(devices)])


def trig_pair(angle_int, period, scale):
    angle = 2.0 * math.pi / period * angle_int.astype(jnp.float32)
    return (scale * jnp.cos(angle), scale * jnp.sin(angle))


def complex_combine(formula, cosine, sine, real_part, imag_part):
    first_term = jnp.einsum(formula, cosine, real_part + imag_part, precision=lax.Precision.HIGHEST)
    second_term = jnp.einsum(formula, cosine + sine, imag_part, precision=lax.Precision.HIGHEST)
    third_term = jnp.einsum(formula, sine - cosine, real_part, precision=lax.Precision.HIGHEST)
    return (first_term - second_term, first_term + third_term)


def forward_imaginary_time(tau_rows, frequency_count):
    freq_index = jnp.arange(frequency_count, dtype=jnp.int32)
    angle_int = (
        (2 * freq_index[None, :] - frequency_count + 1)
        * (2 * tau_rows[:, None] + 1)
        % (4 * frequency_count)
    )
    cosine, sine = trig_pair(angle_int, 4 * frequency_count, frequency_count ** (-0.5))
    return (cosine, -sine)


def tau_backward(tau_rows, frequency_count):
    freq_index = jnp.arange(frequency_count, dtype=jnp.int32)
    angle_int = (
        (freq_index[:, None] - frequency_count // 2)
        * (2 * tau_rows[None, :] + 1)
        % (2 * frequency_count)
    )
    return trig_pair(angle_int, 2 * frequency_count, frequency_count ** (-0.5))


def grid_transform(real_part, imag_part, grid_side, direction):
    shape = real_part.shape
    plane = jnp.arange(grid_side * grid_side, dtype=jnp.int32)
    upper = plane // grid_side
    lower = plane % grid_side
    plane_int = (upper[:, None] * upper[None, :] + lower[:, None] * lower[None, :]) % grid_side
    plane_cos, plane_sin = trig_pair(plane_int, grid_side, 1.0 / grid_side)
    line = jnp.arange(grid_side, dtype=jnp.int32)
    line_cos, line_sin = trig_pair(
        line[:, None] * line[None, :] % grid_side, grid_side, grid_side ** (-0.5)
    )
    real_part = real_part.reshape(shape[:-1] + (grid_side, grid_side * grid_side))
    imag_part = imag_part.reshape(shape[:-1] + (grid_side, grid_side * grid_side))
    real_part, imag_part = complex_combine(
        "pq,...xq->...xp", plane_cos, direction * plane_sin, real_part, imag_part
    )
    real_part, imag_part = complex_combine(
        "ax,...xp->...ap", line_cos, direction * line_sin, real_part, imag_part
    )
    return (real_part.reshape(shape), imag_part.reshape(shape))


def mirror_index(mirror_map, grid_side):
    index_x = mirror_map[0][:, None, None]
    index_y = mirror_map[1][None, :, None]
    index_z = mirror_map[2][None, None, :]
    return (index_x * grid_side * grid_side + index_y * grid_side + index_z).reshape(-1)


def bubble(gr_re, gr_im, mirror_re, mirror_im, pair_table, entries):
    entry_ids = jnp.arange(entries, dtype=jnp.int32)
    pick_left = (pair_table[:, 0][:, None] == entry_ids[None, :]).astype(jnp.float32)
    pick_right = (pair_table[:, 1][:, None] == entry_ids[None, :]).astype(jnp.float32)
    left_re = jnp.einsum("me,e...->m...", pick_left, gr_re, precision=lax.Precision.HIGHEST)
    left_im = jnp.einsum("me,e...->m...", pick_left, gr_im, precision=lax.Precision.HIGHEST)
    right_re = jnp.einsum("me,e...->m...", pick_right, mirror_re, precision=lax.Precision.HIGHEST)
    right_im = jnp.einsum("me,e...->m...", pick_right, mirror_im, precision=lax.Precision.HIGHEST)
    return (left_re * right_re - left_im * right_im, left_re * right_im + left_im * right_re)


def general(green_momentum_grid, pair_table, mirror_map):
    grid_side = mirror_map.shape[1]
    entries = green_momentum_grid.shape[1]
    frequency_count = green_momentum_grid.shape[3]
    position = jnp.arange(frequency_count, dtype=jnp.int32)
    fwd_cos, fwd_sin = forward_imaginary_time(position, frequency_count)
    tau_re, tau_im = complex_combine(
        "qa,fsa->fqs", fwd_cos, fwd_sin, green_momentum_grid[0], green_momentum_grid[1]
    )
    stacked = jnp.stack([tau_re, tau_im])

    def to_real_space(pieces):
        space_re, space_im = grid_transform(pieces[0], pieces[1], grid_side, 1.0)
        return jnp.stack([space_re, space_im])

    mirror_flat = mirror_index(mirror_map, grid_side)
    partner_rows = frequency_count - 1 - position
    reflected_cosine, reflected_sine = forward_imaginary_time(partner_rows, frequency_count)
    partner_real, partner_imaginary = complex_combine(
        "qa,fsa->fqs",
        reflected_cosine,
        reflected_sine,
        green_momentum_grid[0],
        green_momentum_grid[1],
    )
    other_stacked = jnp.stack([partner_real, partner_imaginary])
    pieces = (
        lax.all_to_all(stacked, "kb", split_axis=2, concat_axis=3, tiled=True),
        lax.all_to_all(other_stacked, "kb", split_axis=2, concat_axis=3, tiled=True),
    )
    in_cells = to_real_space(pieces[0])
    partner = to_real_space(pieces[1])
    mirrored = jnp.take(partner, mirror_flat, axis=3)
    chi_re, chi_im = bubble(in_cells[0], in_cells[1], mirrored[0], mirrored[1], pair_table, entries)
    chi_re, chi_im = grid_transform(chi_re, chi_im, grid_side, -1.0)
    momenta = jnp.stack([chi_re, chi_im])
    back_cos, back_sin = tau_backward(position, frequency_count)
    pieces = lax.all_to_all(momenta, "kb", split_axis=3, concat_axis=2, tiled=True)
    out_re, out_im = complex_combine("vj,ejk->ekv", back_cos, back_sin, pieces[0], pieces[1])
    return jnp.stack([out_re, out_im])


def local(green, pair_table, mirror_map):
    side = mirror_map.shape[1]
    plane = side * side
    lanes, count = green.shape[2], green.shape[3]
    devices = side * plane // lanes
    near = devices // 2
    half = ROWS // 2
    shared = near * ROWS
    if lanes != LANES or 2 * lanes != plane or 2 * (shared + devices * half) != count:
        return general(green, pair_table, mirror_map)
    me = lax.axis_index("kb").astype(jnp.int32).reshape(1)
    entries = green.shape[1]

    rows = np.arange(shared)
    both_fermion = fermion_matrix(rows, count).astype(np.float32)
    both_boson = boson_matrix(rows, count).reshape(2, near, ROWS, count).astype(np.float32)
    rows = shared + np.arange(devices * half).reshape(devices, half)
    times = np.concatenate([rows, count - 1 - rows], axis=1).reshape(-1)
    one_fermion = fermion_matrix(times, count).astype(np.float32)
    one_boson = boson_matrix(rows.reshape(-1), count).reshape(2, devices, half, count).swapaxes(0, 1)
    one_boson = one_boson.reshape(devices * ROWS, count).astype(np.float32)

    shape = (near, 2, 2, entries, ROWS, lanes)
    both = to_times(both_times_kernel, green, jnp.asarray(both_fermion), shape, devices, "both_times")
    green, both = lax.optimization_barrier((green, both))
    shape = (devices, 2, entries, ROWS, lanes)
    one = to_times(one_times_kernel, green, jnp.asarray(one_fermion), shape, devices, "one_times")
    both, one = lax.optimization_barrier((exchange(both), one))
    pieces = both_middle(both, pair_table, mirror_map, me, near)
    middle_slot, quarter = near // 2, near // 4
    order = list(range(middle_slot, middle_slot + quarter)) + list(range(1, quarter + 1))
    early = [swap(pieces[slot], slot, devices) for slot in order]
    one, early = lax.optimization_barrier((exchange(one), early))
    one = exchange(one_middle(one, pair_table, mirror_map))
    rest = [slot for slot in reversed(range(near)) if slot not in order]
    moved = dict(zip(order, early)) | {slot: swap(pieces[slot], slot, devices) for slot in rest}
    pieces = [moved[slot] for slot in range(near)]
    return to_frequencies(one, pieces, jnp.asarray(both_boson), jnp.asarray(one_boson), me)


def solution(mesh):
    placed = (P("set", None, "kb", None), P(), P("set", None))
    return jax.shard_map(
        local, mesh=mesh, in_specs=placed, out_specs=P("set", None, "kb", None), check_vma=False
    )
```

```python
import functools
import math

import jax
import jax.numpy as jnp
import ml_dtypes
import numpy as np
from jax import lax
from jax.experimental import pallas as pl
from jax.experimental.pallas import tpu as pltpu
from jax.sharding import PartitionSpec as P

LANES = 128
ROWS = 8
GROUPS = 2


def split_constant(matrix):
    high = matrix.astype(np.float32).astype(ml_dtypes.bfloat16)
    low = (matrix - high.astype(np.float64)).astype(np.float32).astype(ml_dtypes.bfloat16)
    return high, low


def split_value(value):
    high = value.astype(jnp.bfloat16)
    low = (value - high.astype(jnp.float32)).astype(jnp.bfloat16)
    return high, low


def dot3(left, right, dims):
    (k_left,), (k_right,) = dims
    a = jnp.concatenate([left[0], left[0], left[1]], axis=k_left)
    b = jnp.concatenate([right[0], right[1], right[0]], axis=k_right)
    return lax.dot_general(a, b, (dims, ((), ())), preferred_element_type=jnp.float32)


def fermion_matrix(rows, count):
    n = np.arange(count, dtype=np.int64)
    angle = ((2 * n[None, :] - count + 1) * (2 * rows[:, None] + 1)) % (4 * count)
    angle = np.pi * angle / (2 * count)
    return np.concatenate([np.cos(angle), np.sin(angle)], axis=0) * count**-0.5


def boson_matrix(rows, count):
    v = np.arange(count, dtype=np.int64)
    angle = ((v[None, :] - count // 2) * (2 * rows[:, None] + 1)) % (2 * count)
    angle = np.pi * angle / count
    return np.concatenate([np.cos(angle), np.sin(angle)], axis=0) * count**-0.5


def plane_parts(side):
    p = np.arange(side * side, dtype=np.int64)
    angle = ((p[:, None] // side) * (p[None, :] // side) + (p[:, None] % side) * (p[None, :] % side)) % side
    angle = 2 * np.pi * angle / side
    scale = side**-1.5
    return np.cos(angle) * scale, np.sin(angle) * scale


def times_w4(re, im, power, sign):
    power = (power * sign) % 4
    if power == 0:
        return re, im
    if power == 1:
        return -im, re
    if power == 2:
        return -re, -im
    return im, -re


def dft4(values, sign):
    (r0, i0), (r1, i1), (r2, i2), (r3, i3) = values
    sr, si, dr, di = r0 + r2, i0 + i2, r0 - r2, i0 - i2
    tr, ti, er, ei = r1 + r3, i1 + i3, r1 - r3, i1 - i3
    if sign > 0:
        return [(sr + tr, si + ti), (dr - ei, di + er), (sr - tr, si - ti), (dr + ei, di - er)]
    return [(sr + tr, si + ti), (dr + ei, di - er), (sr - tr, si - ti), (dr - ei, di + er)]


def twiddle(value, power, sign, side):
    re, im = value
    if power % (side // 4) == 0:
        return times_w4(re, im, power // (side // 4), sign)
    angle = 2.0 * np.pi * power / side
    c, s = float(np.cos(angle)), float(sign * np.sin(angle))
    return re * c - im * s, re * s + im * c


def dft_line(values, sign):
    side = len(values)
    if side == 1:
        return values
    if side == 2:
        (r0, i0), (r1, i1) = values
        return [(r0 + r1, i0 + i1), (r0 - r1, i0 - i1)]
    if side == 4:
        return dft4(values, sign)
    inner = side // 4
    parts = [dft_line(values[b::4], sign) for b in range(4)]
    out = [None] * side
    for k1 in range(inner):
        column = [twiddle(parts[b][k1], b * k1, sign, side) for b in range(4)]
        for k2, value in enumerate(dft4(column, sign)):
            out[k1 + inner * k2] = value
    return out


def half_line(values, sign, parity):
    side = len(values)
    inner = side // 4
    parts = [dft_line(values[b::4], sign) for b in range(4)]
    out = [None] * (side // 2)
    for k1 in range(inner):
        column = [twiddle(parts[b][k1], b * k1, sign, side) for b in range(4)]
        column = [(re * parity, im * parity) if b % 2 else (re, im) for b, (re, im) in enumerate(column)]
        for k2, value in enumerate(dft4(column, sign)[:2]):
            out[k1 + inner * k2] = value
    return out


def load_inputs(g_hbm, m_hbm, g_ref, m_ref, in_sems, m_sem):
    load = pltpu.make_async_copy(m_hbm, m_ref, m_sem)
    pieces = [
        pltpu.make_async_copy(g_hbm.at[:, pl.ds(e, 1)], g_ref.at[:, pl.ds(e, 1)], in_sems.at[e])
        for e in range(g_ref.shape[1])
    ]
    for copy in [load] + pieces:
        copy.start()
    load.wait()
    return pieces


def sums_of(matrix, g_ref, e):
    lanes = g_ref.shape[2]
    g = jnp.concatenate([g_ref[0, e], g_ref[1, e]], axis=0)
    d = dot3(matrix, split_value(g), ((1,), (1,)))
    half = d.shape[0] // 2
    return d[:half, :lanes], d[:half, lanes:], d[half:, :lanes], d[half:, lanes:]


def both_times_kernel(g_hbm, m_hbm, out_ref, g_ref, m_ref, stage, in_sems, m_sem, out_sems):
    entries, lanes = g_ref.shape[1:3]
    near, _, _, _, rows, _ = stage.shape
    pieces = load_inputs(g_hbm, m_hbm, g_ref, m_ref, in_sems, m_sem)
    matrix = split_value(m_ref[...])
    copies = []
    for e in range(entries):
        pieces[e].wait()
        c_re, c_im, s_re, s_im = sums_of(matrix, g_ref, e)
        for where, value in (
            ((0, 0), c_re + s_im),
            ((0, 1), c_im - s_re),
            ((1, 0), s_im - c_re),
            ((1, 1), -(c_im + s_re)),
        ):
            stage[:, where[0], where[1], e] = value.reshape(near, rows, lanes)
        cut = pl.ds(e, 1)
        for side in range(2):
            target = out_ref.at[pl.ds(side * near, near), :, :, cut]
            copies.append(pltpu.make_async_copy(stage.at[:, :, :, cut], target, out_sems.at[e, side]))
            copies[-1].start()
    for copy in copies:
        copy.wait()


def one_times_kernel(g_hbm, m_hbm, out_ref, g_ref, m_ref, stage, in_sems, m_sem, out_sems):
    entries, lanes = g_ref.shape[1:3]
    devices, _, _, rows, _ = stage.shape
    pieces = load_inputs(g_hbm, m_hbm, g_ref, m_ref, in_sems, m_sem)
    matrix = split_value(m_ref[...])
    copies = []
    for e in range(entries):
        pieces[e].wait()
        c_re, c_im, s_re, s_im = sums_of(matrix, g_ref, e)
        stage[:, 0, e] = (c_re + s_im).reshape(devices, rows, lanes)
        stage[:, 1, e] = (c_im - s_re).reshape(devices, rows, lanes)
        cut = pl.ds(e, 1)
        copies.append(pltpu.make_async_copy(stage.at[:, :, cut], out_ref.at[:, :, cut], out_sems.at[e, 0]))
        copies[-1].start()
    for copy in copies:
        copy.wait()


def to_times(kernel, green, matrix, shape, targets, name):
    entries = green.shape[1]
    hbm = pl.BlockSpec(memory_space=pltpu.HBM)
    return pl.pallas_call(
        kernel,
        in_specs=[hbm, hbm],
        out_specs=hbm,
        out_shape=jax.ShapeDtypeStruct((targets,) + shape[1:], jnp.float32),
        scratch_shapes=[
            pltpu.VMEM(green.shape, jnp.float32),
            pltpu.VMEM(matrix.shape, jnp.float32),
            pltpu.VMEM(shape, jnp.float32),
            pltpu.SemaphoreType.DMA((entries,)),
            pltpu.SemaphoreType.DMA,
            pltpu.SemaphoreType.DMA((entries, 2)),
        ],
        compiler_params=pltpu.CompilerParams(vmem_limit_bytes=63 << 20),
        name=name,
    )(green, matrix)


def fill_block(ref, cosine, sine):
    plane = cosine.shape[0]
    lanes = plane // 2
    for block in range(2):
        cut = slice(block * lanes, (block + 1) * lanes)
        re = slice(2 * block * lanes, (2 * block + 1) * lanes)
        im = slice((2 * block + 1) * lanes, (2 * block + 2) * lanes)
        ref[:plane, re] = cosine[:, cut].astype(jnp.bfloat16)
        ref[plane:, im] = cosine[:, cut].astype(jnp.bfloat16)
        ref[:plane, im] = sine[:, cut].astype(jnp.bfloat16)
        ref[plane:, re] = (-sine[:, cut]).astype(jnp.bfloat16)


def fill_matrices(mirror_ref, parts, forward, backward, turned):
    plane = parts[0].shape[0]
    side = mirror_ref.shape[1]
    row = lax.broadcasted_iota(jnp.int32, (plane, plane), 0)
    column = lax.broadcasted_iota(jnp.int32, (plane, plane), 1)
    upper = (mirror_ref[1, 0] - column // side) & (side - 1)
    lower = (mirror_ref[2, 0] - column % side) & (side - 1)
    pick = (row == upper * side + lower).astype(jnp.float32).astype(jnp.bfloat16)

    def dot(a, b):
        return jnp.dot(a, b, preferred_element_type=jnp.float32)

    for part in range(2):
        c_ref, s_ref = parts[part], parts[2 + part]
        cosine, sine = c_ref[...].astype(jnp.float32), s_ref[...].astype(jnp.float32)
        fill_block(forward.at[0, part], cosine, sine)
        fill_block(backward.at[0, part], turned(cosine), turned(-sine))
        fill_block(forward.at[1, part], dot(c_ref[...], pick), dot(s_ref[...], pick))
        fill_block(backward.at[1, part], turned(dot(pick, c_ref[...])), turned(-dot(pick, s_ref[...])))


def plane_dot(value, matrix, half, block):
    width = matrix.shape[3] // 2
    cut = slice(block * width, (block + 1) * width)
    return dot3(value, (matrix[half, 0, :, cut], matrix[half, 1, :, cut]), ((1,), (0,)))


def one_middle_kernel(table_ref, mirror_ref, ch_ref, cl_ref, sh_ref, sl_ref, x_ref, out_ref, *refs):
    forward, backward, mid, space, other_space, chi, stage, sems = refs
    _, side, _, entries, rows, lanes = space.shape
    plane = 2 * lanes
    groups, _, _, members, _, _ = chi.shape
    fill_matrices(mirror_ref, (ch_ref, cl_ref, sh_ref, sl_ref), forward, backward, lambda value: value)

    def paired(first, second):
        upper = lax.broadcasted_iota(jnp.int32, first.shape, 1) < rows // 2
        turned = [pltpu.roll(part, rows // 2, 1) for part in (first, second)]
        return jnp.where(upper, first, turned[1]), jnp.where(upper, turned[0], second)

    def halves_of(columns):
        value = jnp.concatenate(columns, axis=1)
        count, width = value.shape
        value = value.reshape(count // (2 * rows), 2, rows, width)
        parts = paired(value[:, 0], value[:, 1])
        return [split_value(part.reshape(count // 2, width)) for part in parts]

    def halves_dot(parts, matrix, block):
        shape = (parts[0][0].shape[0] // rows, rows, plane)
        d = paired(*(plane_dot(parts[half], matrix, half, block).reshape(shape) for half in range(2)))
        return jnp.concatenate([part.reshape(shape[0], 1, rows, plane) for part in d], axis=1)

    parts = halves_of([x_ref[:, h, ri].reshape(side * entries * rows, lanes) for ri in range(2) for h in range(2)])
    for block in range(2):
        d = halves_dot(parts, forward, block)
        for ri in range(2):
            piece = d[:, :, :, ri * lanes : (ri + 1) * lanes]
            mid[block, ri] = piece.reshape(side, entries, rows, lanes)
    for block in range(2):
        for e in range(entries):
            values = [(mid[block, 0, x, e], mid[block, 1, x, e]) for x in range(side)]
            for x, parts in enumerate(dft_line(values, 1)):
                for ri in range(2):
                    space[block, x, ri, e] = parts[ri]
                    other_space[block, x, ri, e] = pltpu.roll(parts[ri], rows // 2, 0)

    copies = []
    for group in range(groups):
        for c in range(members):
            left, right = table_ref[0, group * members + c], table_ref[1, group * members + c]
            for block in range(2):
                values = []
                for x in range(side):
                    other = mirror_ref[0, x]
                    a_re, a_im = space[block, x, 0, left], space[block, x, 1, left]
                    b_re, b_im = other_space[block, other, 0, right], other_space[block, other, 1, right]
                    values.append((a_re * b_re - a_im * b_im, a_re * b_im + a_im * b_re))
                cut = slice(block * lanes, (block + 1) * lanes)
                for x, parts in enumerate(dft_line(values, -1)):
                    for ri in range(2):
                        chi[group, ri, x, c, :, cut] = parts[ri]
        whole = (side * members * rows, plane)
        parts = halves_of([chi[group, ri].reshape(whole) for ri in range(2)])
        for h in range(2):
            d = halves_dot(parts, backward, h)
            for ri in range(2):
                piece = d[:, :, :, ri * lanes : (ri + 1) * lanes].reshape(side, members, rows, lanes)
                stage[group, :, h, ri] = piece
        target = out_ref.at[:, :, :, pl.ds(group * members, members)]
        copies.append(pltpu.make_async_copy(stage.at[group], target, sems.at[group]))
        copies[-1].start()
    for copy in copies:
        copy.wait()


def both_middle_kernel(me_ref, table_ref, mirror_ref, ch_ref, cl_ref, sh_ref, sl_ref, x_ref, *refs):
    outs, (forward, backward, mid, space, chi) = refs[:-5], refs[-5:]
    halves, _, side, _, entries, rows, lanes = space.shape
    plane = 2 * lanes
    units, _, kept, members, _, _ = chi.shape
    me, near = me_ref[0], len(outs)
    core, line = me % 2, me // 2 % kept
    parity = (1 - 2 * (me // near)).astype(jnp.float32)

    def turned(value):
        return jnp.where(core == 0, value, jnp.concatenate([value[:, lanes:], value[:, :lanes]], axis=1))

    fill_matrices(mirror_ref, (ch_ref, cl_ref, sh_ref, sl_ref), forward, backward, turned)

    def arrive(half):
        columns = [
            x_ref[:, h, half, ri].reshape(side * entries * rows, lanes) for ri in range(2) for h in range(2)
        ]
        return split_value(jnp.concatenate(columns, axis=1))

    def to_plane(value, half, block):
        d = plane_dot(value, forward, half, block)
        for ri in range(2):
            piece = d[:, ri * lanes : (ri + 1) * lanes]
            mid[half, block, ri] = piece.reshape(side, entries, rows, lanes)

    def along_line(half, block, e):
        values = [(mid[half, block, 0, x, e], mid[half, block, 1, x, e]) for x in range(side)]
        for x, (re, im) in enumerate(dft_line(values, 1)):
            space[half, block, x, 0, e] = re
            space[half, block, x, 1, e] = im

    def product(unit, block, c):
        half, first = unit % halves, unit // halves * members
        left, right = table_ref[0, first + c], table_ref[1, first + c]
        values = []
        for x in range(side):
            other = mirror_ref[0, x]
            a_re, a_im = space[half, block, x, 0, left], space[half, block, x, 1, left]
            b_re, b_im = space[1 - half, block, other, 0, right], space[1 - half, block, other, 1, right]
            values.append((a_re * b_re - a_im * b_im, a_re * b_im + a_im * b_re))
        cut = slice(block * lanes, (block + 1) * lanes)
        for x, (re, im) in enumerate(half_line(values, -1, parity)):
            chi[unit, 0, x ^ line, c, :, cut] = re
            chi[unit, 1, x ^ line, c, :, cut] = im

    def from_plane(unit, value, h):
        half, first = unit % halves, unit // halves * members
        d = plane_dot(value, backward, half, h)
        for ri in range(2):
            piece = d[:, ri * lanes : (ri + 1) * lanes].reshape(kept, members, rows, lanes)
            for x in range(kept):
                outs[2 * x + h][half, ri, first : first + members] = piece[x]

    def collect(unit):
        whole = (kept * members * rows, plane)
        return split_value(jnp.concatenate([chi[unit, ri].reshape(whole) for ri in range(2)], axis=1))

    places = [(half, block) for half in range(halves) for block in range(2)]
    for step in range(len(places) + 1):
        if step < len(places):
            half, block = places[step]
            if block == 0:
                value = arrive(half)
            to_plane(value, half, block)
        if step > 0:
            for e in range(entries):
                along_line(*places[step - 1], e)

    for unit in range(units + 1):
        tasks = [(block, c) for block in range(2) for c in range(members)] if unit < units else []
        if unit > 0:
            value = collect(unit - 1)
        for h in range(2):
            if unit > 0:
                from_plane(unit - 1, value, h)
            for block, c in tasks[h * members : (h + 1) * members]:
                product(unit, block, c)


def middle_inputs(table, mirror_map, x):
    side, plane = x.shape[0] // 2, 2 * x.shape[-1]
    cosine, sine = plane_parts(side)
    parts = [jnp.asarray(part) for part in split_constant(cosine) + split_constant(sine)]
    smem = pl.BlockSpec(memory_space=pltpu.SMEM)
    vmem = pl.BlockSpec(memory_space=pltpu.VMEM)
    args = (table.T, mirror_map, *parts, x.reshape((side, 2) + x.shape[1:]))
    return args, [smem, smem] + [vmem] * 5, pltpu.VMEM((2, 2, 2 * plane, 2 * plane), jnp.bfloat16)


def one_middle(x, table, mirror_map):
    devices, _, entries, rows, lanes = x.shape
    side, components = devices // 2, table.shape[0]
    args, specs, matrices = middle_inputs(table, mirror_map, x)
    spatial = pltpu.VMEM((2, side, 2, entries, rows, lanes), jnp.float32)
    shape = (side, 2, 2, components, rows, lanes)
    out = pl.pallas_call(
        one_middle_kernel,
        in_specs=specs,
        out_specs=pl.BlockSpec(memory_space=pltpu.HBM),
        out_shape=jax.ShapeDtypeStruct(shape, jnp.float32),
        scratch_shapes=[
            matrices,
            matrices,
            pltpu.VMEM((2, 2, side, entries, rows, lanes), jnp.float32),
            spatial,
            spatial,
            pltpu.VMEM((GROUPS, 2, side, components // GROUPS, rows, 2 * lanes), jnp.float32),
            pltpu.VMEM((GROUPS, side, 2, 2, components // GROUPS, rows, lanes), jnp.float32),
            pltpu.SemaphoreType.DMA((GROUPS,)),
        ],
        compiler_params=pltpu.CompilerParams(vmem_limit_bytes=44 << 20),
        name="one_middle",
    )(*args)
    return out.reshape((devices,) + shape[2:])


def both_middle(x, table, mirror_map, me, near):
    devices, halves, _, entries, rows, lanes = x.shape
    side, components = devices // 2, table.shape[0]
    args, specs, matrices = middle_inputs(table, mirror_map, x)
    members = components // GROUPS
    return pl.pallas_call(
        both_middle_kernel,
        in_specs=[pl.BlockSpec(memory_space=pltpu.SMEM)] + specs,
        out_specs=[pl.BlockSpec(memory_space=pltpu.VMEM)] * near,
        out_shape=[jax.ShapeDtypeStruct((halves, 2, components, rows, lanes), jnp.float32)] * near,
        scratch_shapes=[
            matrices,
            matrices,
            pltpu.VMEM((halves, 2, 2, side, entries, rows, lanes), jnp.float32),
            pltpu.VMEM((halves, 2, side, 2, entries, rows, lanes), jnp.float32),
            pltpu.VMEM((halves * GROUPS, 2, near // 2, members, rows, 2 * lanes), jnp.float32),
        ],
        compiler_params=pltpu.CompilerParams(vmem_limit_bytes=60 << 20),
        name="both_middle",
    )(me, *args)


def frequency_kernel(me_ref, y_ref, both_hbm, one_hbm, *refs):
    pieces, (out_ref, both_ref, one_ref, held, stage, m_sems, in_sems, sems) = refs[:-8], refs[-8:]
    near = len(pieces)
    devices, _, components, rows, lanes = y_ref.shape
    groups = sems.shape[0]
    members = components // groups
    matrices = [
        pltpu.make_async_copy(one_hbm, one_ref, m_sems.at[0]),
        pltpu.make_async_copy(both_hbm, both_ref, m_sems.at[1]),
    ]
    loads = [pltpu.make_async_copy(piece, held.at[slot], in_sems.at[slot]) for slot, piece in enumerate(pieces)]
    for copy in matrices + loads:
        copy.start()
    me = me_ref[0] % near
    upper_rows = lax.broadcasted_iota(jnp.int32, (devices, rows, lanes), 1) < rows // 2

    def one_part(group):
        values = []
        for c in range(group * members, (group + 1) * members):
            folded = []
            for ri in range(2):
                tile = y_ref[:, ri, c]
                turned = pltpu.roll(tile, rows // 2, 1)
                folded.append((tile + turned, turned - tile))
            first = jnp.where(upper_rows, folded[0][0], -folded[1][1])
            second = jnp.where(upper_rows, folded[1][0], folded[0][1])
            values.append(first.reshape(devices * rows, lanes).T)
            values.append(second.reshape(devices * rows, lanes).T)
        return dot3(split_value(jnp.concatenate(values, axis=0)), one, ((1,), (0,)))

    def both_part(group):
        values = []
        for c in range(group * members, (group + 1) * members):
            part = [[held[:, half, ri, c].reshape(near * rows, lanes) for ri in range(2)] for half in range(2)]
            sums = [part[0][ri] + part[1][ri] for ri in range(2)]
            differences = [part[0][ri] - part[1][ri] for ri in range(2)]
            values.append(jnp.concatenate([sums[0], -differences[1]], axis=0).T)
            values.append(jnp.concatenate([sums[1], differences[0]], axis=0).T)
        return dot3(split_value(jnp.concatenate(values, axis=0)), both, ((1,), (0,)))

    copies = []
    matrices[0].wait()
    one = split_value(one_ref[...])
    for group in range(groups):
        d = one_part(group)
        if group == 0:
            for copy in matrices[1:] + loads:
                copy.wait()
            ordered = [both_ref[part, slot ^ me] for part in range(2) for slot in range(near)]
            both = split_value(jnp.concatenate(ordered, axis=0))
        d = (d + both_part(group)).reshape(members, 2, lanes, d.shape[1])
        for ri in range(2):
            stage[ri, group * members : (group + 1) * members] = d[:, ri]
        cut = pl.ds(group * members, members)
        copies.append(pltpu.make_async_copy(stage.at[:, cut], out_ref.at[:, cut], sems.at[group]))
        copies[-1].start()
    for copy in copies:
        copy.wait()


def to_frequencies(y, pieces, both, one, me):
    _, _, components, _, lanes = y.shape
    shape = (2, components, lanes, one.shape[1])
    vmem = pl.BlockSpec(memory_space=pltpu.VMEM)
    hbm = pl.BlockSpec(memory_space=pltpu.HBM)
    kept = y.size * 4 + (96 << 10)
    return pl.pallas_call(
        frequency_kernel,
        in_specs=[pl.BlockSpec(memory_space=pltpu.SMEM), vmem] + [hbm] * (2 + len(pieces)),
        out_specs=hbm,
        out_shape=jax.ShapeDtypeStruct(shape, jnp.float32),
        scratch_shapes=[
            pltpu.VMEM(both.shape, jnp.float32),
            pltpu.VMEM(one.shape, jnp.float32),
            pltpu.VMEM((len(pieces),) + pieces[0].shape, jnp.float32),
            pltpu.VMEM(shape, jnp.float32),
            pltpu.SemaphoreType.DMA((2,)),
            pltpu.SemaphoreType.DMA((len(pieces),)),
            pltpu.SemaphoreType.DMA((components // 2,)),
        ],
        compiler_params=pltpu.CompilerParams(vmem_limit_bytes=(64 << 20) - kept),
        name="to_frequencies",
    )(me, y, both, one, *pieces)


def exchange(x):
    flat = x.reshape(x.shape[0], -1, x.shape[-1])
    return lax.all_to_all(flat, "kb", split_axis=0, concat_axis=0, tiled=True).reshape(x.shape)


def swap(piece, slot, devices):
    if slot == 0:
        return piece
    return lax.ppermute(piece, "kb", [(device, device ^ slot) for device in range(devices)])


def trig_pair(angle_int, period, scale):
    angle = 2.0 * math.pi / period * angle_int.astype(jnp.float32)
    return (scale * jnp.cos(angle), scale * jnp.sin(angle))


def complex_combine(formula, cosine, sine, real_part, imag_part):
    first_term = jnp.einsum(formula, cosine, real_part + imag_part, precision=lax.Precision.HIGHEST)
    second_term = jnp.einsum(formula, cosine + sine, imag_part, precision=lax.Precision.HIGHEST)
    third_term = jnp.einsum(formula, sine - cosine, real_part, precision=lax.Precision.HIGHEST)
    return (first_term - second_term, first_term + third_term)


def forward_imaginary_time(tau_rows, frequency_count):
    freq_index = jnp.arange(frequency_count, dtype=jnp.int32)
    angle_int = (
        (2 * freq_index[None, :] - frequency_count + 1)
        * (2 * tau_rows[:, None] + 1)
        % (4 * frequency_count)
    )
    cosine, sine = trig_pair(angle_int, 4 * frequency_count, frequency_count ** (-0.5))
    return (cosine, -sine)


def tau_backward(tau_rows, frequency_count):
    freq_index = jnp.arange(frequency_count, dtype=jnp.int32)
    angle_int = (
        (freq_index[:, None] - frequency_count // 2)
        * (2 * tau_rows[None, :] + 1)
        % (2 * frequency_count)
    )
    return trig_pair(angle_int, 2 * frequency_count, frequency_count ** (-0.5))


def grid_transform(real_part, imag_part, grid_side, direction):
    shape = real_part.shape
    plane = jnp.arange(grid_side * grid_side, dtype=jnp.int32)
    upper = plane // grid_side
    lower = plane % grid_side
    plane_int = (upper[:, None] * upper[None, :] + lower[:, None] * lower[None, :]) % grid_side
    plane_cos, plane_sin = trig_pair(plane_int, grid_side, 1.0 / grid_side)
    line = jnp.arange(grid_side, dtype=jnp.int32)
    line_cos, line_sin = trig_pair(
        line[:, None] * line[None, :] % grid_side, grid_side, grid_side ** (-0.5)
    )
    real_part = real_part.reshape(shape[:-1] + (grid_side, grid_side * grid_side))
    imag_part = imag_part.reshape(shape[:-1] + (grid_side, grid_side * grid_side))
    real_part, imag_part = complex_combine(
        "pq,...xq->...xp", plane_cos, direction * plane_sin, real_part, imag_part
    )
    real_part, imag_part = complex_combine(
        "ax,...xp->...ap", line_cos, direction * line_sin, real_part, imag_part
    )
    return (real_part.reshape(shape), imag_part.reshape(shape))


def mirror_index(mirror_map, grid_side):
    index_x = mirror_map[0][:, None, None]
    index_y = mirror_map[1][None, :, None]
    index_z = mirror_map[2][None, None, :]
    return (index_x * grid_side * grid_side + index_y * grid_side + index_z).reshape(-1)


def bubble(gr_re, gr_im, mirror_re, mirror_im, pair_table, entries):
    entry_ids = jnp.arange(entries, dtype=jnp.int32)
    pick_left = (pair_table[:, 0][:, None] == entry_ids[None, :]).astype(jnp.float32)
    pick_right = (pair_table[:, 1][:, None] == entry_ids[None, :]).astype(jnp.float32)
    left_re = jnp.einsum("me,e...->m...", pick_left, gr_re, precision=lax.Precision.HIGHEST)
    left_im = jnp.einsum("me,e...->m...", pick_left, gr_im, precision=lax.Precision.HIGHEST)
    right_re = jnp.einsum("me,e...->m...", pick_right, mirror_re, precision=lax.Precision.HIGHEST)
    right_im = jnp.einsum("me,e...->m...", pick_right, mirror_im, precision=lax.Precision.HIGHEST)
    return (left_re * right_re - left_im * right_im, left_re * right_im + left_im * right_re)


def general(green_momentum_grid, pair_table, mirror_map):
    grid_side = mirror_map.shape[1]
    entries = green_momentum_grid.shape[1]
    frequency_count = green_momentum_grid.shape[3]
    position = jnp.arange(frequency_count, dtype=jnp.int32)
    fwd_cos, fwd_sin = forward_imaginary_time(position, frequency_count)
    tau_re, tau_im = complex_combine(
        "qa,fsa->fqs", fwd_cos, fwd_sin, green_momentum_grid[0], green_momentum_grid[1]
    )
    stacked = jnp.stack([tau_re, tau_im])

    def to_real_space(pieces):
        space_re, space_im = grid_transform(pieces[0], pieces[1], grid_side, 1.0)
        return jnp.stack([space_re, space_im])

    mirror_flat = mirror_index(mirror_map, grid_side)
    partner_rows = frequency_count - 1 - position
    reflected_cosine, reflected_sine = forward_imaginary_time(partner_rows, frequency_count)
    partner_real, partner_imaginary = complex_combine(
        "qa,fsa->fqs",
        reflected_cosine,
        reflected_sine,
        green_momentum_grid[0],
        green_momentum_grid[1],
    )
    other_stacked = jnp.stack([partner_real, partner_imaginary])
    pieces = (
        lax.all_to_all(stacked, "kb", split_axis=2, concat_axis=3, tiled=True),
        lax.all_to_all(other_stacked, "kb", split_axis=2, concat_axis=3, tiled=True),
    )
    in_cells = to_real_space(pieces[0])
    partner = to_real_space(pieces[1])
    mirrored = jnp.take(partner, mirror_flat, axis=3)
    chi_re, chi_im = bubble(in_cells[0], in_cells[1], mirrored[0], mirrored[1], pair_table, entries)
    chi_re, chi_im = grid_transform(chi_re, chi_im, grid_side, -1.0)
    momenta = jnp.stack([chi_re, chi_im])
    back_cos, back_sin = tau_backward(position, frequency_count)
    pieces = lax.all_to_all(momenta, "kb", split_axis=3, concat_axis=2, tiled=True)
    out_re, out_im = complex_combine("vj,ejk->ekv", back_cos, back_sin, pieces[0], pieces[1])
    return jnp.stack([out_re, out_im])


def local(green, pair_table, mirror_map):
    side = mirror_map.shape[1]
    plane = side * side
    lanes, count = green.shape[2], green.shape[3]
    devices = side * plane // lanes
    near = devices // 2
    half = ROWS // 2
    shared = near * ROWS
    if lanes != LANES or 2 * lanes != plane or 2 * (shared + devices * half) != count:
        return general(green, pair_table, mirror_map)
    me = lax.axis_index("kb").astype(jnp.int32).reshape(1)
    entries = green.shape[1]

    rows = np.arange(shared)
    both_fermion = fermion_matrix(rows, count).astype(np.float32)
    both_boson = boson_matrix(rows, count).reshape(2, near, ROWS, count).astype(np.float32)
    rows = shared + np.arange(devices * half).reshape(devices, half)
    times = np.concatenate([rows, count - 1 - rows], axis=1).reshape(-1)
    one_fermion = fermion_matrix(times, count).astype(np.float32)
    one_boson = boson_matrix(rows.reshape(-1), count).reshape(2, devices, half, count).swapaxes(0, 1)
    one_boson = one_boson.reshape(devices * ROWS, count).astype(np.float32)

    shape = (near, 2, 2, entries, ROWS, lanes)
    both = to_times(both_times_kernel, green, jnp.asarray(both_fermion), shape, devices, "both_times")
    green, both = lax.optimization_barrier((green, both))
    shape = (devices, 2, entries, ROWS, lanes)
    one = to_times(one_times_kernel, green, jnp.asarray(one_fermion), shape, devices, "one_times")
    both, one = lax.optimization_barrier((exchange(both), one))
    pieces = both_middle(both, pair_table, mirror_map, me, near)
    middle_slot, quarter = near // 2, near // 4
    order = list(range(middle_slot, middle_slot + quarter)) + [1]
    early = [swap(pieces[slot], slot, devices) for slot in order]
    one, early = lax.optimization_barrier((exchange(one), early))
    one = exchange(one_middle(one, pair_table, mirror_map))
    rest = [slot for slot in reversed(range(near)) if slot not in order]
    moved = dict(zip(order, early)) | {slot: swap(pieces[slot], slot, devices) for slot in rest}
    pieces = [moved[slot] for slot in range(near)]
    return to_frequencies(one, pieces, jnp.asarray(both_boson), jnp.asarray(one_boson), me)


def solution(mesh):
    placed = (P("set", None, "kb", None), P(), P("set", None))
    return jax.shard_map(
        local, mesh=mesh, in_specs=placed, out_specs=P("set", None, "kb", None), check_vma=False
    )
```

```python
import functools
import math

import jax
import jax.numpy as jnp
import ml_dtypes
import numpy as np
from jax import lax
from jax.experimental import pallas as pl
from jax.experimental.pallas import tpu as pltpu
from jax.sharding import PartitionSpec as P

LANES = 128
ROWS = 8
GROUPS = 2


def split_constant(matrix):
    high = matrix.astype(np.float32).astype(ml_dtypes.bfloat16)
    low = (matrix - high.astype(np.float64)).astype(np.float32).astype(ml_dtypes.bfloat16)
    return high, low


def split_value(value):
    high = value.astype(jnp.bfloat16)
    low = (value - high.astype(jnp.float32)).astype(jnp.bfloat16)
    return high, low


def dot3(left, right, dims):
    (k_left,), (k_right,) = dims
    a = jnp.concatenate([left[0], left[0], left[1]], axis=k_left)
    b = jnp.concatenate([right[0], right[1], right[0]], axis=k_right)
    return lax.dot_general(a, b, (dims, ((), ())), preferred_element_type=jnp.float32)


def fermion_matrix(rows, count):
    n = np.arange(count, dtype=np.int64)
    angle = ((2 * n[None, :] - count + 1) * (2 * rows[:, None] + 1)) % (4 * count)
    angle = np.pi * angle / (2 * count)
    return np.concatenate([np.cos(angle), np.sin(angle)], axis=0) * count**-0.5


def boson_matrix(rows, count):
    v = np.arange(count, dtype=np.int64)
    angle = ((v[None, :] - count // 2) * (2 * rows[:, None] + 1)) % (2 * count)
    angle = np.pi * angle / count
    return np.concatenate([np.cos(angle), np.sin(angle)], axis=0) * count**-0.5


def plane_parts(side):
    p = np.arange(side * side, dtype=np.int64)
    angle = ((p[:, None] // side) * (p[None, :] // side) + (p[:, None] % side) * (p[None, :] % side)) % side
    angle = 2 * np.pi * angle / side
    scale = side**-1.5
    return np.cos(angle) * scale, np.sin(angle) * scale


def times_w4(re, im, power, sign):
    power = (power * sign) % 4
    if power == 0:
        return re, im
    if power == 1:
        return -im, re
    if power == 2:
        return -re, -im
    return im, -re


def dft4(values, sign):
    (r0, i0), (r1, i1), (r2, i2), (r3, i3) = values
    sr, si, dr, di = r0 + r2, i0 + i2, r0 - r2, i0 - i2
    tr, ti, er, ei = r1 + r3, i1 + i3, r1 - r3, i1 - i3
    if sign > 0:
        return [(sr + tr, si + ti), (dr - ei, di + er), (sr - tr, si - ti), (dr + ei, di - er)]
    return [(sr + tr, si + ti), (dr + ei, di - er), (sr - tr, si - ti), (dr - ei, di + er)]


def twiddle(value, power, sign, side):
    re, im = value
    if power % (side // 4) == 0:
        return times_w4(re, im, power // (side // 4), sign)
    angle = 2.0 * np.pi * power / side
    c, s = float(np.cos(angle)), float(sign * np.sin(angle))
    return re * c - im * s, re * s + im * c


def dft_line(values, sign):
    side = len(values)
    if side == 1:
        return values
    if side == 2:
        (r0, i0), (r1, i1) = values
        return [(r0 + r1, i0 + i1), (r0 - r1, i0 - i1)]
    if side == 4:
        return dft4(values, sign)
    inner = side // 4
    parts = [dft_line(values[b::4], sign) for b in range(4)]
    out = [None] * side
    for k1 in range(inner):
        column = [twiddle(parts[b][k1], b * k1, sign, side) for b in range(4)]
        for k2, value in enumerate(dft4(column, sign)):
            out[k1 + inner * k2] = value
    return out


def half_line(values, sign, parity):
    side = len(values)
    inner = side // 4
    parts = [dft_line(values[b::4], sign) for b in range(4)]
    out = [None] * (side // 2)
    for k1 in range(inner):
        column = [twiddle(parts[b][k1], b * k1, sign, side) for b in range(4)]
        column = [(re * parity, im * parity) if b % 2 else (re, im) for b, (re, im) in enumerate(column)]
        for k2, value in enumerate(dft4(column, sign)[:2]):
            out[k1 + inner * k2] = value
    return out


def load_inputs(g_hbm, m_hbm, g_ref, m_ref, in_sems, m_sem):
    load = pltpu.make_async_copy(m_hbm, m_ref, m_sem)
    pieces = [
        pltpu.make_async_copy(g_hbm.at[:, pl.ds(e, 1)], g_ref.at[:, pl.ds(e, 1)], in_sems.at[e])
        for e in range(g_ref.shape[1])
    ]
    for copy in [load] + pieces:
        copy.start()
    load.wait()
    return pieces


def sums_of(matrix, g_ref, e):
    lanes = g_ref.shape[2]
    g = jnp.concatenate([g_ref[0, e], g_ref[1, e]], axis=0)
    d = dot3(matrix, split_value(g), ((1,), (1,)))
    half = d.shape[0] // 2
    return d[:half, :lanes], d[:half, lanes:], d[half:, :lanes], d[half:, lanes:]


def both_times_kernel(g_hbm, m_hbm, out_ref, g_ref, m_ref, stage, in_sems, m_sem, out_sems):
    entries, lanes = g_ref.shape[1:3]
    near, _, _, _, rows, _ = stage.shape
    pieces = load_inputs(g_hbm, m_hbm, g_ref, m_ref, in_sems, m_sem)
    matrix = split_value(m_ref[...])
    copies = []
    for e in range(entries):
        pieces[e].wait()
        c_re, c_im, s_re, s_im = sums_of(matrix, g_ref, e)
        for where, value in (
            ((0, 0), c_re + s_im),
            ((0, 1), c_im - s_re),
            ((1, 0), s_im - c_re),
            ((1, 1), -(c_im + s_re)),
        ):
            stage[:, where[0], where[1], e] = value.reshape(near, rows, lanes)
        cut = pl.ds(e, 1)
        for side in range(2):
            target = out_ref.at[pl.ds(side * near, near), :, :, cut]
            copies.append(pltpu.make_async_copy(stage.at[:, :, :, cut], target, out_sems.at[e, side]))
            copies[-1].start()
    for copy in copies:
        copy.wait()


def one_times_kernel(g_hbm, m_hbm, out_ref, g_ref, m_ref, stage, in_sems, m_sem, out_sems):
    entries, lanes = g_ref.shape[1:3]
    devices, _, _, rows, _ = stage.shape
    pieces = load_inputs(g_hbm, m_hbm, g_ref, m_ref, in_sems, m_sem)
    matrix = split_value(m_ref[...])
    copies = []
    for e in range(entries):
        pieces[e].wait()
        c_re, c_im, s_re, s_im = sums_of(matrix, g_ref, e)
        stage[:, 0, e] = (c_re + s_im).reshape(devices, rows, lanes)
        stage[:, 1, e] = (c_im - s_re).reshape(devices, rows, lanes)
        cut = pl.ds(e, 1)
        copies.append(pltpu.make_async_copy(stage.at[:, :, cut], out_ref.at[:, :, cut], out_sems.at[e, 0]))
        copies[-1].start()
    for copy in copies:
        copy.wait()


def to_times(kernel, green, matrix, shape, targets, name):
    entries = green.shape[1]
    hbm = pl.BlockSpec(memory_space=pltpu.HBM)
    return pl.pallas_call(
        kernel,
        in_specs=[hbm, hbm],
        out_specs=hbm,
        out_shape=jax.ShapeDtypeStruct((targets,) + shape[1:], jnp.float32),
        scratch_shapes=[
            pltpu.VMEM(green.shape, jnp.float32),
            pltpu.VMEM(matrix.shape, jnp.float32),
            pltpu.VMEM(shape, jnp.float32),
            pltpu.SemaphoreType.DMA((entries,)),
            pltpu.SemaphoreType.DMA,
            pltpu.SemaphoreType.DMA((entries, 2)),
        ],
        compiler_params=pltpu.CompilerParams(vmem_limit_bytes=63 << 20),
        name=name,
    )(green, matrix)


def fill_block(ref, cosine, sine):
    plane = cosine.shape[0]
    lanes = plane // 2
    for block in range(2):
        cut = slice(block * lanes, (block + 1) * lanes)
        re = slice(2 * block * lanes, (2 * block + 1) * lanes)
        im = slice((2 * block + 1) * lanes, (2 * block + 2) * lanes)
        ref[:plane, re] = cosine[:, cut].astype(jnp.bfloat16)
        ref[plane:, im] = cosine[:, cut].astype(jnp.bfloat16)
        ref[:plane, im] = sine[:, cut].astype(jnp.bfloat16)
        ref[plane:, re] = (-sine[:, cut]).astype(jnp.bfloat16)


def fill_matrices(mirror_ref, parts, forward, backward, turned):
    plane = parts[0].shape[0]
    side = mirror_ref.shape[1]
    row = lax.broadcasted_iota(jnp.int32, (plane, plane), 0)
    column = lax.broadcasted_iota(jnp.int32, (plane, plane), 1)
    upper = (mirror_ref[1, 0] - column // side) & (side - 1)
    lower = (mirror_ref[2, 0] - column % side) & (side - 1)
    pick = (row == upper * side + lower).astype(jnp.float32).astype(jnp.bfloat16)

    def dot(a, b):
        return jnp.dot(a, b, preferred_element_type=jnp.float32)

    for part in range(2):
        c_ref, s_ref = parts[part], parts[2 + part]
        cosine, sine = c_ref[...].astype(jnp.float32), s_ref[...].astype(jnp.float32)
        fill_block(forward.at[0, part], cosine, sine)
        fill_block(backward.at[0, part], turned(cosine), turned(-sine))
        fill_block(forward.at[1, part], dot(c_ref[...], pick), dot(s_ref[...], pick))
        fill_block(backward.at[1, part], turned(dot(pick, c_ref[...])), turned(-dot(pick, s_ref[...])))


def plane_dot(value, matrix, half, block):
    width = matrix.shape[3] // 2
    cut = slice(block * width, (block + 1) * width)
    return dot3(value, (matrix[half, 0, :, cut], matrix[half, 1, :, cut]), ((1,), (0,)))


def one_middle_kernel(table_ref, mirror_ref, ch_ref, cl_ref, sh_ref, sl_ref, x_ref, out_ref, *refs):
    forward, backward, mid, space, other_space, chi, stage, sems = refs
    _, side, _, entries, rows, lanes = space.shape
    plane = 2 * lanes
    groups, _, _, members, _, _ = chi.shape
    fill_matrices(mirror_ref, (ch_ref, cl_ref, sh_ref, sl_ref), forward, backward, lambda value: value)

    def paired(first, second):
        upper = lax.broadcasted_iota(jnp.int32, first.shape, 1) < rows // 2
        turned = [pltpu.roll(part, rows // 2, 1) for part in (first, second)]
        return jnp.where(upper, first, turned[1]), jnp.where(upper, turned[0], second)

    def halves_of(columns):
        value = jnp.concatenate(columns, axis=1)
        count, width = value.shape
        value = value.reshape(count // (2 * rows), 2, rows, width)
        parts = paired(value[:, 0], value[:, 1])
        return [split_value(part.reshape(count // 2, width)) for part in parts]

    def halves_dot(parts, matrix, block):
        shape = (parts[0][0].shape[0] // rows, rows, plane)
        d = paired(*(plane_dot(parts[half], matrix, half, block).reshape(shape) for half in range(2)))
        return jnp.concatenate([part.reshape(shape[0], 1, rows, plane) for part in d], axis=1)

    parts = halves_of([x_ref[:, h, ri].reshape(side * entries * rows, lanes) for ri in range(2) for h in range(2)])
    for block in range(2):
        d = halves_dot(parts, forward, block)
        for ri in range(2):
            piece = d[:, :, :, ri * lanes : (ri + 1) * lanes]
            mid[block, ri] = piece.reshape(side, entries, rows, lanes)
    for block in range(2):
        for e in range(entries):
            values = [(mid[block, 0, x, e], mid[block, 1, x, e]) for x in range(side)]
            for x, parts in enumerate(dft_line(values, 1)):
                for ri in range(2):
                    space[block, x, ri, e] = parts[ri]
                    other_space[block, x, ri, e] = pltpu.roll(parts[ri], rows // 2, 0)

    copies = []
    for group in range(groups):
        for c in range(members):
            left, right = table_ref[0, group * members + c], table_ref[1, group * members + c]
            for block in range(2):
                values = []
                for x in range(side):
                    other = mirror_ref[0, x]
                    a_re, a_im = space[block, x, 0, left], space[block, x, 1, left]
                    b_re, b_im = other_space[block, other, 0, right], other_space[block, other, 1, right]
                    values.append((a_re * b_re - a_im * b_im, a_re * b_im + a_im * b_re))
                cut = slice(block * lanes, (block + 1) * lanes)
                for x, parts in enumerate(dft_line(values, -1)):
                    for ri in range(2):
                        chi[group, ri, x, c, :, cut] = parts[ri]
        whole = (side * members * rows, plane)
        parts = halves_of([chi[group, ri].reshape(whole) for ri in range(2)])
        for h in range(2):
            d = halves_dot(parts, backward, h)
            for ri in range(2):
                piece = d[:, :, :, ri * lanes : (ri + 1) * lanes].reshape(side, members, rows, lanes)
                stage[group, :, h, ri] = piece
        target = out_ref.at[:, :, :, pl.ds(group * members, members)]
        copies.append(pltpu.make_async_copy(stage.at[group], target, sems.at[group]))
        copies[-1].start()
    for copy in copies:
        copy.wait()


def both_middle_kernel(me_ref, table_ref, mirror_ref, ch_ref, cl_ref, sh_ref, sl_ref, x_ref, *refs):
    outs, (forward, backward, mid, space, chi) = refs[:-5], refs[-5:]
    halves, _, side, _, entries, rows, lanes = space.shape
    plane = 2 * lanes
    units, _, kept, members, _, _ = chi.shape
    me, near = me_ref[0], len(outs)
    core, line = me % 2, me // 2 % kept
    parity = (1 - 2 * (me // near)).astype(jnp.float32)

    def turned(value):
        return jnp.where(core == 0, value, jnp.concatenate([value[:, lanes:], value[:, :lanes]], axis=1))

    fill_matrices(mirror_ref, (ch_ref, cl_ref, sh_ref, sl_ref), forward, backward, turned)

    def arrive(half):
        columns = [
            x_ref[:, h, half, ri].reshape(side * entries * rows, lanes) for ri in range(2) for h in range(2)
        ]
        return split_value(jnp.concatenate(columns, axis=1))

    def to_plane(value, half, block):
        d = plane_dot(value, forward, half, block)
        for ri in range(2):
            piece = d[:, ri * lanes : (ri + 1) * lanes]
            mid[half, block, ri] = piece.reshape(side, entries, rows, lanes)

    def along_line(half, block, e):
        values = [(mid[half, block, 0, x, e], mid[half, block, 1, x, e]) for x in range(side)]
        for x, (re, im) in enumerate(dft_line(values, 1)):
            space[half, block, x, 0, e] = re
            space[half, block, x, 1, e] = im

    def product(unit, block, c):
        half, first = unit % halves, unit // halves * members
        left, right = table_ref[0, first + c], table_ref[1, first + c]
        values = []
        for x in range(side):
            other = mirror_ref[0, x]
            a_re, a_im = space[half, block, x, 0, left], space[half, block, x, 1, left]
            b_re, b_im = space[1 - half, block, other, 0, right], space[1 - half, block, other, 1, right]
            values.append((a_re * b_re - a_im * b_im, a_re * b_im + a_im * b_re))
        cut = slice(block * lanes, (block + 1) * lanes)
        for x, (re, im) in enumerate(half_line(values, -1, parity)):
            chi[unit, 0, x ^ line, c, :, cut] = re
            chi[unit, 1, x ^ line, c, :, cut] = im

    def from_plane(unit, value, h):
        half, first = unit % halves, unit // halves * members
        d = plane_dot(value, backward, half, h)
        for ri in range(2):
            piece = d[:, ri * lanes : (ri + 1) * lanes].reshape(kept, members, rows, lanes)
            for x in range(kept):
                outs[2 * x + h][half, ri, first : first + members] = piece[x]

    def collect(unit):
        whole = (kept * members * rows, plane)
        return split_value(jnp.concatenate([chi[unit, ri].reshape(whole) for ri in range(2)], axis=1))

    places = [(half, block) for half in range(halves) for block in range(2)]
    for step in range(len(places) + 1):
        if step < len(places):
            half, block = places[step]
            if block == 0:
                value = arrive(half)
            to_plane(value, half, block)
        if step > 0:
            for e in range(entries):
                along_line(*places[step - 1], e)

    for unit in range(units + 1):
        tasks = [(block, c) for block in range(2) for c in range(members)] if unit < units else []
        if unit > 0:
            value = collect(unit - 1)
        for h in range(2):
            if unit > 0:
                from_plane(unit - 1, value, h)
            for block, c in tasks[h * members : (h + 1) * members]:
                product(unit, block, c)


def middle_inputs(table, mirror_map, x):
    side, plane = x.shape[0] // 2, 2 * x.shape[-1]
    cosine, sine = plane_parts(side)
    parts = [jnp.asarray(part) for part in split_constant(cosine) + split_constant(sine)]
    smem = pl.BlockSpec(memory_space=pltpu.SMEM)
    vmem = pl.BlockSpec(memory_space=pltpu.VMEM)
    args = (table.T, mirror_map, *parts, x.reshape((side, 2) + x.shape[1:]))
    return args, [smem, smem] + [vmem] * 5, pltpu.VMEM((2, 2, 2 * plane, 2 * plane), jnp.bfloat16)


def one_middle(x, table, mirror_map):
    devices, _, entries, rows, lanes = x.shape
    side, components = devices // 2, table.shape[0]
    args, specs, matrices = middle_inputs(table, mirror_map, x)
    spatial = pltpu.VMEM((2, side, 2, entries, rows, lanes), jnp.float32)
    shape = (side, 2, 2, components, rows, lanes)
    out = pl.pallas_call(
        one_middle_kernel,
        in_specs=specs,
        out_specs=pl.BlockSpec(memory_space=pltpu.HBM),
        out_shape=jax.ShapeDtypeStruct(shape, jnp.float32),
        scratch_shapes=[
            matrices,
            matrices,
            pltpu.VMEM((2, 2, side, entries, rows, lanes), jnp.float32),
            spatial,
            spatial,
            pltpu.VMEM((GROUPS, 2, side, components // GROUPS, rows, 2 * lanes), jnp.float32),
            pltpu.VMEM((GROUPS, side, 2, 2, components // GROUPS, rows, lanes), jnp.float32),
            pltpu.SemaphoreType.DMA((GROUPS,)),
        ],
        compiler_params=pltpu.CompilerParams(vmem_limit_bytes=44 << 20),
        name="one_middle",
    )(*args)
    return out.reshape((devices,) + shape[2:])


def both_middle(x, table, mirror_map, me, near):
    devices, halves, _, entries, rows, lanes = x.shape
    side, components = devices // 2, table.shape[0]
    args, specs, matrices = middle_inputs(table, mirror_map, x)
    members = components // GROUPS
    return pl.pallas_call(
        both_middle_kernel,
        in_specs=[pl.BlockSpec(memory_space=pltpu.SMEM)] + specs,
        out_specs=[pl.BlockSpec(memory_space=pltpu.VMEM)] * near,
        out_shape=[jax.ShapeDtypeStruct((halves, 2, components, rows, lanes), jnp.float32)] * near,
        scratch_shapes=[
            matrices,
            matrices,
            pltpu.VMEM((halves, 2, 2, side, entries, rows, lanes), jnp.float32),
            pltpu.VMEM((halves, 2, side, 2, entries, rows, lanes), jnp.float32),
            pltpu.VMEM((halves * GROUPS, 2, near // 2, members, rows, 2 * lanes), jnp.float32),
        ],
        compiler_params=pltpu.CompilerParams(vmem_limit_bytes=60 << 20),
        name="both_middle",
    )(me, *args)


def prepare_kernel(me_ref, both_ref, one_ref, out_ref):
    near = both_ref.shape[1]
    me = me_ref[0] % near
    ordered = [both_ref[part, slot ^ me] for part in range(2) for slot in range(near)]
    for part, value in enumerate(split_value(jnp.concatenate([one_ref[...]] + ordered, axis=0))):
        out_ref[part] = value


def prepare(me, both, one):
    smem = pl.BlockSpec(memory_space=pltpu.SMEM)
    vmem = pl.BlockSpec(memory_space=pltpu.VMEM)
    depth = both.size // both.shape[3] + one.shape[0]
    return pl.pallas_call(
        prepare_kernel,
        in_specs=[smem, vmem, vmem],
        out_specs=vmem,
        out_shape=jax.ShapeDtypeStruct((2, depth, one.shape[1]), jnp.bfloat16),
        compiler_params=pltpu.CompilerParams(vmem_limit_bytes=63 << 20),
        name="prepare",
    )(me, both, one)


def frequency_kernel(order, y_hbm, m_hbm, *refs):
    pieces, (out_ref, y_ref, m_ref, held, stage, y_sems, m_sems, in_sems, sems) = refs[:-9], refs[-9:]
    near = len(pieces)
    devices, _, components, rows, lanes = y_ref.shape
    groups = sems.shape[0]
    members = components // groups
    depth = devices * rows
    cuts = [pl.ds(group * members, members) for group in range(groups)]
    matrices = [
        pltpu.make_async_copy(m_hbm.at[:, pl.ds(start, depth)], m_ref.at[:, pl.ds(start, depth)], m_sems.at[part])
        for part, start in enumerate((0, depth))
    ]
    blocks = [
        pltpu.make_async_copy(y_hbm.at[:, :, cut], y_ref.at[:, :, cut], y_sems.at[group])
        for group, cut in enumerate(cuts)
    ]
    loads = [pltpu.make_async_copy(piece, held.at[slot], in_sems.at[slot]) for slot, piece in zip(order, pieces)]
    for copy in [matrices[0], blocks[0], matrices[1]] + loads + blocks[1:]:
        copy.start()
    upper_rows = lax.broadcasted_iota(jnp.int32, (devices, rows, lanes), 1) < rows // 2

    def part_of(values, start):
        matrix = [m_ref[part, start : start + depth] for part in range(2)]
        return dot3(split_value(jnp.concatenate(values, axis=0)), matrix, ((1,), (0,)))

    def one_part(group):
        values = []
        for c in range(group * members, (group + 1) * members):
            folded = []
            for ri in range(2):
                tile = y_ref[:, ri, c]
                turned = pltpu.roll(tile, rows // 2, 1)
                folded.append((tile + turned, turned - tile))
            first = jnp.where(upper_rows, folded[0][0], -folded[1][1])
            second = jnp.where(upper_rows, folded[1][0], folded[0][1])
            values.append(first.reshape(devices * rows, lanes).T)
            values.append(second.reshape(devices * rows, lanes).T)
        return part_of(values, 0)

    def both_part(group):
        values = []
        for c in range(group * members, (group + 1) * members):
            part = [[held[:, half, ri, c].reshape(near * rows, lanes) for ri in range(2)] for half in range(2)]
            sums = [part[0][ri] + part[1][ri] for ri in range(2)]
            differences = [part[0][ri] - part[1][ri] for ri in range(2)]
            values.append(jnp.concatenate([sums[0], -differences[1]], axis=0).T)
            values.append(jnp.concatenate([sums[1], differences[0]], axis=0).T)
        return part_of(values, depth)

    copies = []
    matrices[0].wait()
    for group in range(groups):
        blocks[group].wait()
        d = one_part(group)
        if group == 0:
            for copy in matrices[1:] + loads:
                copy.wait()
        d = (d + both_part(group)).reshape(members, 2, lanes, d.shape[1])
        for ri in range(2):
            stage[ri, group * members : (group + 1) * members] = d[:, ri]
        copies.append(pltpu.make_async_copy(stage.at[:, cuts[group]], out_ref.at[:, cuts[group]], sems.at[group]))
        copies[-1].start()
    for copy in copies:
        copy.wait()


def to_frequencies(y, pieces, order, matrix):
    _, _, components, _, lanes = y.shape
    shape = (2, components, lanes, matrix.shape[2])
    hbm = pl.BlockSpec(memory_space=pltpu.HBM)
    groups = components // 2
    return pl.pallas_call(
        functools.partial(frequency_kernel, order),
        in_specs=[hbm] * (2 + len(pieces)),
        out_specs=hbm,
        out_shape=jax.ShapeDtypeStruct(shape, jnp.float32),
        scratch_shapes=[
            pltpu.VMEM(y.shape, jnp.float32),
            pltpu.VMEM(matrix.shape, jnp.bfloat16),
            pltpu.VMEM((len(pieces),) + pieces[0].shape, jnp.float32),
            pltpu.VMEM(shape, jnp.float32),
            pltpu.SemaphoreType.DMA((groups,)),
            pltpu.SemaphoreType.DMA((2,)),
            pltpu.SemaphoreType.DMA((len(pieces),)),
            pltpu.SemaphoreType.DMA((groups,)),
        ],
        compiler_params=pltpu.CompilerParams(vmem_limit_bytes=63 << 20),
        name="to_frequencies",
    )(y, matrix, *pieces)


def exchange(x):
    flat = x.reshape(x.shape[0], -1, x.shape[-1])
    return lax.all_to_all(flat, "kb", split_axis=0, concat_axis=0, tiled=True).reshape(x.shape)


def swap(piece, slot, devices):
    if slot == 0:
        return piece
    return lax.ppermute(piece, "kb", [(device, device ^ slot) for device in range(devices)])


def trig_pair(angle_int, period, scale):
    angle = 2.0 * math.pi / period * angle_int.astype(jnp.float32)
    return (scale * jnp.cos(angle), scale * jnp.sin(angle))


def complex_combine(formula, cosine, sine, real_part, imag_part):
    first_term = jnp.einsum(formula, cosine, real_part + imag_part, precision=lax.Precision.HIGHEST)
    second_term = jnp.einsum(formula, cosine + sine, imag_part, precision=lax.Precision.HIGHEST)
    third_term = jnp.einsum(formula, sine - cosine, real_part, precision=lax.Precision.HIGHEST)
    return (first_term - second_term, first_term + third_term)


def forward_imaginary_time(tau_rows, frequency_count):
    freq_index = jnp.arange(frequency_count, dtype=jnp.int32)
    angle_int = (
        (2 * freq_index[None, :] - frequency_count + 1)
        * (2 * tau_rows[:, None] + 1)
        % (4 * frequency_count)
    )
    cosine, sine = trig_pair(angle_int, 4 * frequency_count, frequency_count ** (-0.5))
    return (cosine, -sine)


def tau_backward(tau_rows, frequency_count):
    freq_index = jnp.arange(frequency_count, dtype=jnp.int32)
    angle_int = (
        (freq_index[:, None] - frequency_count // 2)
        * (2 * tau_rows[None, :] + 1)
        % (2 * frequency_count)
    )
    return trig_pair(angle_int, 2 * frequency_count, frequency_count ** (-0.5))


def grid_transform(real_part, imag_part, grid_side, direction):
    shape = real_part.shape
    plane = jnp.arange(grid_side * grid_side, dtype=jnp.int32)
    upper = plane // grid_side
    lower = plane % grid_side
    plane_int = (upper[:, None] * upper[None, :] + lower[:, None] * lower[None, :]) % grid_side
    plane_cos, plane_sin = trig_pair(plane_int, grid_side, 1.0 / grid_side)
    line = jnp.arange(grid_side, dtype=jnp.int32)
    line_cos, line_sin = trig_pair(
        line[:, None] * line[None, :] % grid_side, grid_side, grid_side ** (-0.5)
    )
    real_part = real_part.reshape(shape[:-1] + (grid_side, grid_side * grid_side))
    imag_part = imag_part.reshape(shape[:-1] + (grid_side, grid_side * grid_side))
    real_part, imag_part = complex_combine(
        "pq,...xq->...xp", plane_cos, direction * plane_sin, real_part, imag_part
    )
    real_part, imag_part = complex_combine(
        "ax,...xp->...ap", line_cos, direction * line_sin, real_part, imag_part
    )
    return (real_part.reshape(shape), imag_part.reshape(shape))


def mirror_index(mirror_map, grid_side):
    index_x = mirror_map[0][:, None, None]
    index_y = mirror_map[1][None, :, None]
    index_z = mirror_map[2][None, None, :]
    return (index_x * grid_side * grid_side + index_y * grid_side + index_z).reshape(-1)


def bubble(gr_re, gr_im, mirror_re, mirror_im, pair_table, entries):
    entry_ids = jnp.arange(entries, dtype=jnp.int32)
    pick_left = (pair_table[:, 0][:, None] == entry_ids[None, :]).astype(jnp.float32)
    pick_right = (pair_table[:, 1][:, None] == entry_ids[None, :]).astype(jnp.float32)
    left_re = jnp.einsum("me,e...->m...", pick_left, gr_re, precision=lax.Precision.HIGHEST)
    left_im = jnp.einsum("me,e...->m...", pick_left, gr_im, precision=lax.Precision.HIGHEST)
    right_re = jnp.einsum("me,e...->m...", pick_right, mirror_re, precision=lax.Precision.HIGHEST)
    right_im = jnp.einsum("me,e...->m...", pick_right, mirror_im, precision=lax.Precision.HIGHEST)
    return (left_re * right_re - left_im * right_im, left_re * right_im + left_im * right_re)


def general(green_momentum_grid, pair_table, mirror_map):
    grid_side = mirror_map.shape[1]
    entries = green_momentum_grid.shape[1]
    frequency_count = green_momentum_grid.shape[3]
    position = jnp.arange(frequency_count, dtype=jnp.int32)
    fwd_cos, fwd_sin = forward_imaginary_time(position, frequency_count)
    tau_re, tau_im = complex_combine(
        "qa,fsa->fqs", fwd_cos, fwd_sin, green_momentum_grid[0], green_momentum_grid[1]
    )
    stacked = jnp.stack([tau_re, tau_im])

    def to_real_space(pieces):
        space_re, space_im = grid_transform(pieces[0], pieces[1], grid_side, 1.0)
        return jnp.stack([space_re, space_im])

    mirror_flat = mirror_index(mirror_map, grid_side)
    partner_rows = frequency_count - 1 - position
    reflected_cosine, reflected_sine = forward_imaginary_time(partner_rows, frequency_count)
    partner_real, partner_imaginary = complex_combine(
        "qa,fsa->fqs",
        reflected_cosine,
        reflected_sine,
        green_momentum_grid[0],
        green_momentum_grid[1],
    )
    other_stacked = jnp.stack([partner_real, partner_imaginary])
    pieces = (
        lax.all_to_all(stacked, "kb", split_axis=2, concat_axis=3, tiled=True),
        lax.all_to_all(other_stacked, "kb", split_axis=2, concat_axis=3, tiled=True),
    )
    in_cells = to_real_space(pieces[0])
    partner = to_real_space(pieces[1])
    mirrored = jnp.take(partner, mirror_flat, axis=3)
    chi_re, chi_im = bubble(in_cells[0], in_cells[1], mirrored[0], mirrored[1], pair_table, entries)
    chi_re, chi_im = grid_transform(chi_re, chi_im, grid_side, -1.0)
    momenta = jnp.stack([chi_re, chi_im])
    back_cos, back_sin = tau_backward(position, frequency_count)
    pieces = lax.all_to_all(momenta, "kb", split_axis=3, concat_axis=2, tiled=True)
    out_re, out_im = complex_combine("vj,ejk->ekv", back_cos, back_sin, pieces[0], pieces[1])
    return jnp.stack([out_re, out_im])


def local(green, pair_table, mirror_map):
    side = mirror_map.shape[1]
    plane = side * side
    lanes, count = green.shape[2], green.shape[3]
    devices = side * plane // lanes
    near = devices // 2
    half = ROWS // 2
    shared = near * ROWS
    if lanes != LANES or 2 * lanes != plane or 2 * (shared + devices * half) != count:
        return general(green, pair_table, mirror_map)
    me = lax.axis_index("kb").astype(jnp.int32).reshape(1)
    entries = green.shape[1]

    rows = np.arange(shared)
    both_fermion = fermion_matrix(rows, count).astype(np.float32)
    both_boson = boson_matrix(rows, count).reshape(2, near, ROWS, count).astype(np.float32)
    rows = shared + np.arange(devices * half).reshape(devices, half)
    times = np.concatenate([rows, count - 1 - rows], axis=1).reshape(-1)
    one_fermion = fermion_matrix(times, count).astype(np.float32)
    one_boson = boson_matrix(rows.reshape(-1), count).reshape(2, devices, half, count).swapaxes(0, 1)
    one_boson = one_boson.reshape(devices * ROWS, count).astype(np.float32)

    shape = (near, 2, 2, entries, ROWS, lanes)
    both = to_times(both_times_kernel, green, jnp.asarray(both_fermion), shape, devices, "both_times")
    green, both = lax.optimization_barrier((green, both))
    shape = (devices, 2, entries, ROWS, lanes)
    one = to_times(one_times_kernel, green, jnp.asarray(one_fermion), shape, devices, "one_times")
    both, one = lax.optimization_barrier((exchange(both), one))
    pieces = both_middle(both, pair_table, mirror_map, me, near)
    middle_slot, quarter = near // 2, near // 4
    order = list(range(middle_slot, middle_slot + quarter)) + [1]
    early = [swap(pieces[slot], slot, devices) for slot in order]
    one, early = lax.optimization_barrier((exchange(one), early))
    one = one_middle(one, pair_table, mirror_map)
    one, both_boson, one_boson = lax.optimization_barrier((one, jnp.asarray(both_boson), jnp.asarray(one_boson)))
    matrix = prepare(me, both_boson, one_boson)
    rest = [slot for slot in reversed(range(1, near)) if slot not in order]
    late = [swap(pieces[slot], slot, devices) for slot in rest]
    return to_frequencies(exchange(one), [pieces[0]] + early + late, [0] + order + rest, matrix)


def solution(mesh):
    placed = (P("set", None, "kb", None), P(), P("set", None))
    return jax.shard_map(
        local, mesh=mesh, in_specs=placed, out_specs=P("set", None, "kb", None), check_vma=False
    )
```

```python
import functools
import math

import jax
import jax.numpy as jnp
import ml_dtypes
import numpy as np
from jax import lax
from jax.experimental import pallas as pl
from jax.experimental.pallas import tpu as pltpu
from jax.sharding import PartitionSpec as P

LANES = 128
ROWS = 8
GROUPS = 2


def split_constant(matrix):
    high = matrix.astype(np.float32).astype(ml_dtypes.bfloat16)
    low = (matrix - high.astype(np.float64)).astype(np.float32).astype(ml_dtypes.bfloat16)
    return high, low


def split_value(value):
    high = value.astype(jnp.bfloat16)
    low = (value - high.astype(jnp.float32)).astype(jnp.bfloat16)
    return high, low


def dot3(left, right, dims):
    (k_left,), (k_right,) = dims
    a = jnp.concatenate([left[0], left[0], left[1]], axis=k_left)
    b = jnp.concatenate([right[0], right[1], right[0]], axis=k_right)
    return lax.dot_general(a, b, (dims, ((), ())), preferred_element_type=jnp.float32)


def fermion_matrix(rows, count):
    n = np.arange(count, dtype=np.int64)
    angle = ((2 * n[None, :] - count + 1) * (2 * rows[:, None] + 1)) % (4 * count)
    angle = np.pi * angle / (2 * count)
    return np.concatenate([np.cos(angle), np.sin(angle)], axis=0) * count**-0.5


def boson_matrix(rows, count):
    v = np.arange(count, dtype=np.int64)
    angle = ((v[None, :] - count // 2) * (2 * rows[:, None] + 1)) % (2 * count)
    angle = np.pi * angle / count
    return np.concatenate([np.cos(angle), np.sin(angle)], axis=0) * count**-0.5


def plane_parts(side):
    p = np.arange(side * side, dtype=np.int64)
    angle = ((p[:, None] // side) * (p[None, :] // side) + (p[:, None] % side) * (p[None, :] % side)) % side
    angle = 2 * np.pi * angle / side
    scale = side**-1.5
    return np.cos(angle) * scale, np.sin(angle) * scale


def times_w4(re, im, power, sign):
    power = (power * sign) % 4
    if power == 0:
        return re, im
    if power == 1:
        return -im, re
    if power == 2:
        return -re, -im
    return im, -re


def dft4(values, sign):
    (r0, i0), (r1, i1), (r2, i2), (r3, i3) = values
    sr, si, dr, di = r0 + r2, i0 + i2, r0 - r2, i0 - i2
    tr, ti, er, ei = r1 + r3, i1 + i3, r1 - r3, i1 - i3
    if sign > 0:
        return [(sr + tr, si + ti), (dr - ei, di + er), (sr - tr, si - ti), (dr + ei, di - er)]
    return [(sr + tr, si + ti), (dr + ei, di - er), (sr - tr, si - ti), (dr - ei, di + er)]


def twiddle(value, power, sign, side):
    re, im = value
    if power % (side // 4) == 0:
        return times_w4(re, im, power // (side // 4), sign)
    angle = 2.0 * np.pi * power / side
    c, s = float(np.cos(angle)), float(sign * np.sin(angle))
    return re * c - im * s, re * s + im * c


def dft_line(values, sign):
    side = len(values)
    if side == 1:
        return values
    if side == 2:
        (r0, i0), (r1, i1) = values
        return [(r0 + r1, i0 + i1), (r0 - r1, i0 - i1)]
    if side == 4:
        return dft4(values, sign)
    inner = side // 4
    parts = [dft_line(values[b::4], sign) for b in range(4)]
    out = [None] * side
    for k1 in range(inner):
        column = [twiddle(parts[b][k1], b * k1, sign, side) for b in range(4)]
        for k2, value in enumerate(dft4(column, sign)):
            out[k1 + inner * k2] = value
    return out


def half_line(values, sign, parity):
    side = len(values)
    inner = side // 4
    parts = [dft_line(values[b::4], sign) for b in range(4)]
    out = [None] * (side // 2)
    for k1 in range(inner):
        column = [twiddle(parts[b][k1], b * k1, sign, side) for b in range(4)]
        column = [(re * parity, im * parity) if b % 2 else (re, im) for b, (re, im) in enumerate(column)]
        for k2, value in enumerate(dft4(column, sign)[:2]):
            out[k1 + inner * k2] = value
    return out


def load_inputs(g_hbm, m_hbm, g_ref, m_ref, in_sems, m_sem):
    load = pltpu.make_async_copy(m_hbm, m_ref, m_sem)
    pieces = [
        pltpu.make_async_copy(g_hbm.at[:, pl.ds(e, 1)], g_ref.at[:, pl.ds(e, 1)], in_sems.at[e])
        for e in range(g_ref.shape[1])
    ]
    for copy in [load] + pieces:
        copy.start()
    load.wait()
    return pieces


def sums_of(matrix, g_ref, e):
    lanes = g_ref.shape[2]
    g = jnp.concatenate([g_ref[0, e], g_ref[1, e]], axis=0)
    d = dot3(matrix, split_value(g), ((1,), (1,)))
    half = d.shape[0] // 2
    return d[:half, :lanes], d[:half, lanes:], d[half:, :lanes], d[half:, lanes:]


def both_times_kernel(g_hbm, m_hbm, out_ref, g_ref, m_ref, stage, in_sems, m_sem, out_sems):
    entries, lanes = g_ref.shape[1:3]
    near, _, _, _, rows, _ = stage.shape
    pieces = load_inputs(g_hbm, m_hbm, g_ref, m_ref, in_sems, m_sem)
    matrix = split_value(m_ref[...])
    copies = []
    for e in range(entries):
        pieces[e].wait()
        c_re, c_im, s_re, s_im = sums_of(matrix, g_ref, e)
        for where, value in (
            ((0, 0), c_re + s_im),
            ((0, 1), c_im - s_re),
            ((1, 0), s_im - c_re),
            ((1, 1), -(c_im + s_re)),
        ):
            stage[:, where[0], where[1], e] = value.reshape(near, rows, lanes)
        cut = pl.ds(e, 1)
        for side in range(2):
            target = out_ref.at[pl.ds(side * near, near), :, :, cut]
            copies.append(pltpu.make_async_copy(stage.at[:, :, :, cut], target, out_sems.at[e, side]))
            copies[-1].start()
    for copy in copies:
        copy.wait()


def one_times_kernel(g_hbm, m_hbm, out_ref, g_ref, m_ref, stage, in_sems, m_sem, out_sems):
    entries, lanes = g_ref.shape[1:3]
    devices, _, _, rows, _ = stage.shape
    pieces = load_inputs(g_hbm, m_hbm, g_ref, m_ref, in_sems, m_sem)
    matrix = split_value(m_ref[...])
    copies = []
    for e in range(entries):
        pieces[e].wait()
        c_re, c_im, s_re, s_im = sums_of(matrix, g_ref, e)
        stage[:, 0, e] = (c_re + s_im).reshape(devices, rows, lanes)
        stage[:, 1, e] = (c_im - s_re).reshape(devices, rows, lanes)
        cut = pl.ds(e, 1)
        copies.append(pltpu.make_async_copy(stage.at[:, :, cut], out_ref.at[:, :, cut], out_sems.at[e, 0]))
        copies[-1].start()
    for copy in copies:
        copy.wait()


def to_times(kernel, green, matrix, shape, targets, name):
    entries = green.shape[1]
    hbm = pl.BlockSpec(memory_space=pltpu.HBM)
    return pl.pallas_call(
        kernel,
        in_specs=[hbm, hbm],
        out_specs=hbm,
        out_shape=jax.ShapeDtypeStruct((targets,) + shape[1:], jnp.float32),
        scratch_shapes=[
            pltpu.VMEM(green.shape, jnp.float32),
            pltpu.VMEM(matrix.shape, jnp.float32),
            pltpu.VMEM(shape, jnp.float32),
            pltpu.SemaphoreType.DMA((entries,)),
            pltpu.SemaphoreType.DMA,
            pltpu.SemaphoreType.DMA((entries, 2)),
        ],
        compiler_params=pltpu.CompilerParams(vmem_limit_bytes=63 << 20),
        name=name,
    )(green, matrix)


def fill_block(ref, cosine, sine):
    plane = cosine.shape[0]
    lanes = plane // 2
    for block in range(2):
        cut = slice(block * lanes, (block + 1) * lanes)
        re = slice(2 * block * lanes, (2 * block + 1) * lanes)
        im = slice((2 * block + 1) * lanes, (2 * block + 2) * lanes)
        ref[:plane, re] = cosine[:, cut].astype(jnp.bfloat16)
        ref[plane:, im] = cosine[:, cut].astype(jnp.bfloat16)
        ref[:plane, im] = sine[:, cut].astype(jnp.bfloat16)
        ref[plane:, re] = (-sine[:, cut]).astype(jnp.bfloat16)


def fill_matrices(mirror_ref, parts, forward, backward, turned):
    plane = parts[0].shape[0]
    side = mirror_ref.shape[1]
    row = lax.broadcasted_iota(jnp.int32, (plane, plane), 0)
    column = lax.broadcasted_iota(jnp.int32, (plane, plane), 1)
    upper = (mirror_ref[1, 0] - column // side) & (side - 1)
    lower = (mirror_ref[2, 0] - column % side) & (side - 1)
    pick = (row == upper * side + lower).astype(jnp.float32).astype(jnp.bfloat16)

    def dot(a, b):
        return jnp.dot(a, b, preferred_element_type=jnp.float32)

    for part in range(2):
        c_ref, s_ref = parts[part], parts[2 + part]
        cosine, sine = c_ref[...].astype(jnp.float32), s_ref[...].astype(jnp.float32)
        fill_block(forward.at[0, part], cosine, sine)
        fill_block(backward.at[0, part], turned(cosine), turned(-sine))
        fill_block(forward.at[1, part], dot(c_ref[...], pick), dot(s_ref[...], pick))
        fill_block(backward.at[1, part], turned(dot(pick, c_ref[...])), turned(-dot(pick, s_ref[...])))


def plane_dot(value, matrix, half, block):
    width = matrix.shape[3] // 2
    cut = slice(block * width, (block + 1) * width)
    return dot3(value, (matrix[half, 0, :, cut], matrix[half, 1, :, cut]), ((1,), (0,)))


def one_middle_kernel(table_ref, mirror_ref, ch_ref, cl_ref, sh_ref, sl_ref, x_ref, out_ref, *refs):
    forward, backward, mid, space, other_space, chi, stage, sems = refs
    _, side, _, entries, rows, lanes = space.shape
    plane = 2 * lanes
    groups, _, _, members, _, _ = chi.shape
    fill_matrices(mirror_ref, (ch_ref, cl_ref, sh_ref, sl_ref), forward, backward, lambda value: value)

    def paired(first, second):
        upper = lax.broadcasted_iota(jnp.int32, first.shape, 1) < rows // 2
        turned = [pltpu.roll(part, rows // 2, 1) for part in (first, second)]
        return jnp.where(upper, first, turned[1]), jnp.where(upper, turned[0], second)

    def halves_of(columns):
        value = jnp.concatenate(columns, axis=1)
        count, width = value.shape
        value = value.reshape(count // (2 * rows), 2, rows, width)
        parts = paired(value[:, 0], value[:, 1])
        return [split_value(part.reshape(count // 2, width)) for part in parts]

    def halves_dot(parts, matrix, block):
        shape = (parts[0][0].shape[0] // rows, rows, plane)
        d = paired(*(plane_dot(parts[half], matrix, half, block).reshape(shape) for half in range(2)))
        return jnp.concatenate([part.reshape(shape[0], 1, rows, plane) for part in d], axis=1)

    parts = halves_of([x_ref[:, h, ri].reshape(side * entries * rows, lanes) for ri in range(2) for h in range(2)])
    for block in range(2):
        d = halves_dot(parts, forward, block)
        for ri in range(2):
            piece = d[:, :, :, ri * lanes : (ri + 1) * lanes]
            mid[block, ri] = piece.reshape(side, entries, rows, lanes)
    for block in range(2):
        for e in range(entries):
            values = [(mid[block, 0, x, e], mid[block, 1, x, e]) for x in range(side)]
            for x, parts in enumerate(dft_line(values, 1)):
                for ri in range(2):
                    space[block, x, ri, e] = parts[ri]
                    other_space[block, x, ri, e] = pltpu.roll(parts[ri], rows // 2, 0)

    copies = []
    for group in range(groups):
        for c in range(members):
            left, right = table_ref[0, group * members + c], table_ref[1, group * members + c]
            for block in range(2):
                values = []
                for x in range(side):
                    other = mirror_ref[0, x]
                    a_re, a_im = space[block, x, 0, left], space[block, x, 1, left]
                    b_re, b_im = other_space[block, other, 0, right], other_space[block, other, 1, right]
                    values.append((a_re * b_re - a_im * b_im, a_re * b_im + a_im * b_re))
                cut = slice(block * lanes, (block + 1) * lanes)
                for x, parts in enumerate(dft_line(values, -1)):
                    for ri in range(2):
                        chi[group, ri, x, c, :, cut] = parts[ri]
        whole = (side * members * rows, plane)
        parts = halves_of([chi[group, ri].reshape(whole) for ri in range(2)])
        for h in range(2):
            d = halves_dot(parts, backward, h)
            for ri in range(2):
                piece = d[:, :, :, ri * lanes : (ri + 1) * lanes].reshape(side, members, rows, lanes)
                stage[group, :, h, ri] = piece
        target = out_ref.at[:, :, :, pl.ds(group * members, members)]
        copies.append(pltpu.make_async_copy(stage.at[group], target, sems.at[group]))
        copies[-1].start()
    for copy in copies:
        copy.wait()


def both_middle_kernel(me_ref, table_ref, mirror_ref, ch_ref, cl_ref, sh_ref, sl_ref, x_ref, *refs):
    outs, (forward, backward, mid, space, chi) = refs[:-5], refs[-5:]
    halves, _, side, _, entries, rows, lanes = space.shape
    plane = 2 * lanes
    units, _, kept, members, _, _ = chi.shape
    me, near = me_ref[0], len(outs)
    core, line = me % 2, me // 2 % kept
    parity = (1 - 2 * (me // near)).astype(jnp.float32)

    def turned(value):
        return jnp.where(core == 0, value, jnp.concatenate([value[:, lanes:], value[:, :lanes]], axis=1))

    fill_matrices(mirror_ref, (ch_ref, cl_ref, sh_ref, sl_ref), forward, backward, turned)

    def arrive(half):
        columns = [
            x_ref[:, h, half, ri].reshape(side * entries * rows, lanes) for ri in range(2) for h in range(2)
        ]
        return split_value(jnp.concatenate(columns, axis=1))

    def to_plane(value, half, block):
        d = plane_dot(value, forward, half, block)
        for ri in range(2):
            piece = d[:, ri * lanes : (ri + 1) * lanes]
            mid[half, block, ri] = piece.reshape(side, entries, rows, lanes)

    def along_line(half, block, e):
        values = [(mid[half, block, 0, x, e], mid[half, block, 1, x, e]) for x in range(side)]
        for x, (re, im) in enumerate(dft_line(values, 1)):
            space[half, block, x, 0, e] = re
            space[half, block, x, 1, e] = im

    def product(unit, block, c):
        half, first = unit % halves, unit // halves * members
        left, right = table_ref[0, first + c], table_ref[1, first + c]
        values = []
        for x in range(side):
            other = mirror_ref[0, x]
            a_re, a_im = space[half, block, x, 0, left], space[half, block, x, 1, left]
            b_re, b_im = space[1 - half, block, other, 0, right], space[1 - half, block, other, 1, right]
            values.append((a_re * b_re - a_im * b_im, a_re * b_im + a_im * b_re))
        cut = slice(block * lanes, (block + 1) * lanes)
        for x, (re, im) in enumerate(half_line(values, -1, parity)):
            chi[unit, 0, x ^ line, c, :, cut] = re
            chi[unit, 1, x ^ line, c, :, cut] = im

    def from_plane(unit, value, h):
        half, first = unit % halves, unit // halves * members
        d = plane_dot(value, backward, half, h)
        for ri in range(2):
            piece = d[:, ri * lanes : (ri + 1) * lanes].reshape(kept, members, rows, lanes)
            for x in range(kept):
                outs[2 * x + h][half, ri, first : first + members] = piece[x]

    def collect(unit):
        whole = (kept * members * rows, plane)
        return split_value(jnp.concatenate([chi[unit, ri].reshape(whole) for ri in range(2)], axis=1))

    places = [(half, block) for half in range(halves) for block in range(2)]
    for step in range(len(places) + 1):
        if step < len(places):
            half, block = places[step]
            if block == 0:
                value = arrive(half)
            to_plane(value, half, block)
        if step > 0:
            for e in range(entries):
                along_line(*places[step - 1], e)

    for unit in range(units + 1):
        tasks = [(block, c) for block in range(2) for c in range(members)] if unit < units else []
        if unit > 0:
            value = collect(unit - 1)
        for h in range(2):
            if unit > 0:
                from_plane(unit - 1, value, h)
            for block, c in tasks[h * members : (h + 1) * members]:
                product(unit, block, c)


def middle_inputs(table, mirror_map, x):
    side, plane = x.shape[0] // 2, 2 * x.shape[-1]
    cosine, sine = plane_parts(side)
    parts = [jnp.asarray(part) for part in split_constant(cosine) + split_constant(sine)]
    smem = pl.BlockSpec(memory_space=pltpu.SMEM)
    vmem = pl.BlockSpec(memory_space=pltpu.VMEM)
    args = (table.T, mirror_map, *parts, x.reshape((side, 2) + x.shape[1:]))
    return args, [smem, smem] + [vmem] * 5, pltpu.VMEM((2, 2, 2 * plane, 2 * plane), jnp.bfloat16)


def one_middle(x, table, mirror_map):
    devices, _, entries, rows, lanes = x.shape
    side, components = devices // 2, table.shape[0]
    args, specs, matrices = middle_inputs(table, mirror_map, x)
    spatial = pltpu.VMEM((2, side, 2, entries, rows, lanes), jnp.float32)
    shape = (side, 2, 2, components, rows, lanes)
    out = pl.pallas_call(
        one_middle_kernel,
        in_specs=specs,
        out_specs=pl.BlockSpec(memory_space=pltpu.HBM),
        out_shape=jax.ShapeDtypeStruct(shape, jnp.float32),
        scratch_shapes=[
            matrices,
            matrices,
            pltpu.VMEM((2, 2, side, entries, rows, lanes), jnp.float32),
            spatial,
            spatial,
            pltpu.VMEM((GROUPS, 2, side, components // GROUPS, rows, 2 * lanes), jnp.float32),
            pltpu.VMEM((GROUPS, side, 2, 2, components // GROUPS, rows, lanes), jnp.float32),
            pltpu.SemaphoreType.DMA((GROUPS,)),
        ],
        compiler_params=pltpu.CompilerParams(vmem_limit_bytes=44 << 20),
        cost_estimate=pl.CostEstimate(flops=6_000_000_000, bytes_accessed=12_000_000, transcendentals=0),
        name="one_middle",
    )(*args)
    return out.reshape((devices,) + shape[2:])


def both_middle(x, table, mirror_map, me, near):
    devices, halves, _, entries, rows, lanes = x.shape
    side, components = devices // 2, table.shape[0]
    args, specs, matrices = middle_inputs(table, mirror_map, x)
    members = components // GROUPS
    return pl.pallas_call(
        both_middle_kernel,
        in_specs=[pl.BlockSpec(memory_space=pltpu.SMEM)] + specs,
        out_specs=[pl.BlockSpec(memory_space=pltpu.VMEM)] * near,
        out_shape=[jax.ShapeDtypeStruct((halves, 2, components, rows, lanes), jnp.float32)] * near,
        scratch_shapes=[
            matrices,
            matrices,
            pltpu.VMEM((halves, 2, 2, side, entries, rows, lanes), jnp.float32),
            pltpu.VMEM((halves, 2, side, 2, entries, rows, lanes), jnp.float32),
            pltpu.VMEM((halves * GROUPS, 2, near // 2, members, rows, 2 * lanes), jnp.float32),
        ],
        compiler_params=pltpu.CompilerParams(vmem_limit_bytes=60 << 20),
        name="both_middle",
    )(me, *args)


def prepare_kernel(me_ref, both_ref, one_ref, out_ref):
    near = both_ref.shape[1]
    me = me_ref[0] % near
    ordered = [both_ref[part, slot ^ me] for part in range(2) for slot in range(near)]
    for part, value in enumerate(split_value(jnp.concatenate([one_ref[...]] + ordered, axis=0))):
        out_ref[part] = value


def prepare(me, both, one):
    smem = pl.BlockSpec(memory_space=pltpu.SMEM)
    vmem = pl.BlockSpec(memory_space=pltpu.VMEM)
    depth = both.size // both.shape[3] + one.shape[0]
    return pl.pallas_call(
        prepare_kernel,
        in_specs=[smem, vmem, vmem],
        out_specs=vmem,
        out_shape=jax.ShapeDtypeStruct((2, depth, one.shape[1]), jnp.bfloat16),
        compiler_params=pltpu.CompilerParams(vmem_limit_bytes=63 << 20),
        name="prepare",
    )(me, both, one)


def frequency_kernel(order, y_hbm, m_hbm, *refs):
    pieces, (out_ref, y_ref, m_ref, held, stage, y_sems, m_sems, in_sems, sems) = refs[:-9], refs[-9:]
    near = len(pieces)
    devices, _, components, rows, lanes = y_ref.shape
    groups = sems.shape[0]
    members = components // groups
    depth = devices * rows
    cuts = [pl.ds(group * members, members) for group in range(groups)]
    matrices = [
        pltpu.make_async_copy(m_hbm.at[:, pl.ds(start, depth)], m_ref.at[:, pl.ds(start, depth)], m_sems.at[part])
        for part, start in enumerate((0, depth))
    ]
    blocks = [
        pltpu.make_async_copy(y_hbm.at[:, :, cut], y_ref.at[:, :, cut], y_sems.at[group])
        for group, cut in enumerate(cuts)
    ]
    spans = [pl.ds(part * components // 2, components // 2) for part in range(2)]
    loads = [
        [
            pltpu.make_async_copy(piece.at[:, :, span], held.at[slot, :, :, span], in_sems.at[part, slot])
            for slot, piece in zip(order, pieces)
        ]
        for part, span in enumerate(spans)
    ]
    for copy in [matrices[0], blocks[0], matrices[1]] + loads[0] + blocks[1:] + loads[1]:
        copy.start()
    upper_rows = lax.broadcasted_iota(jnp.int32, (devices, rows, lanes), 1) < rows // 2

    def part_of(values, start):
        matrix = [m_ref[part, start : start + depth] for part in range(2)]
        return dot3(split_value(jnp.concatenate(values, axis=0)), matrix, ((1,), (0,)))

    def one_part(group):
        values = []
        for c in range(group * members, (group + 1) * members):
            folded = []
            for ri in range(2):
                tile = y_ref[:, ri, c]
                turned = pltpu.roll(tile, rows // 2, 1)
                folded.append((tile + turned, turned - tile))
            first = jnp.where(upper_rows, folded[0][0], -folded[1][1])
            second = jnp.where(upper_rows, folded[1][0], folded[0][1])
            values.append(first.reshape(devices * rows, lanes).T)
            values.append(second.reshape(devices * rows, lanes).T)
        return part_of(values, 0)

    def both_part(group):
        values = []
        for c in range(group * members, (group + 1) * members):
            part = [[held[:, half, ri, c].reshape(near * rows, lanes) for ri in range(2)] for half in range(2)]
            sums = [part[0][ri] + part[1][ri] for ri in range(2)]
            differences = [part[0][ri] - part[1][ri] for ri in range(2)]
            values.append(jnp.concatenate([sums[0], -differences[1]], axis=0).T)
            values.append(jnp.concatenate([sums[1], differences[0]], axis=0).T)
        return part_of(values, depth)

    copies = []
    matrices[0].wait()
    for group in range(groups):
        blocks[group].wait()
        d = one_part(group)
        if group == 0:
            matrices[1].wait()
        if group % (groups // 2) == 0:
            for copy in loads[group // (groups // 2)]:
                copy.wait()
        d = (d + both_part(group)).reshape(members, 2, lanes, d.shape[1])
        for ri in range(2):
            stage[ri, group * members : (group + 1) * members] = d[:, ri]
        copies.append(pltpu.make_async_copy(stage.at[:, cuts[group]], out_ref.at[:, cuts[group]], sems.at[group]))
        copies[-1].start()
    for copy in copies:
        copy.wait()


def to_frequencies(y, pieces, order, matrix):
    _, _, components, _, lanes = y.shape
    shape = (2, components, lanes, matrix.shape[2])
    hbm = pl.BlockSpec(memory_space=pltpu.HBM)
    groups = components // 2
    return pl.pallas_call(
        functools.partial(frequency_kernel, order),
        in_specs=[hbm] * (2 + len(pieces)),
        out_specs=hbm,
        out_shape=jax.ShapeDtypeStruct(shape, jnp.float32),
        scratch_shapes=[
            pltpu.VMEM(y.shape, jnp.float32),
            pltpu.VMEM(matrix.shape, jnp.bfloat16),
            pltpu.VMEM((len(pieces),) + pieces[0].shape, jnp.float32),
            pltpu.VMEM(shape, jnp.float32),
            pltpu.SemaphoreType.DMA((groups,)),
            pltpu.SemaphoreType.DMA((2,)),
            pltpu.SemaphoreType.DMA((2, len(pieces))),
            pltpu.SemaphoreType.DMA((groups,)),
        ],
        compiler_params=pltpu.CompilerParams(vmem_limit_bytes=63 << 20),
        name="to_frequencies",
    )(y, matrix, *pieces)


def exchange(x):
    flat = x.reshape(x.shape[0], -1, x.shape[-1])
    return lax.all_to_all(flat, "kb", split_axis=0, concat_axis=0, tiled=True).reshape(x.shape)


def swap(piece, slot, devices):
    if slot == 0:
        return piece
    return lax.ppermute(piece, "kb", [(device, device ^ slot) for device in range(devices)])


def trig_pair(angle_int, period, scale):
    angle = 2.0 * math.pi / period * angle_int.astype(jnp.float32)
    return (scale * jnp.cos(angle), scale * jnp.sin(angle))


def complex_combine(formula, cosine, sine, real_part, imag_part):
    first_term = jnp.einsum(formula, cosine, real_part + imag_part, precision=lax.Precision.HIGHEST)
    second_term = jnp.einsum(formula, cosine + sine, imag_part, precision=lax.Precision.HIGHEST)
    third_term = jnp.einsum(formula, sine - cosine, real_part, precision=lax.Precision.HIGHEST)
    return (first_term - second_term, first_term + third_term)


def forward_imaginary_time(tau_rows, frequency_count):
    freq_index = jnp.arange(frequency_count, dtype=jnp.int32)
    angle_int = (
        (2 * freq_index[None, :] - frequency_count + 1)
        * (2 * tau_rows[:, None] + 1)
        % (4 * frequency_count)
    )
    cosine, sine = trig_pair(angle_int, 4 * frequency_count, frequency_count ** (-0.5))
    return (cosine, -sine)


def tau_backward(tau_rows, frequency_count):
    freq_index = jnp.arange(frequency_count, dtype=jnp.int32)
    angle_int = (
        (freq_index[:, None] - frequency_count // 2)
        * (2 * tau_rows[None, :] + 1)
        % (2 * frequency_count)
    )
    return trig_pair(angle_int, 2 * frequency_count, frequency_count ** (-0.5))


def grid_transform(real_part, imag_part, grid_side, direction):
    shape = real_part.shape
    plane = jnp.arange(grid_side * grid_side, dtype=jnp.int32)
    upper = plane // grid_side
    lower = plane % grid_side
    plane_int = (upper[:, None] * upper[None, :] + lower[:, None] * lower[None, :]) % grid_side
    plane_cos, plane_sin = trig_pair(plane_int, grid_side, 1.0 / grid_side)
    line = jnp.arange(grid_side, dtype=jnp.int32)
    line_cos, line_sin = trig_pair(
        line[:, None] * line[None, :] % grid_side, grid_side, grid_side ** (-0.5)
    )
    real_part = real_part.reshape(shape[:-1] + (grid_side, grid_side * grid_side))
    imag_part = imag_part.reshape(shape[:-1] + (grid_side, grid_side * grid_side))
    real_part, imag_part = complex_combine(
        "pq,...xq->...xp", plane_cos, direction * plane_sin, real_part, imag_part
    )
    real_part, imag_part = complex_combine(
        "ax,...xp->...ap", line_cos, direction * line_sin, real_part, imag_part
    )
    return (real_part.reshape(shape), imag_part.reshape(shape))


def mirror_index(mirror_map, grid_side):
    index_x = mirror_map[0][:, None, None]
    index_y = mirror_map[1][None, :, None]
    index_z = mirror_map[2][None, None, :]
    return (index_x * grid_side * grid_side + index_y * grid_side + index_z).reshape(-1)


def bubble(gr_re, gr_im, mirror_re, mirror_im, pair_table, entries):
    entry_ids = jnp.arange(entries, dtype=jnp.int32)
    pick_left = (pair_table[:, 0][:, None] == entry_ids[None, :]).astype(jnp.float32)
    pick_right = (pair_table[:, 1][:, None] == entry_ids[None, :]).astype(jnp.float32)
    left_re = jnp.einsum("me,e...->m...", pick_left, gr_re, precision=lax.Precision.HIGHEST)
    left_im = jnp.einsum("me,e...->m...", pick_left, gr_im, precision=lax.Precision.HIGHEST)
    right_re = jnp.einsum("me,e...->m...", pick_right, mirror_re, precision=lax.Precision.HIGHEST)
    right_im = jnp.einsum("me,e...->m...", pick_right, mirror_im, precision=lax.Precision.HIGHEST)
    return (left_re * right_re - left_im * right_im, left_re * right_im + left_im * right_re)


def general(green_momentum_grid, pair_table, mirror_map):
    grid_side = mirror_map.shape[1]
    entries = green_momentum_grid.shape[1]
    frequency_count = green_momentum_grid.shape[3]
    position = jnp.arange(frequency_count, dtype=jnp.int32)
    fwd_cos, fwd_sin = forward_imaginary_time(position, frequency_count)
    tau_re, tau_im = complex_combine(
        "qa,fsa->fqs", fwd_cos, fwd_sin, green_momentum_grid[0], green_momentum_grid[1]
    )
    stacked = jnp.stack([tau_re, tau_im])

    def to_real_space(pieces):
        space_re, space_im = grid_transform(pieces[0], pieces[1], grid_side, 1.0)
        return jnp.stack([space_re, space_im])

    mirror_flat = mirror_index(mirror_map, grid_side)
    partner_rows = frequency_count - 1 - position
    reflected_cosine, reflected_sine = forward_imaginary_time(partner_rows, frequency_count)
    partner_real, partner_imaginary = complex_combine(
        "qa,fsa->fqs",
        reflected_cosine,
        reflected_sine,
        green_momentum_grid[0],
        green_momentum_grid[1],
    )
    other_stacked = jnp.stack([partner_real, partner_imaginary])
    pieces = (
        lax.all_to_all(stacked, "kb", split_axis=2, concat_axis=3, tiled=True),
        lax.all_to_all(other_stacked, "kb", split_axis=2, concat_axis=3, tiled=True),
    )
    in_cells = to_real_space(pieces[0])
    partner = to_real_space(pieces[1])
    mirrored = jnp.take(partner, mirror_flat, axis=3)
    chi_re, chi_im = bubble(in_cells[0], in_cells[1], mirrored[0], mirrored[1], pair_table, entries)
    chi_re, chi_im = grid_transform(chi_re, chi_im, grid_side, -1.0)
    momenta = jnp.stack([chi_re, chi_im])
    back_cos, back_sin = tau_backward(position, frequency_count)
    pieces = lax.all_to_all(momenta, "kb", split_axis=3, concat_axis=2, tiled=True)
    out_re, out_im = complex_combine("vj,ejk->ekv", back_cos, back_sin, pieces[0], pieces[1])
    return jnp.stack([out_re, out_im])


def local(green, pair_table, mirror_map):
    side = mirror_map.shape[1]
    plane = side * side
    lanes, count = green.shape[2], green.shape[3]
    devices = side * plane // lanes
    near = devices // 2
    half = ROWS // 2
    shared = near * ROWS
    if lanes != LANES or 2 * lanes != plane or 2 * (shared + devices * half) != count:
        return general(green, pair_table, mirror_map)
    me = lax.axis_index("kb").astype(jnp.int32).reshape(1)
    entries = green.shape[1]

    rows = np.arange(shared)
    both_fermion = fermion_matrix(rows, count).astype(np.float32)
    both_boson = boson_matrix(rows, count).reshape(2, near, ROWS, count).astype(np.float32)
    rows = shared + np.arange(devices * half).reshape(devices, half)
    times = np.concatenate([rows, count - 1 - rows], axis=1).reshape(-1)
    one_fermion = fermion_matrix(times, count).astype(np.float32)
    one_boson = boson_matrix(rows.reshape(-1), count).reshape(2, devices, half, count).swapaxes(0, 1)
    one_boson = one_boson.reshape(devices * ROWS, count).astype(np.float32)

    shape = (near, 2, 2, entries, ROWS, lanes)
    both = to_times(both_times_kernel, green, jnp.asarray(both_fermion), shape, devices, "both_times")
    green, both = lax.optimization_barrier((green, both))
    shape = (devices, 2, entries, ROWS, lanes)
    one = to_times(one_times_kernel, green, jnp.asarray(one_fermion), shape, devices, "one_times")
    both, one = lax.optimization_barrier((exchange(both), one))
    pieces = both_middle(both, pair_table, mirror_map, me, near)
    first = near // 2
    early = list(range(first, first + near // 4)) + [1]
    beside = [first + near // 4, first + near // 4 + 1, 2, 3]
    late = [slot for slot in range(1, near) if slot not in early + beside]
    moved = {0: pieces[0]}

    one, arrived = lax.optimization_barrier((exchange(one), [swap(pieces[slot], slot, devices) for slot in early]))
    moved |= zip(early, arrived)
    arrived = [swap(pieces[slot], slot, devices) for slot in beside]
    one, arrived, both_boson, one_boson = lax.optimization_barrier(
        (one_middle(one, pair_table, mirror_map), arrived, jnp.asarray(both_boson), jnp.asarray(one_boson))
    )
    moved |= zip(beside, arrived)
    matrix, sent = lax.optimization_barrier((prepare(me, both_boson, one_boson), [pieces[slot] for slot in late]))
    moved |= zip(late, [swap(piece, slot, devices) for slot, piece in zip(late, sent)])
    order = [0] + early + beside + late
    return to_frequencies(exchange(one), [moved[slot] for slot in order], order, matrix)


def solution(mesh):
    placed = (P("set", None, "kb", None), P(), P("set", None))
    return jax.shard_map(
        local, mesh=mesh, in_specs=placed, out_specs=P("set", None, "kb", None), check_vma=False
    )
```

```python
import functools
import math

import jax
import jax.numpy as jnp
import ml_dtypes
import numpy as np
from jax import lax
from jax.experimental import pallas as pl
from jax.experimental.pallas import tpu as pltpu
from jax.sharding import PartitionSpec as P

LANES = 128
ROWS = 8
GROUPS = 2


def split_constant(matrix):
    high = matrix.astype(np.float32).astype(ml_dtypes.bfloat16)
    low = (matrix - high.astype(np.float64)).astype(np.float32).astype(ml_dtypes.bfloat16)
    return high, low


def split_value(value):
    high = value.astype(jnp.bfloat16)
    low = (value - high.astype(jnp.float32)).astype(jnp.bfloat16)
    return high, low


def dot3(left, right, dims):
    (k_left,), (k_right,) = dims
    a = jnp.concatenate([left[0], left[0], left[1]], axis=k_left)
    b = jnp.concatenate([right[0], right[1], right[0]], axis=k_right)
    return lax.dot_general(a, b, (dims, ((), ())), preferred_element_type=jnp.float32)


def fermion_matrix(rows, count):
    n = np.arange(count, dtype=np.int64)
    angle = ((2 * n[None, :] - count + 1) * (2 * rows[:, None] + 1)) % (4 * count)
    angle = np.pi * angle / (2 * count)
    return np.concatenate([np.cos(angle), np.sin(angle)], axis=0) * count**-0.5


def boson_matrix(rows, count):
    v = np.arange(count, dtype=np.int64)
    angle = ((v[None, :] - count // 2) * (2 * rows[:, None] + 1)) % (2 * count)
    angle = np.pi * angle / count
    return np.concatenate([np.cos(angle), np.sin(angle)], axis=0) * count**-0.5


def plane_parts(side):
    p = np.arange(side * side, dtype=np.int64)
    angle = ((p[:, None] // side) * (p[None, :] // side) + (p[:, None] % side) * (p[None, :] % side)) % side
    angle = 2 * np.pi * angle / side
    scale = side**-1.5
    return np.cos(angle) * scale, np.sin(angle) * scale


def times_w4(re, im, power, sign):
    power = (power * sign) % 4
    if power == 0:
        return re, im
    if power == 1:
        return -im, re
    if power == 2:
        return -re, -im
    return im, -re


def dft4(values, sign):
    (r0, i0), (r1, i1), (r2, i2), (r3, i3) = values
    sr, si, dr, di = r0 + r2, i0 + i2, r0 - r2, i0 - i2
    tr, ti, er, ei = r1 + r3, i1 + i3, r1 - r3, i1 - i3
    if sign > 0:
        return [(sr + tr, si + ti), (dr - ei, di + er), (sr - tr, si - ti), (dr + ei, di - er)]
    return [(sr + tr, si + ti), (dr + ei, di - er), (sr - tr, si - ti), (dr - ei, di + er)]


def twiddle(value, power, sign, side):
    re, im = value
    if power % (side // 4) == 0:
        return times_w4(re, im, power // (side // 4), sign)
    angle = 2.0 * np.pi * power / side
    c, s = float(np.cos(angle)), float(sign * np.sin(angle))
    return re * c - im * s, re * s + im * c


def dft_line(values, sign):
    side = len(values)
    if side == 1:
        return values
    if side == 2:
        (r0, i0), (r1, i1) = values
        return [(r0 + r1, i0 + i1), (r0 - r1, i0 - i1)]
    if side == 4:
        return dft4(values, sign)
    inner = side // 4
    parts = [dft_line(values[b::4], sign) for b in range(4)]
    out = [None] * side
    for k1 in range(inner):
        column = [twiddle(parts[b][k1], b * k1, sign, side) for b in range(4)]
        for k2, value in enumerate(dft4(column, sign)):
            out[k1 + inner * k2] = value
    return out


def half_line(values, sign, parity):
    side = len(values)
    inner = side // 4
    parts = [dft_line(values[b::4], sign) for b in range(4)]
    out = [None] * (side // 2)
    for k1 in range(inner):
        column = [twiddle(parts[b][k1], b * k1, sign, side) for b in range(4)]
        column = [(re * parity, im * parity) if b % 2 else (re, im) for b, (re, im) in enumerate(column)]
        for k2, value in enumerate(dft4(column, sign)[:2]):
            out[k1 + inner * k2] = value
    return out


def load_inputs(g_hbm, m_hbm, g_ref, m_ref, in_sems, m_sem):
    load = pltpu.make_async_copy(m_hbm, m_ref, m_sem)
    pieces = [
        pltpu.make_async_copy(g_hbm.at[:, pl.ds(e, 1)], g_ref.at[:, pl.ds(e, 1)], in_sems.at[e])
        for e in range(g_ref.shape[1])
    ]
    for copy in [load] + pieces:
        copy.start()
    load.wait()
    return pieces


def sums_of(matrix, g_ref, e):
    lanes = g_ref.shape[2]
    g = jnp.concatenate([g_ref[0, e], g_ref[1, e]], axis=0)
    d = dot3(matrix, split_value(g), ((1,), (1,)))
    half = d.shape[0] // 2
    return d[:half, :lanes], d[:half, lanes:], d[half:, :lanes], d[half:, lanes:]


def both_times_kernel(g_hbm, m_hbm, out_ref, g_ref, m_ref, stage, in_sems, m_sem, out_sems):
    entries, lanes = g_ref.shape[1:3]
    near, _, _, _, rows, _ = stage.shape
    pieces = load_inputs(g_hbm, m_hbm, g_ref, m_ref, in_sems, m_sem)
    matrix = split_value(m_ref[...])
    copies = []
    for e in range(entries):
        pieces[e].wait()
        c_re, c_im, s_re, s_im = sums_of(matrix, g_ref, e)
        for where, value in (
            ((0, 0), c_re + s_im),
            ((0, 1), c_im - s_re),
            ((1, 0), s_im - c_re),
            ((1, 1), -(c_im + s_re)),
        ):
            stage[:, where[0], where[1], e] = value.reshape(near, rows, lanes)
        cut = pl.ds(e, 1)
        for side in range(2):
            target = out_ref.at[pl.ds(side * near, near), :, :, cut]
            copies.append(pltpu.make_async_copy(stage.at[:, :, :, cut], target, out_sems.at[e, side]))
            copies[-1].start()
    for copy in copies:
        copy.wait()


def one_times_kernel(g_hbm, m_hbm, out_ref, g_ref, m_ref, stage, in_sems, m_sem, out_sems):
    entries, lanes = g_ref.shape[1:3]
    devices, _, _, rows, _ = stage.shape
    pieces = load_inputs(g_hbm, m_hbm, g_ref, m_ref, in_sems, m_sem)
    matrix = split_value(m_ref[...])
    copies = []
    for e in range(entries):
        pieces[e].wait()
        c_re, c_im, s_re, s_im = sums_of(matrix, g_ref, e)
        stage[:, 0, e] = (c_re + s_im).reshape(devices, rows, lanes)
        stage[:, 1, e] = (c_im - s_re).reshape(devices, rows, lanes)
        cut = pl.ds(e, 1)
        copies.append(pltpu.make_async_copy(stage.at[:, :, cut], out_ref.at[:, :, cut], out_sems.at[e, 0]))
        copies[-1].start()
    for copy in copies:
        copy.wait()


def to_times(kernel, green, matrix, shape, targets, name):
    entries = green.shape[1]
    hbm = pl.BlockSpec(memory_space=pltpu.HBM)
    return pl.pallas_call(
        kernel,
        in_specs=[hbm, hbm],
        out_specs=hbm,
        out_shape=jax.ShapeDtypeStruct((targets,) + shape[1:], jnp.float32),
        scratch_shapes=[
            pltpu.VMEM(green.shape, jnp.float32),
            pltpu.VMEM(matrix.shape, jnp.float32),
            pltpu.VMEM(shape, jnp.float32),
            pltpu.SemaphoreType.DMA((entries,)),
            pltpu.SemaphoreType.DMA,
            pltpu.SemaphoreType.DMA((entries, 2)),
        ],
        compiler_params=pltpu.CompilerParams(vmem_limit_bytes=63 << 20),
        name=name,
    )(green, matrix)


def fill_block(ref, cosine, sine):
    plane = cosine.shape[0]
    lanes = plane // 2
    for block in range(2):
        cut = slice(block * lanes, (block + 1) * lanes)
        re = slice(2 * block * lanes, (2 * block + 1) * lanes)
        im = slice((2 * block + 1) * lanes, (2 * block + 2) * lanes)
        ref[:plane, re] = cosine[:, cut].astype(jnp.bfloat16)
        ref[plane:, im] = cosine[:, cut].astype(jnp.bfloat16)
        ref[:plane, im] = sine[:, cut].astype(jnp.bfloat16)
        ref[plane:, re] = (-sine[:, cut]).astype(jnp.bfloat16)


def fill_matrices(mirror_ref, parts, forward, backward, turned):
    plane = parts[0].shape[0]
    side = mirror_ref.shape[1]
    row = lax.broadcasted_iota(jnp.int32, (plane, plane), 0)
    column = lax.broadcasted_iota(jnp.int32, (plane, plane), 1)
    upper = (mirror_ref[1, 0] - column // side) & (side - 1)
    lower = (mirror_ref[2, 0] - column % side) & (side - 1)
    pick = (row == upper * side + lower).astype(jnp.float32).astype(jnp.bfloat16)

    def dot(a, b):
        return jnp.dot(a, b, preferred_element_type=jnp.float32)

    for part in range(2):
        c_ref, s_ref = parts[part], parts[2 + part]
        cosine, sine = c_ref[...].astype(jnp.float32), s_ref[...].astype(jnp.float32)
        fill_block(forward.at[0, part], cosine, sine)
        fill_block(backward.at[0, part], turned(cosine), turned(-sine))
        fill_block(forward.at[1, part], dot(c_ref[...], pick), dot(s_ref[...], pick))
        fill_block(backward.at[1, part], turned(dot(pick, c_ref[...])), turned(-dot(pick, s_ref[...])))


def plane_dot(value, matrix, half, block):
    width = matrix.shape[3] // 2
    cut = slice(block * width, (block + 1) * width)
    return dot3(value, (matrix[half, 0, :, cut], matrix[half, 1, :, cut]), ((1,), (0,)))


def one_middle_kernel(table_ref, mirror_ref, ch_ref, cl_ref, sh_ref, sl_ref, x_ref, out_ref, *refs):
    forward, backward, mid, space, other_space, chi, stage, sems = refs
    _, side, _, entries, rows, lanes = space.shape
    plane = 2 * lanes
    groups, _, _, members, _, _ = chi.shape
    fill_matrices(mirror_ref, (ch_ref, cl_ref, sh_ref, sl_ref), forward, backward, lambda value: value)

    def paired(first, second):
        upper = lax.broadcasted_iota(jnp.int32, first.shape, 1) < rows // 2
        turned = [pltpu.roll(part, rows // 2, 1) for part in (first, second)]
        return jnp.where(upper, first, turned[1]), jnp.where(upper, turned[0], second)

    def halves_of(columns):
        value = jnp.concatenate(columns, axis=1)
        count, width = value.shape
        value = value.reshape(count // (2 * rows), 2, rows, width)
        parts = paired(value[:, 0], value[:, 1])
        return [split_value(part.reshape(count // 2, width)) for part in parts]

    def halves_dot(parts, matrix, block):
        shape = (parts[0][0].shape[0] // rows, rows, plane)
        d = paired(*(plane_dot(parts[half], matrix, half, block).reshape(shape) for half in range(2)))
        return jnp.concatenate([part.reshape(shape[0], 1, rows, plane) for part in d], axis=1)

    parts = halves_of([x_ref[:, h, ri].reshape(side * entries * rows, lanes) for ri in range(2) for h in range(2)])
    for block in range(2):
        d = halves_dot(parts, forward, block)
        for ri in range(2):
            piece = d[:, :, :, ri * lanes : (ri + 1) * lanes]
            mid[block, ri] = piece.reshape(side, entries, rows, lanes)
    for block in range(2):
        for e in range(entries):
            values = [(mid[block, 0, x, e], mid[block, 1, x, e]) for x in range(side)]
            for x, parts in enumerate(dft_line(values, 1)):
                for ri in range(2):
                    space[block, x, ri, e] = parts[ri]
                    other_space[block, x, ri, e] = pltpu.roll(parts[ri], rows // 2, 0)

    copies = []
    for group in range(groups):
        for c in range(members):
            left, right = table_ref[0, group * members + c], table_ref[1, group * members + c]
            for block in range(2):
                values = []
                for x in range(side):
                    other = mirror_ref[0, x]
                    a_re, a_im = space[block, x, 0, left], space[block, x, 1, left]
                    b_re, b_im = other_space[block, other, 0, right], other_space[block, other, 1, right]
                    values.append((a_re * b_re - a_im * b_im, a_re * b_im + a_im * b_re))
                cut = slice(block * lanes, (block + 1) * lanes)
                for x, parts in enumerate(dft_line(values, -1)):
                    for ri in range(2):
                        chi[group, ri, x, c, :, cut] = parts[ri]
        whole = (side * members * rows, plane)
        parts = halves_of([chi[group, ri].reshape(whole) for ri in range(2)])
        for h in range(2):
            d = halves_dot(parts, backward, h)
            for ri in range(2):
                piece = d[:, :, :, ri * lanes : (ri + 1) * lanes].reshape(side, members, rows, lanes)
                stage[group, :, h, ri] = piece
        target = out_ref.at[:, :, :, pl.ds(group * members, members)]
        copies.append(pltpu.make_async_copy(stage.at[group], target, sems.at[group]))
        copies[-1].start()
    for copy in copies:
        copy.wait()


def both_middle_kernel(me_ref, table_ref, mirror_ref, ch_ref, cl_ref, sh_ref, sl_ref, x_ref, *refs):
    outs, (forward, backward, mid, space, chi) = refs[:-5], refs[-5:]
    halves, _, side, _, entries, rows, lanes = space.shape
    plane = 2 * lanes
    units, _, kept, members, _, _ = chi.shape
    me, near = me_ref[0], len(outs)
    core, line = me % 2, me // 2 % kept
    parity = (1 - 2 * (me // near)).astype(jnp.float32)

    def turned(value):
        return jnp.where(core == 0, value, jnp.concatenate([value[:, lanes:], value[:, :lanes]], axis=1))

    fill_matrices(mirror_ref, (ch_ref, cl_ref, sh_ref, sl_ref), forward, backward, turned)

    def arrive(half):
        columns = [
            x_ref[:, h, half, ri].reshape(side * entries * rows, lanes) for ri in range(2) for h in range(2)
        ]
        return split_value(jnp.concatenate(columns, axis=1))

    def to_plane(value, half, block):
        d = plane_dot(value, forward, half, block)
        for ri in range(2):
            piece = d[:, ri * lanes : (ri + 1) * lanes]
            mid[half, block, ri] = piece.reshape(side, entries, rows, lanes)

    def along_line(half, block, e):
        values = [(mid[half, block, 0, x, e], mid[half, block, 1, x, e]) for x in range(side)]
        for x, (re, im) in enumerate(dft_line(values, 1)):
            space[half, block, x, 0, e] = re
            space[half, block, x, 1, e] = im

    def product(unit, block, c):
        half, first = unit % halves, unit // halves * members
        left, right = table_ref[0, first + c], table_ref[1, first + c]
        values = []
        for x in range(side):
            other = mirror_ref[0, x]
            a_re, a_im = space[half, block, x, 0, left], space[half, block, x, 1, left]
            b_re, b_im = space[1 - half, block, other, 0, right], space[1 - half, block, other, 1, right]
            values.append((a_re * b_re - a_im * b_im, a_re * b_im + a_im * b_re))
        cut = slice(block * lanes, (block + 1) * lanes)
        for x, (re, im) in enumerate(half_line(values, -1, parity)):
            chi[unit, 0, x ^ line, c, :, cut] = re
            chi[unit, 1, x ^ line, c, :, cut] = im

    def from_plane(unit, value, h):
        half, first = unit % halves, unit // halves * members
        d = plane_dot(value, backward, half, h)
        for ri in range(2):
            piece = d[:, ri * lanes : (ri + 1) * lanes].reshape(kept, members, rows, lanes)
            for x in range(kept):
                outs[2 * x + h][half, ri, first : first + members] = piece[x]

    def collect(unit):
        whole = (kept * members * rows, plane)
        return split_value(jnp.concatenate([chi[unit, ri].reshape(whole) for ri in range(2)], axis=1))

    places = [(half, block) for half in range(halves) for block in range(2)]
    for step in range(len(places) + 1):
        if step < len(places):
            half, block = places[step]
            if block == 0:
                value = arrive(half)
            to_plane(value, half, block)
        if step > 0:
            for e in range(entries):
                along_line(*places[step - 1], e)

    for unit in range(units + 1):
        tasks = [(block, c) for block in range(2) for c in range(members)] if unit < units else []
        if unit > 0:
            value = collect(unit - 1)
        for h in range(2):
            if unit > 0:
                from_plane(unit - 1, value, h)
            for block, c in tasks[h * members : (h + 1) * members]:
                product(unit, block, c)


def middle_inputs(table, mirror_map, x):
    side, plane = x.shape[0] // 2, 2 * x.shape[-1]
    cosine, sine = plane_parts(side)
    parts = [jnp.asarray(part) for part in split_constant(cosine) + split_constant(sine)]
    smem = pl.BlockSpec(memory_space=pltpu.SMEM)
    vmem = pl.BlockSpec(memory_space=pltpu.VMEM)
    args = (table.T, mirror_map, *parts, x.reshape((side, 2) + x.shape[1:]))
    return args, [smem, smem] + [vmem] * 5, pltpu.VMEM((2, 2, 2 * plane, 2 * plane), jnp.bfloat16)


def one_middle(x, table, mirror_map):
    devices, _, entries, rows, lanes = x.shape
    side, components = devices // 2, table.shape[0]
    args, specs, matrices = middle_inputs(table, mirror_map, x)
    spatial = pltpu.VMEM((2, side, 2, entries, rows, lanes), jnp.float32)
    shape = (side, 2, 2, components, rows, lanes)
    out = pl.pallas_call(
        one_middle_kernel,
        in_specs=specs,
        out_specs=pl.BlockSpec(memory_space=pltpu.HBM),
        out_shape=jax.ShapeDtypeStruct(shape, jnp.float32),
        scratch_shapes=[
            matrices,
            matrices,
            pltpu.VMEM((2, 2, side, entries, rows, lanes), jnp.float32),
            spatial,
            spatial,
            pltpu.VMEM((GROUPS, 2, side, components // GROUPS, rows, 2 * lanes), jnp.float32),
            pltpu.VMEM((GROUPS, side, 2, 2, components // GROUPS, rows, lanes), jnp.float32),
            pltpu.SemaphoreType.DMA((GROUPS,)),
        ],
        compiler_params=pltpu.CompilerParams(vmem_limit_bytes=44 << 20),
        cost_estimate=pl.CostEstimate(flops=6_000_000_000, bytes_accessed=12_000_000, transcendentals=0),
        name="one_middle",
    )(*args)
    return out.reshape((devices,) + shape[2:])


def both_middle(x, table, mirror_map, me, near):
    devices, halves, _, entries, rows, lanes = x.shape
    side, components = devices // 2, table.shape[0]
    args, specs, matrices = middle_inputs(table, mirror_map, x)
    members = components // GROUPS
    return pl.pallas_call(
        both_middle_kernel,
        in_specs=[pl.BlockSpec(memory_space=pltpu.SMEM)] + specs,
        out_specs=[pl.BlockSpec(memory_space=pltpu.VMEM)] * near,
        out_shape=[jax.ShapeDtypeStruct((halves, 2, components, rows, lanes), jnp.float32)] * near,
        scratch_shapes=[
            matrices,
            matrices,
            pltpu.VMEM((halves, 2, 2, side, entries, rows, lanes), jnp.float32),
            pltpu.VMEM((halves, 2, side, 2, entries, rows, lanes), jnp.float32),
            pltpu.VMEM((halves * GROUPS, 2, near // 2, members, rows, 2 * lanes), jnp.float32),
        ],
        compiler_params=pltpu.CompilerParams(vmem_limit_bytes=60 << 20),
        name="both_middle",
    )(me, *args)


def prepare_kernel(me_ref, both_ref, one_ref, out_ref):
    near = both_ref.shape[1]
    me = me_ref[0] % near
    ordered = [both_ref[part, slot ^ me] for part in range(2) for slot in range(near)]
    for part, value in enumerate(split_value(jnp.concatenate([one_ref[...]] + ordered, axis=0))):
        out_ref[part] = value


def prepare(me, both, one):
    smem = pl.BlockSpec(memory_space=pltpu.SMEM)
    vmem = pl.BlockSpec(memory_space=pltpu.VMEM)
    depth = both.size // both.shape[3] + one.shape[0]
    return pl.pallas_call(
        prepare_kernel,
        in_specs=[smem, vmem, vmem],
        out_specs=vmem,
        out_shape=jax.ShapeDtypeStruct((2, depth, one.shape[1]), jnp.bfloat16),
        compiler_params=pltpu.CompilerParams(vmem_limit_bytes=63 << 20),
        name="prepare",
    )(me, both, one)


def frequency_kernel(order, y_hbm, m_hbm, *refs):
    pieces, (out_ref, y_ref, m_ref, held, stage, y_sems, m_sems, in_sems, sems) = refs[:-9], refs[-9:]
    near = len(pieces)
    devices, _, components, rows, lanes = y_ref.shape
    groups = sems.shape[0]
    members = components // groups
    depth = devices * rows
    cuts = [pl.ds(group * members, members) for group in range(groups)]
    matrices = [
        pltpu.make_async_copy(m_hbm.at[:, pl.ds(start, depth)], m_ref.at[:, pl.ds(start, depth)], m_sems.at[part])
        for part, start in enumerate((0, depth))
    ]
    blocks = [
        pltpu.make_async_copy(y_hbm.at[:, :, cut], y_ref.at[:, :, cut], y_sems.at[group])
        for group, cut in enumerate(cuts)
    ]
    spans = [pl.ds(part * components // 2, components // 2) for part in range(2)]
    loads = [
        [
            pltpu.make_async_copy(piece.at[:, :, span], held.at[slot, :, :, span], in_sems.at[part, slot])
            for slot, piece in zip(order, pieces)
        ]
        for part, span in enumerate(spans)
    ]
    for copy in [matrices[0], blocks[0], matrices[1]] + loads[0] + blocks[1:] + loads[1]:
        copy.start()
    upper_rows = lax.broadcasted_iota(jnp.int32, (devices, rows, lanes), 1) < rows // 2

    def one_values(c):
        folded = []
        for ri in range(2):
            tile = y_ref[:, ri, c]
            turned = pltpu.roll(tile, rows // 2, 1)
            folded.append((tile + turned, turned - tile))
        first = jnp.where(upper_rows, folded[0][0], -folded[1][1])
        second = jnp.where(upper_rows, folded[1][0], folded[0][1])
        return first.reshape(depth, lanes), second.reshape(depth, lanes)

    def both_values(c):
        part = [[held[:, half, ri, c].reshape(near * rows, lanes) for ri in range(2)] for half in range(2)]
        sums = [part[0][ri] + part[1][ri] for ri in range(2)]
        differences = [part[0][ri] - part[1][ri] for ri in range(2)]
        return [sums[0], -differences[1]], [sums[1], differences[0]]

    copies = []
    for copy in matrices:
        copy.wait()
    matrix = (m_ref[0], m_ref[1])
    for group in range(groups):
        blocks[group].wait()
        if group % (groups // 2) == 0:
            for copy in loads[group // (groups // 2)]:
                copy.wait()
        values = []
        for c in range(group * members, (group + 1) * members):
            for one, both in zip(one_values(c), both_values(c)):
                values.append(jnp.concatenate([one] + both, axis=0).T)
        d = dot3(split_value(jnp.concatenate(values, axis=0)), matrix, ((1,), (0,)))
        d = d.reshape(members, 2, lanes, d.shape[1])
        for ri in range(2):
            stage[ri, group * members : (group + 1) * members] = d[:, ri]
        copies.append(pltpu.make_async_copy(stage.at[:, cuts[group]], out_ref.at[:, cuts[group]], sems.at[group]))
        copies[-1].start()
    for copy in copies:
        copy.wait()


def to_frequencies(y, pieces, order, matrix):
    _, _, components, _, lanes = y.shape
    shape = (2, components, lanes, matrix.shape[2])
    hbm = pl.BlockSpec(memory_space=pltpu.HBM)
    groups = components // 2
    return pl.pallas_call(
        functools.partial(frequency_kernel, order),
        in_specs=[hbm] * (2 + len(pieces)),
        out_specs=hbm,
        out_shape=jax.ShapeDtypeStruct(shape, jnp.float32),
        scratch_shapes=[
            pltpu.VMEM(y.shape, jnp.float32),
            pltpu.VMEM(matrix.shape, jnp.bfloat16),
            pltpu.VMEM((len(pieces),) + pieces[0].shape, jnp.float32),
            pltpu.VMEM(shape, jnp.float32),
            pltpu.SemaphoreType.DMA((groups,)),
            pltpu.SemaphoreType.DMA((2,)),
            pltpu.SemaphoreType.DMA((2, len(pieces))),
            pltpu.SemaphoreType.DMA((groups,)),
        ],
        compiler_params=pltpu.CompilerParams(vmem_limit_bytes=63 << 20),
        name="to_frequencies",
    )(y, matrix, *pieces)


def exchange(x):
    flat = x.reshape(x.shape[0], -1, x.shape[-1])
    return lax.all_to_all(flat, "kb", split_axis=0, concat_axis=0, tiled=True).reshape(x.shape)


def swap(piece, slot, devices):
    if slot == 0:
        return piece
    return lax.ppermute(piece, "kb", [(device, device ^ slot) for device in range(devices)])


def trig_pair(angle_int, period, scale):
    angle = 2.0 * math.pi / period * angle_int.astype(jnp.float32)
    return (scale * jnp.cos(angle), scale * jnp.sin(angle))


def complex_combine(formula, cosine, sine, real_part, imag_part):
    first_term = jnp.einsum(formula, cosine, real_part + imag_part, precision=lax.Precision.HIGHEST)
    second_term = jnp.einsum(formula, cosine + sine, imag_part, precision=lax.Precision.HIGHEST)
    third_term = jnp.einsum(formula, sine - cosine, real_part, precision=lax.Precision.HIGHEST)
    return (first_term - second_term, first_term + third_term)


def forward_imaginary_time(tau_rows, frequency_count):
    freq_index = jnp.arange(frequency_count, dtype=jnp.int32)
    angle_int = (
        (2 * freq_index[None, :] - frequency_count + 1)
        * (2 * tau_rows[:, None] + 1)
        % (4 * frequency_count)
    )
    cosine, sine = trig_pair(angle_int, 4 * frequency_count, frequency_count ** (-0.5))
    return (cosine, -sine)


def tau_backward(tau_rows, frequency_count):
    freq_index = jnp.arange(frequency_count, dtype=jnp.int32)
    angle_int = (
        (freq_index[:, None] - frequency_count // 2)
        * (2 * tau_rows[None, :] + 1)
        % (2 * frequency_count)
    )
    return trig_pair(angle_int, 2 * frequency_count, frequency_count ** (-0.5))


def grid_transform(real_part, imag_part, grid_side, direction):
    shape = real_part.shape
    plane = jnp.arange(grid_side * grid_side, dtype=jnp.int32)
    upper = plane // grid_side
    lower = plane % grid_side
    plane_int = (upper[:, None] * upper[None, :] + lower[:, None] * lower[None, :]) % grid_side
    plane_cos, plane_sin = trig_pair(plane_int, grid_side, 1.0 / grid_side)
    line = jnp.arange(grid_side, dtype=jnp.int32)
    line_cos, line_sin = trig_pair(
        line[:, None] * line[None, :] % grid_side, grid_side, grid_side ** (-0.5)
    )
    real_part = real_part.reshape(shape[:-1] + (grid_side, grid_side * grid_side))
    imag_part = imag_part.reshape(shape[:-1] + (grid_side, grid_side * grid_side))
    real_part, imag_part = complex_combine(
        "pq,...xq->...xp", plane_cos, direction * plane_sin, real_part, imag_part
    )
    real_part, imag_part = complex_combine(
        "ax,...xp->...ap", line_cos, direction * line_sin, real_part, imag_part
    )
    return (real_part.reshape(shape), imag_part.reshape(shape))


def mirror_index(mirror_map, grid_side):
    index_x = mirror_map[0][:, None, None]
    index_y = mirror_map[1][None, :, None]
    index_z = mirror_map[2][None, None, :]
    return (index_x * grid_side * grid_side + index_y * grid_side + index_z).reshape(-1)


def bubble(gr_re, gr_im, mirror_re, mirror_im, pair_table, entries):
    entry_ids = jnp.arange(entries, dtype=jnp.int32)
    pick_left = (pair_table[:, 0][:, None] == entry_ids[None, :]).astype(jnp.float32)
    pick_right = (pair_table[:, 1][:, None] == entry_ids[None, :]).astype(jnp.float32)
    left_re = jnp.einsum("me,e...->m...", pick_left, gr_re, precision=lax.Precision.HIGHEST)
    left_im = jnp.einsum("me,e...->m...", pick_left, gr_im, precision=lax.Precision.HIGHEST)
    right_re = jnp.einsum("me,e...->m...", pick_right, mirror_re, precision=lax.Precision.HIGHEST)
    right_im = jnp.einsum("me,e...->m...", pick_right, mirror_im, precision=lax.Precision.HIGHEST)
    return (left_re * right_re - left_im * right_im, left_re * right_im + left_im * right_re)


def general(green_momentum_grid, pair_table, mirror_map):
    grid_side = mirror_map.shape[1]
    entries = green_momentum_grid.shape[1]
    frequency_count = green_momentum_grid.shape[3]
    position = jnp.arange(frequency_count, dtype=jnp.int32)
    fwd_cos, fwd_sin = forward_imaginary_time(position, frequency_count)
    tau_re, tau_im = complex_combine(
        "qa,fsa->fqs", fwd_cos, fwd_sin, green_momentum_grid[0], green_momentum_grid[1]
    )
    stacked = jnp.stack([tau_re, tau_im])

    def to_real_space(pieces):
        space_re, space_im = grid_transform(pieces[0], pieces[1], grid_side, 1.0)
        return jnp.stack([space_re, space_im])

    mirror_flat = mirror_index(mirror_map, grid_side)
    partner_rows = frequency_count - 1 - position
    reflected_cosine, reflected_sine = forward_imaginary_time(partner_rows, frequency_count)
    partner_real, partner_imaginary = complex_combine(
        "qa,fsa->fqs",
        reflected_cosine,
        reflected_sine,
        green_momentum_grid[0],
        green_momentum_grid[1],
    )
    other_stacked = jnp.stack([partner_real, partner_imaginary])
    pieces = (
        lax.all_to_all(stacked, "kb", split_axis=2, concat_axis=3, tiled=True),
        lax.all_to_all(other_stacked, "kb", split_axis=2, concat_axis=3, tiled=True),
    )
    in_cells = to_real_space(pieces[0])
    partner = to_real_space(pieces[1])
    mirrored = jnp.take(partner, mirror_flat, axis=3)
    chi_re, chi_im = bubble(in_cells[0], in_cells[1], mirrored[0], mirrored[1], pair_table, entries)
    chi_re, chi_im = grid_transform(chi_re, chi_im, grid_side, -1.0)
    momenta = jnp.stack([chi_re, chi_im])
    back_cos, back_sin = tau_backward(position, frequency_count)
    pieces = lax.all_to_all(momenta, "kb", split_axis=3, concat_axis=2, tiled=True)
    out_re, out_im = complex_combine("vj,ejk->ekv", back_cos, back_sin, pieces[0], pieces[1])
    return jnp.stack([out_re, out_im])


def local(green, pair_table, mirror_map):
    side = mirror_map.shape[1]
    plane = side * side
    lanes, count = green.shape[2], green.shape[3]
    devices = side * plane // lanes
    near = devices // 2
    half = ROWS // 2
    shared = near * ROWS
    if lanes != LANES or 2 * lanes != plane or 2 * (shared + devices * half) != count:
        return general(green, pair_table, mirror_map)
    me = lax.axis_index("kb").astype(jnp.int32).reshape(1)
    entries = green.shape[1]

    rows = np.arange(shared)
    both_fermion = fermion_matrix(rows, count).astype(np.float32)
    both_boson = boson_matrix(rows, count).reshape(2, near, ROWS, count).astype(np.float32)
    rows = shared + np.arange(devices * half).reshape(devices, half)
    times = np.concatenate([rows, count - 1 - rows], axis=1).reshape(-1)
    one_fermion = fermion_matrix(times, count).astype(np.float32)
    one_boson = boson_matrix(rows.reshape(-1), count).reshape(2, devices, half, count).swapaxes(0, 1)
    one_boson = one_boson.reshape(devices * ROWS, count).astype(np.float32)

    shape = (near, 2, 2, entries, ROWS, lanes)
    both = to_times(both_times_kernel, green, jnp.asarray(both_fermion), shape, devices, "both_times")
    green, both = lax.optimization_barrier((green, both))
    shape = (devices, 2, entries, ROWS, lanes)
    one = to_times(one_times_kernel, green, jnp.asarray(one_fermion), shape, devices, "one_times")
    both, one = lax.optimization_barrier((exchange(both), one))
    pieces = both_middle(both, pair_table, mirror_map, me, near)
    first, count = near // 2, 3 * near // 16
    early = list(range(first, first + count)) + [1, 2]
    beside = list(range(first + count, first + 2 * count)) + [3, 4]
    late = [slot for slot in range(1, near) if slot not in early + beside]
    moved = {0: pieces[0]}

    one, arrived = lax.optimization_barrier((exchange(one), [swap(pieces[slot], slot, devices) for slot in early]))
    moved |= zip(early, arrived)
    arrived = [swap(pieces[slot], slot, devices) for slot in beside]
    one, arrived, both_boson, one_boson = lax.optimization_barrier(
        (one_middle(one, pair_table, mirror_map), arrived, jnp.asarray(both_boson), jnp.asarray(one_boson))
    )
    moved |= zip(beside, arrived)
    matrix, sent = lax.optimization_barrier((prepare(me, both_boson, one_boson), [pieces[slot] for slot in late]))
    moved |= zip(late, [swap(piece, slot, devices) for slot, piece in zip(late, sent)])
    order = [0] + early + beside + late
    return to_frequencies(exchange(one), [moved[slot] for slot in order], order, matrix)


def solution(mesh):
    placed = (P("set", None, "kb", None), P(), P("set", None))
    return jax.shard_map(
        local, mesh=mesh, in_specs=placed, out_specs=P("set", None, "kb", None), check_vma=False
    )
```

```python
import functools
import math

import jax
import jax.numpy as jnp
import ml_dtypes
import numpy as np
from jax import lax
from jax.experimental import pallas as pl
from jax.experimental.pallas import tpu as pltpu
from jax.sharding import PartitionSpec as P

LANES = 128
ROWS = 8
GROUPS = 2


def split_constant(matrix):
    high = matrix.astype(np.float32).astype(ml_dtypes.bfloat16)
    low = (matrix - high.astype(np.float64)).astype(np.float32).astype(ml_dtypes.bfloat16)
    return high, low


def split_value(value):
    high = value.astype(jnp.bfloat16)
    low = (value - high.astype(jnp.float32)).astype(jnp.bfloat16)
    return high, low


def dot3(left, right, dims):
    (k_left,), (k_right,) = dims
    a = jnp.concatenate([left[0], left[0], left[1]], axis=k_left)
    b = jnp.concatenate([right[0], right[1], right[0]], axis=k_right)
    return lax.dot_general(a, b, (dims, ((), ())), preferred_element_type=jnp.float32)


def fermion_matrix(rows, count):
    n = np.arange(count, dtype=np.int64)
    angle = ((2 * n[None, :] - count + 1) * (2 * rows[:, None] + 1)) % (4 * count)
    angle = np.pi * angle / (2 * count)
    return np.concatenate([np.cos(angle), np.sin(angle)], axis=0) * count**-0.5


def boson_matrix(rows, count):
    v = np.arange(count, dtype=np.int64)
    angle = ((v[None, :] - count // 2) * (2 * rows[:, None] + 1)) % (2 * count)
    angle = np.pi * angle / count
    return np.concatenate([np.cos(angle), np.sin(angle)], axis=0) * count**-0.5


def plane_parts(side):
    p = np.arange(side * side, dtype=np.int64)
    angle = ((p[:, None] // side) * (p[None, :] // side) + (p[:, None] % side) * (p[None, :] % side)) % side
    angle = 2 * np.pi * angle / side
    scale = side**-1.5
    return np.cos(angle) * scale, np.sin(angle) * scale


def times_w4(re, im, power, sign):
    power = (power * sign) % 4
    if power == 0:
        return re, im
    if power == 1:
        return -im, re
    if power == 2:
        return -re, -im
    return im, -re


def dft4(values, sign):
    (r0, i0), (r1, i1), (r2, i2), (r3, i3) = values
    sr, si, dr, di = r0 + r2, i0 + i2, r0 - r2, i0 - i2
    tr, ti, er, ei = r1 + r3, i1 + i3, r1 - r3, i1 - i3
    if sign > 0:
        return [(sr + tr, si + ti), (dr - ei, di + er), (sr - tr, si - ti), (dr + ei, di - er)]
    return [(sr + tr, si + ti), (dr + ei, di - er), (sr - tr, si - ti), (dr - ei, di + er)]


def twiddle(value, power, sign, side):
    re, im = value
    if power % (side // 4) == 0:
        return times_w4(re, im, power // (side // 4), sign)
    angle = 2.0 * np.pi * power / side
    c, s = float(np.cos(angle)), float(sign * np.sin(angle))
    return re * c - im * s, re * s + im * c


def dft_line(values, sign):
    side = len(values)
    if side == 1:
        return values
    if side == 2:
        (r0, i0), (r1, i1) = values
        return [(r0 + r1, i0 + i1), (r0 - r1, i0 - i1)]
    if side == 4:
        return dft4(values, sign)
    inner = side // 4
    parts = [dft_line(values[b::4], sign) for b in range(4)]
    out = [None] * side
    for k1 in range(inner):
        column = [twiddle(parts[b][k1], b * k1, sign, side) for b in range(4)]
        for k2, value in enumerate(dft4(column, sign)):
            out[k1 + inner * k2] = value
    return out


def half_line(values, sign, parity):
    side = len(values)
    inner = side // 4
    parts = [dft_line(values[b::4], sign) for b in range(4)]
    out = [None] * (side // 2)
    for k1 in range(inner):
        column = [twiddle(parts[b][k1], b * k1, sign, side) for b in range(4)]
        column = [(re * parity, im * parity) if b % 2 else (re, im) for b, (re, im) in enumerate(column)]
        for k2, value in enumerate(dft4(column, sign)[:2]):
            out[k1 + inner * k2] = value
    return out


def load_inputs(g_hbm, m_hbm, g_ref, m_ref, in_sems, m_sem):
    load = pltpu.make_async_copy(m_hbm, m_ref, m_sem)
    pieces = [
        pltpu.make_async_copy(g_hbm.at[:, pl.ds(e, 1)], g_ref.at[:, pl.ds(e, 1)], in_sems.at[e])
        for e in range(g_ref.shape[1])
    ]
    for copy in [load] + pieces:
        copy.start()
    load.wait()
    return pieces


def sums_of(matrix, g_ref, e):
    lanes = g_ref.shape[2]
    g = jnp.concatenate([g_ref[0, e], g_ref[1, e]], axis=0)
    d = dot3(matrix, split_value(g), ((1,), (1,)))
    half = d.shape[0] // 2
    return d[:half, :lanes], d[:half, lanes:], d[half:, :lanes], d[half:, lanes:]


def both_times_kernel(g_hbm, m_hbm, out_ref, g_ref, m_ref, stage, in_sems, m_sem, out_sems):
    entries, lanes = g_ref.shape[1:3]
    near, _, _, _, rows, _ = stage.shape
    pieces = load_inputs(g_hbm, m_hbm, g_ref, m_ref, in_sems, m_sem)
    matrix = split_value(m_ref[...])
    copies = []
    for e in range(entries):
        pieces[e].wait()
        c_re, c_im, s_re, s_im = sums_of(matrix, g_ref, e)
        for where, value in (
            ((0, 0), c_re + s_im),
            ((0, 1), c_im - s_re),
            ((1, 0), s_im - c_re),
            ((1, 1), -(c_im + s_re)),
        ):
            stage[:, where[0], where[1], e] = value.reshape(near, rows, lanes)
        cut = pl.ds(e, 1)
        for side in range(2):
            target = out_ref.at[pl.ds(side * near, near), :, :, cut]
            copies.append(pltpu.make_async_copy(stage.at[:, :, :, cut], target, out_sems.at[e, side]))
            copies[-1].start()
    for copy in copies:
        copy.wait()


def one_times_kernel(g_hbm, m_hbm, out_ref, g_ref, m_ref, stage, in_sems, m_sem, out_sems):
    entries, lanes = g_ref.shape[1:3]
    devices, _, _, rows, _ = stage.shape
    pieces = load_inputs(g_hbm, m_hbm, g_ref, m_ref, in_sems, m_sem)
    matrix = split_value(m_ref[...])
    copies = []
    for e in range(entries):
        pieces[e].wait()
        c_re, c_im, s_re, s_im = sums_of(matrix, g_ref, e)
        stage[:, 0, e] = (c_re + s_im).reshape(devices, rows, lanes)
        stage[:, 1, e] = (c_im - s_re).reshape(devices, rows, lanes)
        cut = pl.ds(e, 1)
        copies.append(pltpu.make_async_copy(stage.at[:, :, cut], out_ref.at[:, :, cut], out_sems.at[e, 0]))
        copies[-1].start()
    for copy in copies:
        copy.wait()


def to_times(kernel, green, matrix, shape, targets, name):
    entries = green.shape[1]
    hbm = pl.BlockSpec(memory_space=pltpu.HBM)
    return pl.pallas_call(
        kernel,
        in_specs=[hbm, hbm],
        out_specs=hbm,
        out_shape=jax.ShapeDtypeStruct((targets,) + shape[1:], jnp.float32),
        scratch_shapes=[
            pltpu.VMEM(green.shape, jnp.float32),
            pltpu.VMEM(matrix.shape, jnp.float32),
            pltpu.VMEM(shape, jnp.float32),
            pltpu.SemaphoreType.DMA((entries,)),
            pltpu.SemaphoreType.DMA,
            pltpu.SemaphoreType.DMA((entries, 2)),
        ],
        compiler_params=pltpu.CompilerParams(vmem_limit_bytes=63 << 20),
        name=name,
    )(green, matrix)


def fill_block(ref, cosine, sine):
    plane = cosine.shape[0]
    lanes = plane // 2
    for block in range(2):
        cut = slice(block * lanes, (block + 1) * lanes)
        re = slice(2 * block * lanes, (2 * block + 1) * lanes)
        im = slice((2 * block + 1) * lanes, (2 * block + 2) * lanes)
        ref[:plane, re] = cosine[:, cut].astype(jnp.bfloat16)
        ref[plane:, im] = cosine[:, cut].astype(jnp.bfloat16)
        ref[:plane, im] = sine[:, cut].astype(jnp.bfloat16)
        ref[plane:, re] = (-sine[:, cut]).astype(jnp.bfloat16)


def fill_matrices(mirror_ref, parts, forward, backward, turned):
    plane = parts[0].shape[0]
    side = mirror_ref.shape[1]
    row = lax.broadcasted_iota(jnp.int32, (plane, plane), 0)
    column = lax.broadcasted_iota(jnp.int32, (plane, plane), 1)
    upper = (mirror_ref[1, 0] - column // side) & (side - 1)
    lower = (mirror_ref[2, 0] - column % side) & (side - 1)
    pick = (row == upper * side + lower).astype(jnp.float32).astype(jnp.bfloat16)

    def dot(a, b):
        return jnp.dot(a, b, preferred_element_type=jnp.float32)

    for part in range(2):
        c_ref, s_ref = parts[part], parts[2 + part]
        cosine, sine = c_ref[...].astype(jnp.float32), s_ref[...].astype(jnp.float32)
        fill_block(forward.at[0, part], cosine, sine)
        fill_block(backward.at[0, part], turned(cosine), turned(-sine))
        fill_block(forward.at[1, part], dot(c_ref[...], pick), dot(s_ref[...], pick))
        fill_block(backward.at[1, part], turned(dot(pick, c_ref[...])), turned(-dot(pick, s_ref[...])))


def plane_dot(value, matrix, half, block):
    width = matrix.shape[3] // 2
    cut = slice(block * width, (block + 1) * width)
    return dot3(value, (matrix[half, 0, :, cut], matrix[half, 1, :, cut]), ((1,), (0,)))


def one_middle_kernel(table_ref, mirror_ref, ch_ref, cl_ref, sh_ref, sl_ref, x_ref, out_ref, *refs):
    forward, backward, mid, space, other_space, chi, stage, sems = refs
    _, side, _, entries, rows, lanes = space.shape
    plane = 2 * lanes
    groups, _, _, members, _, _ = chi.shape
    fill_matrices(mirror_ref, (ch_ref, cl_ref, sh_ref, sl_ref), forward, backward, lambda value: value)

    def paired(first, second):
        upper = lax.broadcasted_iota(jnp.int32, first.shape, 1) < rows // 2
        turned = [pltpu.roll(part, rows // 2, 1) for part in (first, second)]
        return jnp.where(upper, first, turned[1]), jnp.where(upper, turned[0], second)

    def halves_of(columns):
        value = jnp.concatenate(columns, axis=1)
        count, width = value.shape
        value = value.reshape(count // (2 * rows), 2, rows, width)
        parts = paired(value[:, 0], value[:, 1])
        return [split_value(part.reshape(count // 2, width)) for part in parts]

    def halves_dot(parts, matrix, block):
        shape = (parts[0][0].shape[0] // rows, rows, plane)
        d = paired(*(plane_dot(parts[half], matrix, half, block).reshape(shape) for half in range(2)))
        return jnp.concatenate([part.reshape(shape[0], 1, rows, plane) for part in d], axis=1)

    parts = halves_of([x_ref[:, h, ri].reshape(side * entries * rows, lanes) for ri in range(2) for h in range(2)])
    for block in range(2):
        d = halves_dot(parts, forward, block)
        for ri in range(2):
            piece = d[:, :, :, ri * lanes : (ri + 1) * lanes]
            mid[block, ri] = piece.reshape(side, entries, rows, lanes)
    for block in range(2):
        for e in range(entries):
            values = [(mid[block, 0, x, e], mid[block, 1, x, e]) for x in range(side)]
            for x, parts in enumerate(dft_line(values, 1)):
                for ri in range(2):
                    space[block, x, ri, e] = parts[ri]
                    other_space[block, x, ri, e] = pltpu.roll(parts[ri], rows // 2, 0)

    copies = []
    for group in range(groups):
        for c in range(members):
            left, right = table_ref[0, group * members + c], table_ref[1, group * members + c]
            for block in range(2):
                values = []
                for x in range(side):
                    other = mirror_ref[0, x]
                    a_re, a_im = space[block, x, 0, left], space[block, x, 1, left]
                    b_re, b_im = other_space[block, other, 0, right], other_space[block, other, 1, right]
                    values.append((a_re * b_re - a_im * b_im, a_re * b_im + a_im * b_re))
                cut = slice(block * lanes, (block + 1) * lanes)
                for x, parts in enumerate(dft_line(values, -1)):
                    for ri in range(2):
                        chi[group, ri, x, c, :, cut] = parts[ri]
        whole = (side * members * rows, plane)
        parts = halves_of([chi[group, ri].reshape(whole) for ri in range(2)])
        for h in range(2):
            d = halves_dot(parts, backward, h)
            for ri in range(2):
                piece = d[:, :, :, ri * lanes : (ri + 1) * lanes].reshape(side, members, rows, lanes)
                stage[group, :, h, ri] = piece
        target = out_ref.at[:, :, :, pl.ds(group * members, members)]
        copies.append(pltpu.make_async_copy(stage.at[group], target, sems.at[group]))
        copies[-1].start()
    for copy in copies:
        copy.wait()


def both_middle_kernel(me_ref, table_ref, mirror_ref, ch_ref, cl_ref, sh_ref, sl_ref, x_ref, *refs):
    outs, (forward, backward, mid, space, chi) = refs[:-5], refs[-5:]
    halves, _, side, _, entries, rows, lanes = space.shape
    plane = 2 * lanes
    units, _, kept, members, _, _ = chi.shape
    me, near = me_ref[0], len(outs)
    core, line = me % 2, me // 2 % kept
    parity = (1 - 2 * (me // near)).astype(jnp.float32)

    def turned(value):
        return jnp.where(core == 0, value, jnp.concatenate([value[:, lanes:], value[:, :lanes]], axis=1))

    fill_matrices(mirror_ref, (ch_ref, cl_ref, sh_ref, sl_ref), forward, backward, turned)

    def arrive(half):
        columns = [
            x_ref[:, h, half, ri].reshape(side * entries * rows, lanes) for ri in range(2) for h in range(2)
        ]
        return split_value(jnp.concatenate(columns, axis=1))

    def to_plane(value, half, block):
        d = plane_dot(value, forward, half, block)
        for ri in range(2):
            piece = d[:, ri * lanes : (ri + 1) * lanes]
            mid[half, block, ri] = piece.reshape(side, entries, rows, lanes)

    def along_line(half, block, e):
        values = [(mid[half, block, 0, x, e], mid[half, block, 1, x, e]) for x in range(side)]
        for x, (re, im) in enumerate(dft_line(values, 1)):
            space[half, block, x, 0, e] = re
            space[half, block, x, 1, e] = im

    def product(unit, block, c):
        half, first = unit % halves, unit // halves * members
        left, right = table_ref[0, first + c], table_ref[1, first + c]
        values = []
        for x in range(side):
            other = mirror_ref[0, x]
            a_re, a_im = space[half, block, x, 0, left], space[half, block, x, 1, left]
            b_re, b_im = space[1 - half, block, other, 0, right], space[1 - half, block, other, 1, right]
            values.append((a_re * b_re - a_im * b_im, a_re * b_im + a_im * b_re))
        cut = slice(block * lanes, (block + 1) * lanes)
        for x, (re, im) in enumerate(half_line(values, -1, parity)):
            chi[unit, 0, x ^ line, c, :, cut] = re
            chi[unit, 1, x ^ line, c, :, cut] = im

    def from_plane(unit, value, h):
        half, first = unit % halves, unit // halves * members
        d = plane_dot(value, backward, half, h)
        for ri in range(2):
            piece = d[:, ri * lanes : (ri + 1) * lanes].reshape(kept, members, rows, lanes)
            for x in range(kept):
                outs[2 * x + h][half, ri, first : first + members] = piece[x]

    def collect(unit):
        whole = (kept * members * rows, plane)
        return split_value(jnp.concatenate([chi[unit, ri].reshape(whole) for ri in range(2)], axis=1))

    places = [(half, block) for half in range(halves) for block in range(2)]
    for step in range(len(places) + 1):
        if step < len(places):
            half, block = places[step]
            if block == 0:
                value = arrive(half)
            to_plane(value, half, block)
        if step > 0:
            for e in range(entries):
                along_line(*places[step - 1], e)

    for unit in range(units + 1):
        tasks = [(block, c) for block in range(2) for c in range(members)] if unit < units else []
        if unit > 0:
            value = collect(unit - 1)
        for h in range(2):
            if unit > 0:
                from_plane(unit - 1, value, h)
            for block, c in tasks[h * members : (h + 1) * members]:
                product(unit, block, c)


def middle_inputs(table, mirror_map, x):
    side, plane = x.shape[0] // 2, 2 * x.shape[-1]
    cosine, sine = plane_parts(side)
    parts = [jnp.asarray(part) for part in split_constant(cosine) + split_constant(sine)]
    smem = pl.BlockSpec(memory_space=pltpu.SMEM)
    vmem = pl.BlockSpec(memory_space=pltpu.VMEM)
    args = (table.T, mirror_map, *parts, x.reshape((side, 2) + x.shape[1:]))
    return args, [smem, smem] + [vmem] * 5, pltpu.VMEM((2, 2, 2 * plane, 2 * plane), jnp.bfloat16)


def one_middle(x, table, mirror_map):
    devices, _, entries, rows, lanes = x.shape
    side, components = devices // 2, table.shape[0]
    args, specs, matrices = middle_inputs(table, mirror_map, x)
    spatial = pltpu.VMEM((2, side, 2, entries, rows, lanes), jnp.float32)
    shape = (side, 2, 2, components, rows, lanes)
    out = pl.pallas_call(
        one_middle_kernel,
        in_specs=specs,
        out_specs=pl.BlockSpec(memory_space=pltpu.HBM),
        out_shape=jax.ShapeDtypeStruct(shape, jnp.float32),
        scratch_shapes=[
            matrices,
            matrices,
            pltpu.VMEM((2, 2, side, entries, rows, lanes), jnp.float32),
            spatial,
            spatial,
            pltpu.VMEM((GROUPS, 2, side, components // GROUPS, rows, 2 * lanes), jnp.float32),
            pltpu.VMEM((GROUPS, side, 2, 2, components // GROUPS, rows, lanes), jnp.float32),
            pltpu.SemaphoreType.DMA((GROUPS,)),
        ],
        compiler_params=pltpu.CompilerParams(vmem_limit_bytes=44 << 20),
        cost_estimate=pl.CostEstimate(flops=6_000_000_000, bytes_accessed=12_000_000, transcendentals=0),
        name="one_middle",
    )(*args)
    return out.reshape((devices,) + shape[2:])


def both_middle(x, table, mirror_map, me, near):
    devices, halves, _, entries, rows, lanes = x.shape
    side, components = devices // 2, table.shape[0]
    args, specs, matrices = middle_inputs(table, mirror_map, x)
    members = components // GROUPS
    return pl.pallas_call(
        both_middle_kernel,
        in_specs=[pl.BlockSpec(memory_space=pltpu.SMEM)] + specs,
        out_specs=[pl.BlockSpec(memory_space=pltpu.VMEM)] * near,
        out_shape=[jax.ShapeDtypeStruct((halves, 2, components, rows, lanes), jnp.float32)] * near,
        scratch_shapes=[
            matrices,
            matrices,
            pltpu.VMEM((halves, 2, 2, side, entries, rows, lanes), jnp.float32),
            pltpu.VMEM((halves, 2, side, 2, entries, rows, lanes), jnp.float32),
            pltpu.VMEM((halves * GROUPS, 2, near // 2, members, rows, 2 * lanes), jnp.float32),
        ],
        compiler_params=pltpu.CompilerParams(vmem_limit_bytes=60 << 20),
        name="both_middle",
    )(me, *args)


def prepare_kernel(me_ref, both_ref, one_ref, out_ref):
    near = both_ref.shape[1]
    me = me_ref[0] % near
    ordered = [both_ref[part, slot ^ me] for part in range(2) for slot in range(near)]
    for part, value in enumerate(split_value(jnp.concatenate([one_ref[...]] + ordered, axis=0))):
        out_ref[part] = value


def prepare(me, both, one):
    smem = pl.BlockSpec(memory_space=pltpu.SMEM)
    vmem = pl.BlockSpec(memory_space=pltpu.VMEM)
    depth = both.size // both.shape[3] + one.shape[0]
    return pl.pallas_call(
        prepare_kernel,
        in_specs=[smem, vmem, vmem],
        out_specs=vmem,
        out_shape=jax.ShapeDtypeStruct((2, depth, one.shape[1]), jnp.bfloat16),
        compiler_params=pltpu.CompilerParams(vmem_limit_bytes=32 << 20),
        name="prepare",
    )(me, both, one)


def fold_kernel(order, *refs):
    pieces, (out_ref, held, stage, in_sems, sems) = refs[:-5], refs[-5:]
    near, _, _, components, rows, lanes = held.shape
    loads = [pltpu.make_async_copy(piece, held.at[slot], in_sems.at[slot]) for slot, piece in zip(order, pieces)]
    for copy in loads:
        copy.start()
    for copy in loads:
        copy.wait()
    copies = []
    for c in range(components):
        part = [[held[:, half, ri, c].reshape(near * rows, lanes) for ri in range(2)] for half in range(2)]
        sums = [part[0][ri] + part[1][ri] for ri in range(2)]
        differences = [part[0][ri] - part[1][ri] for ri in range(2)]
        first = jnp.concatenate([sums[0], -differences[1]], axis=0).T
        second = jnp.concatenate([sums[1], differences[0]], axis=0).T
        for place, value in enumerate(split_value(jnp.concatenate([first, second], axis=0))):
            stage[c, place] = value
        copies.append(pltpu.make_async_copy(stage.at[c], out_ref.at[c], sems.at[c]))
        copies[-1].start()
    for copy in copies:
        copy.wait()


def fold(pieces, order):
    _, _, components, rows, lanes = pieces[0].shape
    shape = (components, 2, 2 * lanes, 2 * len(pieces) * rows)
    hbm = pl.BlockSpec(memory_space=pltpu.HBM)
    return pl.pallas_call(
        functools.partial(fold_kernel, order),
        in_specs=[hbm] * len(pieces),
        out_specs=hbm,
        out_shape=jax.ShapeDtypeStruct(shape, jnp.bfloat16),
        scratch_shapes=[
            pltpu.VMEM((len(pieces),) + pieces[0].shape, jnp.float32),
            pltpu.VMEM(shape, jnp.bfloat16),
            pltpu.SemaphoreType.DMA((len(pieces),)),
            pltpu.SemaphoreType.DMA((components,)),
        ],
        compiler_params=pltpu.CompilerParams(vmem_limit_bytes=32 << 20),
        name="fold",
    )(*pieces)


def frequency_kernel(y_ref, m_hbm, f_hbm, out_ref, m_ref, f_ref, stage, m_sem, f_sems, sems):
    devices, _, components, rows, lanes = y_ref.shape
    groups = sems.shape[0]
    members = components // groups
    depth = devices * rows
    load = pltpu.make_async_copy(m_hbm, m_ref, m_sem)
    spans = [pl.ds(group * members, members) for group in range(groups)]
    loads = [pltpu.make_async_copy(f_hbm.at[span], f_ref.at[span], f_sems.at[k]) for k, span in enumerate(spans)]
    for copy in [load] + loads:
        copy.start()
    upper_rows = lax.broadcasted_iota(jnp.int32, (devices, rows, lanes), 1) < rows // 2

    def one_values(group):
        values = []
        for c in range(group * members, (group + 1) * members):
            folded = []
            for ri in range(2):
                tile = y_ref[:, ri, c]
                turned = pltpu.roll(tile, rows // 2, 1)
                folded.append((tile + turned, turned - tile))
            first = jnp.where(upper_rows, folded[0][0], -folded[1][1])
            second = jnp.where(upper_rows, folded[1][0], folded[0][1])
            values.append(first.reshape(depth, lanes).T)
            values.append(second.reshape(depth, lanes).T)
        return split_value(jnp.concatenate(values, axis=0))

    copies = []
    for group, span in enumerate(spans):
        parts = one_values(group)
        if group == 0:
            load.wait()
            matrix = (m_ref[0], m_ref[1])
        loads[group].wait()
        own = range(group * members, (group + 1) * members)
        value = [
            jnp.concatenate([parts[place], jnp.concatenate([f_ref[c, place] for c in own], axis=0)], axis=1)
            for place in range(2)
        ]
        d = dot3(value, matrix, ((1,), (0,))).reshape(members, 2, lanes, stage.shape[3])
        for ri in range(2):
            stage[ri, group * members : (group + 1) * members] = d[:, ri]
        copies.append(pltpu.make_async_copy(stage.at[:, span], out_ref.at[:, span], sems.at[group]))
        copies[-1].start()
    for copy in copies:
        copy.wait()


def to_frequencies(y, matrix, folded):
    _, _, components, _, lanes = y.shape
    shape = (2, components, lanes, matrix.shape[2])
    hbm = pl.BlockSpec(memory_space=pltpu.HBM)
    groups = components // 2
    return pl.pallas_call(
        frequency_kernel,
        in_specs=[pl.BlockSpec(memory_space=pltpu.VMEM), hbm, hbm],
        out_specs=hbm,
        out_shape=jax.ShapeDtypeStruct(shape, jnp.float32),
        scratch_shapes=[
            pltpu.VMEM(matrix.shape, jnp.bfloat16),
            pltpu.VMEM(folded.shape, jnp.bfloat16),
            pltpu.VMEM(shape, jnp.float32),
            pltpu.SemaphoreType.DMA,
            pltpu.SemaphoreType.DMA((groups,)),
            pltpu.SemaphoreType.DMA((groups,)),
        ],
        compiler_params=pltpu.CompilerParams(vmem_limit_bytes=44 << 20),
        name="to_frequencies",
    )(y, matrix, folded)


def exchange(x):
    flat = x.reshape(x.shape[0], -1, x.shape[-1])
    return lax.all_to_all(flat, "kb", split_axis=0, concat_axis=0, tiled=True).reshape(x.shape)


def swap(piece, slot, devices):
    if slot == 0:
        return piece
    return lax.ppermute(piece, "kb", [(device, device ^ slot) for device in range(devices)])


def trig_pair(angle_int, period, scale):
    angle = 2.0 * math.pi / period * angle_int.astype(jnp.float32)
    return (scale * jnp.cos(angle), scale * jnp.sin(angle))


def complex_combine(formula, cosine, sine, real_part, imag_part):
    first_term = jnp.einsum(formula, cosine, real_part + imag_part, precision=lax.Precision.HIGHEST)
    second_term = jnp.einsum(formula, cosine + sine, imag_part, precision=lax.Precision.HIGHEST)
    third_term = jnp.einsum(formula, sine - cosine, real_part, precision=lax.Precision.HIGHEST)
    return (first_term - second_term, first_term + third_term)


def forward_imaginary_time(tau_rows, frequency_count):
    freq_index = jnp.arange(frequency_count, dtype=jnp.int32)
    angle_int = (
        (2 * freq_index[None, :] - frequency_count + 1)
        * (2 * tau_rows[:, None] + 1)
        % (4 * frequency_count)
    )
    cosine, sine = trig_pair(angle_int, 4 * frequency_count, frequency_count ** (-0.5))
    return (cosine, -sine)


def tau_backward(tau_rows, frequency_count):
    freq_index = jnp.arange(frequency_count, dtype=jnp.int32)
    angle_int = (
        (freq_index[:, None] - frequency_count // 2)
        * (2 * tau_rows[None, :] + 1)
        % (2 * frequency_count)
    )
    return trig_pair(angle_int, 2 * frequency_count, frequency_count ** (-0.5))


def grid_transform(real_part, imag_part, grid_side, direction):
    shape = real_part.shape
    plane = jnp.arange(grid_side * grid_side, dtype=jnp.int32)
    upper = plane // grid_side
    lower = plane % grid_side
    plane_int = (upper[:, None] * upper[None, :] + lower[:, None] * lower[None, :]) % grid_side
    plane_cos, plane_sin = trig_pair(plane_int, grid_side, 1.0 / grid_side)
    line = jnp.arange(grid_side, dtype=jnp.int32)
    line_cos, line_sin = trig_pair(
        line[:, None] * line[None, :] % grid_side, grid_side, grid_side ** (-0.5)
    )
    real_part = real_part.reshape(shape[:-1] + (grid_side, grid_side * grid_side))
    imag_part = imag_part.reshape(shape[:-1] + (grid_side, grid_side * grid_side))
    real_part, imag_part = complex_combine(
        "pq,...xq->...xp", plane_cos, direction * plane_sin, real_part, imag_part
    )
    real_part, imag_part = complex_combine(
        "ax,...xp->...ap", line_cos, direction * line_sin, real_part, imag_part
    )
    return (real_part.reshape(shape), imag_part.reshape(shape))


def mirror_index(mirror_map, grid_side):
    index_x = mirror_map[0][:, None, None]
    index_y = mirror_map[1][None, :, None]
    index_z = mirror_map[2][None, None, :]
    return (index_x * grid_side * grid_side + index_y * grid_side + index_z).reshape(-1)


def bubble(gr_re, gr_im, mirror_re, mirror_im, pair_table, entries):
    entry_ids = jnp.arange(entries, dtype=jnp.int32)
    pick_left = (pair_table[:, 0][:, None] == entry_ids[None, :]).astype(jnp.float32)
    pick_right = (pair_table[:, 1][:, None] == entry_ids[None, :]).astype(jnp.float32)
    left_re = jnp.einsum("me,e...->m...", pick_left, gr_re, precision=lax.Precision.HIGHEST)
    left_im = jnp.einsum("me,e...->m...", pick_left, gr_im, precision=lax.Precision.HIGHEST)
    right_re = jnp.einsum("me,e...->m...", pick_right, mirror_re, precision=lax.Precision.HIGHEST)
    right_im = jnp.einsum("me,e...->m...", pick_right, mirror_im, precision=lax.Precision.HIGHEST)
    return (left_re * right_re - left_im * right_im, left_re * right_im + left_im * right_re)


def general(green_momentum_grid, pair_table, mirror_map):
    grid_side = mirror_map.shape[1]
    entries = green_momentum_grid.shape[1]
    frequency_count = green_momentum_grid.shape[3]
    position = jnp.arange(frequency_count, dtype=jnp.int32)
    fwd_cos, fwd_sin = forward_imaginary_time(position, frequency_count)
    tau_re, tau_im = complex_combine(
        "qa,fsa->fqs", fwd_cos, fwd_sin, green_momentum_grid[0], green_momentum_grid[1]
    )
    stacked = jnp.stack([tau_re, tau_im])

    def to_real_space(pieces):
        space_re, space_im = grid_transform(pieces[0], pieces[1], grid_side, 1.0)
        return jnp.stack([space_re, space_im])

    mirror_flat = mirror_index(mirror_map, grid_side)
    partner_rows = frequency_count - 1 - position
    reflected_cosine, reflected_sine = forward_imaginary_time(partner_rows, frequency_count)
    partner_real, partner_imaginary = complex_combine(
        "qa,fsa->fqs",
        reflected_cosine,
        reflected_sine,
        green_momentum_grid[0],
        green_momentum_grid[1],
    )
    other_stacked = jnp.stack([partner_real, partner_imaginary])
    pieces = (
        lax.all_to_all(stacked, "kb", split_axis=2, concat_axis=3, tiled=True),
        lax.all_to_all(other_stacked, "kb", split_axis=2, concat_axis=3, tiled=True),
    )
    in_cells = to_real_space(pieces[0])
    partner = to_real_space(pieces[1])
    mirrored = jnp.take(partner, mirror_flat, axis=3)
    chi_re, chi_im = bubble(in_cells[0], in_cells[1], mirrored[0], mirrored[1], pair_table, entries)
    chi_re, chi_im = grid_transform(chi_re, chi_im, grid_side, -1.0)
    momenta = jnp.stack([chi_re, chi_im])
    back_cos, back_sin = tau_backward(position, frequency_count)
    pieces = lax.all_to_all(momenta, "kb", split_axis=3, concat_axis=2, tiled=True)
    out_re, out_im = complex_combine("vj,ejk->ekv", back_cos, back_sin, pieces[0], pieces[1])
    return jnp.stack([out_re, out_im])


def local(green, pair_table, mirror_map):
    side = mirror_map.shape[1]
    plane = side * side
    lanes, count = green.shape[2], green.shape[3]
    devices = side * plane // lanes
    near = devices // 2
    half = ROWS // 2
    shared = near * ROWS
    if lanes != LANES or 2 * lanes != plane or 2 * (shared + devices * half) != count:
        return general(green, pair_table, mirror_map)
    me = lax.axis_index("kb").astype(jnp.int32).reshape(1)
    entries = green.shape[1]

    rows = np.arange(shared)
    both_fermion = fermion_matrix(rows, count).astype(np.float32)
    both_boson = boson_matrix(rows, count).reshape(2, near, ROWS, count).astype(np.float32)
    rows = shared + np.arange(devices * half).reshape(devices, half)
    times = np.concatenate([rows, count - 1 - rows], axis=1).reshape(-1)
    one_fermion = fermion_matrix(times, count).astype(np.float32)
    one_boson = boson_matrix(rows.reshape(-1), count).reshape(2, devices, half, count).swapaxes(0, 1)
    one_boson = one_boson.reshape(devices * ROWS, count).astype(np.float32)

    shape = (near, 2, 2, entries, ROWS, lanes)
    both = to_times(both_times_kernel, green, jnp.asarray(both_fermion), shape, devices, "both_times")
    green, both = lax.optimization_barrier((green, both))
    shape = (devices, 2, entries, ROWS, lanes)
    one = to_times(one_times_kernel, green, jnp.asarray(one_fermion), shape, devices, "one_times")
    both, one = lax.optimization_barrier((exchange(both), one))
    pieces = both_middle(both, pair_table, mirror_map, me, near)
    first, count = near // 2, near // 4
    early = list(range(first, first + count)) + [1]
    beside = [first + count, first + count + 1, 2, 3]
    late = [slot for slot in range(1, near) if slot not in early + beside]
    moved = {0: pieces[0]}

    one, arrived = lax.optimization_barrier((exchange(one), [swap(pieces[slot], slot, devices) for slot in early]))
    moved |= zip(early, arrived)
    arrived = [swap(pieces[slot], slot, devices) for slot in beside]
    one, arrived, both_boson, one_boson = lax.optimization_barrier(
        (one_middle(one, pair_table, mirror_map), arrived, jnp.asarray(both_boson), jnp.asarray(one_boson))
    )
    moved |= zip(beside, arrived)
    matrix, sent = lax.optimization_barrier((prepare(me, both_boson, one_boson), [pieces[slot] for slot in late]))
    moved |= zip(late, [swap(piece, slot, devices) for slot, piece in zip(late, sent)])
    order = [0] + early + beside + late
    return to_frequencies(exchange(one), matrix, fold([moved[slot] for slot in order], order))


def solution(mesh):
    placed = (P("set", None, "kb", None), P(), P("set", None))
    return jax.shard_map(
        local, mesh=mesh, in_specs=placed, out_specs=P("set", None, "kb", None), check_vma=False
    )
```

```python
import functools
import math

import jax
import jax.numpy as jnp
import ml_dtypes
import numpy as np
from jax import lax
from jax.experimental import pallas as pl
from jax.experimental.pallas import tpu as pltpu
from jax.sharding import PartitionSpec as P

LANES = 128
ROWS = 8
GROUPS = 2


def split_constant(matrix):
    high = matrix.astype(np.float32).astype(ml_dtypes.bfloat16)
    low = (matrix - high.astype(np.float64)).astype(np.float32).astype(ml_dtypes.bfloat16)
    return high, low


def split_value(value):
    high = value.astype(jnp.bfloat16)
    low = (value - high.astype(jnp.float32)).astype(jnp.bfloat16)
    return high, low


def dot3(left, right, dims):
    (k_left,), (k_right,) = dims
    a = jnp.concatenate([left[0], left[0], left[1]], axis=k_left)
    b = jnp.concatenate([right[0], right[1], right[0]], axis=k_right)
    return lax.dot_general(a, b, (dims, ((), ())), preferred_element_type=jnp.float32)


def fermion_matrix(rows, count):
    n = np.arange(count, dtype=np.int64)
    angle = ((2 * n[None, :] - count + 1) * (2 * rows[:, None] + 1)) % (4 * count)
    angle = np.pi * angle / (2 * count)
    return np.concatenate([np.cos(angle), np.sin(angle)], axis=0) * count**-0.5


def boson_matrix(rows, count):
    v = np.arange(count, dtype=np.int64)
    angle = ((v[None, :] - count // 2) * (2 * rows[:, None] + 1)) % (2 * count)
    angle = np.pi * angle / count
    return np.concatenate([np.cos(angle), np.sin(angle)], axis=0) * count**-0.5


def plane_parts(side):
    p = np.arange(side * side, dtype=np.int64)
    angle = ((p[:, None] // side) * (p[None, :] // side) + (p[:, None] % side) * (p[None, :] % side)) % side
    angle = 2 * np.pi * angle / side
    scale = side**-1.5
    return np.cos(angle) * scale, np.sin(angle) * scale


def times_w4(re, im, power, sign):
    power = (power * sign) % 4
    if power == 0:
        return re, im
    if power == 1:
        return -im, re
    if power == 2:
        return -re, -im
    return im, -re


def dft4(values, sign):
    (r0, i0), (r1, i1), (r2, i2), (r3, i3) = values
    sr, si, dr, di = r0 + r2, i0 + i2, r0 - r2, i0 - i2
    tr, ti, er, ei = r1 + r3, i1 + i3, r1 - r3, i1 - i3
    if sign > 0:
        return [(sr + tr, si + ti), (dr - ei, di + er), (sr - tr, si - ti), (dr + ei, di - er)]
    return [(sr + tr, si + ti), (dr + ei, di - er), (sr - tr, si - ti), (dr - ei, di + er)]


def twiddle(value, power, sign, side):
    re, im = value
    if power % (side // 4) == 0:
        return times_w4(re, im, power // (side // 4), sign)
    angle = 2.0 * np.pi * power / side
    c, s = float(np.cos(angle)), float(sign * np.sin(angle))
    return re * c - im * s, re * s + im * c


def dft_line(values, sign):
    side = len(values)
    if side == 1:
        return values
    if side == 2:
        (r0, i0), (r1, i1) = values
        return [(r0 + r1, i0 + i1), (r0 - r1, i0 - i1)]
    if side == 4:
        return dft4(values, sign)
    inner = side // 4
    parts = [dft_line(values[b::4], sign) for b in range(4)]
    out = [None] * side
    for k1 in range(inner):
        column = [twiddle(parts[b][k1], b * k1, sign, side) for b in range(4)]
        for k2, value in enumerate(dft4(column, sign)):
            out[k1 + inner * k2] = value
    return out


def half_line(values, sign, parity):
    side = len(values)
    inner = side // 4
    parts = [dft_line(values[b::4], sign) for b in range(4)]
    out = [None] * (side // 2)
    for k1 in range(inner):
        column = [twiddle(parts[b][k1], b * k1, sign, side) for b in range(4)]
        column = [(re * parity, im * parity) if b % 2 else (re, im) for b, (re, im) in enumerate(column)]
        for k2, value in enumerate(dft4(column, sign)[:2]):
            out[k1 + inner * k2] = value
    return out


def load_inputs(g_hbm, m_hbm, g_ref, m_ref, in_sems, m_sem):
    load = pltpu.make_async_copy(m_hbm, m_ref, m_sem)
    pieces = [
        pltpu.make_async_copy(g_hbm.at[:, pl.ds(e, 1)], g_ref.at[:, pl.ds(e, 1)], in_sems.at[e])
        for e in range(g_ref.shape[1])
    ]
    for copy in [load] + pieces:
        copy.start()
    load.wait()
    return pieces


def sums_of(matrix, g_ref, e):
    lanes = g_ref.shape[2]
    g = jnp.concatenate([g_ref[0, e], g_ref[1, e]], axis=0)
    d = dot3(matrix, split_value(g), ((1,), (1,)))
    half = d.shape[0] // 2
    return d[:half, :lanes], d[:half, lanes:], d[half:, :lanes], d[half:, lanes:]


def both_times_kernel(g_hbm, m_hbm, out_ref, g_ref, m_ref, stage, in_sems, m_sem, out_sems):
    entries, lanes = g_ref.shape[1:3]
    near, _, _, _, rows, _ = stage.shape
    pieces = load_inputs(g_hbm, m_hbm, g_ref, m_ref, in_sems, m_sem)
    matrix = split_value(m_ref[...])
    copies = []
    for e in range(entries):
        pieces[e].wait()
        c_re, c_im, s_re, s_im = sums_of(matrix, g_ref, e)
        for where, value in (
            ((0, 0), c_re + s_im),
            ((0, 1), c_im - s_re),
            ((1, 0), s_im - c_re),
            ((1, 1), -(c_im + s_re)),
        ):
            stage[:, where[0], where[1], e] = value.reshape(near, rows, lanes)
        cut = pl.ds(e, 1)
        for side in range(2):
            target = out_ref.at[pl.ds(side * near, near), :, :, cut]
            copies.append(pltpu.make_async_copy(stage.at[:, :, :, cut], target, out_sems.at[e, side]))
            copies[-1].start()
    for copy in copies:
        copy.wait()


def one_times_kernel(g_hbm, m_hbm, out_ref, g_ref, m_ref, stage, in_sems, m_sem, out_sems):
    entries, lanes = g_ref.shape[1:3]
    devices, _, _, rows, _ = stage.shape
    pieces = load_inputs(g_hbm, m_hbm, g_ref, m_ref, in_sems, m_sem)
    matrix = split_value(m_ref[...])
    copies = []
    for e in range(entries):
        pieces[e].wait()
        c_re, c_im, s_re, s_im = sums_of(matrix, g_ref, e)
        stage[:, 0, e] = (c_re + s_im).reshape(devices, rows, lanes)
        stage[:, 1, e] = (c_im - s_re).reshape(devices, rows, lanes)
        cut = pl.ds(e, 1)
        copies.append(pltpu.make_async_copy(stage.at[:, :, cut], out_ref.at[:, :, cut], out_sems.at[e, 0]))
        copies[-1].start()
    for copy in copies:
        copy.wait()


def to_times(kernel, green, matrix, shape, targets, name):
    entries = green.shape[1]
    hbm = pl.BlockSpec(memory_space=pltpu.HBM)
    return pl.pallas_call(
        kernel,
        in_specs=[hbm, hbm],
        out_specs=hbm,
        out_shape=jax.ShapeDtypeStruct((targets,) + shape[1:], jnp.float32),
        scratch_shapes=[
            pltpu.VMEM(green.shape, jnp.float32),
            pltpu.VMEM(matrix.shape, jnp.float32),
            pltpu.VMEM(shape, jnp.float32),
            pltpu.SemaphoreType.DMA((entries,)),
            pltpu.SemaphoreType.DMA,
            pltpu.SemaphoreType.DMA((entries, 2)),
        ],
        compiler_params=pltpu.CompilerParams(vmem_limit_bytes=63 << 20),
        name=name,
    )(green, matrix)


def fill_block(ref, cosine, sine):
    plane = cosine.shape[0]
    lanes = plane // 2
    for block in range(2):
        cut = slice(block * lanes, (block + 1) * lanes)
        re = slice(2 * block * lanes, (2 * block + 1) * lanes)
        im = slice((2 * block + 1) * lanes, (2 * block + 2) * lanes)
        ref[:plane, re] = cosine[:, cut].astype(jnp.bfloat16)
        ref[plane:, im] = cosine[:, cut].astype(jnp.bfloat16)
        ref[:plane, im] = sine[:, cut].astype(jnp.bfloat16)
        ref[plane:, re] = (-sine[:, cut]).astype(jnp.bfloat16)


def fill_matrices(mirror_ref, parts, forward, backward, turned):
    plane = parts[0].shape[0]
    side = mirror_ref.shape[1]
    row = lax.broadcasted_iota(jnp.int32, (plane, plane), 0)
    column = lax.broadcasted_iota(jnp.int32, (plane, plane), 1)
    upper = (mirror_ref[1, 0] - column // side) & (side - 1)
    lower = (mirror_ref[2, 0] - column % side) & (side - 1)
    pick = (row == upper * side + lower).astype(jnp.float32).astype(jnp.bfloat16)

    def dot(a, b):
        return jnp.dot(a, b, preferred_element_type=jnp.float32)

    for part in range(2):
        c_ref, s_ref = parts[part], parts[2 + part]
        cosine, sine = c_ref[...].astype(jnp.float32), s_ref[...].astype(jnp.float32)
        fill_block(forward.at[0, part], cosine, sine)
        fill_block(backward.at[0, part], turned(cosine), turned(-sine))
        fill_block(forward.at[1, part], dot(c_ref[...], pick), dot(s_ref[...], pick))
        fill_block(backward.at[1, part], turned(dot(pick, c_ref[...])), turned(-dot(pick, s_ref[...])))


def plane_dot(value, matrix, half, block):
    width = matrix.shape[3] // 2
    cut = slice(block * width, (block + 1) * width)
    return dot3(value, (matrix[half, 0, :, cut], matrix[half, 1, :, cut]), ((1,), (0,)))


def one_middle_kernel(table_ref, mirror_ref, ch_ref, cl_ref, sh_ref, sl_ref, x_ref, out_ref, *refs):
    forward, backward, mid, space, other_space, chi, stage, sems = refs
    _, side, _, entries, rows, lanes = space.shape
    plane = 2 * lanes
    groups, _, _, members, _, _ = chi.shape
    fill_matrices(mirror_ref, (ch_ref, cl_ref, sh_ref, sl_ref), forward, backward, lambda value: value)

    def paired(first, second):
        upper = lax.broadcasted_iota(jnp.int32, first.shape, 1) < rows // 2
        turned = [pltpu.roll(part, rows // 2, 1) for part in (first, second)]
        return jnp.where(upper, first, turned[1]), jnp.where(upper, turned[0], second)

    def halves_of(columns):
        value = jnp.concatenate(columns, axis=1)
        count, width = value.shape
        value = value.reshape(count // (2 * rows), 2, rows, width)
        parts = paired(value[:, 0], value[:, 1])
        return [split_value(part.reshape(count // 2, width)) for part in parts]

    def halves_dot(parts, matrix, block):
        shape = (parts[0][0].shape[0] // rows, rows, plane)
        d = paired(*(plane_dot(parts[half], matrix, half, block).reshape(shape) for half in range(2)))
        return jnp.concatenate([part.reshape(shape[0], 1, rows, plane) for part in d], axis=1)

    parts = halves_of([x_ref[:, h, ri].reshape(side * entries * rows, lanes) for ri in range(2) for h in range(2)])
    for block in range(2):
        d = halves_dot(parts, forward, block)
        for ri in range(2):
            piece = d[:, :, :, ri * lanes : (ri + 1) * lanes]
            mid[block, ri] = piece.reshape(side, entries, rows, lanes)
    for block in range(2):
        for e in range(entries):
            values = [(mid[block, 0, x, e], mid[block, 1, x, e]) for x in range(side)]
            for x, parts in enumerate(dft_line(values, 1)):
                for ri in range(2):
                    space[block, x, ri, e] = parts[ri]
                    other_space[block, x, ri, e] = pltpu.roll(parts[ri], rows // 2, 0)

    copies = []
    for group in range(groups):
        for c in range(members):
            left, right = table_ref[0, group * members + c], table_ref[1, group * members + c]
            for block in range(2):
                values = []
                for x in range(side):
                    other = mirror_ref[0, x]
                    a_re, a_im = space[block, x, 0, left], space[block, x, 1, left]
                    b_re, b_im = other_space[block, other, 0, right], other_space[block, other, 1, right]
                    values.append((a_re * b_re - a_im * b_im, a_re * b_im + a_im * b_re))
                cut = slice(block * lanes, (block + 1) * lanes)
                for x, parts in enumerate(dft_line(values, -1)):
                    for ri in range(2):
                        chi[group, ri, x, c, :, cut] = parts[ri]
        whole = (side * members * rows, plane)
        parts = halves_of([chi[group, ri].reshape(whole) for ri in range(2)])
        for h in range(2):
            d = halves_dot(parts, backward, h)
            for ri in range(2):
                piece = d[:, :, :, ri * lanes : (ri + 1) * lanes].reshape(side, members, rows, lanes)
                stage[group, :, h, ri] = piece
        target = out_ref.at[:, :, :, pl.ds(group * members, members)]
        copies.append(pltpu.make_async_copy(stage.at[group], target, sems.at[group]))
        copies[-1].start()
    for copy in copies:
        copy.wait()


def both_middle_kernel(me_ref, table_ref, mirror_ref, ch_ref, cl_ref, sh_ref, sl_ref, x_ref, *refs):
    outs, (forward, backward, mid, space, chi) = refs[:-5], refs[-5:]
    halves, _, side, _, entries, rows, lanes = space.shape
    plane = 2 * lanes
    units, _, kept, members, _, _ = chi.shape
    me, near = me_ref[0], len(outs)
    core, line = me % 2, me // 2 % kept
    parity = (1 - 2 * (me // near)).astype(jnp.float32)

    def turned(value):
        return jnp.where(core == 0, value, jnp.concatenate([value[:, lanes:], value[:, :lanes]], axis=1))

    fill_matrices(mirror_ref, (ch_ref, cl_ref, sh_ref, sl_ref), forward, backward, turned)

    def arrive(half):
        columns = [
            x_ref[:, h, half, ri].reshape(side * entries * rows, lanes) for ri in range(2) for h in range(2)
        ]
        return split_value(jnp.concatenate(columns, axis=1))

    def to_plane(value, half, block):
        d = plane_dot(value, forward, half, block)
        for ri in range(2):
            piece = d[:, ri * lanes : (ri + 1) * lanes]
            mid[half, block, ri] = piece.reshape(side, entries, rows, lanes)

    def along_line(half, block, e):
        values = [(mid[half, block, 0, x, e], mid[half, block, 1, x, e]) for x in range(side)]
        for x, (re, im) in enumerate(dft_line(values, 1)):
            space[half, block, x, 0, e] = re
            space[half, block, x, 1, e] = im

    def product(unit, block, c):
        half, first = unit % halves, unit // halves * members
        left, right = table_ref[0, first + c], table_ref[1, first + c]
        values = []
        for x in range(side):
            other = mirror_ref[0, x]
            a_re, a_im = space[half, block, x, 0, left], space[half, block, x, 1, left]
            b_re, b_im = space[1 - half, block, other, 0, right], space[1 - half, block, other, 1, right]
            values.append((a_re * b_re - a_im * b_im, a_re * b_im + a_im * b_re))
        cut = slice(block * lanes, (block + 1) * lanes)
        for x, (re, im) in enumerate(half_line(values, -1, parity)):
            chi[unit, 0, x ^ line, c, :, cut] = re
            chi[unit, 1, x ^ line, c, :, cut] = im

    def from_plane(unit, value, h):
        half, first = unit % halves, unit // halves * members
        d = plane_dot(value, backward, half, h)
        for ri in range(2):
            piece = d[:, ri * lanes : (ri + 1) * lanes].reshape(kept, members, rows, lanes)
            for x in range(kept):
                outs[2 * x + h][half, ri, first : first + members] = piece[x]

    def collect(unit):
        whole = (kept * members * rows, plane)
        return split_value(jnp.concatenate([chi[unit, ri].reshape(whole) for ri in range(2)], axis=1))

    places = [(half, block) for half in range(halves) for block in range(2)]
    for step in range(len(places) + 1):
        if step < len(places):
            half, block = places[step]
            if block == 0:
                value = arrive(half)
            to_plane(value, half, block)
        if step > 0:
            for e in range(entries):
                along_line(*places[step - 1], e)

    for unit in range(units + 1):
        tasks = [(block, c) for block in range(2) for c in range(members)] if unit < units else []
        if unit > 0:
            value = collect(unit - 1)
        for h in range(2):
            if unit > 0:
                from_plane(unit - 1, value, h)
            for block, c in tasks[h * members : (h + 1) * members]:
                product(unit, block, c)


def middle_inputs(table, mirror_map, x):
    side, plane = x.shape[0] // 2, 2 * x.shape[-1]
    cosine, sine = plane_parts(side)
    parts = [jnp.asarray(part) for part in split_constant(cosine) + split_constant(sine)]
    smem = pl.BlockSpec(memory_space=pltpu.SMEM)
    vmem = pl.BlockSpec(memory_space=pltpu.VMEM)
    args = (table.T, mirror_map, *parts, x.reshape((side, 2) + x.shape[1:]))
    return args, [smem, smem] + [vmem] * 5, pltpu.VMEM((2, 2, 2 * plane, 2 * plane), jnp.bfloat16)


def one_middle(x, table, mirror_map):
    devices, _, entries, rows, lanes = x.shape
    side, components = devices // 2, table.shape[0]
    args, specs, matrices = middle_inputs(table, mirror_map, x)
    spatial = pltpu.VMEM((2, side, 2, entries, rows, lanes), jnp.float32)
    shape = (side, 2, 2, components, rows, lanes)
    out = pl.pallas_call(
        one_middle_kernel,
        in_specs=specs,
        out_specs=pl.BlockSpec(memory_space=pltpu.HBM),
        out_shape=jax.ShapeDtypeStruct(shape, jnp.float32),
        scratch_shapes=[
            matrices,
            matrices,
            pltpu.VMEM((2, 2, side, entries, rows, lanes), jnp.float32),
            spatial,
            spatial,
            pltpu.VMEM((GROUPS, 2, side, components // GROUPS, rows, 2 * lanes), jnp.float32),
            pltpu.VMEM((GROUPS, side, 2, 2, components // GROUPS, rows, lanes), jnp.float32),
            pltpu.SemaphoreType.DMA((GROUPS,)),
        ],
        compiler_params=pltpu.CompilerParams(vmem_limit_bytes=60416 << 10),
        cost_estimate=pl.CostEstimate(flops=6_000_000_000, bytes_accessed=12_000_000, transcendentals=0),
        name="one_middle",
    )(*args)
    return out.reshape((devices,) + shape[2:])


def both_middle(x, table, mirror_map, me, near):
    devices, halves, _, entries, rows, lanes = x.shape
    side, components = devices // 2, table.shape[0]
    args, specs, matrices = middle_inputs(table, mirror_map, x)
    members = components // GROUPS
    return pl.pallas_call(
        both_middle_kernel,
        in_specs=[pl.BlockSpec(memory_space=pltpu.SMEM)] + specs,
        out_specs=[pl.BlockSpec(memory_space=pltpu.VMEM)] * near,
        out_shape=[jax.ShapeDtypeStruct((halves, 2, components, rows, lanes), jnp.float32)] * near,
        scratch_shapes=[
            matrices,
            matrices,
            pltpu.VMEM((halves, 2, 2, side, entries, rows, lanes), jnp.float32),
            pltpu.VMEM((halves, 2, side, 2, entries, rows, lanes), jnp.float32),
            pltpu.VMEM((halves * GROUPS, 2, near // 2, members, rows, 2 * lanes), jnp.float32),
        ],
        compiler_params=pltpu.CompilerParams(vmem_limit_bytes=60 << 20),
        name="both_middle",
    )(me, *args)


def prepare_kernel(me_ref, both_ref, one_ref, out_ref):
    near = both_ref.shape[1]
    me = me_ref[0] % near
    ordered = [both_ref[part, slot ^ me] for part in range(2) for slot in range(near)]
    for part, value in enumerate(split_value(jnp.concatenate([one_ref[...]] + ordered, axis=0))):
        out_ref[part] = value


def prepare(me, both, one):
    smem = pl.BlockSpec(memory_space=pltpu.SMEM)
    vmem = pl.BlockSpec(memory_space=pltpu.VMEM)
    depth = both.size // both.shape[3] + one.shape[0]
    return pl.pallas_call(
        prepare_kernel,
        in_specs=[smem, vmem, vmem],
        out_specs=vmem,
        out_shape=jax.ShapeDtypeStruct((2, depth, one.shape[1]), jnp.bfloat16),
        compiler_params=pltpu.CompilerParams(vmem_limit_bytes=60620 << 10),
        name="prepare",
    )(me, both, one)


def fold_kernel(order, *refs):
    pieces, (out_ref, held, stage, in_sems, sems) = refs[:-5], refs[-5:]
    near, _, _, components, rows, lanes = held.shape
    loads = [pltpu.make_async_copy(piece, held.at[slot], in_sems.at[slot]) for slot, piece in zip(order, pieces)]
    for copy in loads:
        copy.start()
    for copy in loads:
        copy.wait()
    copies = []
    for c in range(components):
        part = [[held[:, half, ri, c].reshape(near * rows, lanes) for ri in range(2)] for half in range(2)]
        sums = [part[0][ri] + part[1][ri] for ri in range(2)]
        differences = [part[0][ri] - part[1][ri] for ri in range(2)]
        first = jnp.concatenate([sums[0], -differences[1]], axis=0).T
        second = jnp.concatenate([sums[1], differences[0]], axis=0).T
        for place, value in enumerate(split_value(jnp.concatenate([first, second], axis=0))):
            stage[c, place] = value
        copies.append(pltpu.make_async_copy(stage.at[c], out_ref.at[c], sems.at[c]))
        copies[-1].start()
    for copy in copies:
        copy.wait()


def fold(pieces, order):
    _, _, components, rows, lanes = pieces[0].shape
    shape = (components, 2, 2 * lanes, 2 * len(pieces) * rows)
    hbm = pl.BlockSpec(memory_space=pltpu.HBM)
    return pl.pallas_call(
        functools.partial(fold_kernel, order),
        in_specs=[hbm] * len(pieces),
        out_specs=hbm,
        out_shape=jax.ShapeDtypeStruct(shape, jnp.bfloat16),
        scratch_shapes=[
            pltpu.VMEM((len(pieces),) + pieces[0].shape, jnp.float32),
            pltpu.VMEM(shape, jnp.bfloat16),
            pltpu.SemaphoreType.DMA((len(pieces),)),
            pltpu.SemaphoreType.DMA((components,)),
        ],
        compiler_params=pltpu.CompilerParams(vmem_limit_bytes=59699 << 10),
        name="fold",
    )(*pieces)


def frequency_kernel(y_ref, m_hbm, f_hbm, out_ref, m_ref, f_ref, stage, m_sem, f_sems, sems):
    devices, _, components, rows, lanes = y_ref.shape
    groups = sems.shape[0]
    members = components // groups
    depth = devices * rows
    load = pltpu.make_async_copy(m_hbm, m_ref, m_sem)
    spans = [pl.ds(group * members, members) for group in range(groups)]
    loads = [pltpu.make_async_copy(f_hbm.at[span], f_ref.at[span], f_sems.at[k]) for k, span in enumerate(spans)]
    for copy in [load] + loads:
        copy.start()
    upper_rows = lax.broadcasted_iota(jnp.int32, (devices, rows, lanes), 1) < rows // 2

    def one_values(group):
        values = []
        for c in range(group * members, (group + 1) * members):
            folded = []
            for ri in range(2):
                tile = y_ref[:, ri, c]
                turned = pltpu.roll(tile, rows // 2, 1)
                folded.append((tile + turned, turned - tile))
            first = jnp.where(upper_rows, folded[0][0], -folded[1][1])
            second = jnp.where(upper_rows, folded[1][0], folded[0][1])
            values.append(first.reshape(depth, lanes).T)
            values.append(second.reshape(depth, lanes).T)
        return split_value(jnp.concatenate(values, axis=0))

    copies = []
    for group, span in enumerate(spans):
        parts = one_values(group)
        if group == 0:
            load.wait()
            matrix = (m_ref[0], m_ref[1])
        loads[group].wait()
        own = range(group * members, (group + 1) * members)
        value = [
            jnp.concatenate([parts[place], jnp.concatenate([f_ref[c, place] for c in own], axis=0)], axis=1)
            for place in range(2)
        ]
        d = dot3(value, matrix, ((1,), (0,))).reshape(members, 2, lanes, stage.shape[3])
        for ri in range(2):
            stage[ri, group * members : (group + 1) * members] = d[:, ri]
        copies.append(pltpu.make_async_copy(stage.at[:, span], out_ref.at[:, span], sems.at[group]))
        copies[-1].start()
    for copy in copies:
        copy.wait()


def to_frequencies(y, matrix, folded):
    _, _, components, _, lanes = y.shape
    shape = (2, components, lanes, matrix.shape[2])
    hbm = pl.BlockSpec(memory_space=pltpu.HBM)
    groups = components // 2
    return pl.pallas_call(
        frequency_kernel,
        in_specs=[pl.BlockSpec(memory_space=pltpu.VMEM), hbm, hbm],
        out_specs=hbm,
        out_shape=jax.ShapeDtypeStruct(shape, jnp.float32),
        scratch_shapes=[
            pltpu.VMEM(matrix.shape, jnp.bfloat16),
            pltpu.VMEM(folded.shape, jnp.bfloat16),
            pltpu.VMEM(shape, jnp.float32),
            pltpu.SemaphoreType.DMA,
            pltpu.SemaphoreType.DMA((groups,)),
            pltpu.SemaphoreType.DMA((groups,)),
        ],
        compiler_params=pltpu.CompilerParams(vmem_limit_bytes=59904 << 10),
        name="to_frequencies",
    )(y, matrix, folded)


def exchange(x):
    flat = x.reshape(x.shape[0], -1, x.shape[-1])
    return lax.all_to_all(flat, "kb", split_axis=0, concat_axis=0, tiled=True).reshape(x.shape)


def swap(piece, slot, devices):
    if slot == 0:
        return piece
    return lax.ppermute(piece, "kb", [(device, device ^ slot) for device in range(devices)])


def trig_pair(angle_int, period, scale):
    angle = 2.0 * math.pi / period * angle_int.astype(jnp.float32)
    return (scale * jnp.cos(angle), scale * jnp.sin(angle))


def complex_combine(formula, cosine, sine, real_part, imag_part):
    first_term = jnp.einsum(formula, cosine, real_part + imag_part, precision=lax.Precision.HIGHEST)
    second_term = jnp.einsum(formula, cosine + sine, imag_part, precision=lax.Precision.HIGHEST)
    third_term = jnp.einsum(formula, sine - cosine, real_part, precision=lax.Precision.HIGHEST)
    return (first_term - second_term, first_term + third_term)


def forward_imaginary_time(tau_rows, frequency_count):
    freq_index = jnp.arange(frequency_count, dtype=jnp.int32)
    angle_int = (
        (2 * freq_index[None, :] - frequency_count + 1)
        * (2 * tau_rows[:, None] + 1)
        % (4 * frequency_count)
    )
    cosine, sine = trig_pair(angle_int, 4 * frequency_count, frequency_count ** (-0.5))
    return (cosine, -sine)


def tau_backward(tau_rows, frequency_count):
    freq_index = jnp.arange(frequency_count, dtype=jnp.int32)
    angle_int = (
        (freq_index[:, None] - frequency_count // 2)
        * (2 * tau_rows[None, :] + 1)
        % (2 * frequency_count)
    )
    return trig_pair(angle_int, 2 * frequency_count, frequency_count ** (-0.5))


def grid_transform(real_part, imag_part, grid_side, direction):
    shape = real_part.shape
    plane = jnp.arange(grid_side * grid_side, dtype=jnp.int32)
    upper = plane // grid_side
    lower = plane % grid_side
    plane_int = (upper[:, None] * upper[None, :] + lower[:, None] * lower[None, :]) % grid_side
    plane_cos, plane_sin = trig_pair(plane_int, grid_side, 1.0 / grid_side)
    line = jnp.arange(grid_side, dtype=jnp.int32)
    line_cos, line_sin = trig_pair(
        line[:, None] * line[None, :] % grid_side, grid_side, grid_side ** (-0.5)
    )
    real_part = real_part.reshape(shape[:-1] + (grid_side, grid_side * grid_side))
    imag_part = imag_part.reshape(shape[:-1] + (grid_side, grid_side * grid_side))
    real_part, imag_part = complex_combine(
        "pq,...xq->...xp", plane_cos, direction * plane_sin, real_part, imag_part
    )
    real_part, imag_part = complex_combine(
        "ax,...xp->...ap", line_cos, direction * line_sin, real_part, imag_part
    )
    return (real_part.reshape(shape), imag_part.reshape(shape))


def mirror_index(mirror_map, grid_side):
    index_x = mirror_map[0][:, None, None]
    index_y = mirror_map[1][None, :, None]
    index_z = mirror_map[2][None, None, :]
    return (index_x * grid_side * grid_side + index_y * grid_side + index_z).reshape(-1)


def bubble(gr_re, gr_im, mirror_re, mirror_im, pair_table, entries):
    entry_ids = jnp.arange(entries, dtype=jnp.int32)
    pick_left = (pair_table[:, 0][:, None] == entry_ids[None, :]).astype(jnp.float32)
    pick_right = (pair_table[:, 1][:, None] == entry_ids[None, :]).astype(jnp.float32)
    left_re = jnp.einsum("me,e...->m...", pick_left, gr_re, precision=lax.Precision.HIGHEST)
    left_im = jnp.einsum("me,e...->m...", pick_left, gr_im, precision=lax.Precision.HIGHEST)
    right_re = jnp.einsum("me,e...->m...", pick_right, mirror_re, precision=lax.Precision.HIGHEST)
    right_im = jnp.einsum("me,e...->m...", pick_right, mirror_im, precision=lax.Precision.HIGHEST)
    return (left_re * right_re - left_im * right_im, left_re * right_im + left_im * right_re)


def general(green_momentum_grid, pair_table, mirror_map):
    grid_side = mirror_map.shape[1]
    entries = green_momentum_grid.shape[1]
    frequency_count = green_momentum_grid.shape[3]
    position = jnp.arange(frequency_count, dtype=jnp.int32)
    fwd_cos, fwd_sin = forward_imaginary_time(position, frequency_count)
    tau_re, tau_im = complex_combine(
        "qa,fsa->fqs", fwd_cos, fwd_sin, green_momentum_grid[0], green_momentum_grid[1]
    )
    stacked = jnp.stack([tau_re, tau_im])

    def to_real_space(pieces):
        space_re, space_im = grid_transform(pieces[0], pieces[1], grid_side, 1.0)
        return jnp.stack([space_re, space_im])

    mirror_flat = mirror_index(mirror_map, grid_side)
    partner_rows = frequency_count - 1 - position
    reflected_cosine, reflected_sine = forward_imaginary_time(partner_rows, frequency_count)
    partner_real, partner_imaginary = complex_combine(
        "qa,fsa->fqs",
        reflected_cosine,
        reflected_sine,
        green_momentum_grid[0],
        green_momentum_grid[1],
    )
    other_stacked = jnp.stack([partner_real, partner_imaginary])
    pieces = (
        lax.all_to_all(stacked, "kb", split_axis=2, concat_axis=3, tiled=True),
        lax.all_to_all(other_stacked, "kb", split_axis=2, concat_axis=3, tiled=True),
    )
    in_cells = to_real_space(pieces[0])
    partner = to_real_space(pieces[1])
    mirrored = jnp.take(partner, mirror_flat, axis=3)
    chi_re, chi_im = bubble(in_cells[0], in_cells[1], mirrored[0], mirrored[1], pair_table, entries)
    chi_re, chi_im = grid_transform(chi_re, chi_im, grid_side, -1.0)
    momenta = jnp.stack([chi_re, chi_im])
    back_cos, back_sin = tau_backward(position, frequency_count)
    pieces = lax.all_to_all(momenta, "kb", split_axis=3, concat_axis=2, tiled=True)
    out_re, out_im = complex_combine("vj,ejk->ekv", back_cos, back_sin, pieces[0], pieces[1])
    return jnp.stack([out_re, out_im])


def local(green, pair_table, mirror_map):
    side = mirror_map.shape[1]
    plane = side * side
    lanes, count = green.shape[2], green.shape[3]
    devices = side * plane // lanes
    near = devices // 2
    half = ROWS // 2
    shared = near * ROWS
    if lanes != LANES or 2 * lanes != plane or 2 * (shared + devices * half) != count:
        return general(green, pair_table, mirror_map)
    me = lax.axis_index("kb").astype(jnp.int32).reshape(1)
    entries = green.shape[1]

    rows = np.arange(shared)
    both_fermion = fermion_matrix(rows, count).astype(np.float32)
    both_boson = boson_matrix(rows, count).reshape(2, near, ROWS, count).astype(np.float32)
    rows = shared + np.arange(devices * half).reshape(devices, half)
    times = np.concatenate([rows, count - 1 - rows], axis=1).reshape(-1)
    one_fermion = fermion_matrix(times, count).astype(np.float32)
    one_boson = boson_matrix(rows.reshape(-1), count).reshape(2, devices, half, count).swapaxes(0, 1)
    one_boson = one_boson.reshape(devices * ROWS, count).astype(np.float32)

    shape = (near, 2, 2, entries, ROWS, lanes)
    both = to_times(both_times_kernel, green, jnp.asarray(both_fermion), shape, devices, "both_times")
    green, both = lax.optimization_barrier((green, both))
    shape = (devices, 2, entries, ROWS, lanes)
    one = to_times(one_times_kernel, green, jnp.asarray(one_fermion), shape, devices, "one_times")
    both, one = lax.optimization_barrier((exchange(both), one))
    pieces = both_middle(both, pair_table, mirror_map, me, near)
    first, count = near // 2, near // 4
    early = list(range(first, first + count)) + [1]
    beside = [first + count, first + count + 1, 2, 3]
    late = [slot for slot in range(1, near) if slot not in early + beside]
    moved = {0: pieces[0]}

    one, arrived = lax.optimization_barrier((exchange(one), [swap(pieces[slot], slot, devices) for slot in early]))
    moved |= zip(early, arrived)
    arrived = [swap(pieces[slot], slot, devices) for slot in beside]
    one, arrived, both_boson, one_boson = lax.optimization_barrier(
        (one_middle(one, pair_table, mirror_map), arrived, jnp.asarray(both_boson), jnp.asarray(one_boson))
    )
    moved |= zip(beside, arrived)
    matrix, sent = lax.optimization_barrier((prepare(me, both_boson, one_boson), [pieces[slot] for slot in late]))
    moved |= zip(late, [swap(piece, slot, devices) for slot, piece in zip(late, sent)])
    order = [0] + early + beside + late
    return to_frequencies(exchange(one), matrix, fold([moved[slot] for slot in order], order))


def solution(mesh):
    placed = (P("set", None, "kb", None), P(), P("set", None))
    return jax.shard_map(
        local, mesh=mesh, in_specs=placed, out_specs=P("set", None, "kb", None), check_vma=False
    )
```

```python
import functools
import math

import jax
import jax.numpy as jnp
import ml_dtypes
import numpy as np
from jax import lax
from jax.experimental import pallas as pl
from jax.experimental.pallas import tpu as pltpu
from jax.sharding import PartitionSpec as P

LANES = 128
ROWS = 8
GROUPS = 2


def split_constant(matrix):
    high = matrix.astype(np.float32).astype(ml_dtypes.bfloat16)
    low = (matrix - high.astype(np.float64)).astype(np.float32).astype(ml_dtypes.bfloat16)
    return high, low


def split_value(value):
    high = value.astype(jnp.bfloat16)
    low = (value - high.astype(jnp.float32)).astype(jnp.bfloat16)
    return high, low


def dot3(left, right, dims):
    (k_left,), (k_right,) = dims
    a = jnp.concatenate([left[0], left[0], left[1]], axis=k_left)
    b = jnp.concatenate([right[0], right[1], right[0]], axis=k_right)
    return lax.dot_general(a, b, (dims, ((), ())), preferred_element_type=jnp.float32)


def fermion_matrix(rows, count):
    n = np.arange(count, dtype=np.int64)
    angle = ((2 * n[None, :] - count + 1) * (2 * rows[:, None] + 1)) % (4 * count)
    angle = np.pi * angle / (2 * count)
    return np.concatenate([np.cos(angle), np.sin(angle)], axis=0) * count**-0.5


def boson_matrix(rows, count):
    v = np.arange(count, dtype=np.int64)
    angle = ((v[None, :] - count // 2) * (2 * rows[:, None] + 1)) % (2 * count)
    angle = np.pi * angle / count
    return np.concatenate([np.cos(angle), np.sin(angle)], axis=0) * count**-0.5


def plane_parts(side):
    p = np.arange(side * side, dtype=np.int64)
    angle = ((p[:, None] // side) * (p[None, :] // side) + (p[:, None] % side) * (p[None, :] % side)) % side
    angle = 2 * np.pi * angle / side
    scale = side**-1.5
    return np.cos(angle) * scale, np.sin(angle) * scale


def times_w4(re, im, power, sign):
    power = (power * sign) % 4
    if power == 0:
        return re, im
    if power == 1:
        return -im, re
    if power == 2:
        return -re, -im
    return im, -re


def dft4(values, sign):
    (r0, i0), (r1, i1), (r2, i2), (r3, i3) = values
    sr, si, dr, di = r0 + r2, i0 + i2, r0 - r2, i0 - i2
    tr, ti, er, ei = r1 + r3, i1 + i3, r1 - r3, i1 - i3
    if sign > 0:
        return [(sr + tr, si + ti), (dr - ei, di + er), (sr - tr, si - ti), (dr + ei, di - er)]
    return [(sr + tr, si + ti), (dr + ei, di - er), (sr - tr, si - ti), (dr - ei, di + er)]


def twiddle(value, power, sign, side):
    re, im = value
    if power % (side // 4) == 0:
        return times_w4(re, im, power // (side // 4), sign)
    angle = 2.0 * np.pi * power / side
    c, s = float(np.cos(angle)), float(sign * np.sin(angle))
    return re * c - im * s, re * s + im * c


def dft_line(values, sign):
    side = len(values)
    if side == 1:
        return values
    if side == 2:
        (r0, i0), (r1, i1) = values
        return [(r0 + r1, i0 + i1), (r0 - r1, i0 - i1)]
    if side == 4:
        return dft4(values, sign)
    inner = side // 4
    parts = [dft_line(values[b::4], sign) for b in range(4)]
    out = [None] * side
    for k1 in range(inner):
        column = [twiddle(parts[b][k1], b * k1, sign, side) for b in range(4)]
        for k2, value in enumerate(dft4(column, sign)):
            out[k1 + inner * k2] = value
    return out


def half_line(values, sign, parity):
    side = len(values)
    inner = side // 4
    parts = [dft_line(values[b::4], sign) for b in range(4)]
    out = [None] * (side // 2)
    for k1 in range(inner):
        column = [twiddle(parts[b][k1], b * k1, sign, side) for b in range(4)]
        column = [(re * parity, im * parity) if b % 2 else (re, im) for b, (re, im) in enumerate(column)]
        for k2, value in enumerate(dft4(column, sign)[:2]):
            out[k1 + inner * k2] = value
    return out


def load_inputs(g_hbm, m_hbm, g_ref, m_ref, in_sems, m_sem):
    load = pltpu.make_async_copy(m_hbm, m_ref, m_sem)
    pieces = [
        pltpu.make_async_copy(g_hbm.at[:, pl.ds(e, 1)], g_ref.at[:, pl.ds(e, 1)], in_sems.at[e])
        for e in range(g_ref.shape[1])
    ]
    for copy in [load] + pieces:
        copy.start()
    load.wait()
    return pieces


def sums_of(matrix, g_ref, e):
    lanes = g_ref.shape[2]
    g = jnp.concatenate([g_ref[0, e], g_ref[1, e]], axis=0)
    d = dot3(matrix, split_value(g), ((1,), (1,)))
    half = d.shape[0] // 2
    return d[:half, :lanes], d[:half, lanes:], d[half:, :lanes], d[half:, lanes:]


def both_times_kernel(g_hbm, m_hbm, out_ref, g_ref, m_ref, stage, in_sems, m_sem, out_sems):
    entries, lanes = g_ref.shape[1:3]
    near, _, _, _, rows, _ = stage.shape
    pieces = load_inputs(g_hbm, m_hbm, g_ref, m_ref, in_sems, m_sem)
    matrix = split_value(m_ref[...])
    copies = []
    for e in range(entries):
        pieces[e].wait()
        c_re, c_im, s_re, s_im = sums_of(matrix, g_ref, e)
        for where, value in (
            ((0, 0), c_re + s_im),
            ((0, 1), c_im - s_re),
            ((1, 0), s_im - c_re),
            ((1, 1), -(c_im + s_re)),
        ):
            stage[:, where[0], where[1], e] = value.reshape(near, rows, lanes)
        cut = pl.ds(e, 1)
        for side in range(2):
            target = out_ref.at[pl.ds(side * near, near), :, :, cut]
            copies.append(pltpu.make_async_copy(stage.at[:, :, :, cut], target, out_sems.at[e, side]))
            copies[-1].start()
    for copy in copies:
        copy.wait()


def one_times_kernel(g_hbm, m_hbm, out_ref, g_ref, m_ref, stage, in_sems, m_sem, out_sems):
    entries, lanes = g_ref.shape[1:3]
    devices, _, _, rows, _ = stage.shape
    pieces = load_inputs(g_hbm, m_hbm, g_ref, m_ref, in_sems, m_sem)
    matrix = split_value(m_ref[...])
    copies = []
    for e in range(entries):
        pieces[e].wait()
        c_re, c_im, s_re, s_im = sums_of(matrix, g_ref, e)
        stage[:, 0, e] = (c_re + s_im).reshape(devices, rows, lanes)
        stage[:, 1, e] = (c_im - s_re).reshape(devices, rows, lanes)
        cut = pl.ds(e, 1)
        copies.append(pltpu.make_async_copy(stage.at[:, :, cut], out_ref.at[:, :, cut], out_sems.at[e, 0]))
        copies[-1].start()
    for copy in copies:
        copy.wait()


def to_times(kernel, green, matrix, shape, targets, name):
    entries = green.shape[1]
    hbm = pl.BlockSpec(memory_space=pltpu.HBM)
    return pl.pallas_call(
        kernel,
        in_specs=[hbm, hbm],
        out_specs=hbm,
        out_shape=jax.ShapeDtypeStruct((targets,) + shape[1:], jnp.float32),
        scratch_shapes=[
            pltpu.VMEM(green.shape, jnp.float32),
            pltpu.VMEM(matrix.shape, jnp.float32),
            pltpu.VMEM(shape, jnp.float32),
            pltpu.SemaphoreType.DMA((entries,)),
            pltpu.SemaphoreType.DMA,
            pltpu.SemaphoreType.DMA((entries, 2)),
        ],
        compiler_params=pltpu.CompilerParams(vmem_limit_bytes=63 << 20),
        name=name,
    )(green, matrix)


def fill_block(ref, cosine, sine):
    plane = cosine.shape[0]
    lanes = plane // 2
    for block in range(2):
        cut = slice(block * lanes, (block + 1) * lanes)
        re = slice(2 * block * lanes, (2 * block + 1) * lanes)
        im = slice((2 * block + 1) * lanes, (2 * block + 2) * lanes)
        ref[:plane, re] = cosine[:, cut].astype(jnp.bfloat16)
        ref[plane:, im] = cosine[:, cut].astype(jnp.bfloat16)
        ref[:plane, im] = sine[:, cut].astype(jnp.bfloat16)
        ref[plane:, re] = (-sine[:, cut]).astype(jnp.bfloat16)


def fill_matrices(mirror_ref, parts, forward, backward, turned):
    plane = parts[0].shape[0]
    side = mirror_ref.shape[1]
    row = lax.broadcasted_iota(jnp.int32, (plane, plane), 0)
    column = lax.broadcasted_iota(jnp.int32, (plane, plane), 1)
    upper = (mirror_ref[1, 0] - column // side) & (side - 1)
    lower = (mirror_ref[2, 0] - column % side) & (side - 1)
    pick = (row == upper * side + lower).astype(jnp.float32).astype(jnp.bfloat16)

    def dot(a, b):
        return jnp.dot(a, b, preferred_element_type=jnp.float32)

    for part in range(2):
        c_ref, s_ref = parts[part], parts[2 + part]
        cosine, sine = c_ref[...].astype(jnp.float32), s_ref[...].astype(jnp.float32)
        fill_block(forward.at[0, part], cosine, sine)
        fill_block(backward.at[0, part], turned(cosine), turned(-sine))
        fill_block(forward.at[1, part], dot(c_ref[...], pick), dot(s_ref[...], pick))
        fill_block(backward.at[1, part], turned(dot(pick, c_ref[...])), turned(-dot(pick, s_ref[...])))


def plane_dot(value, matrix, half, block):
    width = matrix.shape[3] // 2
    cut = slice(block * width, (block + 1) * width)
    return dot3(value, (matrix[half, 0, :, cut], matrix[half, 1, :, cut]), ((1,), (0,)))


def one_middle_kernel(table_ref, mirror_ref, ch_ref, cl_ref, sh_ref, sl_ref, x_ref, out_ref, *refs):
    forward, backward, mid, space, other_space, chi, stage, sems = refs
    _, side, _, entries, rows, lanes = space.shape
    plane = 2 * lanes
    groups, _, _, members, _, _ = chi.shape
    fill_matrices(mirror_ref, (ch_ref, cl_ref, sh_ref, sl_ref), forward, backward, lambda value: value)

    def paired(first, second):
        upper = lax.broadcasted_iota(jnp.int32, first.shape, 1) < rows // 2
        turned = [pltpu.roll(part, rows // 2, 1) for part in (first, second)]
        return jnp.where(upper, first, turned[1]), jnp.where(upper, turned[0], second)

    def halves_of(columns):
        value = jnp.concatenate(columns, axis=1)
        count, width = value.shape
        value = value.reshape(count // (2 * rows), 2, rows, width)
        parts = paired(value[:, 0], value[:, 1])
        return [split_value(part.reshape(count // 2, width)) for part in parts]

    def halves_dot(parts, matrix, block):
        shape = (parts[0][0].shape[0] // rows, rows, plane)
        d = paired(*(plane_dot(parts[half], matrix, half, block).reshape(shape) for half in range(2)))
        return jnp.concatenate([part.reshape(shape[0], 1, rows, plane) for part in d], axis=1)

    parts = halves_of([x_ref[:, h, ri].reshape(side * entries * rows, lanes) for ri in range(2) for h in range(2)])
    for block in range(2):
        d = halves_dot(parts, forward, block)
        for ri in range(2):
            piece = d[:, :, :, ri * lanes : (ri + 1) * lanes]
            mid[block, ri] = piece.reshape(side, entries, rows, lanes)
    for block in range(2):
        for e in range(entries):
            values = [(mid[block, 0, x, e], mid[block, 1, x, e]) for x in range(side)]
            for x, parts in enumerate(dft_line(values, 1)):
                for ri in range(2):
                    space[block, x, ri, e] = parts[ri]
                    other_space[block, x, ri, e] = pltpu.roll(parts[ri], rows // 2, 0)

    copies = []
    for group in range(groups):
        for c in range(members):
            left, right = table_ref[0, group * members + c], table_ref[1, group * members + c]
            for block in range(2):
                values = []
                for x in range(side):
                    other = mirror_ref[0, x]
                    a_re, a_im = space[block, x, 0, left], space[block, x, 1, left]
                    b_re, b_im = other_space[block, other, 0, right], other_space[block, other, 1, right]
                    values.append((a_re * b_re - a_im * b_im, a_re * b_im + a_im * b_re))
                cut = slice(block * lanes, (block + 1) * lanes)
                for x, parts in enumerate(dft_line(values, -1)):
                    for ri in range(2):
                        chi[group, ri, x, c, :, cut] = parts[ri]
        whole = (side * members * rows, plane)
        parts = halves_of([chi[group, ri].reshape(whole) for ri in range(2)])
        for h in range(2):
            d = halves_dot(parts, backward, h)
            for ri in range(2):
                piece = d[:, :, :, ri * lanes : (ri + 1) * lanes].reshape(side, members, rows, lanes)
                stage[group, :, h, ri] = piece
        target = out_ref.at[:, :, :, pl.ds(group * members, members)]
        copies.append(pltpu.make_async_copy(stage.at[group], target, sems.at[group]))
        copies[-1].start()
    for copy in copies:
        copy.wait()


def both_middle_kernel(me_ref, table_ref, mirror_ref, ch_ref, cl_ref, sh_ref, sl_ref, x_ref, *refs):
    outs, (forward, backward, mid, space, chi) = refs[:-5], refs[-5:]
    halves, _, side, _, entries, rows, lanes = space.shape
    plane = 2 * lanes
    units, _, kept, members, _, _ = chi.shape
    me, near = me_ref[0], len(outs)
    core, line = me % 2, me // 2 % kept
    parity = (1 - 2 * (me // near)).astype(jnp.float32)

    def turned(value):
        return jnp.where(core == 0, value, jnp.concatenate([value[:, lanes:], value[:, :lanes]], axis=1))

    fill_matrices(mirror_ref, (ch_ref, cl_ref, sh_ref, sl_ref), forward, backward, turned)

    def arrive(half):
        columns = [
            x_ref[:, h, half, ri].reshape(side * entries * rows, lanes) for ri in range(2) for h in range(2)
        ]
        return split_value(jnp.concatenate(columns, axis=1))

    def to_plane(value, half, block):
        d = plane_dot(value, forward, half, block)
        for ri in range(2):
            piece = d[:, ri * lanes : (ri + 1) * lanes]
            mid[half, block, ri] = piece.reshape(side, entries, rows, lanes)

    def along_line(half, block, e):
        values = [(mid[half, block, 0, x, e], mid[half, block, 1, x, e]) for x in range(side)]
        for x, (re, im) in enumerate(dft_line(values, 1)):
            space[half, block, x, 0, e] = re
            space[half, block, x, 1, e] = im

    def product(unit, block, c):
        half, first = unit % halves, unit // halves * members
        left, right = table_ref[0, first + c], table_ref[1, first + c]
        values = []
        for x in range(side):
            other = mirror_ref[0, x]
            a_re, a_im = space[half, block, x, 0, left], space[half, block, x, 1, left]
            b_re, b_im = space[1 - half, block, other, 0, right], space[1 - half, block, other, 1, right]
            values.append((a_re * b_re - a_im * b_im, a_re * b_im + a_im * b_re))
        cut = slice(block * lanes, (block + 1) * lanes)
        for x, (re, im) in enumerate(half_line(values, -1, parity)):
            chi[unit, 0, x ^ line, c, :, cut] = re
            chi[unit, 1, x ^ line, c, :, cut] = im

    def from_plane(unit, value, h):
        half, first = unit % halves, unit // halves * members
        d = plane_dot(value, backward, half, h)
        for ri in range(2):
            piece = d[:, ri * lanes : (ri + 1) * lanes].reshape(kept, members, rows, lanes)
            for x in range(kept):
                outs[2 * x + h][half, ri, first : first + members] = piece[x]

    def collect(unit):
        whole = (kept * members * rows, plane)
        return split_value(jnp.concatenate([chi[unit, ri].reshape(whole) for ri in range(2)], axis=1))

    places = [(half, block) for half in range(halves) for block in range(2)]
    for step in range(len(places) + 1):
        if step < len(places):
            half, block = places[step]
            if block == 0:
                value = arrive(half)
            to_plane(value, half, block)
        if step > 0:
            for e in range(entries):
                along_line(*places[step - 1], e)

    for unit in range(units + 1):
        tasks = [(block, c) for block in range(2) for c in range(members)] if unit < units else []
        if unit > 0:
            value = collect(unit - 1)
        for h in range(2):
            if unit > 0:
                from_plane(unit - 1, value, h)
            for block, c in tasks[h * members : (h + 1) * members]:
                product(unit, block, c)


def middle_inputs(table, mirror_map, x):
    side, plane = x.shape[0] // 2, 2 * x.shape[-1]
    cosine, sine = plane_parts(side)
    parts = [jnp.asarray(part) for part in split_constant(cosine) + split_constant(sine)]
    smem = pl.BlockSpec(memory_space=pltpu.SMEM)
    vmem = pl.BlockSpec(memory_space=pltpu.VMEM)
    args = (table.T, mirror_map, *parts, x.reshape((side, 2) + x.shape[1:]))
    return args, [smem, smem] + [vmem] * 5, pltpu.VMEM((2, 2, 2 * plane, 2 * plane), jnp.bfloat16)


def one_middle(x, table, mirror_map):
    devices, _, entries, rows, lanes = x.shape
    side, components = devices // 2, table.shape[0]
    args, specs, matrices = middle_inputs(table, mirror_map, x)
    spatial = pltpu.VMEM((2, side, 2, entries, rows, lanes), jnp.float32)
    shape = (side, 2, 2, components, rows, lanes)
    out = pl.pallas_call(
        one_middle_kernel,
        in_specs=specs,
        out_specs=pl.BlockSpec(memory_space=pltpu.HBM),
        out_shape=jax.ShapeDtypeStruct(shape, jnp.float32),
        scratch_shapes=[
            matrices,
            matrices,
            pltpu.VMEM((2, 2, side, entries, rows, lanes), jnp.float32),
            spatial,
            spatial,
            pltpu.VMEM((GROUPS, 2, side, components // GROUPS, rows, 2 * lanes), jnp.float32),
            pltpu.VMEM((GROUPS, side, 2, 2, components // GROUPS, rows, lanes), jnp.float32),
            pltpu.SemaphoreType.DMA((GROUPS,)),
        ],
        compiler_params=pltpu.CompilerParams(vmem_limit_bytes=59500 << 10),
        cost_estimate=pl.CostEstimate(flops=6_000_000_000, bytes_accessed=12_000_000, transcendentals=0),
        name="one_middle",
    )(*args)
    return out.reshape((devices,) + shape[2:])


def both_middle(x, table, mirror_map, me, near):
    devices, halves, _, entries, rows, lanes = x.shape
    side, components = devices // 2, table.shape[0]
    args, specs, matrices = middle_inputs(table, mirror_map, x)
    members = components // GROUPS
    return pl.pallas_call(
        both_middle_kernel,
        in_specs=[pl.BlockSpec(memory_space=pltpu.SMEM)] + specs,
        out_specs=[pl.BlockSpec(memory_space=pltpu.VMEM)] * near,
        out_shape=[jax.ShapeDtypeStruct((halves, 2, components, rows, lanes), jnp.float32)] * near,
        scratch_shapes=[
            matrices,
            matrices,
            pltpu.VMEM((halves, 2, 2, side, entries, rows, lanes), jnp.float32),
            pltpu.VMEM((halves, 2, side, 2, entries, rows, lanes), jnp.float32),
            pltpu.VMEM((halves * GROUPS, 2, near // 2, members, rows, 2 * lanes), jnp.float32),
        ],
        compiler_params=pltpu.CompilerParams(vmem_limit_bytes=60 << 20),
        name="both_middle",
    )(me, *args)


def prepare_kernel(me_ref, both_ref, one_ref, out_ref):
    near = both_ref.shape[1]
    me = me_ref[0] % near
    ordered = [both_ref[part, slot ^ me] for part in range(2) for slot in range(near)]
    for part, value in enumerate(split_value(jnp.concatenate([one_ref[...]] + ordered, axis=0))):
        out_ref[part] = value


def prepare(me, both, one):
    smem = pl.BlockSpec(memory_space=pltpu.SMEM)
    vmem = pl.BlockSpec(memory_space=pltpu.VMEM)
    depth = both.size // both.shape[3] + one.shape[0]
    return pl.pallas_call(
        prepare_kernel,
        in_specs=[smem, vmem, vmem],
        out_specs=vmem,
        out_shape=jax.ShapeDtypeStruct((2, depth, one.shape[1]), jnp.bfloat16),
        compiler_params=pltpu.CompilerParams(vmem_limit_bytes=59500 << 10),
        name="prepare",
    )(me, both, one)


def fold_kernel(order, *refs):
    pieces, (out_ref, held, stage, in_sems, sems) = refs[:-5], refs[-5:]
    near, _, _, components, rows, lanes = held.shape
    loads = [pltpu.make_async_copy(piece, held.at[slot], in_sems.at[slot]) for slot, piece in zip(order, pieces)]
    for copy in loads:
        copy.start()
    for copy in loads:
        copy.wait()
    copies = []
    for c in range(components):
        part = [[held[:, half, ri, c].reshape(near * rows, lanes) for ri in range(2)] for half in range(2)]
        sums = [part[0][ri] + part[1][ri] for ri in range(2)]
        differences = [part[0][ri] - part[1][ri] for ri in range(2)]
        first = jnp.concatenate([sums[0], -differences[1]], axis=0).T
        second = jnp.concatenate([sums[1], differences[0]], axis=0).T
        for place, value in enumerate(split_value(jnp.concatenate([first, second], axis=0))):
            stage[c, place] = value
        copies.append(pltpu.make_async_copy(stage.at[c], out_ref.at[c], sems.at[c]))
        copies[-1].start()
    for copy in copies:
        copy.wait()


def fold(pieces, order):
    _, _, components, rows, lanes = pieces[0].shape
    shape = (components, 2, 2 * lanes, 2 * len(pieces) * rows)
    hbm = pl.BlockSpec(memory_space=pltpu.HBM)
    return pl.pallas_call(
        functools.partial(fold_kernel, order),
        in_specs=[hbm] * len(pieces),
        out_specs=hbm,
        out_shape=jax.ShapeDtypeStruct(shape, jnp.bfloat16),
        scratch_shapes=[
            pltpu.VMEM((len(pieces),) + pieces[0].shape, jnp.float32),
            pltpu.VMEM(shape, jnp.bfloat16),
            pltpu.SemaphoreType.DMA((len(pieces),)),
            pltpu.SemaphoreType.DMA((components,)),
        ],
        compiler_params=pltpu.CompilerParams(vmem_limit_bytes=59400 << 10),
        name="fold",
    )(*pieces)


def frequency_kernel(y_ref, m_hbm, f_hbm, out_ref, m_ref, f_ref, stage, m_sem, f_sems, sems):
    devices, _, components, rows, lanes = y_ref.shape
    groups = sems.shape[0]
    members = components // groups
    depth = devices * rows
    load = pltpu.make_async_copy(m_hbm, m_ref, m_sem)
    spans = [pl.ds(group * members, members) for group in range(groups)]
    loads = [pltpu.make_async_copy(f_hbm.at[span], f_ref.at[span], f_sems.at[k]) for k, span in enumerate(spans)]
    for copy in [load] + loads:
        copy.start()
    upper_rows = lax.broadcasted_iota(jnp.int32, (devices, rows, lanes), 1) < rows // 2

    def one_values(group):
        values = []
        for c in range(group * members, (group + 1) * members):
            folded = []
            for ri in range(2):
                tile = y_ref[:, ri, c]
                turned = pltpu.roll(tile, rows // 2, 1)
                folded.append((tile + turned, turned - tile))
            first = jnp.where(upper_rows, folded[0][0], -folded[1][1])
            second = jnp.where(upper_rows, folded[1][0], folded[0][1])
            values.append(first.reshape(depth, lanes).T)
            values.append(second.reshape(depth, lanes).T)
        return split_value(jnp.concatenate(values, axis=0))

    copies = []
    for group, span in enumerate(spans):
        parts = one_values(group)
        if group == 0:
            load.wait()
            matrix = (m_ref[0], m_ref[1])
        loads[group].wait()
        own = range(group * members, (group + 1) * members)
        value = [
            jnp.concatenate([parts[place], jnp.concatenate([f_ref[c, place] for c in own], axis=0)], axis=1)
            for place in range(2)
        ]
        d = dot3(value, matrix, ((1,), (0,))).reshape(members, 2, lanes, stage.shape[3])
        for ri in range(2):
            stage[ri, group * members : (group + 1) * members] = d[:, ri]
        copies.append(pltpu.make_async_copy(stage.at[:, span], out_ref.at[:, span], sems.at[group]))
        copies[-1].start()
    for copy in copies:
        copy.wait()


def to_frequencies(y, matrix, folded):
    _, _, components, _, lanes = y.shape
    shape = (2, components, lanes, matrix.shape[2])
    hbm = pl.BlockSpec(memory_space=pltpu.HBM)
    groups = components // 2
    return pl.pallas_call(
        frequency_kernel,
        in_specs=[pl.BlockSpec(memory_space=pltpu.VMEM), hbm, hbm],
        out_specs=hbm,
        out_shape=jax.ShapeDtypeStruct(shape, jnp.float32),
        scratch_shapes=[
            pltpu.VMEM(matrix.shape, jnp.bfloat16),
            pltpu.VMEM(folded.shape, jnp.bfloat16),
            pltpu.VMEM(shape, jnp.float32),
            pltpu.SemaphoreType.DMA,
            pltpu.SemaphoreType.DMA((groups,)),
            pltpu.SemaphoreType.DMA((groups,)),
        ],
        compiler_params=pltpu.CompilerParams(vmem_limit_bytes=59400 << 10),
        name="to_frequencies",
    )(y, matrix, folded)


def exchange(x):
    flat = x.reshape(x.shape[0], -1, x.shape[-1])
    return lax.all_to_all(flat, "kb", split_axis=0, concat_axis=0, tiled=True).reshape(x.shape)


def swap(piece, slot, devices):
    if slot == 0:
        return piece
    return lax.ppermute(piece, "kb", [(device, device ^ slot) for device in range(devices)])


def trig_pair(angle_int, period, scale):
    angle = 2.0 * math.pi / period * angle_int.astype(jnp.float32)
    return (scale * jnp.cos(angle), scale * jnp.sin(angle))


def complex_combine(formula, cosine, sine, real_part, imag_part):
    first_term = jnp.einsum(formula, cosine, real_part + imag_part, precision=lax.Precision.HIGHEST)
    second_term = jnp.einsum(formula, cosine + sine, imag_part, precision=lax.Precision.HIGHEST)
    third_term = jnp.einsum(formula, sine - cosine, real_part, precision=lax.Precision.HIGHEST)
    return (first_term - second_term, first_term + third_term)


def forward_imaginary_time(tau_rows, frequency_count):
    freq_index = jnp.arange(frequency_count, dtype=jnp.int32)
    angle_int = (
        (2 * freq_index[None, :] - frequency_count + 1)
        * (2 * tau_rows[:, None] + 1)
        % (4 * frequency_count)
    )
    cosine, sine = trig_pair(angle_int, 4 * frequency_count, frequency_count ** (-0.5))
    return (cosine, -sine)


def tau_backward(tau_rows, frequency_count):
    freq_index = jnp.arange(frequency_count, dtype=jnp.int32)
    angle_int = (
        (freq_index[:, None] - frequency_count // 2)
        * (2 * tau_rows[None, :] + 1)
        % (2 * frequency_count)
    )
    return trig_pair(angle_int, 2 * frequency_count, frequency_count ** (-0.5))


def grid_transform(real_part, imag_part, grid_side, direction):
    shape = real_part.shape
    plane = jnp.arange(grid_side * grid_side, dtype=jnp.int32)
    upper = plane // grid_side
    lower = plane % grid_side
    plane_int = (upper[:, None] * upper[None, :] + lower[:, None] * lower[None, :]) % grid_side
    plane_cos, plane_sin = trig_pair(plane_int, grid_side, 1.0 / grid_side)
    line = jnp.arange(grid_side, dtype=jnp.int32)
    line_cos, line_sin = trig_pair(
        line[:, None] * line[None, :] % grid_side, grid_side, grid_side ** (-0.5)
    )
    real_part = real_part.reshape(shape[:-1] + (grid_side, grid_side * grid_side))
    imag_part = imag_part.reshape(shape[:-1] + (grid_side, grid_side * grid_side))
    real_part, imag_part = complex_combine(
        "pq,...xq->...xp", plane_cos, direction * plane_sin, real_part, imag_part
    )
    real_part, imag_part = complex_combine(
        "ax,...xp->...ap", line_cos, direction * line_sin, real_part, imag_part
    )
    return (real_part.reshape(shape), imag_part.reshape(shape))


def mirror_index(mirror_map, grid_side):
    index_x = mirror_map[0][:, None, None]
    index_y = mirror_map[1][None, :, None]
    index_z = mirror_map[2][None, None, :]
    return (index_x * grid_side * grid_side + index_y * grid_side + index_z).reshape(-1)


def bubble(gr_re, gr_im, mirror_re, mirror_im, pair_table, entries):
    entry_ids = jnp.arange(entries, dtype=jnp.int32)
    pick_left = (pair_table[:, 0][:, None] == entry_ids[None, :]).astype(jnp.float32)
    pick_right = (pair_table[:, 1][:, None] == entry_ids[None, :]).astype(jnp.float32)
    left_re = jnp.einsum("me,e...->m...", pick_left, gr_re, precision=lax.Precision.HIGHEST)
    left_im = jnp.einsum("me,e...->m...", pick_left, gr_im, precision=lax.Precision.HIGHEST)
    right_re = jnp.einsum("me,e...->m...", pick_right, mirror_re, precision=lax.Precision.HIGHEST)
    right_im = jnp.einsum("me,e...->m...", pick_right, mirror_im, precision=lax.Precision.HIGHEST)
    return (left_re * right_re - left_im * right_im, left_re * right_im + left_im * right_re)


def general(green_momentum_grid, pair_table, mirror_map):
    grid_side = mirror_map.shape[1]
    entries = green_momentum_grid.shape[1]
    frequency_count = green_momentum_grid.shape[3]
    position = jnp.arange(frequency_count, dtype=jnp.int32)
    fwd_cos, fwd_sin = forward_imaginary_time(position, frequency_count)
    tau_re, tau_im = complex_combine(
        "qa,fsa->fqs", fwd_cos, fwd_sin, green_momentum_grid[0], green_momentum_grid[1]
    )
    stacked = jnp.stack([tau_re, tau_im])

    def to_real_space(pieces):
        space_re, space_im = grid_transform(pieces[0], pieces[1], grid_side, 1.0)
        return jnp.stack([space_re, space_im])

    mirror_flat = mirror_index(mirror_map, grid_side)
    partner_rows = frequency_count - 1 - position
    reflected_cosine, reflected_sine = forward_imaginary_time(partner_rows, frequency_count)
    partner_real, partner_imaginary = complex_combine(
        "qa,fsa->fqs",
        reflected_cosine,
        reflected_sine,
        green_momentum_grid[0],
        green_momentum_grid[1],
    )
    other_stacked = jnp.stack([partner_real, partner_imaginary])
    pieces = (
        lax.all_to_all(stacked, "kb", split_axis=2, concat_axis=3, tiled=True),
        lax.all_to_all(other_stacked, "kb", split_axis=2, concat_axis=3, tiled=True),
    )
    in_cells = to_real_space(pieces[0])
    partner = to_real_space(pieces[1])
    mirrored = jnp.take(partner, mirror_flat, axis=3)
    chi_re, chi_im = bubble(in_cells[0], in_cells[1], mirrored[0], mirrored[1], pair_table, entries)
    chi_re, chi_im = grid_transform(chi_re, chi_im, grid_side, -1.0)
    momenta = jnp.stack([chi_re, chi_im])
    back_cos, back_sin = tau_backward(position, frequency_count)
    pieces = lax.all_to_all(momenta, "kb", split_axis=3, concat_axis=2, tiled=True)
    out_re, out_im = complex_combine("vj,ejk->ekv", back_cos, back_sin, pieces[0], pieces[1])
    return jnp.stack([out_re, out_im])


def local(green, pair_table, mirror_map):
    side = mirror_map.shape[1]
    plane = side * side
    lanes, count = green.shape[2], green.shape[3]
    devices = side * plane // lanes
    near = devices // 2
    half = ROWS // 2
    shared = near * ROWS
    if lanes != LANES or 2 * lanes != plane or 2 * (shared + devices * half) != count:
        return general(green, pair_table, mirror_map)
    me = lax.axis_index("kb").astype(jnp.int32).reshape(1)
    entries = green.shape[1]

    rows = np.arange(shared)
    both_fermion = fermion_matrix(rows, count).astype(np.float32)
    both_boson = boson_matrix(rows, count).reshape(2, near, ROWS, count).astype(np.float32)
    rows = shared + np.arange(devices * half).reshape(devices, half)
    times = np.concatenate([rows, count - 1 - rows], axis=1).reshape(-1)
    one_fermion = fermion_matrix(times, count).astype(np.float32)
    one_boson = boson_matrix(rows.reshape(-1), count).reshape(2, devices, half, count).swapaxes(0, 1)
    one_boson = one_boson.reshape(devices * ROWS, count).astype(np.float32)

    shape = (near, 2, 2, entries, ROWS, lanes)
    both = to_times(both_times_kernel, green, jnp.asarray(both_fermion), shape, devices, "both_times")
    green, both = lax.optimization_barrier((green, both))
    shape = (devices, 2, entries, ROWS, lanes)
    one = to_times(one_times_kernel, green, jnp.asarray(one_fermion), shape, devices, "one_times")
    both, one = lax.optimization_barrier((exchange(both), one))
    pieces = both_middle(both, pair_table, mirror_map, me, near)
    first, count = near // 2, near // 4
    early = list(range(first, first + count)) + [1]
    beside = [first + count, first + count + 1, 2, 3]
    late = [slot for slot in range(1, near) if slot not in early + beside]
    moved = {0: pieces[0]}

    one, arrived = lax.optimization_barrier((exchange(one), [swap(pieces[slot], slot, devices) for slot in early]))
    moved |= zip(early, arrived)
    arrived = [swap(pieces[slot], slot, devices) for slot in beside]
    one, arrived, both_boson, one_boson = lax.optimization_barrier(
        (one_middle(one, pair_table, mirror_map), arrived, jnp.asarray(both_boson), jnp.asarray(one_boson))
    )
    moved |= zip(beside, arrived)
    matrix, sent = lax.optimization_barrier((prepare(me, both_boson, one_boson), [pieces[slot] for slot in late]))
    moved |= zip(late, [swap(piece, slot, devices) for slot, piece in zip(late, sent)])
    order = [0] + early + beside + late
    return to_frequencies(exchange(one), matrix, fold([moved[slot] for slot in order], order))


def solution(mesh):
    placed = (P("set", None, "kb", None), P(), P("set", None))
    return jax.shard_map(
        local, mesh=mesh, in_specs=placed, out_specs=P("set", None, "kb", None), check_vma=False
    )
```

```python
import functools
import math

import jax
import jax.numpy as jnp
import ml_dtypes
import numpy as np
from jax import lax
from jax.experimental import pallas as pl
from jax.experimental.pallas import tpu as pltpu
from jax.sharding import PartitionSpec as P

LANES = 128
ROWS = 8
GROUPS = 2


def split_constant(matrix):
    high = matrix.astype(np.float32).astype(ml_dtypes.bfloat16)
    low = (matrix - high.astype(np.float64)).astype(np.float32).astype(ml_dtypes.bfloat16)
    return high, low


def split_value(value):
    high = value.astype(jnp.bfloat16)
    low = (value - high.astype(jnp.float32)).astype(jnp.bfloat16)
    return high, low


def dot3(left, right, dims):
    (k_left,), (k_right,) = dims
    a = jnp.concatenate([left[0], left[0], left[1]], axis=k_left)
    b = jnp.concatenate([right[0], right[1], right[0]], axis=k_right)
    return lax.dot_general(a, b, (dims, ((), ())), preferred_element_type=jnp.float32)


def fermion_matrix(rows, count):
    n = np.arange(count, dtype=np.int64)
    angle = ((2 * n[None, :] - count + 1) * (2 * rows[:, None] + 1)) % (4 * count)
    angle = np.pi * angle / (2 * count)
    return np.concatenate([np.cos(angle), np.sin(angle)], axis=0) * count**-0.5


def boson_matrix(rows, count):
    v = np.arange(count, dtype=np.int64)
    angle = ((v[None, :] - count // 2) * (2 * rows[:, None] + 1)) % (2 * count)
    angle = np.pi * angle / count
    return np.concatenate([np.cos(angle), np.sin(angle)], axis=0) * count**-0.5


def plane_parts(side):
    p = np.arange(side * side, dtype=np.int64)
    angle = ((p[:, None] // side) * (p[None, :] // side) + (p[:, None] % side) * (p[None, :] % side)) % side
    angle = 2 * np.pi * angle / side
    scale = side**-1.5
    return np.cos(angle) * scale, np.sin(angle) * scale


def times_w4(re, im, power, sign):
    power = (power * sign) % 4
    if power == 0:
        return re, im
    if power == 1:
        return -im, re
    if power == 2:
        return -re, -im
    return im, -re


def dft4(values, sign):
    (r0, i0), (r1, i1), (r2, i2), (r3, i3) = values
    sr, si, dr, di = r0 + r2, i0 + i2, r0 - r2, i0 - i2
    tr, ti, er, ei = r1 + r3, i1 + i3, r1 - r3, i1 - i3
    if sign > 0:
        return [(sr + tr, si + ti), (dr - ei, di + er), (sr - tr, si - ti), (dr + ei, di - er)]
    return [(sr + tr, si + ti), (dr + ei, di - er), (sr - tr, si - ti), (dr - ei, di + er)]


def twiddle(value, power, sign, side):
    re, im = value
    if power % (side // 4) == 0:
        return times_w4(re, im, power // (side // 4), sign)
    angle = 2.0 * np.pi * power / side
    c, s = float(np.cos(angle)), float(sign * np.sin(angle))
    return re * c - im * s, re * s + im * c


def dft_line(values, sign):
    side = len(values)
    if side == 1:
        return values
    if side == 2:
        (r0, i0), (r1, i1) = values
        return [(r0 + r1, i0 + i1), (r0 - r1, i0 - i1)]
    if side == 4:
        return dft4(values, sign)
    inner = side // 4
    parts = [dft_line(values[b::4], sign) for b in range(4)]
    out = [None] * side
    for k1 in range(inner):
        column = [twiddle(parts[b][k1], b * k1, sign, side) for b in range(4)]
        for k2, value in enumerate(dft4(column, sign)):
            out[k1 + inner * k2] = value
    return out


def half_line(values, sign, parity):
    side = len(values)
    inner = side // 4
    parts = [dft_line(values[b::4], sign) for b in range(4)]
    out = [None] * (side // 2)
    for k1 in range(inner):
        column = [twiddle(parts[b][k1], b * k1, sign, side) for b in range(4)]
        column = [(re * parity, im * parity) if b % 2 else (re, im) for b, (re, im) in enumerate(column)]
        for k2, value in enumerate(dft4(column, sign)[:2]):
            out[k1 + inner * k2] = value
    return out


def load_inputs(g_hbm, m_hbm, g_ref, m_ref, in_sems, m_sem):
    load = pltpu.make_async_copy(m_hbm, m_ref, m_sem)
    pieces = [
        pltpu.make_async_copy(g_hbm.at[:, pl.ds(e, 1)], g_ref.at[:, pl.ds(e, 1)], in_sems.at[e])
        for e in range(g_ref.shape[1])
    ]
    for copy in [load] + pieces:
        copy.start()
    load.wait()
    return pieces


def sums_of(matrix, g_ref, e):
    lanes = g_ref.shape[2]
    g = jnp.concatenate([g_ref[0, e], g_ref[1, e]], axis=0)
    d = dot3(matrix, split_value(g), ((1,), (1,)))
    half = d.shape[0] // 2
    return d[:half, :lanes], d[:half, lanes:], d[half:, :lanes], d[half:, lanes:]


def both_times_kernel(g_hbm, m_hbm, out_ref, g_ref, m_ref, stage, in_sems, m_sem, out_sems):
    entries, lanes = g_ref.shape[1:3]
    near, _, _, _, rows, _ = stage.shape
    pieces = load_inputs(g_hbm, m_hbm, g_ref, m_ref, in_sems, m_sem)
    matrix = split_value(m_ref[...])
    copies = []
    for e in range(entries):
        pieces[e].wait()
        c_re, c_im, s_re, s_im = sums_of(matrix, g_ref, e)
        for where, value in (
            ((0, 0), c_re + s_im),
            ((0, 1), c_im - s_re),
            ((1, 0), s_im - c_re),
            ((1, 1), -(c_im + s_re)),
        ):
            stage[:, where[0], where[1], e] = value.reshape(near, rows, lanes)
        cut = pl.ds(e, 1)
        for side in range(2):
            target = out_ref.at[pl.ds(side * near, near), :, :, cut]
            copies.append(pltpu.make_async_copy(stage.at[:, :, :, cut], target, out_sems.at[e, side]))
            copies[-1].start()
    for copy in copies:
        copy.wait()


def one_times_kernel(g_hbm, m_hbm, out_ref, g_ref, m_ref, stage, in_sems, m_sem, out_sems):
    entries, lanes = g_ref.shape[1:3]
    devices, _, _, rows, _ = stage.shape
    pieces = load_inputs(g_hbm, m_hbm, g_ref, m_ref, in_sems, m_sem)
    matrix = split_value(m_ref[...])
    copies = []
    for e in range(entries):
        pieces[e].wait()
        c_re, c_im, s_re, s_im = sums_of(matrix, g_ref, e)
        stage[:, 0, e] = (c_re + s_im).reshape(devices, rows, lanes)
        stage[:, 1, e] = (c_im - s_re).reshape(devices, rows, lanes)
        cut = pl.ds(e, 1)
        copies.append(pltpu.make_async_copy(stage.at[:, :, cut], out_ref.at[:, :, cut], out_sems.at[e, 0]))
        copies[-1].start()
    for copy in copies:
        copy.wait()


def to_times(kernel, green, matrix, shape, targets, name):
    entries = green.shape[1]
    hbm = pl.BlockSpec(memory_space=pltpu.HBM)
    return pl.pallas_call(
        kernel,
        in_specs=[hbm, hbm],
        out_specs=hbm,
        out_shape=jax.ShapeDtypeStruct((targets,) + shape[1:], jnp.float32),
        scratch_shapes=[
            pltpu.VMEM(green.shape, jnp.float32),
            pltpu.VMEM(matrix.shape, jnp.float32),
            pltpu.VMEM(shape, jnp.float32),
            pltpu.SemaphoreType.DMA((entries,)),
            pltpu.SemaphoreType.DMA,
            pltpu.SemaphoreType.DMA((entries, 2)),
        ],
        compiler_params=pltpu.CompilerParams(vmem_limit_bytes=63 << 20),
        name=name,
    )(green, matrix)


def fill_block(ref, cosine, sine):
    plane = cosine.shape[0]
    lanes = plane // 2
    for block in range(2):
        cut = slice(block * lanes, (block + 1) * lanes)
        re = slice(2 * block * lanes, (2 * block + 1) * lanes)
        im = slice((2 * block + 1) * lanes, (2 * block + 2) * lanes)
        ref[:plane, re] = cosine[:, cut].astype(jnp.bfloat16)
        ref[plane:, im] = cosine[:, cut].astype(jnp.bfloat16)
        ref[:plane, im] = sine[:, cut].astype(jnp.bfloat16)
        ref[plane:, re] = (-sine[:, cut]).astype(jnp.bfloat16)


def fill_matrices(mirror_ref, parts, forward, backward, turned):
    plane = parts[0].shape[0]
    side = mirror_ref.shape[1]
    row = lax.broadcasted_iota(jnp.int32, (plane, plane), 0)
    column = lax.broadcasted_iota(jnp.int32, (plane, plane), 1)
    upper = (mirror_ref[1, 0] - column // side) & (side - 1)
    lower = (mirror_ref[2, 0] - column % side) & (side - 1)
    pick = (row == upper * side + lower).astype(jnp.float32).astype(jnp.bfloat16)

    def dot(a, b):
        return jnp.dot(a, b, preferred_element_type=jnp.float32)

    for part in range(2):
        c_ref, s_ref = parts[part], parts[2 + part]
        cosine, sine = c_ref[...].astype(jnp.float32), s_ref[...].astype(jnp.float32)
        fill_block(forward.at[0, part], cosine, sine)
        fill_block(backward.at[0, part], turned(cosine), turned(-sine))
        fill_block(forward.at[1, part], dot(c_ref[...], pick), dot(s_ref[...], pick))
        fill_block(backward.at[1, part], turned(dot(pick, c_ref[...])), turned(-dot(pick, s_ref[...])))


def plane_dot(value, matrix, half, block):
    width = matrix.shape[3] // 2
    cut = slice(block * width, (block + 1) * width)
    return dot3(value, (matrix[half, 0, :, cut], matrix[half, 1, :, cut]), ((1,), (0,)))


def one_middle_kernel(table_ref, mirror_ref, ch_ref, cl_ref, sh_ref, sl_ref, x_ref, out_ref, *refs):
    forward, backward, mid, space, other_space, chi, stage, sems = refs
    _, side, _, entries, rows, lanes = space.shape
    plane = 2 * lanes
    groups, _, _, members, _, _ = chi.shape
    fill_matrices(mirror_ref, (ch_ref, cl_ref, sh_ref, sl_ref), forward, backward, lambda value: value)

    def paired(first, second):
        upper = lax.broadcasted_iota(jnp.int32, first.shape, 1) < rows // 2
        turned = [pltpu.roll(part, rows // 2, 1) for part in (first, second)]
        return jnp.where(upper, first, turned[1]), jnp.where(upper, turned[0], second)

    def halves_of(columns):
        value = jnp.concatenate(columns, axis=1)
        count, width = value.shape
        value = value.reshape(count // (2 * rows), 2, rows, width)
        parts = paired(value[:, 0], value[:, 1])
        return [split_value(part.reshape(count // 2, width)) for part in parts]

    def halves_dot(parts, matrix, block):
        shape = (parts[0][0].shape[0] // rows, rows, plane)
        d = paired(*(plane_dot(parts[half], matrix, half, block).reshape(shape) for half in range(2)))
        return jnp.concatenate([part.reshape(shape[0], 1, rows, plane) for part in d], axis=1)

    parts = halves_of([x_ref[:, h, ri].reshape(side * entries * rows, lanes) for ri in range(2) for h in range(2)])
    for block in range(2):
        d = halves_dot(parts, forward, block)
        for ri in range(2):
            piece = d[:, :, :, ri * lanes : (ri + 1) * lanes]
            mid[block, ri] = piece.reshape(side, entries, rows, lanes)
    for block in range(2):
        for e in range(entries):
            values = [(mid[block, 0, x, e], mid[block, 1, x, e]) for x in range(side)]
            for x, parts in enumerate(dft_line(values, 1)):
                for ri in range(2):
                    space[block, x, ri, e] = parts[ri]
                    other_space[block, x, ri, e] = pltpu.roll(parts[ri], rows // 2, 0)

    copies = []
    for group in range(groups):
        for c in range(members):
            left, right = table_ref[0, group * members + c], table_ref[1, group * members + c]
            for block in range(2):
                values = []
                for x in range(side):
                    other = mirror_ref[0, x]
                    a_re, a_im = space[block, x, 0, left], space[block, x, 1, left]
                    b_re, b_im = other_space[block, other, 0, right], other_space[block, other, 1, right]
                    values.append((a_re * b_re - a_im * b_im, a_re * b_im + a_im * b_re))
                cut = slice(block * lanes, (block + 1) * lanes)
                for x, parts in enumerate(dft_line(values, -1)):
                    for ri in range(2):
                        chi[group, ri, x, c, :, cut] = parts[ri]
        whole = (side * members * rows, plane)
        parts = halves_of([chi[group, ri].reshape(whole) for ri in range(2)])
        for h in range(2):
            d = halves_dot(parts, backward, h)
            for ri in range(2):
                piece = d[:, :, :, ri * lanes : (ri + 1) * lanes].reshape(side, members, rows, lanes)
                stage[group, :, h, ri] = piece
        target = out_ref.at[:, :, :, pl.ds(group * members, members)]
        copies.append(pltpu.make_async_copy(stage.at[group], target, sems.at[group]))
        copies[-1].start()
    for copy in copies:
        copy.wait()


def both_middle_kernel(me_ref, table_ref, mirror_ref, ch_ref, cl_ref, sh_ref, sl_ref, x_ref, *refs):
    outs, (forward, backward, mid, space, chi) = refs[:-5], refs[-5:]
    halves, _, side, _, entries, rows, lanes = space.shape
    plane = 2 * lanes
    units, _, kept, members, _, _ = chi.shape
    me, near = me_ref[0], len(outs)
    core, line = me % 2, me // 2 % kept
    parity = (1 - 2 * (me // near)).astype(jnp.float32)

    def turned(value):
        return jnp.where(core == 0, value, jnp.concatenate([value[:, lanes:], value[:, :lanes]], axis=1))

    fill_matrices(mirror_ref, (ch_ref, cl_ref, sh_ref, sl_ref), forward, backward, turned)

    def arrive(half):
        columns = [
            x_ref[:, h, half, ri].reshape(side * entries * rows, lanes) for ri in range(2) for h in range(2)
        ]
        return split_value(jnp.concatenate(columns, axis=1))

    def to_plane(value, half, block):
        d = plane_dot(value, forward, half, block)
        for ri in range(2):
            piece = d[:, ri * lanes : (ri + 1) * lanes]
            mid[half, block, ri] = piece.reshape(side, entries, rows, lanes)

    def along_line(half, block, e):
        values = [(mid[half, block, 0, x, e], mid[half, block, 1, x, e]) for x in range(side)]
        for x, (re, im) in enumerate(dft_line(values, 1)):
            space[half, block, x, 0, e] = re
            space[half, block, x, 1, e] = im

    def product(unit, block, c):
        half, first = unit % halves, unit // halves * members
        left, right = table_ref[0, first + c], table_ref[1, first + c]
        values = []
        for x in range(side):
            other = mirror_ref[0, x]
            a_re, a_im = space[half, block, x, 0, left], space[half, block, x, 1, left]
            b_re, b_im = space[1 - half, block, other, 0, right], space[1 - half, block, other, 1, right]
            values.append((a_re * b_re - a_im * b_im, a_re * b_im + a_im * b_re))
        cut = slice(block * lanes, (block + 1) * lanes)
        for x, (re, im) in enumerate(half_line(values, -1, parity)):
            chi[unit, 0, x ^ line, c, :, cut] = re
            chi[unit, 1, x ^ line, c, :, cut] = im

    def from_plane(unit, value, h):
        half, first = unit % halves, unit // halves * members
        d = plane_dot(value, backward, half, h)
        for ri in range(2):
            piece = d[:, ri * lanes : (ri + 1) * lanes].reshape(kept, members, rows, lanes)
            for x in range(kept):
                outs[2 * x + h][half, ri, first : first + members] = piece[x]

    def collect(unit):
        whole = (kept * members * rows, plane)
        return split_value(jnp.concatenate([chi[unit, ri].reshape(whole) for ri in range(2)], axis=1))

    places = [(half, block) for half in range(halves) for block in range(2)]
    for step in range(len(places) + 1):
        if step < len(places):
            half, block = places[step]
            if block == 0:
                value = arrive(half)
            to_plane(value, half, block)
        if step > 0:
            for e in range(entries):
                along_line(*places[step - 1], e)

    for unit in range(units + 1):
        tasks = [(block, c) for block in range(2) for c in range(members)] if unit < units else []
        if unit > 0:
            value = collect(unit - 1)
        for h in range(2):
            if unit > 0:
                from_plane(unit - 1, value, h)
            for block, c in tasks[h * members : (h + 1) * members]:
                product(unit, block, c)


def middle_inputs(table, mirror_map, x):
    side, plane = x.shape[0] // 2, 2 * x.shape[-1]
    cosine, sine = plane_parts(side)
    parts = [jnp.asarray(part) for part in split_constant(cosine) + split_constant(sine)]
    smem = pl.BlockSpec(memory_space=pltpu.SMEM)
    vmem = pl.BlockSpec(memory_space=pltpu.VMEM)
    args = (table.T, mirror_map, *parts, x.reshape((side, 2) + x.shape[1:]))
    return args, [smem, smem] + [vmem] * 5, pltpu.VMEM((2, 2, 2 * plane, 2 * plane), jnp.bfloat16)


def one_middle(x, table, mirror_map):
    devices, _, entries, rows, lanes = x.shape
    side, components = devices // 2, table.shape[0]
    args, specs, matrices = middle_inputs(table, mirror_map, x)
    spatial = pltpu.VMEM((2, side, 2, entries, rows, lanes), jnp.float32)
    shape = (side, 2, 2, components, rows, lanes)
    out = pl.pallas_call(
        one_middle_kernel,
        in_specs=specs,
        out_specs=pl.BlockSpec(memory_space=pltpu.HBM),
        out_shape=jax.ShapeDtypeStruct(shape, jnp.float32),
        scratch_shapes=[
            matrices,
            matrices,
            pltpu.VMEM((2, 2, side, entries, rows, lanes), jnp.float32),
            spatial,
            spatial,
            pltpu.VMEM((GROUPS, 2, side, components // GROUPS, rows, 2 * lanes), jnp.float32),
            pltpu.VMEM((GROUPS, side, 2, 2, components // GROUPS, rows, lanes), jnp.float32),
            pltpu.SemaphoreType.DMA((GROUPS,)),
        ],
        compiler_params=pltpu.CompilerParams(vmem_limit_bytes=45056 << 10),
        cost_estimate=pl.CostEstimate(flops=6_000_000_000, bytes_accessed=12_000_000, transcendentals=0),
        name="one_middle",
    )(*args)
    return out.reshape((devices,) + shape[2:])


def both_middle(x, table, mirror_map, me, near):
    devices, halves, _, entries, rows, lanes = x.shape
    side, components = devices // 2, table.shape[0]
    args, specs, matrices = middle_inputs(table, mirror_map, x)
    members = components // GROUPS
    return pl.pallas_call(
        both_middle_kernel,
        in_specs=[pl.BlockSpec(memory_space=pltpu.SMEM)] + specs,
        out_specs=[pl.BlockSpec(memory_space=pltpu.VMEM)] * near,
        out_shape=[jax.ShapeDtypeStruct((halves, 2, components, rows, lanes), jnp.float32)] * near,
        scratch_shapes=[
            matrices,
            matrices,
            pltpu.VMEM((halves, 2, 2, side, entries, rows, lanes), jnp.float32),
            pltpu.VMEM((halves, 2, side, 2, entries, rows, lanes), jnp.float32),
            pltpu.VMEM((halves * GROUPS, 2, near // 2, members, rows, 2 * lanes), jnp.float32),
        ],
        compiler_params=pltpu.CompilerParams(vmem_limit_bytes=60 << 20),
        name="both_middle",
    )(me, *args)


def prepare_kernel(me_ref, both_ref, one_ref, out_ref):
    near = both_ref.shape[1]
    me = me_ref[0] % near
    ordered = [both_ref[part, slot ^ me] for part in range(2) for slot in range(near)]
    for part, value in enumerate(split_value(jnp.concatenate([one_ref[...]] + ordered, axis=0))):
        out_ref[part] = value


def prepare(me, both, one):
    smem = pl.BlockSpec(memory_space=pltpu.SMEM)
    vmem = pl.BlockSpec(memory_space=pltpu.VMEM)
    depth = both.size // both.shape[3] + one.shape[0]
    return pl.pallas_call(
        prepare_kernel,
        in_specs=[smem, vmem, vmem],
        out_specs=vmem,
        out_shape=jax.ShapeDtypeStruct((2, depth, one.shape[1]), jnp.bfloat16),
        compiler_params=pltpu.CompilerParams(vmem_limit_bytes=59500 << 10),
        name="prepare",
    )(me, both, one)


def fold_kernel(order, *refs):
    pieces, (out_ref, held, stage, in_sems, sems) = refs[:-5], refs[-5:]
    near, _, _, components, rows, lanes = held.shape
    loads = [pltpu.make_async_copy(piece, held.at[slot], in_sems.at[slot]) for slot, piece in zip(order, pieces)]
    for copy in loads:
        copy.start()
    for copy in loads:
        copy.wait()
    copies = []
    for c in range(components):
        part = [[held[:, half, ri, c].reshape(near * rows, lanes) for ri in range(2)] for half in range(2)]
        sums = [part[0][ri] + part[1][ri] for ri in range(2)]
        differences = [part[0][ri] - part[1][ri] for ri in range(2)]
        first = jnp.concatenate([sums[0], -differences[1]], axis=0).T
        second = jnp.concatenate([sums[1], differences[0]], axis=0).T
        for place, value in enumerate(split_value(jnp.concatenate([first, second], axis=0))):
            stage[c, place] = value
        copies.append(pltpu.make_async_copy(stage.at[c], out_ref.at[c], sems.at[c]))
        copies[-1].start()
    for copy in copies:
        copy.wait()


def fold(pieces, order):
    _, _, components, rows, lanes = pieces[0].shape
    shape = (components, 2, 2 * lanes, 2 * len(pieces) * rows)
    hbm = pl.BlockSpec(memory_space=pltpu.HBM)
    return pl.pallas_call(
        functools.partial(fold_kernel, order),
        in_specs=[hbm] * len(pieces),
        out_specs=hbm,
        out_shape=jax.ShapeDtypeStruct(shape, jnp.bfloat16),
        scratch_shapes=[
            pltpu.VMEM((len(pieces),) + pieces[0].shape, jnp.float32),
            pltpu.VMEM(shape, jnp.bfloat16),
            pltpu.SemaphoreType.DMA((len(pieces),)),
            pltpu.SemaphoreType.DMA((components,)),
        ],
        compiler_params=pltpu.CompilerParams(vmem_limit_bytes=59400 << 10),
        name="fold",
    )(*pieces)


def frequency_kernel(y_ref, m_hbm, f_hbm, out_ref, m_ref, f_ref, stage, m_sem, f_sems, sems):
    devices, _, components, rows, lanes = y_ref.shape
    groups = sems.shape[0]
    members = components // groups
    depth = devices * rows
    load = pltpu.make_async_copy(m_hbm, m_ref, m_sem)
    spans = [pl.ds(group * members, members) for group in range(groups)]
    loads = [pltpu.make_async_copy(f_hbm.at[span], f_ref.at[span], f_sems.at[k]) for k, span in enumerate(spans)]
    for copy in [load] + loads:
        copy.start()
    upper_rows = lax.broadcasted_iota(jnp.int32, (devices, rows, lanes), 1) < rows // 2

    def one_values(group):
        values = []
        for c in range(group * members, (group + 1) * members):
            folded = []
            for ri in range(2):
                tile = y_ref[:, ri, c]
                turned = pltpu.roll(tile, rows // 2, 1)
                folded.append((tile + turned, turned - tile))
            first = jnp.where(upper_rows, folded[0][0], -folded[1][1])
            second = jnp.where(upper_rows, folded[1][0], folded[0][1])
            values.append(first.reshape(depth, lanes).T)
            values.append(second.reshape(depth, lanes).T)
        return split_value(jnp.concatenate(values, axis=0))

    copies = []
    for group, span in enumerate(spans):
        parts = one_values(group)
        if group == 0:
            load.wait()
            matrix = (m_ref[0], m_ref[1])
        loads[group].wait()
        own = range(group * members, (group + 1) * members)
        value = [
            jnp.concatenate([parts[place], jnp.concatenate([f_ref[c, place] for c in own], axis=0)], axis=1)
            for place in range(2)
        ]
        d = dot3(value, matrix, ((1,), (0,))).reshape(members, 2, lanes, stage.shape[3])
        for ri in range(2):
            stage[ri, group * members : (group + 1) * members] = d[:, ri]
        copies.append(pltpu.make_async_copy(stage.at[:, span], out_ref.at[:, span], sems.at[group]))
        copies[-1].start()
    for copy in copies:
        copy.wait()


def to_frequencies(y, matrix, folded):
    _, _, components, _, lanes = y.shape
    shape = (2, components, lanes, matrix.shape[2])
    hbm = pl.BlockSpec(memory_space=pltpu.HBM)
    groups = components // 2
    return pl.pallas_call(
        frequency_kernel,
        in_specs=[pl.BlockSpec(memory_space=pltpu.VMEM), hbm, hbm],
        out_specs=hbm,
        out_shape=jax.ShapeDtypeStruct(shape, jnp.float32),
        scratch_shapes=[
            pltpu.VMEM(matrix.shape, jnp.bfloat16),
            pltpu.VMEM(folded.shape, jnp.bfloat16),
            pltpu.VMEM(shape, jnp.float32),
            pltpu.SemaphoreType.DMA,
            pltpu.SemaphoreType.DMA((groups,)),
            pltpu.SemaphoreType.DMA((groups,)),
        ],
        compiler_params=pltpu.CompilerParams(vmem_limit_bytes=56320 << 10),
        name="to_frequencies",
    )(y, matrix, folded)


def exchange(x):
    flat = x.reshape(x.shape[0], -1, x.shape[-1])
    return lax.all_to_all(flat, "kb", split_axis=0, concat_axis=0, tiled=True).reshape(x.shape)


def swap(piece, slot, devices):
    if slot == 0:
        return piece
    return lax.ppermute(piece, "kb", [(device, device ^ slot) for device in range(devices)])


def trig_pair(angle_int, period, scale):
    angle = 2.0 * math.pi / period * angle_int.astype(jnp.float32)
    return (scale * jnp.cos(angle), scale * jnp.sin(angle))


def complex_combine(formula, cosine, sine, real_part, imag_part):
    first_term = jnp.einsum(formula, cosine, real_part + imag_part, precision=lax.Precision.HIGHEST)
    second_term = jnp.einsum(formula, cosine + sine, imag_part, precision=lax.Precision.HIGHEST)
    third_term = jnp.einsum(formula, sine - cosine, real_part, precision=lax.Precision.HIGHEST)
    return (first_term - second_term, first_term + third_term)


def forward_imaginary_time(tau_rows, frequency_count):
    freq_index = jnp.arange(frequency_count, dtype=jnp.int32)
    angle_int = (
        (2 * freq_index[None, :] - frequency_count + 1)
        * (2 * tau_rows[:, None] + 1)
        % (4 * frequency_count)
    )
    cosine, sine = trig_pair(angle_int, 4 * frequency_count, frequency_count ** (-0.5))
    return (cosine, -sine)


def tau_backward(tau_rows, frequency_count):
    freq_index = jnp.arange(frequency_count, dtype=jnp.int32)
    angle_int = (
        (freq_index[:, None] - frequency_count // 2)
        * (2 * tau_rows[None, :] + 1)
        % (2 * frequency_count)
    )
    return trig_pair(angle_int, 2 * frequency_count, frequency_count ** (-0.5))


def grid_transform(real_part, imag_part, grid_side, direction):
    shape = real_part.shape
    plane = jnp.arange(grid_side * grid_side, dtype=jnp.int32)
    upper = plane // grid_side
    lower = plane % grid_side
    plane_int = (upper[:, None] * upper[None, :] + lower[:, None] * lower[None, :]) % grid_side
    plane_cos, plane_sin = trig_pair(plane_int, grid_side, 1.0 / grid_side)
    line = jnp.arange(grid_side, dtype=jnp.int32)
    line_cos, line_sin = trig_pair(
        line[:, None] * line[None, :] % grid_side, grid_side, grid_side ** (-0.5)
    )
    real_part = real_part.reshape(shape[:-1] + (grid_side, grid_side * grid_side))
    imag_part = imag_part.reshape(shape[:-1] + (grid_side, grid_side * grid_side))
    real_part, imag_part = complex_combine(
        "pq,...xq->...xp", plane_cos, direction * plane_sin, real_part, imag_part
    )
    real_part, imag_part = complex_combine(
        "ax,...xp->...ap", line_cos, direction * line_sin, real_part, imag_part
    )
    return (real_part.reshape(shape), imag_part.reshape(shape))


def mirror_index(mirror_map, grid_side):
    index_x = mirror_map[0][:, None, None]
    index_y = mirror_map[1][None, :, None]
    index_z = mirror_map[2][None, None, :]
    return (index_x * grid_side * grid_side + index_y * grid_side + index_z).reshape(-1)


def bubble(gr_re, gr_im, mirror_re, mirror_im, pair_table, entries):
    entry_ids = jnp.arange(entries, dtype=jnp.int32)
    pick_left = (pair_table[:, 0][:, None] == entry_ids[None, :]).astype(jnp.float32)
    pick_right = (pair_table[:, 1][:, None] == entry_ids[None, :]).astype(jnp.float32)
    left_re = jnp.einsum("me,e...->m...", pick_left, gr_re, precision=lax.Precision.HIGHEST)
    left_im = jnp.einsum("me,e...->m...", pick_left, gr_im, precision=lax.Precision.HIGHEST)
    right_re = jnp.einsum("me,e...->m...", pick_right, mirror_re, precision=lax.Precision.HIGHEST)
    right_im = jnp.einsum("me,e...->m...", pick_right, mirror_im, precision=lax.Precision.HIGHEST)
    return (left_re * right_re - left_im * right_im, left_re * right_im + left_im * right_re)


def general(green_momentum_grid, pair_table, mirror_map):
    grid_side = mirror_map.shape[1]
    entries = green_momentum_grid.shape[1]
    frequency_count = green_momentum_grid.shape[3]
    position = jnp.arange(frequency_count, dtype=jnp.int32)
    fwd_cos, fwd_sin = forward_imaginary_time(position, frequency_count)
    tau_re, tau_im = complex_combine(
        "qa,fsa->fqs", fwd_cos, fwd_sin, green_momentum_grid[0], green_momentum_grid[1]
    )
    stacked = jnp.stack([tau_re, tau_im])

    def to_real_space(pieces):
        space_re, space_im = grid_transform(pieces[0], pieces[1], grid_side, 1.0)
        return jnp.stack([space_re, space_im])

    mirror_flat = mirror_index(mirror_map, grid_side)
    partner_rows = frequency_count - 1 - position
    reflected_cosine, reflected_sine = forward_imaginary_time(partner_rows, frequency_count)
    partner_real, partner_imaginary = complex_combine(
        "qa,fsa->fqs",
        reflected_cosine,
        reflected_sine,
        green_momentum_grid[0],
        green_momentum_grid[1],
    )
    other_stacked = jnp.stack([partner_real, partner_imaginary])
    pieces = (
        lax.all_to_all(stacked, "kb", split_axis=2, concat_axis=3, tiled=True),
        lax.all_to_all(other_stacked, "kb", split_axis=2, concat_axis=3, tiled=True),
    )
    in_cells = to_real_space(pieces[0])
    partner = to_real_space(pieces[1])
    mirrored = jnp.take(partner, mirror_flat, axis=3)
    chi_re, chi_im = bubble(in_cells[0], in_cells[1], mirrored[0], mirrored[1], pair_table, entries)
    chi_re, chi_im = grid_transform(chi_re, chi_im, grid_side, -1.0)
    momenta = jnp.stack([chi_re, chi_im])
    back_cos, back_sin = tau_backward(position, frequency_count)
    pieces = lax.all_to_all(momenta, "kb", split_axis=3, concat_axis=2, tiled=True)
    out_re, out_im = complex_combine("vj,ejk->ekv", back_cos, back_sin, pieces[0], pieces[1])
    return jnp.stack([out_re, out_im])


def local(green, pair_table, mirror_map):
    side = mirror_map.shape[1]
    plane = side * side
    lanes, count = green.shape[2], green.shape[3]
    devices = side * plane // lanes
    near = devices // 2
    half = ROWS // 2
    shared = near * ROWS
    if lanes != LANES or 2 * lanes != plane or 2 * (shared + devices * half) != count:
        return general(green, pair_table, mirror_map)
    me = lax.axis_index("kb").astype(jnp.int32).reshape(1)
    entries = green.shape[1]

    rows = np.arange(shared)
    both_fermion = fermion_matrix(rows, count).astype(np.float32)
    both_boson = boson_matrix(rows, count).reshape(2, near, ROWS, count).astype(np.float32)
    rows = shared + np.arange(devices * half).reshape(devices, half)
    times = np.concatenate([rows, count - 1 - rows], axis=1).reshape(-1)
    one_fermion = fermion_matrix(times, count).astype(np.float32)
    one_boson = boson_matrix(rows.reshape(-1), count).reshape(2, devices, half, count).swapaxes(0, 1)
    one_boson = one_boson.reshape(devices * ROWS, count).astype(np.float32)

    shape = (near, 2, 2, entries, ROWS, lanes)
    both = to_times(both_times_kernel, green, jnp.asarray(both_fermion), shape, devices, "both_times")
    green, both = lax.optimization_barrier((green, both))
    shape = (devices, 2, entries, ROWS, lanes)
    one = to_times(one_times_kernel, green, jnp.asarray(one_fermion), shape, devices, "one_times")
    both, one = lax.optimization_barrier((exchange(both), one))
    pieces = both_middle(both, pair_table, mirror_map, me, near)
    first, count = near // 2, near // 4
    early = list(range(first, first + count)) + [1]
    beside = [first + count, first + count + 1, 2, 3]
    late = [slot for slot in range(1, near) if slot not in early + beside]
    moved = {0: pieces[0]}

    one, arrived = lax.optimization_barrier((exchange(one), [swap(pieces[slot], slot, devices) for slot in early]))
    moved |= zip(early, arrived)
    arrived = [swap(pieces[slot], slot, devices) for slot in beside]
    one, arrived, both_boson, one_boson = lax.optimization_barrier(
        (one_middle(one, pair_table, mirror_map), arrived, jnp.asarray(both_boson), jnp.asarray(one_boson))
    )
    moved |= zip(beside, arrived)
    matrix, sent = lax.optimization_barrier((prepare(me, both_boson, one_boson), [pieces[slot] for slot in late]))
    moved |= zip(late, [swap(piece, slot, devices) for slot, piece in zip(late, sent)])
    order = [0] + early + beside + late
    return to_frequencies(exchange(one), matrix, fold([moved[slot] for slot in order], order))


def solution(mesh):
    placed = (P("set", None, "kb", None), P(), P("set", None))
    return jax.shard_map(
        local, mesh=mesh, in_specs=placed, out_specs=P("set", None, "kb", None), check_vma=False
    )
```

```python
import functools
import math

import jax
import jax.numpy as jnp
import ml_dtypes
import numpy as np
from jax import lax
from jax.experimental import pallas as pl
from jax.experimental.pallas import tpu as pltpu
from jax.sharding import PartitionSpec as P

LANES = 128
ROWS = 8
GROUPS = 2


def split_constant(matrix):
    high = matrix.astype(np.float32).astype(ml_dtypes.bfloat16)
    low = (matrix - high.astype(np.float64)).astype(np.float32).astype(ml_dtypes.bfloat16)
    return high, low


def split_value(value):
    high = value.astype(jnp.bfloat16)
    low = (value - high.astype(jnp.float32)).astype(jnp.bfloat16)
    return high, low


def dot3(left, right, dims):
    (k_left,), (k_right,) = dims
    a = jnp.concatenate([left[0], left[0], left[1]], axis=k_left)
    b = jnp.concatenate([right[0], right[1], right[0]], axis=k_right)
    return lax.dot_general(a, b, (dims, ((), ())), preferred_element_type=jnp.float32)


def fermion_matrix(rows, count):
    n = np.arange(count, dtype=np.int64)
    angle = ((2 * n[None, :] - count + 1) * (2 * rows[:, None] + 1)) % (4 * count)
    angle = np.pi * angle / (2 * count)
    return np.concatenate([np.cos(angle), np.sin(angle)], axis=0) * count**-0.5


def boson_matrix(rows, count):
    v = np.arange(count, dtype=np.int64)
    angle = ((v[None, :] - count // 2) * (2 * rows[:, None] + 1)) % (2 * count)
    angle = np.pi * angle / count
    return np.concatenate([np.cos(angle), np.sin(angle)], axis=0) * count**-0.5


def plane_parts(side):
    p = np.arange(side * side, dtype=np.int64)
    angle = ((p[:, None] // side) * (p[None, :] // side) + (p[:, None] % side) * (p[None, :] % side)) % side
    angle = 2 * np.pi * angle / side
    scale = side**-1.5
    return np.cos(angle) * scale, np.sin(angle) * scale


def times_w4(re, im, power, sign):
    power = (power * sign) % 4
    if power == 0:
        return re, im
    if power == 1:
        return -im, re
    if power == 2:
        return -re, -im
    return im, -re


def dft4(values, sign):
    (r0, i0), (r1, i1), (r2, i2), (r3, i3) = values
    sr, si, dr, di = r0 + r2, i0 + i2, r0 - r2, i0 - i2
    tr, ti, er, ei = r1 + r3, i1 + i3, r1 - r3, i1 - i3
    if sign > 0:
        return [(sr + tr, si + ti), (dr - ei, di + er), (sr - tr, si - ti), (dr + ei, di - er)]
    return [(sr + tr, si + ti), (dr + ei, di - er), (sr - tr, si - ti), (dr - ei, di + er)]


def twiddle(value, power, sign, side):
    re, im = value
    if power % (side // 4) == 0:
        return times_w4(re, im, power // (side // 4), sign)
    angle = 2.0 * np.pi * power / side
    c, s = float(np.cos(angle)), float(sign * np.sin(angle))
    return re * c - im * s, re * s + im * c


def dft_line(values, sign):
    side = len(values)
    if side == 1:
        return values
    if side == 2:
        (r0, i0), (r1, i1) = values
        return [(r0 + r1, i0 + i1), (r0 - r1, i0 - i1)]
    if side == 4:
        return dft4(values, sign)
    inner = side // 4
    parts = [dft_line(values[b::4], sign) for b in range(4)]
    out = [None] * side
    for k1 in range(inner):
        column = [twiddle(parts[b][k1], b * k1, sign, side) for b in range(4)]
        for k2, value in enumerate(dft4(column, sign)):
            out[k1 + inner * k2] = value
    return out


def half_line(values, sign, parity):
    side = len(values)
    inner = side // 4
    parts = [dft_line(values[b::4], sign) for b in range(4)]
    out = [None] * (side // 2)
    for k1 in range(inner):
        column = [twiddle(parts[b][k1], b * k1, sign, side) for b in range(4)]
        column = [(re * parity, im * parity) if b % 2 else (re, im) for b, (re, im) in enumerate(column)]
        for k2, value in enumerate(dft4(column, sign)[:2]):
            out[k1 + inner * k2] = value
    return out


def load_inputs(g_hbm, m_hbm, g_ref, m_ref, in_sems, m_sem):
    load = pltpu.make_async_copy(m_hbm, m_ref, m_sem)
    pieces = [
        pltpu.make_async_copy(g_hbm.at[:, pl.ds(e, 1)], g_ref.at[:, pl.ds(e, 1)], in_sems.at[e])
        for e in range(g_ref.shape[1])
    ]
    for copy in [load] + pieces:
        copy.start()
    load.wait()
    return pieces


def sums_of(matrix, g_ref, e):
    lanes = g_ref.shape[2]
    g = jnp.concatenate([g_ref[0, e], g_ref[1, e]], axis=0)
    d = dot3(matrix, split_value(g), ((1,), (1,)))
    half = d.shape[0] // 2
    return d[:half, :lanes], d[:half, lanes:], d[half:, :lanes], d[half:, lanes:]


def both_times_kernel(g_hbm, m_hbm, out_ref, g_ref, m_ref, stage, in_sems, m_sem, out_sems):
    entries, lanes = g_ref.shape[1:3]
    near, _, _, _, rows, _ = stage.shape
    pieces = load_inputs(g_hbm, m_hbm, g_ref, m_ref, in_sems, m_sem)
    matrix = split_value(m_ref[...])
    copies = []
    for e in range(entries):
        pieces[e].wait()
        c_re, c_im, s_re, s_im = sums_of(matrix, g_ref, e)
        for where, value in (
            ((0, 0), c_re + s_im),
            ((0, 1), c_im - s_re),
            ((1, 0), s_im - c_re),
            ((1, 1), -(c_im + s_re)),
        ):
            stage[:, where[0], where[1], e] = value.reshape(near, rows, lanes)
        cut = pl.ds(e, 1)
        for side in range(2):
            target = out_ref.at[pl.ds(side * near, near), :, :, cut]
            copies.append(pltpu.make_async_copy(stage.at[:, :, :, cut], target, out_sems.at[e, side]))
            copies[-1].start()
    for copy in copies:
        copy.wait()


def one_times_kernel(g_hbm, m_hbm, out_ref, g_ref, m_ref, stage, in_sems, m_sem, out_sems):
    entries, lanes = g_ref.shape[1:3]
    devices, _, _, rows, _ = stage.shape
    pieces = load_inputs(g_hbm, m_hbm, g_ref, m_ref, in_sems, m_sem)
    matrix = split_value(m_ref[...])
    copies = []
    for e in range(entries):
        pieces[e].wait()
        c_re, c_im, s_re, s_im = sums_of(matrix, g_ref, e)
        stage[:, 0, e] = (c_re + s_im).reshape(devices, rows, lanes)
        stage[:, 1, e] = (c_im - s_re).reshape(devices, rows, lanes)
        cut = pl.ds(e, 1)
        copies.append(pltpu.make_async_copy(stage.at[:, :, cut], out_ref.at[:, :, cut], out_sems.at[e, 0]))
        copies[-1].start()
    for copy in copies:
        copy.wait()


def to_times(kernel, green, matrix, shape, targets, name):
    entries = green.shape[1]
    hbm = pl.BlockSpec(memory_space=pltpu.HBM)
    return pl.pallas_call(
        kernel,
        in_specs=[hbm, hbm],
        out_specs=hbm,
        out_shape=jax.ShapeDtypeStruct((targets,) + shape[1:], jnp.float32),
        scratch_shapes=[
            pltpu.VMEM(green.shape, jnp.float32),
            pltpu.VMEM(matrix.shape, jnp.float32),
            pltpu.VMEM(shape, jnp.float32),
            pltpu.SemaphoreType.DMA((entries,)),
            pltpu.SemaphoreType.DMA,
            pltpu.SemaphoreType.DMA((entries, 2)),
        ],
        compiler_params=pltpu.CompilerParams(vmem_limit_bytes=63 << 20),
        name=name,
    )(green, matrix)


def fill_block(ref, cosine, sine):
    plane = cosine.shape[0]
    lanes = plane // 2
    for block in range(2):
        cut = slice(block * lanes, (block + 1) * lanes)
        re = slice(2 * block * lanes, (2 * block + 1) * lanes)
        im = slice((2 * block + 1) * lanes, (2 * block + 2) * lanes)
        ref[:plane, re] = cosine[:, cut].astype(jnp.bfloat16)
        ref[plane:, im] = cosine[:, cut].astype(jnp.bfloat16)
        ref[:plane, im] = sine[:, cut].astype(jnp.bfloat16)
        ref[plane:, re] = (-sine[:, cut]).astype(jnp.bfloat16)


def fill_matrices(mirror_ref, parts, forward, backward, turned):
    plane = parts[0].shape[0]
    side = mirror_ref.shape[1]
    row = lax.broadcasted_iota(jnp.int32, (plane, plane), 0)
    column = lax.broadcasted_iota(jnp.int32, (plane, plane), 1)
    upper = (mirror_ref[1, 0] - column // side) & (side - 1)
    lower = (mirror_ref[2, 0] - column % side) & (side - 1)
    pick = (row == upper * side + lower).astype(jnp.float32).astype(jnp.bfloat16)

    def dot(a, b):
        return jnp.dot(a, b, preferred_element_type=jnp.float32)

    for part in range(2):
        c_ref, s_ref = parts[part], parts[2 + part]
        cosine, sine = c_ref[...].astype(jnp.float32), s_ref[...].astype(jnp.float32)
        fill_block(forward.at[0, part], cosine, sine)
        fill_block(backward.at[0, part], turned(cosine), turned(-sine))
        fill_block(forward.at[1, part], dot(c_ref[...], pick), dot(s_ref[...], pick))
        fill_block(backward.at[1, part], turned(dot(pick, c_ref[...])), turned(-dot(pick, s_ref[...])))


def plane_dot(value, matrix, half, block):
    width = matrix.shape[3] // 2
    cut = slice(block * width, (block + 1) * width)
    return dot3(value, (matrix[half, 0, :, cut], matrix[half, 1, :, cut]), ((1,), (0,)))


def one_middle_kernel(table_ref, mirror_ref, ch_ref, cl_ref, sh_ref, sl_ref, x_ref, out_ref, *refs):
    forward, backward, mid, space, other_space, chi, stage, sems = refs
    _, side, _, entries, rows, lanes = space.shape
    plane = 2 * lanes
    groups, _, _, members, _, _ = chi.shape
    fill_matrices(mirror_ref, (ch_ref, cl_ref, sh_ref, sl_ref), forward, backward, lambda value: value)

    def paired(first, second):
        upper = lax.broadcasted_iota(jnp.int32, first.shape, 1) < rows // 2
        turned = [pltpu.roll(part, rows // 2, 1) for part in (first, second)]
        return jnp.where(upper, first, turned[1]), jnp.where(upper, turned[0], second)

    def halves_of(columns):
        value = jnp.concatenate(columns, axis=1)
        count, width = value.shape
        value = value.reshape(count // (2 * rows), 2, rows, width)
        parts = paired(value[:, 0], value[:, 1])
        return [split_value(part.reshape(count // 2, width)) for part in parts]

    def halves_dot(parts, matrix, block):
        shape = (parts[0][0].shape[0] // rows, rows, plane)
        d = paired(*(plane_dot(parts[half], matrix, half, block).reshape(shape) for half in range(2)))
        return jnp.concatenate([part.reshape(shape[0], 1, rows, plane) for part in d], axis=1)

    parts = halves_of([x_ref[:, h, ri].reshape(side * entries * rows, lanes) for ri in range(2) for h in range(2)])
    for block in range(2):
        d = halves_dot(parts, forward, block)
        for ri in range(2):
            piece = d[:, :, :, ri * lanes : (ri + 1) * lanes]
            mid[block, ri] = piece.reshape(side, entries, rows, lanes)
    for block in range(2):
        for e in range(entries):
            values = [(mid[block, 0, x, e], mid[block, 1, x, e]) for x in range(side)]
            for x, parts in enumerate(dft_line(values, 1)):
                for ri in range(2):
                    space[block, x, ri, e] = parts[ri]
                    other_space[block, x, ri, e] = pltpu.roll(parts[ri], rows // 2, 0)

    copies = []
    for group in range(groups):
        for c in range(members):
            left, right = table_ref[0, group * members + c], table_ref[1, group * members + c]
            for block in range(2):
                values = []
                for x in range(side):
                    other = mirror_ref[0, x]
                    a_re, a_im = space[block, x, 0, left], space[block, x, 1, left]
                    b_re, b_im = other_space[block, other, 0, right], other_space[block, other, 1, right]
                    values.append((a_re * b_re - a_im * b_im, a_re * b_im + a_im * b_re))
                cut = slice(block * lanes, (block + 1) * lanes)
                for x, parts in enumerate(dft_line(values, -1)):
                    for ri in range(2):
                        chi[group, ri, x, c, :, cut] = parts[ri]
        whole = (side * members * rows, plane)
        parts = halves_of([chi[group, ri].reshape(whole) for ri in range(2)])
        for h in range(2):
            d = halves_dot(parts, backward, h)
            for ri in range(2):
                piece = d[:, :, :, ri * lanes : (ri + 1) * lanes].reshape(side, members, rows, lanes)
                stage[group, :, h, ri] = piece
        target = out_ref.at[:, :, :, pl.ds(group * members, members)]
        copies.append(pltpu.make_async_copy(stage.at[group], target, sems.at[group]))
        copies[-1].start()
    for copy in copies:
        copy.wait()


def both_middle_kernel(me_ref, table_ref, mirror_ref, ch_ref, cl_ref, sh_ref, sl_ref, x_ref, *refs):
    outs, (forward, backward, mid, space, chi) = refs[:-5], refs[-5:]
    halves, _, side, _, entries, rows, lanes = space.shape
    plane = 2 * lanes
    units, _, kept, members, _, _ = chi.shape
    me, near = me_ref[0], len(outs)
    core, line = me % 2, me // 2 % kept
    parity = (1 - 2 * (me // near)).astype(jnp.float32)

    def turned(value):
        return jnp.where(core == 0, value, jnp.concatenate([value[:, lanes:], value[:, :lanes]], axis=1))

    fill_matrices(mirror_ref, (ch_ref, cl_ref, sh_ref, sl_ref), forward, backward, turned)

    def arrive(half):
        columns = [
            x_ref[:, h, half, ri].reshape(side * entries * rows, lanes) for ri in range(2) for h in range(2)
        ]
        return split_value(jnp.concatenate(columns, axis=1))

    def to_plane(value, half, block):
        d = plane_dot(value, forward, half, block)
        for ri in range(2):
            piece = d[:, ri * lanes : (ri + 1) * lanes]
            mid[half, block, ri] = piece.reshape(side, entries, rows, lanes)

    def along_line(half, block, e):
        values = [(mid[half, block, 0, x, e], mid[half, block, 1, x, e]) for x in range(side)]
        for x, (re, im) in enumerate(dft_line(values, 1)):
            space[half, block, x, 0, e] = re
            space[half, block, x, 1, e] = im

    def product(unit, block, c):
        half, first = unit % halves, unit // halves * members
        left, right = table_ref[0, first + c], table_ref[1, first + c]
        values = []
        for x in range(side):
            other = mirror_ref[0, x]
            a_re, a_im = space[half, block, x, 0, left], space[half, block, x, 1, left]
            b_re, b_im = space[1 - half, block, other, 0, right], space[1 - half, block, other, 1, right]
            values.append((a_re * b_re - a_im * b_im, a_re * b_im + a_im * b_re))
        cut = slice(block * lanes, (block + 1) * lanes)
        for x, (re, im) in enumerate(half_line(values, -1, parity)):
            chi[unit, 0, x ^ line, c, :, cut] = re
            chi[unit, 1, x ^ line, c, :, cut] = im

    def from_plane(unit, value, h):
        half, first = unit % halves, unit // halves * members
        d = plane_dot(value, backward, half, h)
        for ri in range(2):
            piece = d[:, ri * lanes : (ri + 1) * lanes].reshape(kept, members, rows, lanes)
            for x in range(kept):
                outs[2 * x + h][half, ri, first : first + members] = piece[x]

    def collect(unit):
        whole = (kept * members * rows, plane)
        return split_value(jnp.concatenate([chi[unit, ri].reshape(whole) for ri in range(2)], axis=1))

    places = [(half, block) for half in range(halves) for block in range(2)]
    for step in range(len(places) + 1):
        if step < len(places):
            half, block = places[step]
            if block == 0:
                value = arrive(half)
            to_plane(value, half, block)
        if step > 0:
            for e in range(entries):
                along_line(*places[step - 1], e)

    for unit in range(units + 1):
        tasks = [(block, c) for block in range(2) for c in range(members)] if unit < units else []
        if unit > 0:
            value = collect(unit - 1)
        for h in range(2):
            if unit > 0:
                from_plane(unit - 1, value, h)
            for block, c in tasks[h * members : (h + 1) * members]:
                product(unit, block, c)


def middle_inputs(table, mirror_map, x):
    side, plane = x.shape[0] // 2, 2 * x.shape[-1]
    cosine, sine = plane_parts(side)
    parts = [jnp.asarray(part) for part in split_constant(cosine) + split_constant(sine)]
    smem = pl.BlockSpec(memory_space=pltpu.SMEM)
    vmem = pl.BlockSpec(memory_space=pltpu.VMEM)
    args = (table.T, mirror_map, *parts, x.reshape((side, 2) + x.shape[1:]))
    return args, [smem, smem] + [vmem] * 5, pltpu.VMEM((2, 2, 2 * plane, 2 * plane), jnp.bfloat16)


def one_middle(x, table, mirror_map):
    devices, _, entries, rows, lanes = x.shape
    side, components = devices // 2, table.shape[0]
    args, specs, matrices = middle_inputs(table, mirror_map, x)
    spatial = pltpu.VMEM((2, side, 2, entries, rows, lanes), jnp.float32)
    shape = (side, 2, 2, components, rows, lanes)
    out = pl.pallas_call(
        one_middle_kernel,
        in_specs=specs,
        out_specs=pl.BlockSpec(memory_space=pltpu.HBM),
        out_shape=jax.ShapeDtypeStruct(shape, jnp.float32),
        scratch_shapes=[
            matrices,
            matrices,
            pltpu.VMEM((2, 2, side, entries, rows, lanes), jnp.float32),
            spatial,
            spatial,
            pltpu.VMEM((GROUPS, 2, side, components // GROUPS, rows, 2 * lanes), jnp.float32),
            pltpu.VMEM((GROUPS, side, 2, 2, components // GROUPS, rows, lanes), jnp.float32),
            pltpu.SemaphoreType.DMA((GROUPS,)),
        ],
        compiler_params=pltpu.CompilerParams(vmem_limit_bytes=44 << 20),
        cost_estimate=pl.CostEstimate(flops=6_000_000_000, bytes_accessed=12_000_000, transcendentals=0),
        name="one_middle",
    )(*args)
    return out.reshape((devices,) + shape[2:])


def both_middle(x, table, mirror_map, me, near):
    devices, halves, _, entries, rows, lanes = x.shape
    side, components = devices // 2, table.shape[0]
    args, specs, matrices = middle_inputs(table, mirror_map, x)
    members = components // GROUPS
    return pl.pallas_call(
        both_middle_kernel,
        in_specs=[pl.BlockSpec(memory_space=pltpu.SMEM)] + specs,
        out_specs=[pl.BlockSpec(memory_space=pltpu.VMEM)] * near,
        out_shape=[jax.ShapeDtypeStruct((halves, 2, components, rows, lanes), jnp.float32)] * near,
        scratch_shapes=[
            matrices,
            matrices,
            pltpu.VMEM((halves, 2, 2, side, entries, rows, lanes), jnp.float32),
            pltpu.VMEM((halves, 2, side, 2, entries, rows, lanes), jnp.float32),
            pltpu.VMEM((halves * GROUPS, 2, near // 2, members, rows, 2 * lanes), jnp.float32),
        ],
        compiler_params=pltpu.CompilerParams(vmem_limit_bytes=60 << 20),
        name="both_middle",
    )(me, *args)


def prepare_kernel(me_ref, both_ref, one_ref, out_ref):
    near = both_ref.shape[1]
    me = me_ref[0] % near
    ordered = [both_ref[part, slot ^ me] for part in range(2) for slot in range(near)]
    for part, value in enumerate(split_value(jnp.concatenate([one_ref[...]] + ordered, axis=0))):
        out_ref[part] = value


def prepare(me, both, one):
    smem = pl.BlockSpec(memory_space=pltpu.SMEM)
    vmem = pl.BlockSpec(memory_space=pltpu.VMEM)
    depth = both.size // both.shape[3] + one.shape[0]
    return pl.pallas_call(
        prepare_kernel,
        in_specs=[smem, vmem, vmem],
        out_specs=vmem,
        out_shape=jax.ShapeDtypeStruct((2, depth, one.shape[1]), jnp.bfloat16),
        compiler_params=pltpu.CompilerParams(vmem_limit_bytes=63 << 20),
        name="prepare",
    )(me, both, one)


def fold_kernel(order, *refs):
    pieces, (out_ref, held, stage, in_sems, sems) = refs[:-5], refs[-5:]
    near, _, _, components, rows, lanes = held.shape
    loads = [pltpu.make_async_copy(piece, held.at[slot], in_sems.at[slot]) for slot, piece in zip(order, pieces)]
    for copy in loads:
        copy.start()
    for copy in loads:
        copy.wait()
    copies = []
    for c in range(components):
        part = [[held[:, half, ri, c].reshape(near * rows, lanes) for ri in range(2)] for half in range(2)]
        sums = [part[0][ri] + part[1][ri] for ri in range(2)]
        differences = [part[0][ri] - part[1][ri] for ri in range(2)]
        first = jnp.concatenate([sums[0], -differences[1]], axis=0).T
        second = jnp.concatenate([sums[1], differences[0]], axis=0).T
        for place, value in enumerate(split_value(jnp.concatenate([first, second], axis=0))):
            stage[c, place] = value
        copies.append(pltpu.make_async_copy(stage.at[c], out_ref.at[c], sems.at[c]))
        copies[-1].start()
    for copy in copies:
        copy.wait()


def fold(pieces, order):
    _, _, components, rows, lanes = pieces[0].shape
    shape = (components, 2, 2 * lanes, 2 * len(pieces) * rows)
    hbm = pl.BlockSpec(memory_space=pltpu.HBM)
    return pl.pallas_call(
        functools.partial(fold_kernel, order),
        in_specs=[hbm] * len(pieces),
        out_specs=hbm,
        out_shape=jax.ShapeDtypeStruct(shape, jnp.bfloat16),
        scratch_shapes=[
            pltpu.VMEM((len(pieces),) + pieces[0].shape, jnp.float32),
            pltpu.VMEM(shape, jnp.bfloat16),
            pltpu.SemaphoreType.DMA((len(pieces),)),
            pltpu.SemaphoreType.DMA((components,)),
        ],
        compiler_params=pltpu.CompilerParams(vmem_limit_bytes=63 << 20),
        name="fold",
    )(*pieces)


def frequency_kernel(y_hbm, m_hbm, f_hbm, out_ref, y_ref, m_ref, f_ref, stage, y_sems, m_sem, f_sems, sems):
    devices, _, components, rows, lanes = y_ref.shape
    groups = sems.shape[0]
    members = components // groups
    depth = devices * rows
    load = pltpu.make_async_copy(m_hbm, m_ref, m_sem)
    spans = [pl.ds(group * members, members) for group in range(groups)]
    loads = [pltpu.make_async_copy(f_hbm.at[span], f_ref.at[span], f_sems.at[k]) for k, span in enumerate(spans)]
    blocks = [
        pltpu.make_async_copy(y_hbm.at[:, :, span], y_ref.at[:, :, span], y_sems.at[k]) for k, span in enumerate(spans)
    ]
    load.start()
    for pair in zip(blocks, loads):
        for copy in pair:
            copy.start()
    upper_rows = lax.broadcasted_iota(jnp.int32, (devices, rows, lanes), 1) < rows // 2

    def one_values(group):
        values = []
        for c in range(group * members, (group + 1) * members):
            folded = []
            for ri in range(2):
                tile = y_ref[:, ri, c]
                turned = pltpu.roll(tile, rows // 2, 1)
                folded.append((tile + turned, turned - tile))
            first = jnp.where(upper_rows, folded[0][0], -folded[1][1])
            second = jnp.where(upper_rows, folded[1][0], folded[0][1])
            values.append(first.reshape(depth, lanes).T)
            values.append(second.reshape(depth, lanes).T)
        return split_value(jnp.concatenate(values, axis=0))

    copies = []
    for group, span in enumerate(spans):
        blocks[group].wait()
        parts = one_values(group)
        if group == 0:
            load.wait()
            matrix = (m_ref[0], m_ref[1])
        loads[group].wait()
        own = range(group * members, (group + 1) * members)
        value = [
            jnp.concatenate([parts[place], jnp.concatenate([f_ref[c, place] for c in own], axis=0)], axis=1)
            for place in range(2)
        ]
        d = dot3(value, matrix, ((1,), (0,))).reshape(members, 2, lanes, stage.shape[3])
        for ri in range(2):
            stage[ri, group * members : (group + 1) * members] = d[:, ri]
        copies.append(pltpu.make_async_copy(stage.at[:, span], out_ref.at[:, span], sems.at[group]))
        copies[-1].start()
    for copy in copies:
        copy.wait()


def to_frequencies(y, matrix, folded):
    _, _, components, _, lanes = y.shape
    shape = (2, components, lanes, matrix.shape[2])
    hbm = pl.BlockSpec(memory_space=pltpu.HBM)
    groups = components // 2
    return pl.pallas_call(
        frequency_kernel,
        in_specs=[hbm, hbm, hbm],
        out_specs=hbm,
        out_shape=jax.ShapeDtypeStruct(shape, jnp.float32),
        scratch_shapes=[
            pltpu.VMEM(y.shape, jnp.float32),
            pltpu.VMEM(matrix.shape, jnp.bfloat16),
            pltpu.VMEM(folded.shape, jnp.bfloat16),
            pltpu.VMEM(shape, jnp.float32),
            pltpu.SemaphoreType.DMA((groups,)),
            pltpu.SemaphoreType.DMA,
            pltpu.SemaphoreType.DMA((groups,)),
            pltpu.SemaphoreType.DMA((groups,)),
        ],
        compiler_params=pltpu.CompilerParams(vmem_limit_bytes=63 << 20),
        name="to_frequencies",
    )(y, matrix, folded)


def exchange(x):
    flat = x.reshape(x.shape[0], -1, x.shape[-1])
    return lax.all_to_all(flat, "kb", split_axis=0, concat_axis=0, tiled=True).reshape(x.shape)


def swap(piece, slot, devices):
    if slot == 0:
        return piece
    return lax.ppermute(piece, "kb", [(device, device ^ slot) for device in range(devices)])


def trig_pair(angle_int, period, scale):
    angle = 2.0 * math.pi / period * angle_int.astype(jnp.float32)
    return (scale * jnp.cos(angle), scale * jnp.sin(angle))


def complex_combine(formula, cosine, sine, real_part, imag_part):
    first_term = jnp.einsum(formula, cosine, real_part + imag_part, precision=lax.Precision.HIGHEST)
    second_term = jnp.einsum(formula, cosine + sine, imag_part, precision=lax.Precision.HIGHEST)
    third_term = jnp.einsum(formula, sine - cosine, real_part, precision=lax.Precision.HIGHEST)
    return (first_term - second_term, first_term + third_term)


def forward_imaginary_time(tau_rows, frequency_count):
    freq_index = jnp.arange(frequency_count, dtype=jnp.int32)
    angle_int = (
        (2 * freq_index[None, :] - frequency_count + 1)
        * (2 * tau_rows[:, None] + 1)
        % (4 * frequency_count)
    )
    cosine, sine = trig_pair(angle_int, 4 * frequency_count, frequency_count ** (-0.5))
    return (cosine, -sine)


def tau_backward(tau_rows, frequency_count):
    freq_index = jnp.arange(frequency_count, dtype=jnp.int32)
    angle_int = (
        (freq_index[:, None] - frequency_count // 2)
        * (2 * tau_rows[None, :] + 1)
        % (2 * frequency_count)
    )
    return trig_pair(angle_int, 2 * frequency_count, frequency_count ** (-0.5))


def grid_transform(real_part, imag_part, grid_side, direction):
    shape = real_part.shape
    plane = jnp.arange(grid_side * grid_side, dtype=jnp.int32)
    upper = plane // grid_side
    lower = plane % grid_side
    plane_int = (upper[:, None] * upper[None, :] + lower[:, None] * lower[None, :]) % grid_side
    plane_cos, plane_sin = trig_pair(plane_int, grid_side, 1.0 / grid_side)
    line = jnp.arange(grid_side, dtype=jnp.int32)
    line_cos, line_sin = trig_pair(
        line[:, None] * line[None, :] % grid_side, grid_side, grid_side ** (-0.5)
    )
    real_part = real_part.reshape(shape[:-1] + (grid_side, grid_side * grid_side))
    imag_part = imag_part.reshape(shape[:-1] + (grid_side, grid_side * grid_side))
    real_part, imag_part = complex_combine(
        "pq,...xq->...xp", plane_cos, direction * plane_sin, real_part, imag_part
    )
    real_part, imag_part = complex_combine(
        "ax,...xp->...ap", line_cos, direction * line_sin, real_part, imag_part
    )
    return (real_part.reshape(shape), imag_part.reshape(shape))


def mirror_index(mirror_map, grid_side):
    index_x = mirror_map[0][:, None, None]
    index_y = mirror_map[1][None, :, None]
    index_z = mirror_map[2][None, None, :]
    return (index_x * grid_side * grid_side + index_y * grid_side + index_z).reshape(-1)


def bubble(gr_re, gr_im, mirror_re, mirror_im, pair_table, entries):
    entry_ids = jnp.arange(entries, dtype=jnp.int32)
    pick_left = (pair_table[:, 0][:, None] == entry_ids[None, :]).astype(jnp.float32)
    pick_right = (pair_table[:, 1][:, None] == entry_ids[None, :]).astype(jnp.float32)
    left_re = jnp.einsum("me,e...->m...", pick_left, gr_re, precision=lax.Precision.HIGHEST)
    left_im = jnp.einsum("me,e...->m...", pick_left, gr_im, precision=lax.Precision.HIGHEST)
    right_re = jnp.einsum("me,e...->m...", pick_right, mirror_re, precision=lax.Precision.HIGHEST)
    right_im = jnp.einsum("me,e...->m...", pick_right, mirror_im, precision=lax.Precision.HIGHEST)
    return (left_re * right_re - left_im * right_im, left_re * right_im + left_im * right_re)


def general(green_momentum_grid, pair_table, mirror_map):
    grid_side = mirror_map.shape[1]
    entries = green_momentum_grid.shape[1]
    frequency_count = green_momentum_grid.shape[3]
    position = jnp.arange(frequency_count, dtype=jnp.int32)
    fwd_cos, fwd_sin = forward_imaginary_time(position, frequency_count)
    tau_re, tau_im = complex_combine(
        "qa,fsa->fqs", fwd_cos, fwd_sin, green_momentum_grid[0], green_momentum_grid[1]
    )
    stacked = jnp.stack([tau_re, tau_im])

    def to_real_space(pieces):
        space_re, space_im = grid_transform(pieces[0], pieces[1], grid_side, 1.0)
        return jnp.stack([space_re, space_im])

    mirror_flat = mirror_index(mirror_map, grid_side)
    partner_rows = frequency_count - 1 - position
    reflected_cosine, reflected_sine = forward_imaginary_time(partner_rows, frequency_count)
    partner_real, partner_imaginary = complex_combine(
        "qa,fsa->fqs",
        reflected_cosine,
        reflected_sine,
        green_momentum_grid[0],
        green_momentum_grid[1],
    )
    other_stacked = jnp.stack([partner_real, partner_imaginary])
    pieces = (
        lax.all_to_all(stacked, "kb", split_axis=2, concat_axis=3, tiled=True),
        lax.all_to_all(other_stacked, "kb", split_axis=2, concat_axis=3, tiled=True),
    )
    in_cells = to_real_space(pieces[0])
    partner = to_real_space(pieces[1])
    mirrored = jnp.take(partner, mirror_flat, axis=3)
    chi_re, chi_im = bubble(in_cells[0], in_cells[1], mirrored[0], mirrored[1], pair_table, entries)
    chi_re, chi_im = grid_transform(chi_re, chi_im, grid_side, -1.0)
    momenta = jnp.stack([chi_re, chi_im])
    back_cos, back_sin = tau_backward(position, frequency_count)
    pieces = lax.all_to_all(momenta, "kb", split_axis=3, concat_axis=2, tiled=True)
    out_re, out_im = complex_combine("vj,ejk->ekv", back_cos, back_sin, pieces[0], pieces[1])
    return jnp.stack([out_re, out_im])


def local(green, pair_table, mirror_map):
    side = mirror_map.shape[1]
    plane = side * side
    lanes, count = green.shape[2], green.shape[3]
    devices = side * plane // lanes
    near = devices // 2
    half = ROWS // 2
    shared = near * ROWS
    if lanes != LANES or 2 * lanes != plane or 2 * (shared + devices * half) != count:
        return general(green, pair_table, mirror_map)
    me = lax.axis_index("kb").astype(jnp.int32).reshape(1)
    entries = green.shape[1]

    rows = np.arange(shared)
    both_fermion = fermion_matrix(rows, count).astype(np.float32)
    both_boson = boson_matrix(rows, count).reshape(2, near, ROWS, count).astype(np.float32)
    rows = shared + np.arange(devices * half).reshape(devices, half)
    times = np.concatenate([rows, count - 1 - rows], axis=1).reshape(-1)
    one_fermion = fermion_matrix(times, count).astype(np.float32)
    one_boson = boson_matrix(rows.reshape(-1), count).reshape(2, devices, half, count).swapaxes(0, 1)
    one_boson = one_boson.reshape(devices * ROWS, count).astype(np.float32)

    shape = (near, 2, 2, entries, ROWS, lanes)
    both = to_times(both_times_kernel, green, jnp.asarray(both_fermion), shape, devices, "both_times")
    green, both = lax.optimization_barrier((green, both))
    shape = (devices, 2, entries, ROWS, lanes)
    one = to_times(one_times_kernel, green, jnp.asarray(one_fermion), shape, devices, "one_times")
    both, one = lax.optimization_barrier((exchange(both), one))
    pieces = both_middle(both, pair_table, mirror_map, me, near)
    first, count = near // 2, near // 4
    early = list(range(first, first + count)) + [1]
    beside = [first + count, first + count + 1, 2, 3]
    late = [slot for slot in range(1, near) if slot not in early + beside]
    moved = {0: pieces[0]}

    one, arrived = lax.optimization_barrier((exchange(one), [swap(pieces[slot], slot, devices) for slot in early]))
    moved |= zip(early, arrived)
    arrived = [swap(pieces[slot], slot, devices) for slot in beside]
    one, arrived, both_boson, one_boson = lax.optimization_barrier(
        (one_middle(one, pair_table, mirror_map), arrived, jnp.asarray(both_boson), jnp.asarray(one_boson))
    )
    moved |= zip(beside, arrived)
    matrix, sent = lax.optimization_barrier((prepare(me, both_boson, one_boson), [pieces[slot] for slot in late]))
    moved |= zip(late, [swap(piece, slot, devices) for slot, piece in zip(late, sent)])
    order = [0] + early + beside + late
    return to_frequencies(exchange(one), matrix, fold([moved[slot] for slot in order], order))


def solution(mesh):
    placed = (P("set", None, "kb", None), P(), P("set", None))
    return jax.shard_map(
        local, mesh=mesh, in_specs=placed, out_specs=P("set", None, "kb", None), check_vma=False
    )
```
